32 devices in a mesh: batch: 8 (over y, x, core), mp: 4 (over z).
Axes of the slice: x: 2, y: 2, z: 4, core: 2. Of those that a mesh axis runs over, the one named last changes fastest.
Arguments:
- tokens: bfloat16 [16384, 768], P(('batch', 'mp')), may hold values from -6 to 6
- cotangent: bfloat16 [16384, 768], P(('batch', 'mp')), may hold values from -6 to 6
- lengths: int32 [8, 6], P('batch'), may hold values from 1 to 1024, 2048 in all within a row
- buckets: int32 [2047], replicated, may hold values from 0 to 31
- w_query: bfloat16 [768, 768], P(None, 'mp'), may hold values from -0.046875 to 0.046875
- w_key: bfloat16 [768, 768], P(None, 'mp'), may hold values from -0.21875 to 0.21875
- w_value: bfloat16 [768, 768], P(None, 'mp'), may hold values from -0.21875 to 0.21875
- w_out: bfloat16 [768, 768], P('mp'), may hold values from -0.625 to 0.625
- w_gate: bfloat16 [768, 2048], P(None, 'mp'), may hold values from -0.21875 to 0.21875
- w_up: bfloat16 [768, 2048], P(None, 'mp'), may hold values from -0.21875 to 0.21875
- w_down: bfloat16 [2048, 768], P('mp'), may hold values from -0.125 to 0.125
- rel_table: float32 [32, 12], P(None, 'mp'), may hold values from -3 to 3
- gain_one: float32 [768], replicated, may hold values from 0.25 to 1.75
- gain_two: float32 [768], replicated, may hold values from 0.25 to 1.75
Outputs:
- layer_out: bfloat16 [16384, 768], P(('batch', 'mp'))
- grad_tokens: bfloat16 [16384, 768], P(('batch', 'mp'))
- grad_w_query: float32 [768, 768], P(None, 'mp')
- grad_w_key: float32 [768, 768], P(None, 'mp')
- grad_w_value: float32 [768, 768], P(None, 'mp')
- grad_w_out: float32 [768, 768], P('mp')
- grad_w_gate: float32 [768, 2048], P(None, 'mp')
- grad_w_up: float32 [768, 2048], P(None, 'mp')
- grad_w_down: float32 [2048, 768], P('mp')
- grad_rel_table: float32 [32, 12], P(None, 'mp')
- grad_gain_one: float32 [768], replicated
- grad_gain_two: float32 [768], replicated
- stat_model: float32 [5, 768], replicated
- stat_heads: float32 [4, 768], P(None, 'mp')
- stat_hidden: float32 [3, 2048], P(None, 'mp')
- stat_ffn_rows: float32 [2, 768], replicated
The draws below stay inside these ranges and needn't reach their ends.
Inputs may be any that keep to these rules, and one draw needn't show every extreme that they name: Each row's entries sum to 2048; the first 5 are the lengths of its sequences in order, the last is the padding at its end; some entry of each row is exactly 1024. `buckets`: entry o holds the bucket of the relative offset o - 1023.
All inputs are finite; a program needn't handle non-finite values.
Results may differ from the reference program's by a relative error of at most 0.02.
Values may be sent and summed in bfloat16 or wider, within the bound.
A program may use at most 384 MiB of HBM per device.

```python
import math
import jax
import jax.numpy as jnp
import numpy as np
from jax import lax

D = 768
H = 12
DK = 64
FF = 2048
NB = 32
LMAX = 1024
NSEQ = 6
ROW = 2048
QB = 512
NROWS = 8
TOKENS = 16384


def plant(values, own_key, least, high):
    longest = values.shape.index(max(values.shape))
    spots = []
    for shift in (0, 1):
        where = [jax.random.randint(jax.random.fold_in(own_key, axis), (), 0, length) for axis, length in enumerate(values.shape)]
        where[longest] = (where[longest] + shift) % values.shape[longest]
        spots.append(tuple(where))
    return values.at[spots[0]].set(least).at[spots[1]].set(high)


def shard_levels(rng, extent, cuts, low, largest):
    def one(position, blocks):
        draws = jax.random.uniform(jax.random.fold_in(jax.random.fold_in(rng, 6), position), (blocks,), jnp.float32, low / len(cuts), largest / len(cuts))
        return jnp.repeat(jnp.exp(draws), extent[position] // blocks).reshape((-1,) + (1,) * (len(extent) - position - 1))

    level = one(*cuts[0])
    for cut in cuts[1:]:
        level = level * one(*cut)
    return level


def length_profile(amount, total, reach, lean):
    loads = [(1 << 20) // math.isqrt(standing ** lean) + 1 for standing in range(2, amount + 1)]
    rest, given = total - reach - (amount - 1), [1] * (amount - 1)
    while rest > 0:
        free = [i for i in range(amount - 1) if given[i] < reach]
        mass, left = sum([loads[i] for i in free]), rest
        for i in free:
            extra = min(reach - given[i], max(1, left * loads[i] // mass), rest)
            given[i] = given[i] + extra
            rest = rest - extra
    return np.array([reach] + given)


def ragged_sizes(key, amount, total, bound, skew):
    if amount == 2:
        one = jax.random.randint(key, (), max(1, total - bound), min(bound, total - 1) + 1)
        return jnp.stack([one, total - one])
    sizes = jnp.asarray(length_profile(amount, total, bound, skew), jnp.int32)
    couples = (amount - 1) // 2
    donor, receiver = sizes[1:1 + 2 * couples:2], sizes[2:2 + 2 * couples:2]
    slack = jnp.minimum(donor - 1, bound - receiver)
    shifted = jax.random.randint(jax.random.fold_in(key, 1), (couples,), 0, 1 << 20) % (slack + 1)
    sizes = sizes.at[1:1 + 2 * couples:2].set(donor - shifted).at[2:2 + 2 * couples:2].set(receiver + shifted)
    return sizes[jax.random.permutation(jax.random.fold_in(key, 2), amount)]


def bell_draw(own_key, shape, deviation, most, shards=(), kind=jnp.bfloat16):
    factor_of = shard_levels(own_key, shape, shards, -0.22, 0.18) if shards else 1.0
    values = jax.random.normal(own_key, shape, jnp.float32) * deviation * factor_of
    return jnp.minimum(jnp.maximum(values, -most), most).astype(kind)


def setup_inputs(seed: int = 0) -> dict:
    arg_keys = jax.random.split(jax.random.key(seed), 15)
    tokens = bell_draw(arg_keys[0], (TOKENS, D), 1.0, 6.0, ((0, 32),))
    cotangent = bell_draw(arg_keys[1], (TOKENS, D), 1.0, 6.0, ((0, 32),))
    lengths = jax.vmap(lambda own: ragged_sizes(own, NSEQ, ROW, LMAX, 2))(jax.random.split(arg_keys[2], NROWS)).reshape((NROWS, NSEQ)).astype(jnp.int32)
    buckets = plant(jax.random.randint(arg_keys[3], (2 * LMAX - 1,), 0, NB), jax.random.fold_in(arg_keys[3], 1), 0, NB - 1).astype(jnp.int32)
    w_query = bell_draw(arg_keys[4], (D, H * DK), (25 * D) ** -0.5, 0.046875, ((1, 4),))
    w_key = bell_draw(arg_keys[5], (D, H * DK), D ** -0.5, 0.21875, ((1, 4),))
    w_value = bell_draw(arg_keys[6], (D, H * DK), D ** -0.5, 0.21875, ((1, 4),))
    w_out = bell_draw(arg_keys[7], (H * DK, D), (H * DK // 8) ** -0.5, 0.625, ((0, 4),))
    w_gate = bell_draw(arg_keys[8], (D, FF), D ** -0.5, 0.21875, ((1, 4),))
    w_up = bell_draw(arg_keys[9], (D, FF), D ** -0.5, 0.21875, ((1, 4),))
    w_down = bell_draw(arg_keys[10], (FF, D), FF ** -0.5, 0.125, ((0, 4),))
    rel_table = bell_draw(arg_keys[11], (NB, H), 0.5, 3.0, ((1, 4),), jnp.float32)
    gain_one = jnp.clip(1.0 + 0.15 * jax.random.normal(arg_keys[12], (D,), jnp.float32), 0.25, 1.75)
    gain_two = jnp.clip(1.0 + 0.15 * jax.random.normal(arg_keys[13], (D,), jnp.float32), 0.25, 1.75)
    return dict(tokens=tokens, cotangent=cotangent, lengths=lengths, buckets=buckets, w_query=w_query, w_key=w_key, w_value=w_value, w_out=w_out, w_gate=w_gate, w_up=w_up, w_down=w_down, rel_table=rel_table, gain_one=gain_one, gain_two=gain_two)


@jax.custom_vjp
def low(v):
    return lax.optimization_barrier(v.astype(jnp.bfloat16)).astype(jnp.float32)

@jax.custom_vjp
def low_back(v):
    return v

def low_keep(v):
    return (low(v), None)

def low_pass(kept, grad):
    return (grad,)

def back_keep(v):
    return (v, None)

def back_low(kept, grad):
    return (low(grad),)
low.defvjp(low_keep, low_pass)
low_back.defvjp(back_keep, back_low)
EPS = 1e-06
NEG = -1000000000.0
TINY = 1e-30
HIGH = lax.Precision.HIGHEST

def low_both(values):
    return low_back(low(values))

def norm_rows(values, gain_vec):
    return values * lax.rsqrt(lax.optimization_barrier(jnp.mean(values * values, axis=-1, keepdims=True)) + EPS) * gain_vec

def segment_ids(lengths_row):
    ends_at = jnp.cumsum(lengths_row)
    places = jnp.arange(ROW, dtype=jnp.int32)
    return lax.optimization_barrier(jnp.sum((places[:, None] >= ends_at[None, :]).astype(jnp.int32), axis=1))

def attend_block(queries, key_rows, value_rows, rel_table, buckets, segments, token_valid, start_row):
    scores = jnp.einsum('hqd,hkd->hqk', queries, key_rows, precision=HIGH)
    row_index = start_row + jnp.arange(QB, dtype=jnp.int32)
    col_index = jnp.arange(ROW, dtype=jnp.int32)
    offsets = jnp.clip(col_index[None, :] - row_index[:, None] + LMAX - 1, 0, 2 * LMAX - 2)
    rel_bias = jnp.transpose(rel_table[buckets[offsets]], (2, 0, 1))
    scores = low_back(scores + rel_bias)
    seg_rows = lax.dynamic_slice_in_dim(segments, start_row, QB)
    allowed = (seg_rows[:, None] == segments[None, :]) & token_valid[None, :] | (row_index[:, None] == col_index[None, :])
    scores = jnp.where(allowed[None], scores, NEG)
    row_max = lax.optimization_barrier(jnp.max(scores, axis=-1, keepdims=True))
    weights = jnp.exp(scores - row_max)
    probs_low = low(weights / lax.optimization_barrier(jnp.sum(weights, axis=-1, keepdims=True)))
    return jnp.einsum('hqk,hkd->hqd', probs_low, value_rows, precision=HIGH)

def split_heads(matrix):
    return jnp.transpose(matrix.reshape(ROW, H, DK), (1, 0, 2))

def layer_row(inputs, w_query, w_key, w_value, w_out, w_gate, w_up, w_down, rel_table, gain_one, gain_two, buckets, segments, token_valid):
    normed_one = low(norm_rows(inputs, gain_one))
    queries = split_heads(low_both(jnp.dot(normed_one, w_query, precision=HIGH)))
    key_rows = split_heads(low_both(jnp.dot(normed_one, w_key, precision=HIGH)))
    value_rows = split_heads(low_both(jnp.dot(normed_one, w_value, precision=HIGH)))
    blocks = jnp.transpose(queries.reshape(H, ROW // QB, QB, DK), (1, 0, 2, 3))
    starts = jnp.arange(ROW // QB, dtype=jnp.int32) * QB
    block_fn = jax.checkpoint(attend_block)

    def one_block(entry):
        return block_fn(entry[0], key_rows, value_rows, rel_table, buckets, segments, token_valid, entry[1])
    block_out = lax.map(one_block, (blocks, starts))
    context = low_both(jnp.transpose(block_out, (0, 2, 1, 3)).reshape(ROW, H * DK))
    attn_out = low_back(jnp.dot(context, w_out, precision=HIGH))
    middle = inputs + attn_out
    normed_two = low(norm_rows(middle, gain_two))
    gate_pre = low_back(jnp.dot(normed_two, w_gate, precision=HIGH))
    up_proj = low_back(jnp.dot(normed_two, w_up, precision=HIGH))
    hidden = low(jax.nn.gelu(gate_pre, approximate=True) * up_proj)
    return middle + jnp.dot(hidden, w_down, precision=HIGH)

def row_mean(matrix):
    return lax.optimization_barrier(jnp.mean(matrix * matrix + TINY, axis=1))

def col_mean(matrix):
    return lax.optimization_barrier(jnp.mean(matrix * matrix + TINY, axis=0))

def reference(tokens, cotangent, lengths, buckets, w_query, w_key, w_value, w_out, w_gate, w_up, w_down, rel_table, gain_one, gain_two):
    params = tuple((member.astype(jnp.float32) for member in (w_query, w_key, w_value, w_out, w_gate, w_up, w_down))) + (rel_table, gain_one, gain_two)
    rows_in = tokens.astype(jnp.float32).reshape(NROWS, ROW, D)
    rows_cot = cotangent.astype(jnp.float32).reshape(NROWS, ROW, D)

    def row_step(totals, entry):
        row_in, row_cot, row_lengths = entry
        segments = segment_ids(row_lengths)
        token_valid = segments < NSEQ - 1

        def forward(inputs, *weights):
            return layer_row(inputs, *weights, buckets, segments, token_valid)
        result, pullback = jax.vjp(forward, row_in, *params)
        gradients = pullback(row_cot)
        totals = tuple((left_side + right_side for left_side, right_side in zip(totals, gradients[1:])))
        return (totals, (result.astype(jnp.bfloat16), gradients[0].astype(jnp.bfloat16)))
    zero_sums = tuple((jnp.zeros_like(member) for member in params))
    totals, (outputs, grad_rows) = lax.scan(row_step, zero_sums, (rows_in, rows_cot, lengths))
    scale = lax.rsqrt(jnp.float32(TOKENS))
    g_query, g_key, g_value, g_out, g_gate, g_up, g_down, g_rel, g_one, g_two = tuple((member * scale for member in totals))
    stat_model = jnp.stack([row_mean(g_query), row_mean(g_key), row_mean(g_value), col_mean(g_out), col_mean(g_down)])
    stat_heads = jnp.stack([col_mean(g_query), col_mean(g_key), col_mean(g_value), row_mean(g_out)])
    stat_hidden = jnp.stack([col_mean(g_gate), col_mean(g_up), row_mean(g_down)])
    stat_ffn_rows = jnp.stack([row_mean(g_gate), row_mean(g_up)])
    return (outputs.reshape(TOKENS, D), grad_rows.reshape(TOKENS, D), g_query, g_key, g_value, g_out, g_gate, g_up, g_down, g_rel, g_one, g_two, stat_model, stat_heads, stat_hidden, stat_ffn_rows)
```

```python
import functools

import jax
import jax.numpy as jnp
from jax import lax
from jax.experimental import pallas as pl
from jax.experimental.pallas import tpu as pltpu
from jax.sharding import PartitionSpec as P

NEG = -1e9
LANES = 128

def strip_sizes(limit, tq):
    reach = -(-limit // LANES)
    nq = tq // LANES
    off = LANES * (reach + nq)
    return reach, off, off + LANES * reach + tq

def bucket_hot(buckets, count, tq):
    limit = (buckets.shape[0] + 1) // 2
    _, off, width = strip_sizes(limit, tq)
    back = lax.rev(buckets, (0,))
    shift = off - (limit - 1)
    left = jnp.broadcast_to(back[:1], (shift,))
    right = jnp.broadcast_to(back[-1:], (width - shift - back.shape[0],))
    kinds = jnp.concatenate([left, back, right])
    return (kinds[:, None] == jnp.arange(count, dtype=jnp.int32)[None, :]).astype(jnp.float32)

def ends_list(lens_ref, rows_dev, count):
    total = jnp.int32(0)
    ends = []
    for r in range(rows_dev):
        for c in range(count):
            total = total + lens_ref[r, c]
            ends.append(total)
    return ends

def segment_of(place, ends, count):
    seg = jnp.zeros_like(place)
    pad = jnp.zeros_like(place)
    for n, end in enumerate(ends):
        past = place >= end
        seg = seg + jnp.where(past, 1, 0)
        if n % count == count - 2:
            pad = pad + jnp.where(past, 1, 0)
        if n % count == count - 1:
            pad = pad - jnp.where(past, 1, 0)
    return jnp.where(pad > 0, place + 4096, seg)

def key_range(first, last, ends, count, low_end, high_end, tk):
    low = jnp.int32(0)
    high = ends[-1]
    for n, end in enumerate(ends):
        is_pad_next = n % count == count - 2
        low = jnp.where(first >= end, jnp.maximum(low, first if is_pad_next else end), low)
    for n in range(len(ends) - 1, -1, -1):
        is_pad = n % count == count - 1
        high = jnp.where(last < ends[n], (last + 1) if is_pad else ends[n], high)
    low = (low // LANES) * LANES
    steps = (high - low + tk - 1) // tk
    low = jnp.minimum(low, high_end - steps * tk)
    return pl.multiple_of(low, LANES), steps

def window(place_ref, own, total, limit):
    first = place_ref[0]
    radius = -(-(limit - 1) // own)
    return jnp.maximum(first - radius * own, 0), jnp.minimum(first + (radius + 1) * own, total)

def build_strip(strip, table_ref, hh, width):
    row = table_ref[0, hh : hh + 1, :]
    strip[hh] = pltpu.roll(jnp.broadcast_to(row, (LANES, width)), 0, 1, stride=1, stride_axis=0)

def fill_segments(kseg, ends, count, total):
    def one(n, _):
        at = pl.multiple_of(n * 256, 256)
        place = at + lax.broadcasted_iota(jnp.int32, (256, LANES), 0)
        kseg[pl.ds(at, 256), :] = segment_of(place, ends, count)
        return 0
    lax.fori_loop(0, total // 256, one, 0)

def tile_lanes(x, n):
    return x if n == 1 else jnp.concatenate([x] * n, axis=1)

def lane_start(ks, q_at, g, reach, off, nq):
    d = (ks - q_at) // LANES + g
    return pl.multiple_of(off - LANES * jnp.clip(d, -reach, reach + nq - 1), LANES)

def fwd_kernel(cfg, lens_ref, place_ref, table_ref, q_ref, k_ref, vt_ref, ctx_ref, lse_ref, strip, kseg):
    tq, tk, limit, rows_dev, count, own, total = cfg
    reach, off, width = strip_sizes(limit, tq)
    nq = tq // LANES
    ends = ends_list(lens_ref, rows_dev, count)
    @pl.when(pl.program_id(0) == 0)
    def _():
        fill_segments(kseg, ends, count, total)
    for hh in range(2):
        build_strip(strip, table_ref, hh, width)
    w_low, w_high = window(place_ref, own, total, limit)
    lane = lax.broadcasted_iota(jnp.int32, (tq, LANES), 1)
    for qt in range(own // tq):
        q_at = place_ref[0] + qt * tq
        q2 = q_ref[qt * tq : (qt + 1) * tq, :]
        halves = [jnp.where((lane < 64) == (hh == 0), q2, jnp.zeros_like(q2)) for hh in range(2)]
        qseg = segment_of(q_at + lax.broadcasted_iota(jnp.int32, (1, tq), 1), ends, count)
        low, steps = key_range(q_at, q_at + tq - 1, ends, count, w_low, w_high, tk)
        def step(c, carry):
            ks = pl.multiple_of(low + c * tk, LANES)
            kc = k_ref[pl.ds(ks, tk), :]
            same = tile_lanes(kseg[pl.ds(ks, tk), :], nq) == qseg
            out = []
            for hh in range(2):
                top, tot, acc = carry[hh]
                s = lax.dot_general(kc, halves[hh], (((1,), (1,)), ((), ())), preferred_element_type=jnp.float32)
                bias = jnp.concatenate([strip[hh, :, pl.ds(lane_start(ks, q_at, g, reach, off, nq), tq)] for g in range(tk // LANES)], axis=0)
                s = jnp.where(same, s + bias, NEG)
                new = jnp.maximum(top, jnp.max(s, axis=0, keepdims=True))
                p = jnp.exp(s - new)
                fade = jnp.exp(top - new)
                tot = tot * fade + jnp.sum(p, axis=0, keepdims=True)
                acc = acc * fade + jnp.dot(vt_ref[hh * 64 : hh * 64 + 64, pl.ds(ks, tk)], p.astype(jnp.bfloat16), preferred_element_type=jnp.float32)
                out.append((new, tot, acc))
            return tuple(out)
        zero = (jnp.full((1, tq), 2 * NEG, jnp.float32), jnp.zeros((1, tq), jnp.float32), jnp.zeros((64, tq), jnp.float32))
        res = lax.fori_loop(0, steps, step, (zero, zero))
        both = jnp.concatenate([res[hh][2] / res[hh][1] for hh in range(2)], axis=0)
        ctx_ref[qt * tq : (qt + 1) * tq, :] = both.T.astype(jnp.bfloat16)
        for hh in range(2):
            lse_ref[0, hh : hh + 1, qt * tq : (qt + 1) * tq] = res[hh][0] + jnp.log(res[hh][1])

def attend(lengths, place, table, q, k, vt, limit, tq=256, tk=256):
    own, inner = q.shape
    total = k.shape[0]
    pairs = inner // LANES
    rows_dev, count = lengths.shape
    width = strip_sizes(limit, tq)[2]
    cfg = (tq, tk, limit, rows_dev, count, own, total)
    smem = pl.BlockSpec(memory_space=pltpu.SMEM)
    return pl.pallas_call(
        functools.partial(fwd_kernel, cfg),
        grid=(pairs,),
        in_specs=[smem, smem,
            pl.BlockSpec((1, 2, width), lambda p: (p, 0, 0)),
            pl.BlockSpec((own, LANES), lambda p: (0, p)),
            pl.BlockSpec((total, LANES), lambda p: (0, p)),
            pl.BlockSpec((LANES, total), lambda p: (p, 0))],
        out_specs=[pl.BlockSpec((own, LANES), lambda p: (0, p)),
                   pl.BlockSpec((1, 2, own), lambda p: (p, 0, 0))],
        out_shape=[jax.ShapeDtypeStruct((own, inner), jnp.bfloat16), jax.ShapeDtypeStruct((pairs, 2, own), jnp.float32)],
        scratch_shapes=[pltpu.VMEM((2, LANES, width), jnp.float32), pltpu.VMEM((total, LANES), jnp.int32)],
        compiler_params=pltpu.CompilerParams(vmem_limit_bytes=56 * 2**20),
        name="attend",
    )(lengths, place, table, q, k, vt)

def bwd_kernel(cfg, lens_ref, place_ref, table_ref, q_ref, k_ref, kt_ref, v_ref, ctx_ref, do_ref, lse_ref,
               dq_ref, dk_ref, dv_ref, diag_ref, strip, dstrip, kseg, dk_acc, dv_acc):
    tq, tk, limit, rows_dev, count, own, total = cfg
    reach, off, width = strip_sizes(limit, tq)
    nq = tq // LANES
    ends = ends_list(lens_ref, rows_dev, count)
    @pl.when(pl.program_id(0) == 0)
    def _():
        fill_segments(kseg, ends, count, total)
    for hh in range(2):
        build_strip(strip, table_ref, hh, width)
    dstrip[...] = jnp.zeros_like(dstrip)
    dk_acc[...] = jnp.zeros_like(dk_acc)
    dv_acc[...] = jnp.zeros_like(dv_acc)
    w_low, w_high = window(place_ref, own, total, limit)
    lane = lax.broadcasted_iota(jnp.int32, (tq, LANES), 1)
    for qt in range(own // tq):
        rows = slice(qt * tq, (qt + 1) * tq)
        q_at = place_ref[0] + qt * tq
        q2 = q_ref[rows, :]
        do2 = do_ref[rows, :]
        prod = (do2.astype(jnp.float32) * ctx_ref[rows, :].astype(jnp.float32)).T
        q_half = [jnp.where((lane < 64) == (hh == 0), q2, jnp.zeros_like(q2)) for hh in range(2)]
        do_half = [jnp.where((lane < 64) == (hh == 0), do2, jnp.zeros_like(do2)) for hh in range(2)]
        delta = [jnp.sum(prod[hh * 64 : hh * 64 + 64], axis=0, keepdims=True) for hh in range(2)]
        lse = [lse_ref[0, hh : hh + 1, rows] for hh in range(2)]
        qseg = segment_of(q_at + lax.broadcasted_iota(jnp.int32, (1, tq), 1), ends, count)
        low, steps = key_range(q_at, q_at + tq - 1, ends, count, w_low, w_high, tk)
        def step(c, carry):
            ks = pl.multiple_of(low + c * tk, LANES)
            kc = k_ref[pl.ds(ks, tk), :]
            vc = v_ref[pl.ds(ks, tk), :]
            same = tile_lanes(kseg[pl.ds(ks, tk), :], nq) == qseg
            out = []
            dk_part = dv_part = None
            for hh in range(2):
                s = lax.dot_general(kc, q_half[hh], (((1,), (1,)), ((), ())), preferred_element_type=jnp.float32)
                starts = [lane_start(ks, q_at, g, reach, off, nq) for g in range(tk // LANES)]
                bias = jnp.concatenate([strip[hh, :, pl.ds(at, tq)] for at in starts], axis=0)
                p = jnp.exp(jnp.where(same, s + (bias - lse[hh]), NEG))
                dp = lax.dot_general(vc, do_half[hh], (((1,), (1,)), ((), ())), preferred_element_type=jnp.float32)
                ds = p * (dp - delta[hh])
                for g, at in enumerate(starts):
                    dstrip[hh, :, pl.ds(at, tq)] += ds[g * LANES : (g + 1) * LANES, :]
                pb = p.astype(jnp.bfloat16)
                dsb = ds.astype(jnp.bfloat16)
                dv_one = jnp.dot(pb, do_half[hh], preferred_element_type=jnp.float32)
                dk_one = jnp.dot(dsb, q_half[hh], preferred_element_type=jnp.float32)
                dv_part = dv_one if dv_part is None else dv_part + dv_one
                dk_part = dk_one if dk_part is None else dk_part + dk_one
                out.append(carry[hh] + jnp.dot(kt_ref[hh * 64 : hh * 64 + 64, pl.ds(ks, tk)], dsb, preferred_element_type=jnp.float32))
            dv_acc[pl.ds(ks, tk), :] += dv_part
            dk_acc[pl.ds(ks, tk), :] += dk_part
            return tuple(out)
        zero = jnp.zeros((64, tq), jnp.float32)
        res = lax.fori_loop(0, steps, step, (zero, zero))
        dq_ref[rows, :] = jnp.concatenate(res, axis=0).T.astype(jnp.bfloat16)
    dk_ref[...] = dk_acc[...].astype(jnp.bfloat16)
    dv_ref[...] = dv_acc[...].astype(jnp.bfloat16)
    for hh in range(2):
        eight = dstrip[hh, 0:8, :]
        for g in range(1, LANES // 8):
            eight = eight + pltpu.roll(dstrip[hh, 8 * g : 8 * g + 8, :], width - 8 * g, 1)
        flat = eight[0:1, :]
        for r in range(1, 8):
            flat = flat + pltpu.roll(eight[r : r + 1, :], width - r, 1)
        diag_ref[0, hh : hh + 1, :] = flat

def attend_back(lengths, place, table, q, k, kt, v, ctx, do, lse, limit, tq=256, tk=256):
    own, inner = q.shape
    total = k.shape[0]
    pairs = inner // LANES
    rows_dev, count = lengths.shape
    width = strip_sizes(limit, tq)[2]
    cfg = (tq, tk, limit, rows_dev, count, own, total)
    smem = pl.BlockSpec(memory_space=pltpu.SMEM)
    tall = pl.BlockSpec((total, LANES), lambda p: (0, p))
    short = pl.BlockSpec((own, LANES), lambda p: (0, p))
    return pl.pallas_call(
        functools.partial(bwd_kernel, cfg),
        grid=(pairs,),
        in_specs=[smem, smem,
            pl.BlockSpec((1, 2, width), lambda p: (p, 0, 0)),
            short, tall, pl.BlockSpec((LANES, total), lambda p: (p, 0)), tall, short, short,
            pl.BlockSpec((1, 2, own), lambda p: (p, 0, 0))],
        out_specs=[short, tall, tall, pl.BlockSpec((1, 2, width), lambda p: (p, 0, 0))],
        out_shape=[jax.ShapeDtypeStruct((own, inner), jnp.bfloat16), jax.ShapeDtypeStruct((total, inner), jnp.bfloat16),
                   jax.ShapeDtypeStruct((total, inner), jnp.bfloat16), jax.ShapeDtypeStruct((pairs, 2, width), jnp.float32)],
        scratch_shapes=[pltpu.VMEM((2, LANES, width), jnp.float32), pltpu.VMEM((2, LANES, width), jnp.float32), pltpu.VMEM((total, LANES), jnp.int32),
                        pltpu.VMEM((total, LANES), jnp.float32), pltpu.VMEM((total, LANES), jnp.float32)],
        compiler_params=pltpu.CompilerParams(vmem_limit_bytes=56 * 2**20),
        name="attend_back",
    )(lengths, place, table, q, k, kt, v, ctx, do, lse)


MESH = pl.DeviceIdType.MESH
GROUP = 8


def flip(index, bit):
    return index + bit * (1 - 2 * ((index // bit) % 2))


class Links:
    def __init__(self, send_sems, recv_sems, batch, place):
        self.send_sems, self.recv_sems = send_sems, recv_sems
        self.batch, self.place = batch, place
        self.slots = {}
        self.sent = []

    def slot(self, key):
        return self.slots.setdefault(key, len(self.slots))

    def copy(self, key, src, dst, target):
        n = self.slot(key)
        return pltpu.make_async_remote_copy(
            src_ref=src, dst_ref=dst, send_sem=self.send_sems.at[n], recv_sem=self.recv_sems.at[n],
            device_id=target, device_id_type=MESH)

    def send(self, key, src, dst, target, when=None):
        def go():
            self.copy(key, src, dst, target).start()
        self.sent.append((key, src, dst, target, when))
        if when is None:
            go()
        else:
            pl.when(when)(go)

    def take(self, key, dst, when=None, then=None):
        def go():
            self.copy(key, dst, dst, (self.batch, self.place)).wait_recv()
            if then is not None:
                then()
        if when is None:
            go()
        else:
            pl.when(when)(go)

    def drain(self):
        for key, src, dst, target, when in self.sent:
            def go():
                self.copy(key, src, dst, target).wait_send()
            if when is None:
                go()
            else:
                pl.when(when)(go)


def greet(batch, place, count):
    bar = pltpu.get_barrier_semaphore()
    for bit in (1, 2, 4):
        pl.semaphore_signal(bar, inc=1, device_id=(flip(batch, bit), place), device_id_type=MESH)
    for way in range(1 - count, count):
        if way != 0:
            @pl.when((place + way >= 0) & (place + way < count))
            def _():
                pl.semaphore_signal(bar, inc=1, device_id=(batch, place + way), device_id_type=MESH)
    pl.semaphore_wait(bar, 3 + count - 1)


def both(a, b):
    return a if b is None else (b if a is None else a & b)


class PlaneGather:
    def __init__(self, links, key, view, ref, sub, when=None):
        self.l, self.key, self.view, self.ref, self.sub, self.when = links, key, view, ref, sub, when

    def put(self, path, sub, half, bit):
        region = self.view(self.ref, sub, half)
        self.l.send((self.key, path), region, region, (flip(self.l.batch, bit), self.l.place), self.when)

    def start(self):
        self.put("x", self.sub, None, 2)
        self.put("y", self.sub, None, 4)
        self.put("c", self.sub, None, 1)

    def middle(self):
        sub = self.sub
        self.l.take((self.key, "x"), self.view(self.ref, flip(sub, 2), None), self.when)
        self.put("xy", flip(sub, 2), 0, 4)
        self.put("xc", flip(sub, 2), None, 1)
        self.l.take((self.key, "y"), self.view(self.ref, flip(sub, 4), None), self.when)
        self.put("yx", flip(sub, 4), 1, 2)
        self.put("yc", flip(sub, 4), None, 1)

    def far(self):
        sub = self.sub
        diagonal = flip(flip(sub, 2), 4)
        self.l.take((self.key, "xy"), self.view(self.ref, diagonal, 0), self.when)
        self.put("0c", diagonal, 0, 1)
        self.l.take((self.key, "yx"), self.view(self.ref, diagonal, 1), self.when)
        self.put("1c", diagonal, 1, 1)

    def end(self):
        sub = flip(self.sub, 1)
        diagonal = flip(flip(sub, 2), 4)
        self.l.take((self.key, "c"), self.view(self.ref, sub, None), self.when)
        self.l.take((self.key, "xc"), self.view(self.ref, flip(sub, 2), None), self.when)
        self.l.take((self.key, "yc"), self.view(self.ref, flip(sub, 4), None), self.when)
        self.l.take((self.key, "0c"), self.view(self.ref, diagonal, 0), self.when)
        self.l.take((self.key, "1c"), self.view(self.ref, diagonal, 1), self.when)


def half_rows(half, rows):
    return pl.ds(0, rows) if half is None else pl.ds(half * (rows // 2), rows // 2)


PIECES = 4


def gather_kernel(count, radius, x_ref, wa_ref, wf_ref, xs_ref, was_ref, wfs_ref, blank, send_sems, recv_sems, local_sems):
    batch, place = lax.axis_index("batch"), lax.axis_index("mp")
    sub = batch % GROUP
    links = Links(send_sems, recv_sems, batch, place)
    own = x_ref.shape[0]
    rows_a = wa_ref.shape[2]
    rows_f = wf_ref.shape[2]
    step = own // PIECES
    local = [
        pltpu.make_async_copy(wa_ref, was_ref.at[:, place], local_sems.at[0]),
        pltpu.make_async_copy(wf_ref, wfs_ref.at[:, place], local_sems.at[1]),
        pltpu.make_async_copy(x_ref, xs_ref.at[place], local_sems.at[2]),
    ]
    for one in local:
        one.start()
    blank[...] = jnp.zeros_like(blank)
    outside = []
    for n in range(count):
        far = (n - place > radius) | (place - n > radius)
        outside.append((far, pltpu.make_async_copy(blank, xs_ref.at[n], local_sems.at[3 + n])))
    for far, one in outside:
        pl.when(far)(one.start)
    greet(batch, place, count)

    def view_a(mm):
        return lambda ref, s, half: ref.at[s // 2, mm, s % 2, half_rows(half, rows_a)]

    def view_f(mm):
        return lambda ref, s, half: ref.at[:, mm, s, half_rows(half, rows_f)]

    def inside(n):
        return (n >= 0) & (n < count)

    for way in (1, -1):
        ok = inside(place + way)
        target = (batch, place + way)
        links.send(("a", way, 1), wa_ref.at[sub // 2, sub % 2], view_a(place)(was_ref, sub, None), target, ok)
        links.send(("f", way, 1), wf_ref.at[:, sub], view_f(place)(wfs_ref, sub, None), target, ok)
    for way in (1, -1):
        ok = inside(place + way)
        target = (batch, place + way)
        for p in range(PIECES):
            rows = pl.ds(p * step, step)
            links.send(("x", way, 1, p), x_ref.at[rows], xs_ref.at[place, rows], target, ok)

    gathers = {}

    def weights_arrive(kind, dist):
        for way in (1, -1):
            source = place - way * dist
            ok = inside(source)
            view, ref = (view_a(source), was_ref) if kind == "a" else (view_f(source), wfs_ref)
            region = view(ref, sub, None)
            links.take((kind, way, dist), region, ok)
            if dist < count - 1:
                links.send((kind, way, dist + 1), region, region, (batch, place + way), ok & inside(place + way))
            gather = PlaneGather(links, ("g", kind, way, dist), view, ref, sub, ok)
            gather.start()
            gathers[kind, way, dist] = gather

    def x_arrive(dist, p):
        for way in (1, -1):
            source = place - way * dist
            ok = inside(source)
            region = xs_ref.at[source, pl.ds(p * step, step)]
            links.take(("x", way, dist, p), region, ok)
            if dist < radius:
                links.send(("x", way, dist + 1, p), region, region, (batch, place + way), ok & inside(place + way))

    def stage(name, kind, dist):
        for way in (1, -1):
            getattr(gathers[kind, way, dist], name)()

    dists = range(1, count)
    for d in dists:
        weights_arrive("a", d)
    weights_arrive("f", 1)
    for d in dists:
        stage("middle", "a", d)
    for p in range(PIECES):
        x_arrive(1, p)
        if p + 2 < count:
            weights_arrive("f", p + 2)
        if p == 1:
            stage("middle", "f", 1)
    for d in dists:
        stage("far", "a", d)
    for d in range(2, count):
        stage("middle", "f", d)
    for d in dists:
        stage("far", "f", d)
    for r in range(2, radius + 1):
        for p in range(PIECES):
            x_arrive(r, p)
    for kind in ("a", "f"):
        for d in dists:
            stage("end", kind, d)
    links.drain()
    for one in local:
        one.wait()
    for far, one in outside:
        pl.when(far)(one.wait)


def gather(x, wa, wf, count, radius):
    own, width = x.shape
    return pl.pallas_call(
        functools.partial(gather_kernel, count, radius),
        in_specs=[pl.BlockSpec(memory_space=pl.ANY)] * 3,
        out_specs=[pl.BlockSpec(memory_space=pl.ANY)] * 3,
        out_shape=[
            jax.ShapeDtypeStruct((count, own, width), x.dtype),
            jax.ShapeDtypeStruct((wa.shape[0], count) + wa.shape[1:], wa.dtype),
            jax.ShapeDtypeStruct((wf.shape[0], count) + wf.shape[1:], wf.dtype),
        ],
        scratch_shapes=[
            pltpu.VMEM((own, width), x.dtype),
            pltpu.SemaphoreType.DMA((160,)),
            pltpu.SemaphoreType.DMA((160,)),
            pltpu.SemaphoreType.DMA((8 + count,)),
        ],
        compiler_params=pltpu.CompilerParams(collective_id=1, has_side_effects=True, vmem_limit_bytes=32 * 2**20),
        name="gather",
    )(x, wa, wf)


def add_blocks(count, target, extra):
    def one(n, _):
        t, e = target(n), extra(n)
        t[...] = t[...] + e[...]
        return 0
    lax.fori_loop(0, count, one, 0)


def reduce_kernel(count, radius, scale, final, gx_ref, ga_ref, gg_ref, gu_ref, gd_ref, small_ref,
                  gn_ref, oa_ref, of_ref, side_ref, total_ref,
                  keep_a, got_a1, got_ax, got_ay, got_ay2, got_ax2, keep_f, got_f1, got_fx, got_fy, got_fy2, got_fx2,
                  from_a, from_f, full_a, full_f, got_x, tiny, tiny_z, side_z, send_sems, recv_sems, local_sems):
    batch, place = lax.axis_index("batch"), lax.axis_index("mp")
    sub = batch % GROUP
    core, xx, yy = sub % 2, (sub // 2) % 2, sub // 4
    links = Links(send_sems, recv_sems, batch, place)
    gf_refs = [gg_ref, gu_ref, gd_ref]
    rows_a, rows_f = keep_a.shape[3], keep_f.shape[4]
    ha, hf = rows_a // 2, rows_f // 2
    own = gn_ref.shape[0]
    step = own // PIECES

    def inside(n):
        return (n >= 0) & (n < count)

    sibling, x_near, y_near = [(flip(batch, bit), place) for bit in (1, 2, 4)]
    local_f = [pltpu.make_async_copy(gf_refs[t].at[:, :, :, core], keep_f.at[t], local_sems.at[t]) for t in range(3)]
    local_a = pltpu.make_async_copy(ga_ref.at[:, :, :, core], keep_a, local_sems.at[3])
    for one in local_f + [local_a]:
        one.start()
    greet(batch, place, count)
    for t in range(3):
        links.send(("f1", t), gf_refs[t].at[:, :, :, 1 - core], got_f1.at[t], sibling)
    links.send(("a1",), ga_ref.at[:, :, :, 1 - core], got_a1, sibling)
    for way in (1, -1):
        for p in range(PIECES):
            rows = pl.ds(p * step, step)
            dest = place + way * radius
            links.send(("x", way, radius, p), gx_ref.at[jnp.clip(dest, 0, count - 1), rows],
                       got_x.at[0 if way > 0 else 1, radius - 1, rows], (batch, place + way), inside(dest))
    links.send(("s", 0), small_ref, tiny.at[1], sibling)

    def start_a(t):
        if t == "a":
            links.send(("ax",), keep_a.at[:, 1 - xx, :, pl.ds(0, ha)], got_ax, x_near)
            links.send(("ay",), keep_a.at[1 - yy, :, :, pl.ds(ha, ha)], got_ay, y_near)
        else:
            links.send(("fx", t), keep_f.at[t, :, :, 1 - xx, pl.ds(0, hf)], got_fx.at[t], x_near)
            links.send(("fy", t), keep_f.at[t, :, 1 - yy, :, pl.ds(hf, hf)], got_fy.at[t], y_near)

    for t in range(3):
        local_f[t].wait()
        links.take(("f1", t), got_f1.at[t])
        def one(n, _):
            for i in range(2):
                for j in range(2):
                    keep_f[t, n, i, j] = keep_f[t, n, i, j] + got_f1[t, n, i, j]
            return 0
        lax.fori_loop(0, count, one, 0)
        start_a(t)
    local_a.wait()
    links.take(("a1",), got_a1)
    def one_a(n, _):
        for i in range(2):
            for j in range(2):
                keep_a[i, j, n] = keep_a[i, j, n] + got_a1[i, j, n]
        return 0
    lax.fori_loop(0, count, one_a, 0)
    start_a("a")

    def tiny_step(n):
        links.take(("s", n), tiny.at[2 * n + 1])
        before = small_ref if n == 0 else tiny.at[2 * n]
        tiny[2 * n + 2] = before[...] + tiny[2 * n + 1]
        if n < 2:
            links.send(("s", n + 1), tiny.at[2 * n + 2], tiny.at[2 * n + 3], (flip(batch, 2 << n), place))
        else:
            tiny_z[place] = tiny[6]
            for d in range(1, count):
                for way in (1, -1):
                    links.send(("sz", way, d), tiny.at[6], tiny_z.at[place], (batch, place + way * d), inside(place + way * d))

    tiny_step(0)

    def x_step(level, p):
        rows = pl.ds(p * step, step)
        for side, way in ((0, 1), (1, -1)):
            dest = place + way * (level - 1)
            ok = inside(place - way) & inside(dest)
            def add():
                got_x[side, level - 1, rows] = got_x[side, level - 1, rows] + gx_ref[dest, rows]
            links.take(("x", way, level, p), got_x.at[side, level - 1, rows], ok, add if level > 1 else None)
            if level > 1:
                ok2 = inside(place - way) & inside(dest)
                links.send(("x", way, level - 1, p), got_x.at[side, level - 1, rows], got_x.at[side, level - 2, rows],
                           (batch, place + way), ok2)
                links.send(("x0", way, level - 1, p), gx_ref.at[jnp.clip(dest, 0, count - 1), rows], got_x.at[side, level - 2, rows],
                           (batch, place + way), jnp.logical_not(inside(place - way)) & inside(dest))

    for level in range(radius, 1, -1):
        for p in range(PIECES):
            x_step(level, p)
    tiny_step(1)

    def middle(t):
        if t == "a":
            links.take(("ax",), got_ax)
            links.take(("ay",), got_ay)
            def one(n, _):
                for i in range(2):
                    keep_a[i, xx, n, pl.ds(0, ha)] = keep_a[i, xx, n, pl.ds(0, ha)] + got_ax[i, n]
                    keep_a[yy, i, n, pl.ds(ha, ha)] = keep_a[yy, i, n, pl.ds(ha, ha)] + got_ay[i, n]
                return 0
            lax.fori_loop(0, count, one, 0)
            links.send(("ay2",), keep_a.at[1 - yy, xx, :, pl.ds(0, ha)], got_ay2, y_near)
            links.send(("ax2",), keep_a.at[yy, 1 - xx, :, pl.ds(ha, ha)], got_ax2, x_near)
        else:
            links.take(("fx", t), got_fx.at[t])
            links.take(("fy", t), got_fy.at[t])
            def one(n, _):
                for i in range(2):
                    keep_f[t, n, i, xx, pl.ds(0, hf)] = keep_f[t, n, i, xx, pl.ds(0, hf)] + got_fx[t, n, i]
                    keep_f[t, n, yy, i, pl.ds(hf, hf)] = keep_f[t, n, yy, i, pl.ds(hf, hf)] + got_fy[t, n, i]
                return 0
            lax.fori_loop(0, count, one, 0)
            links.send(("fy2", t), keep_f.at[t, :, 1 - yy, xx, pl.ds(0, hf)], got_fy2.at[t], y_near)
            links.send(("fx2", t), keep_f.at[t, :, yy, 1 - xx, pl.ds(hf, hf)], got_fx2.at[t], x_near)

    def unit(t, n):
        return keep_a.at[yy, xx, n] if t == "a" else keep_f.at[t, n, yy, xx]

    def arrived(t, side, n):
        return from_a.at[side, n] if t == "a" else from_f.at[t, side, n]

    def last(t):
        if t == "a":
            links.take(("ay2",), got_ay2)
            links.take(("ax2",), got_ax2)
            def one(n, _):
                keep_a[yy, xx, n, pl.ds(0, ha)] = keep_a[yy, xx, n, pl.ds(0, ha)] + got_ay2[n]
                keep_a[yy, xx, n, pl.ds(ha, ha)] = keep_a[yy, xx, n, pl.ds(ha, ha)] + got_ax2[n]
                return 0
        else:
            links.take(("fy2", t), got_fy2.at[t])
            links.take(("fx2", t), got_fx2.at[t])
            def one(n, _):
                keep_f[t, n, yy, xx, pl.ds(0, hf)] = keep_f[t, n, yy, xx, pl.ds(0, hf)] + got_fy2[t, n]
                keep_f[t, n, yy, xx, pl.ds(hf, hf)] = keep_f[t, n, yy, xx, pl.ds(hf, hf)] + got_fx2[t, n]
                return 0
        lax.fori_loop(0, count, one, 0)

    def line(t, hop):
        for side, way in ((0, 1), (1, -1)):
            for n in (range(count - 1, 0, -1) if way > 0 else range(count - 1)):
                first = place == (0 if way > 0 else count - 1)
                beyond = (n > place) if way > 0 else (n < place)
                here = place == (hop if way > 0 else count - 1 - hop)
                if hop > 0:
                    def add():
                        ref, more = unit(t, n), arrived(t, side, n)
                        ref[...] = ref[...] + more[...]
                    links.take(("z", t, side, n, hop - 1), arrived(t, side, n), here & beyond, add)
                links.send(("z", t, side, n, hop), unit(t, n), arrived(t, side, n), (batch, place + way), here & beyond)

    def view_a(ref, s, half):
        return ref.at[s // 2, s % 2, half_rows(half, rows_a)]

    def view_f(t):
        return lambda ref, s, half: ref.at[t, s, half_rows(half, rows_f)]

    gathers = {}

    def finish(t):
        for side, way in ((0, 1), (1, -1)):
            for hop in range(count - 1):
                def add():
                    ref, more = unit(t, place), arrived(t, side, place)
                    ref[...] = ref[...] + more[...]
                for n in range(count):
                    here = (place == n) & (place == (hop + 1 if way > 0 else count - 2 - hop))
                    if (n == hop + 1) if way > 0 else (n == count - 2 - hop):
                        links.take(("z", t, side, n, hop), arrived(t, side, n), here, add)
        if t == "a":
            view, ref = view_a, full_a
            full_a[sub // 2, sub % 2] = keep_a[yy, xx, place]
        else:
            view, ref = view_f(t), full_f
            full_f[t, sub] = keep_f[t, place, yy, xx]
        gathers[t] = PlaneGather(links, ("g", t), view, ref, sub)
        gathers[t].start()

    order = [0, 1, 2, "a"]
    for t in order:
        middle(t)
    tiny_step(2)
    for t in order:
        last(t)
        line(t, 0)
    for p in range(PIECES):
        for side, way in ((0, 1), (1, -1)):
            rows = pl.ds(p * step, step)
            ok = inside(place - way)
            near = inside(place - 2 * way)
            if radius > 1:
                links.take(("x", way, 1, p), got_x.at[side, 0, rows], ok & near)
                links.take(("x0", way, 1, p), got_x.at[side, 0, rows], ok & jnp.logical_not(near))
            else:
                links.take(("x", way, 1, p), got_x.at[side, 0, rows], ok)
            def fill():
                got_x[side, 0, rows] = jnp.zeros((step, got_x.shape[3]), got_x.dtype)
            pl.when(jnp.logical_not(ok))(fill)
        rows = pl.ds(p * step, step)
        gn_ref[rows, :] = (gx_ref[place, rows].astype(jnp.float32) + got_x[0, 0, rows].astype(jnp.float32)
                           + got_x[1, 0, rows].astype(jnp.float32))
    for hop in range(1, count - 1):
        for t in order:
            line(t, hop)
    for t in order:
        finish(t)
    for d in range(1, count):
        for way in (1, -1):
            links.take(("sz", way, d), tiny_z.at[place - way * d], inside(place - way * d))
    summed = tiny_z[0]
    for n in range(1, count):
        summed = summed + tiny_z[n]
    total_ref[...] = summed
    for name in ("middle", "far", "end"):
        for t in order:
            getattr(gathers[t], name)()

    def scaled(value):
        return value.astype(jnp.float32) * scale if final else value.astype(jnp.float32)

    sums = []
    for s in range(4):
        acc = jnp.zeros((8, full_a.shape[3]), jnp.float32)
        for j in range(2):
            def one(r, acc):
                rows = pl.ds(pl.multiple_of(r * 32, 32), 32)
                value = scaled(full_a[s, j, rows])
                oa_ref[s, j, rows] = value
                sq = value * value
                return acc + sq[0:8] + sq[8:16] + sq[16:24] + sq[24:32]
            acc = lax.fori_loop(0, rows_a // 32, one, acc)
        sums.append(jnp.sum(acc, axis=0, keepdims=True))
    for t in range(3):
        def one(n, acc):
            for r in range(rows_f // 32):
                rows = pl.ds(r * 32, 32)
                value = scaled(full_f[t, n, rows])
                of_ref[t, n, rows] = value
                sq = value * value
                acc = acc + sq[0:8] + sq[8:16] + sq[16:24] + sq[24:32]
            return acc
        sums.append(jnp.sum(lax.fori_loop(0, GROUP, one, jnp.zeros((8, full_a.shape[3]), jnp.float32)), axis=0, keepdims=True))
    sums.append(jnp.zeros_like(sums[0]))
    side_z[place] = jnp.concatenate(sums, axis=0)
    for d in range(1, count):
        for way in (1, -1):
            links.send(("q", way, d), side_z.at[place], side_z.at[place], (batch, place + way * d), inside(place + way * d))
    for d in range(1, count):
        for way in (1, -1):
            links.take(("q", way, d), side_z.at[place - way * d], inside(place - way * d))
    summed = side_z[0]
    for n in range(1, count):
        summed = summed + side_z[n]
    side_ref[...] = summed
    links.drain()


def reduce(gx, ga, gfs, small, count, radius, scale, final):
    _, own, width = gx.shape
    bf = jnp.bfloat16
    ra, rf = ga.shape[4], gfs[0].shape[4]
    vm = pl.BlockSpec(memory_space=pltpu.VMEM)
    hb = pl.BlockSpec(memory_space=pl.ANY)
    V = lambda *s: pltpu.VMEM(s + (width,), bf)
    S = small.shape[0]
    return pl.pallas_call(
        functools.partial(reduce_kernel, count, radius, scale, final),
        in_specs=[vm, hb, hb, hb, hb, vm],
        out_specs=[vm] * 5,
        out_shape=[
            jax.ShapeDtypeStruct((own, width), jnp.float32),
            jax.ShapeDtypeStruct((4, 2, ra, width), jnp.float32),
            jax.ShapeDtypeStruct((3, GROUP, rf, width), jnp.float32),
            jax.ShapeDtypeStruct((8, width), jnp.float32),
            jax.ShapeDtypeStruct((S, width), jnp.float32),
        ],
        scratch_shapes=[
            V(2, 2, count, ra), V(2, 2, count, ra), V(2, count, ra // 2), V(2, count, ra // 2), V(count, ra // 2), V(count, ra // 2),
            V(3, count, 2, 2, rf), V(3, count, 2, 2, rf), V(3, count, 2, rf // 2), V(3, count, 2, rf // 2), V(3, count, rf // 2), V(3, count, rf // 2),
            V(2, count, ra), V(3, 2, count, rf), V(4, 2, ra), V(3, GROUP, rf), V(2, radius, own),
            pltpu.VMEM((7, S, width), jnp.float32), pltpu.VMEM((count, S, width), jnp.float32), pltpu.VMEM((count, 8, width), jnp.float32),
            pltpu.SemaphoreType.DMA((240,)), pltpu.SemaphoreType.DMA((240,)), pltpu.SemaphoreType.DMA((4,)),
        ],
        compiler_params=pltpu.CompilerParams(collective_id=2, has_side_effects=True, vmem_limit_bytes=56 * 2**20),
        name="reduce",
    )(gx, ga, *gfs, small)


EPS = 1e-06
TINY = 1e-30
HIGH = lax.Precision.HIGHEST


def norm_rows(values, gain_vec):
    return values * lax.rsqrt(jnp.mean(values * values, axis=-1, keepdims=True) + EPS) * gain_vec


def mm(a, b, ca, cb):
    return lax.dot_general(a, b, (((ca,), (cb,)), ((), ())), preferred_element_type=jnp.float32)


def on_device(tokens, cotangent, lengths, buckets, w_query, w_key, w_value, w_out, w_gate, w_up, w_down, rel_table, gain_one, gain_two):
    bf = jnp.bfloat16
    count = lax.axis_size("mp")
    batches = lax.axis_size("batch")
    own, width = tokens.shape
    total = own * count
    inner = w_query.shape[1]
    hidden_rows = w_gate.shape[1]
    limit = (buckets.shape[0] + 1) // 2
    radius = min(count - 1, -(-(limit - 1) // own))
    place = jnp.reshape(lax.axis_index("mp") * own, (1,)).astype(jnp.int32)
    kinds = rel_table.shape[0]
    heads = rel_table.shape[1] * count

    wa = jnp.concatenate([w_query.T, w_key.T, w_value.T, w_out], axis=0).reshape(4, 2, inner // 2, width)
    wf = jnp.stack([w_gate.T, w_up.T, w_down]).reshape(3, GROUP, hidden_rows // GROUP, width)
    inputs = tokens.astype(jnp.float32)
    normed_one = norm_rows(inputs, gain_one).astype(bf)
    rel_all = lax.all_gather(rel_table, "mp", axis=1, tiled=True)
    hot = bucket_hot(buckets, kinds, TQ)
    table = jnp.dot(hot, rel_all, precision=HIGH).T.reshape(heads // 2, 2, -1)

    rows_one, wa_all, wf_all = gather(normed_one, wa, wf, count, radius)
    rows_one = rows_one.reshape(total, width)
    wa_all = wa_all.reshape(4, count * inner, width)
    wf_all = wf_all.reshape(3, count * hidden_rows, width)
    wq, wk, wv, wo = [wa_all[n] for n in range(4)]
    wg, wu, wd = [wf_all[n] for n in range(3)]

    q = mm(normed_one, wq, 1, 1).astype(bf)
    k = mm(rows_one, wk, 1, 1).astype(bf)
    kt = mm(wk, rows_one, 1, 1).astype(bf)
    v = mm(rows_one, wv, 1, 1).astype(bf)
    vt = mm(wv, rows_one, 1, 1).astype(bf)
    context, lse = attend(lengths, place, table, q, k, vt, limit, TQ, TK)

    middle = inputs + mm(context, wo, 1, 0)
    normed_two = norm_rows(middle, gain_two).astype(bf)
    gate_pre = mm(normed_two, wg, 1, 1)
    up_proj = mm(normed_two, wu, 1, 1)

    def gated_unit(gate_in, up_in):
        return jax.nn.gelu(gate_in, approximate=True) * up_in

    hidden, unit_back = jax.vjp(gated_unit, gate_pre, up_proj)
    hidden = hidden.astype(bf)
    layer_out = (middle + mm(hidden, wd, 1, 0)).astype(bf)
    grad_gate, grad_up = unit_back(mm(cotangent, wd, 1, 1))
    grad_gate = grad_gate.astype(bf)
    grad_up = grad_up.astype(bf)
    raw_down = mm(hidden, cotangent, 0, 0).astype(bf)
    raw_gate = mm(grad_gate, normed_two, 0, 0).astype(bf)
    raw_up = mm(grad_up, normed_two, 0, 0).astype(bf)
    grad_norm_two = mm(grad_gate, wg, 1, 0) + mm(grad_up, wu, 1, 0)
    grad_middle_part, gain_two_part = jax.vjp(norm_rows, middle, gain_two)[1](grad_norm_two)
    grad_middle = cotangent.astype(jnp.float32) + grad_middle_part
    grad_attn = grad_middle.astype(bf)
    grad_context = mm(grad_attn, wo, 1, 1).astype(bf)
    raw_out = mm(context, grad_attn, 0, 0).astype(bf)

    grad_q, grad_k, grad_v, diag = attend_back(lengths, place, table, q, k, kt, v, context, grad_context, lse, limit, TQ, TK)
    grad_rel = jnp.dot(hot.T, diag.reshape(heads, -1).T, precision=HIGH)
    raw_q = mm(grad_q, normed_one, 0, 0).astype(bf)
    raw_k = mm(grad_k, rows_one, 0, 0).astype(bf)
    raw_v = mm(grad_v, rows_one, 0, 0).astype(bf)
    grad_rows = (mm(grad_k, wk, 1, 0) + mm(grad_v, wv, 1, 0)).astype(bf)
    own_part = mm(grad_q, wq, 1, 0)
    gain_one_part = (
        jnp.sum(grad_rows.astype(jnp.float32) * rows_one.astype(jnp.float32), axis=0)
        + jnp.sum(own_part * normed_one.astype(jnp.float32), axis=0)
    ) / gain_one

    rel_rows = -(-(kinds * heads) // width)
    rel_flat = jnp.pad(grad_rel.reshape(-1), (0, rel_rows * width - kinds * heads)).reshape(rel_rows, width)
    small = jnp.concatenate([gain_one_part[None], gain_two_part[None], rel_flat], axis=0)
    small_rows = -(-small.shape[0] // 8) * 8
    small = jnp.pad(small, ((0, small_rows - small.shape[0]), (0, 0)))
    scale = (total * batches) ** -0.5
    one_group = batches == GROUP
    half = inner // 2
    part = hidden_rows // GROUP
    grads_a = jnp.stack([raw_q, raw_k, raw_v, raw_out]).reshape(2, 2, count, 2, half, width)
    grads_f = [one.reshape(count, 2, 2, 2, part, width) for one in (raw_gate, raw_up, raw_down)]
    grad_norm_one, full_a, full_f, side, summed = reduce(
        grad_rows.reshape(count, own, width), grads_a, grads_f, small, count, radius, scale, one_group
    )
    full_a = full_a.reshape(4, inner, width)
    full_f = full_f.reshape(3, hidden_rows, width)
    summed = summed * scale
    if not one_group:
        full_a, full_f, summed = lax.psum((full_a, full_f, summed), "batch")
        full_a, full_f, summed = full_a * (scale / GROUP), full_f * (scale / GROUP), summed / GROUP
        side = lax.psum(jnp.concatenate([jnp.sum(full_a * full_a, axis=1), jnp.sum(full_f * full_f, axis=1)]), "mp")
    grad_input_part = jax.vjp(lambda one: norm_rows(one, gain_one), inputs)[1](grad_norm_one + own_part)[0]
    grad_tokens = (grad_middle + grad_input_part).astype(bf)

    inner_total = float(inner * count)
    hidden_total = float(hidden_rows * count)
    stat_model = jnp.stack([side[0] / inner_total, side[1] / inner_total, side[2] / inner_total, side[3] / inner_total, side[6] / hidden_total]) + TINY
    stat_ffn_rows = side[4:6] / hidden_total + TINY
    stat_heads = jnp.mean(full_a * full_a, axis=2) + TINY
    stat_hidden = jnp.mean(full_f * full_f, axis=2) + TINY
    rel_sum = summed[2 : 2 + rel_rows].reshape(-1)[: kinds * heads].reshape(kinds, heads)
    rel_own = lax.dynamic_slice_in_dim(rel_sum, lax.axis_index("mp") * rel_table.shape[1], rel_table.shape[1], 1)
    return (
        layer_out,
        grad_tokens,
        full_a[0].T,
        full_a[1].T,
        full_a[2].T,
        full_a[3],
        full_f[0].T,
        full_f[1].T,
        full_f[2],
        rel_own,
        summed[0],
        summed[1],
        stat_model,
        stat_heads,
        stat_hidden,
        stat_ffn_rows,
    )


TQ = 256
TK = 256


def solution(mesh):
    in_specs = (
        P(("batch", "mp"), None),
        P(("batch", "mp"), None),
        P("batch", None),
        P(),
        P(None, "mp"),
        P(None, "mp"),
        P(None, "mp"),
        P("mp", None),
        P(None, "mp"),
        P(None, "mp"),
        P("mp", None),
        P(None, "mp"),
        P(),
        P(),
    )
    out_specs = (
        P(("batch", "mp"), None),
        P(("batch", "mp"), None),
        P(None, "mp"),
        P(None, "mp"),
        P(None, "mp"),
        P("mp", None),
        P(None, "mp"),
        P(None, "mp"),
        P("mp", None),
        P(None, "mp"),
        P(),
        P(),
        P(),
        P(None, "mp"),
        P(None, "mp"),
        P(),
    )
    return jax.shard_map(
        on_device, mesh=mesh, in_specs=in_specs, out_specs=out_specs, check_vma=False
    )
```

```python
import functools

import jax
import jax.numpy as jnp
from jax import lax
from jax.experimental import pallas as pl
from jax.experimental.pallas import tpu as pltpu
from jax.sharding import PartitionSpec as P

NEG = -1e9
LANES = 128

def strip_sizes(limit, tq):
    reach = -(-limit // LANES)
    nq = tq // LANES
    off = LANES * (reach + nq)
    return reach, off, off + LANES * reach + tq

def bucket_kinds(buckets, tq):
    limit = (buckets.shape[0] + 1) // 2
    _, off, width = strip_sizes(limit, tq)
    back = lax.rev(buckets, (0,))
    shift = off - (limit - 1)
    left = jnp.broadcast_to(back[:1], (shift,))
    right = jnp.broadcast_to(back[-1:], (width - shift - back.shape[0],))
    return jnp.concatenate([left, back, right])


def ends_list(lens_ref, rows_dev, count):
    total = jnp.int32(0)
    ends = []
    for r in range(rows_dev):
        for c in range(count):
            total = total + lens_ref[r, c]
            ends.append(total)
    return ends

def segment_of(place, ends, count):
    seg = jnp.zeros_like(place)
    pad = jnp.zeros_like(place)
    for n, end in enumerate(ends):
        past = place >= end
        seg = seg + jnp.where(past, 1, 0)
        if n % count == count - 2:
            pad = pad + jnp.where(past, 1, 0)
        if n % count == count - 1:
            pad = pad - jnp.where(past, 1, 0)
    return jnp.where(pad > 0, place + 4096, seg)

def key_range(first, last, ends, count, low_end, high_end, tk):
    low = jnp.int32(0)
    high = ends[-1]
    for n, end in enumerate(ends):
        is_pad_next = n % count == count - 2
        low = jnp.where(first >= end, jnp.maximum(low, first if is_pad_next else end), low)
    for n in range(len(ends) - 1, -1, -1):
        is_pad = n % count == count - 1
        high = jnp.where(last < ends[n], (last + 1) if is_pad else ends[n], high)
    low = (low // LANES) * LANES
    steps = (high - low + tk - 1) // tk
    low = jnp.minimum(low, high_end - steps * tk)
    return pl.multiple_of(low, LANES), steps

def window(place_ref, own, total, limit):
    first = place_ref[0]
    radius = -(-(limit - 1) // own)
    return jnp.maximum(first - radius * own, 0), jnp.minimum(first + (radius + 1) * own, total)

def fill_segments(kseg, ends, count, total):
    def one(n, _):
        at = pl.multiple_of(n * 256, 256)
        place = at + lax.broadcasted_iota(jnp.int32, (256, LANES), 0)
        kseg[pl.ds(at, 256), :] = segment_of(place, ends, count)
        return 0
    lax.fori_loop(0, total // 256, one, 0)

def tile_lanes(x, n):
    return x if n == 1 else jnp.concatenate([x] * n, axis=1)

def lane_start(ks, q_at, g, reach, off, nq):
    d = (ks - q_at) // LANES + g
    return pl.multiple_of(off - LANES * jnp.clip(d, -reach, reach + nq - 1), LANES)

def fwd_kernel(cfg, lens_ref, place_ref, strip, q_ref, k_ref, vt_ref, ctx_ref, lse_ref, kseg):
    tq, tk, limit, rows_dev, count, own, total, hp = cfg
    reach, off, width = strip_sizes(limit, tq)
    nq = tq // LANES
    ends = ends_list(lens_ref, rows_dev, count)
    @pl.when(pl.program_id(0) == 0)
    def _():
        fill_segments(kseg, ends, count, total)
    w_low, w_high = window(place_ref, own, total, limit)
    lane = lax.broadcasted_iota(jnp.int32, (tq, LANES), 1)
    for qt in range(own // tq):
        rows = slice(qt * tq, (qt + 1) * tq)
        q_at = place_ref[0] + qt * tq
        halves = []
        for h in range(hp):
            q2 = q_ref[rows, h // 2 * LANES : h // 2 * LANES + LANES]
            halves.append(jnp.where((lane < 64) == (h % 2 == 0), q2, jnp.zeros_like(q2)))
        qseg = segment_of(q_at + lax.broadcasted_iota(jnp.int32, (1, tq), 1), ends, count)
        low, steps = key_range(q_at, q_at + tq - 1, ends, count, w_low, w_high, tk)
        def step(c, carry):
            ks = pl.multiple_of(low + c * tk, LANES)
            same = tile_lanes(kseg[pl.ds(ks, tk), :], nq) == qseg
            starts = [lane_start(ks, q_at, g, reach, off, nq) for g in range(tk // LANES)]
            out = []
            for h in range(hp):
                top, tot, acc = carry[h]
                kc = k_ref[pl.ds(ks, tk), h // 2 * LANES : h // 2 * LANES + LANES]
                s = lax.dot_general(kc, halves[h], (((1,), (1,)), ((), ())), preferred_element_type=jnp.float32)
                bias = jnp.concatenate([strip[h, :, pl.ds(at, tq)] for at in starts], axis=0)
                s = jnp.where(same, s + bias, NEG)
                new = jnp.maximum(top, jnp.max(s, axis=0, keepdims=True))
                p = jnp.exp(s - new)
                fade = jnp.exp(top - new)
                tot = tot * fade + jnp.sum(p, axis=0, keepdims=True)
                acc = acc * fade + jnp.dot(vt_ref[h * 64 : h * 64 + 64, pl.ds(ks, tk)], p.astype(jnp.bfloat16), preferred_element_type=jnp.float32)
                out.append((new, tot, acc))
            return tuple(out)
        zero = (jnp.full((1, tq), 2 * NEG, jnp.float32), jnp.zeros((1, tq), jnp.float32), jnp.zeros((64, tq), jnp.float32))
        res = lax.fori_loop(0, steps, step, (zero,) * hp)
        for pair in range(hp // 2):
            both = jnp.concatenate([res[h][2] / res[h][1] for h in (2 * pair, 2 * pair + 1)], axis=0)
            ctx_ref[rows, pair * LANES : pair * LANES + LANES] = both.T.astype(jnp.bfloat16)
        for h in range(hp):
            lse_ref[0, h : h + 1, rows] = res[h][0] + jnp.log(res[h][1])


def attend(lengths, place, strips, q, k, vt, limit, tq, tk, hp):
    own, inner = q.shape
    total = k.shape[0]
    steps = inner // 64 // hp
    lanes = hp * 64
    rows_dev, count = lengths.shape
    width = strips.shape[2]
    cfg = (tq, tk, limit, rows_dev, count, own, total, hp)
    smem = pl.BlockSpec(memory_space=pltpu.SMEM)
    return pl.pallas_call(
        functools.partial(fwd_kernel, cfg),
        grid=(steps,),
        in_specs=[smem, smem,
            pl.BlockSpec((hp, LANES, width), lambda p: (p, 0, 0)),
            pl.BlockSpec((own, lanes), lambda p: (0, p)),
            pl.BlockSpec((total, lanes), lambda p: (0, p)),
            pl.BlockSpec((lanes, total), lambda p: (p, 0))],
        out_specs=[pl.BlockSpec((own, lanes), lambda p: (0, p)),
                   pl.BlockSpec((1, hp, own), lambda p: (p, 0, 0))],
        out_shape=[jax.ShapeDtypeStruct((own, inner), jnp.bfloat16), jax.ShapeDtypeStruct((steps, hp, own), jnp.float32)],
        scratch_shapes=[pltpu.VMEM((total, LANES), jnp.int32)],
        compiler_params=pltpu.CompilerParams(vmem_limit_bytes=56 * 2**20),
        name="attend",
    )(lengths, place, strips, q, k, vt)


def bwd_kernel(cfg, lens_ref, place_ref, strip, q_ref, k_ref, kt_ref, v_ref, ctx_ref, do_ref, lse_ref,
               dq_ref, dk_ref, dv_ref, dstrip, kseg, dk_acc, dv_acc):
    tq, tk, limit, rows_dev, count, own, total, hp = cfg
    reach, off, width = strip_sizes(limit, tq)
    nq = tq // LANES
    ends = ends_list(lens_ref, rows_dev, count)
    @pl.when(pl.program_id(0) == 0)
    def _():
        fill_segments(kseg, ends, count, total)
    dstrip[...] = jnp.zeros_like(dstrip)
    dk_acc[...] = jnp.zeros_like(dk_acc)
    dv_acc[...] = jnp.zeros_like(dv_acc)
    w_low, w_high = window(place_ref, own, total, limit)
    lane = lax.broadcasted_iota(jnp.int32, (tq, LANES), 1)
    for qt in range(own // tq):
        rows = slice(qt * tq, (qt + 1) * tq)
        q_at = place_ref[0] + qt * tq
        q_half, do_half, delta, lse = [], [], [], []
        for pair in range(hp // 2):
            lanes = slice(pair * LANES, pair * LANES + LANES)
            q2 = q_ref[rows, lanes]
            do2 = do_ref[rows, lanes]
            prod = (do2.astype(jnp.float32) * ctx_ref[rows, lanes].astype(jnp.float32)).T
            for hh in range(2):
                keep = (lane < 64) == (hh == 0)
                q_half.append(jnp.where(keep, q2, jnp.zeros_like(q2)))
                do_half.append(jnp.where(keep, do2, jnp.zeros_like(do2)))
                delta.append(jnp.sum(prod[hh * 64 : hh * 64 + 64], axis=0, keepdims=True))
                lse.append(lse_ref[0, 2 * pair + hh : 2 * pair + hh + 1, rows])
        qseg = segment_of(q_at + lax.broadcasted_iota(jnp.int32, (1, tq), 1), ends, count)
        low, steps = key_range(q_at, q_at + tq - 1, ends, count, w_low, w_high, tk)
        def step(c, carry):
            ks = pl.multiple_of(low + c * tk, LANES)
            same = tile_lanes(kseg[pl.ds(ks, tk), :], nq) == qseg
            starts = [lane_start(ks, q_at, g, reach, off, nq) for g in range(tk // LANES)]
            out = []
            for pair in range(hp // 2):
                lanes = slice(pair * LANES, pair * LANES + LANES)
                kc = k_ref[pl.ds(ks, tk), lanes]
                vc = v_ref[pl.ds(ks, tk), lanes]
                dk_part = dv_part = None
                for h in (2 * pair, 2 * pair + 1):
                    s = lax.dot_general(kc, q_half[h], (((1,), (1,)), ((), ())), preferred_element_type=jnp.float32)
                    bias = jnp.concatenate([strip[h, :, pl.ds(at, tq)] for at in starts], axis=0)
                    p = jnp.exp(jnp.where(same, s + (bias - lse[h]), NEG))
                    dp = lax.dot_general(vc, do_half[h], (((1,), (1,)), ((), ())), preferred_element_type=jnp.float32)
                    ds = p * (dp - delta[h])
                    for g, at in enumerate(starts):
                        dstrip[h, :, pl.ds(at, tq)] += ds[g * LANES : (g + 1) * LANES, :]
                    pb = p.astype(jnp.bfloat16)
                    dsb = ds.astype(jnp.bfloat16)
                    dv_one = jnp.dot(pb, do_half[h], preferred_element_type=jnp.float32)
                    dk_one = jnp.dot(dsb, q_half[h], preferred_element_type=jnp.float32)
                    dv_part = dv_one if dv_part is None else dv_part + dv_one
                    dk_part = dk_one if dk_part is None else dk_part + dk_one
                    out.append(carry[h] + jnp.dot(kt_ref[h * 64 : h * 64 + 64, pl.ds(ks, tk)], dsb, preferred_element_type=jnp.float32))
                dv_acc[pl.ds(ks, tk), lanes] += dv_part
                dk_acc[pl.ds(ks, tk), lanes] += dk_part
            return tuple(out)
        zero = jnp.zeros((64, tq), jnp.float32)
        res = lax.fori_loop(0, steps, step, (zero,) * hp)
        for pair in range(hp // 2):
            dq_ref[rows, pair * LANES : pair * LANES + LANES] = jnp.concatenate(res[2 * pair : 2 * pair + 2], axis=0).T.astype(jnp.bfloat16)
    dk_ref[...] = dk_acc[...].astype(jnp.bfloat16)
    dv_ref[...] = dv_acc[...].astype(jnp.bfloat16)


def attend_back(lengths, place, strips, q, k, kt, v, ctx, do, lse, limit, tq, tk, hp):
    own, inner = q.shape
    total = k.shape[0]
    steps = inner // 64 // hp
    lanes = hp * 64
    rows_dev, count = lengths.shape
    width = strips.shape[2]
    cfg = (tq, tk, limit, rows_dev, count, own, total, hp)
    smem = pl.BlockSpec(memory_space=pltpu.SMEM)
    tall = pl.BlockSpec((total, lanes), lambda p: (0, p))
    short = pl.BlockSpec((own, lanes), lambda p: (0, p))
    band = pl.BlockSpec((hp, LANES, width), lambda p: (p, 0, 0))
    return pl.pallas_call(
        functools.partial(bwd_kernel, cfg),
        grid=(steps,),
        in_specs=[smem, smem, band,
            short, tall, pl.BlockSpec((lanes, total), lambda p: (p, 0)), tall, short, short,
            pl.BlockSpec((1, hp, own), lambda p: (p, 0, 0))],
        out_specs=[short, tall, tall, band],
        out_shape=[jax.ShapeDtypeStruct((own, inner), jnp.bfloat16), jax.ShapeDtypeStruct((total, inner), jnp.bfloat16),
                   jax.ShapeDtypeStruct((total, inner), jnp.bfloat16), jax.ShapeDtypeStruct(strips.shape, jnp.float32)],
        scratch_shapes=[pltpu.VMEM((total, LANES), jnp.int32),
                        pltpu.VMEM((total, lanes), jnp.float32), pltpu.VMEM((total, lanes), jnp.float32)],
        compiler_params=pltpu.CompilerParams(vmem_limit_bytes=60 * 2**20),
        name="attend_back",
    )(lengths, place, strips, q, k, kt, v, ctx, do, lse)


def sum_strip(block, width):
    eight = block[0:8, :]
    for g in range(1, LANES // 8):
        eight = eight + pltpu.roll(block[8 * g : 8 * g + 8, :], width - 8 * g, 1)
    flat = eight[0:1, :]
    for r in range(1, 8):
        flat = flat + pltpu.roll(eight[r : r + 1, :], width - r, 1)
    return flat


def sums_kernel(in_ref, out_ref):
    for h in range(in_ref.shape[0]):
        out_ref[0, h : h + 1, :] = sum_strip(in_ref[h], in_ref.shape[2])


def sum_strips(strips):
    heads, _, width = strips.shape
    return pl.pallas_call(
        sums_kernel, grid=(heads // 2,),
        in_specs=[pl.BlockSpec((2, LANES, width), lambda p: (p, 0, 0))],
        out_specs=pl.BlockSpec((1, 2, width), lambda p: (p, 0, 0)),
        out_shape=jax.ShapeDtypeStruct((heads // 2, 2, width), jnp.float32), name="attend_sums",
    )(strips).reshape(heads, width)


MESH = pl.DeviceIdType.MESH
GROUP = 8


def flip(index, bit):
    return index + bit * (1 - 2 * ((index // bit) % 2))


class Links:
    def __init__(self, send_sems, recv_sems, batch, place):
        self.send_sems, self.recv_sems = send_sems, recv_sems
        self.batch, self.place = batch, place
        self.slots = {}
        self.sent = []

    def slot(self, key):
        return self.slots.setdefault(key, len(self.slots))

    def copy(self, key, src, dst, target):
        n = self.slot(key)
        return pltpu.make_async_remote_copy(
            src_ref=src, dst_ref=dst, send_sem=self.send_sems.at[n], recv_sem=self.recv_sems.at[n],
            device_id=target, device_id_type=MESH)

    def send(self, key, src, dst, target, when=None):
        def go():
            self.copy(key, src, dst, target).start()
        self.sent.append((key, src, dst, target, when))
        if when is None:
            go()
        else:
            pl.when(when)(go)

    def take(self, key, dst, when=None, then=None):
        def go():
            self.copy(key, dst, dst, (self.batch, self.place)).wait_recv()
            if then is not None:
                then()
        if when is None:
            go()
        else:
            pl.when(when)(go)

    def drain(self):
        for key, src, dst, target, when in self.sent:
            def go():
                self.copy(key, src, dst, target).wait_send()
            if when is None:
                go()
            else:
                pl.when(when)(go)


def greet(batch, place, count):
    bar = pltpu.get_barrier_semaphore()
    for bit in (1, 2, 4):
        pl.semaphore_signal(bar, inc=1, device_id=(flip(batch, bit), place), device_id_type=MESH)
    for way in range(1 - count, count):
        if way != 0:
            @pl.when((place + way >= 0) & (place + way < count))
            def _():
                pl.semaphore_signal(bar, inc=1, device_id=(batch, place + way), device_id_type=MESH)
    pl.semaphore_wait(bar, 3 + count - 1)


def both(a, b):
    return a if b is None else (b if a is None else a & b)


class PlaneGather:
    def __init__(self, links, key, view, ref, sub, when=None):
        self.l, self.key, self.view, self.ref, self.sub, self.when = links, key, view, ref, sub, when

    def put(self, path, sub, half, bit):
        region = self.view(self.ref, sub, half)
        self.l.send((self.key, path), region, region, (flip(self.l.batch, bit), self.l.place), self.when)

    def start(self):
        self.put("x", self.sub, None, 2)
        self.put("y", self.sub, None, 4)
        self.put("c", self.sub, None, 1)

    def middle(self):
        sub = self.sub
        self.l.take((self.key, "x"), self.view(self.ref, flip(sub, 2), None), self.when)
        self.put("xy", flip(sub, 2), 0, 4)
        self.put("xc", flip(sub, 2), None, 1)
        self.l.take((self.key, "y"), self.view(self.ref, flip(sub, 4), None), self.when)
        self.put("yx", flip(sub, 4), 1, 2)
        self.put("yc", flip(sub, 4), None, 1)

    def far(self):
        sub = self.sub
        diagonal = flip(flip(sub, 2), 4)
        self.l.take((self.key, "xy"), self.view(self.ref, diagonal, 0), self.when)
        self.put("0c", diagonal, 0, 1)
        self.l.take((self.key, "yx"), self.view(self.ref, diagonal, 1), self.when)
        self.put("1c", diagonal, 1, 1)

    def end(self):
        sub = flip(self.sub, 1)
        diagonal = flip(flip(sub, 2), 4)
        self.l.take((self.key, "c"), self.view(self.ref, sub, None), self.when)
        self.l.take((self.key, "xc"), self.view(self.ref, flip(sub, 2), None), self.when)
        self.l.take((self.key, "yc"), self.view(self.ref, flip(sub, 4), None), self.when)
        self.l.take((self.key, "0c"), self.view(self.ref, diagonal, 0), self.when)
        self.l.take((self.key, "1c"), self.view(self.ref, diagonal, 1), self.when)


def half_rows(half, rows):
    return pl.ds(0, rows) if half is None else pl.ds(half * (rows // 2), rows // 2)


PIECES = 4
EPS = 1e-06


def unit_norm(values):
    return lax.rsqrt(jnp.mean(values * values, axis=1, keepdims=True) + EPS)


def dot_nt(a, b):
    return lax.dot_general(a, b, (((1,), (1,)), ((), ())), preferred_element_type=jnp.float32)


def dot_nn(a, b):
    return jnp.dot(a, b, preferred_element_type=jnp.float32)


def gather_kernel(count, radius, tok_ref, gain_ref, wa_ref, wf_ref, rel_ref, kinds_ref,
                  xs_out, was_out, wfs_ref, q_out, k_out, kt_out, v_out, vt_out, strips_out,
                  xs, was, q_v, k_v, kt_v, v_v, vt_v, rel_all, table, strip_v, send_sems, recv_sems, local_sems):
    batch, place = lax.axis_index("batch"), lax.axis_index("mp")
    sub = batch % GROUP
    links = Links(send_sems, recv_sems, batch, place)
    own, width = tok_ref.shape
    rows_a = wa_ref.shape[2]
    rows_f = wf_ref.shape[2]
    step = own // PIECES
    local = []

    def copy_local(src, dst):
        one = pltpu.make_async_copy(src, dst, local_sems.at[len(local)])
        local.append(one)
        return one

    own_a = copy_local(wa_ref, was.at[:, place])
    own_a.start()
    copy_local(wf_ref, wfs_ref.at[:, place]).start()
    for p in range(PIECES):
        rows = pl.ds(p * step, step)
        values = tok_ref[rows, :].astype(jnp.float32)
        xs[place, rows] = (values * unit_norm(values) * gain_ref[...]).astype(xs.dtype)
    greet(batch, place, count)

    def view_a(mm):
        return lambda ref, s, half: ref.at[s // 2, mm, s % 2, half_rows(half, rows_a)]

    def view_f(mm):
        return lambda ref, s, half: ref.at[:, mm, s, half_rows(half, rows_f)]

    def inside(n):
        return (n >= 0) & (n < count)

    for way in (1, -1):
        ok = inside(place + way)
        target = (batch, place + way)
        links.send(("a", way, 1), wa_ref.at[sub // 2, sub % 2], view_a(place)(was, sub, None), target, ok)
        links.send(("f", way, 1), wf_ref.at[:, sub], view_f(place)(wfs_ref, sub, None), target, ok)
    for d in range(1, count):
        for way in (1, -1):
            links.send(("r", way, d), rel_ref, rel_all.at[place], (batch, place + way * d), inside(place + way * d))
    for way in (1, -1):
        ok = inside(place + way)
        target = (batch, place + way)
        for p in range(PIECES):
            rows = pl.ds(p * step, step)
            links.send(("x", way, 1, p), xs.at[place, rows], xs.at[place, rows], target, ok)
    for n in range(count):
        @pl.when((n - place > radius) | (place - n > radius))
        def _():
            def blank(p, _):
                xs[n, pl.ds(p * step, step)] = jnp.zeros((step, width), xs.dtype)
                return 0
            lax.fori_loop(0, PIECES, blank, 0)
            for ref in (k_v, v_v):
                ref[pl.ds(n * own, own)] = jnp.zeros((own, ref.shape[1]), ref.dtype)
            for ref in (kt_v, vt_v):
                ref[:, pl.ds(n * own, own)] = jnp.zeros((ref.shape[0], own), ref.dtype)

    gathers = {}

    def weights_arrive(kind, dist):
        for way in (1, -1):
            source = place - way * dist
            ok = inside(source)
            view, ref = (view_a(source), was) if kind == "a" else (view_f(source), wfs_ref)
            region = view(ref, sub, None)
            links.take((kind, way, dist), region, ok)
            if dist < count - 1:
                links.send((kind, way, dist + 1), region, region, (batch, place + way), ok & inside(place + way))
            gather = PlaneGather(links, ("g", kind, way, dist), view, ref, sub, ok)
            gather.start()
            gathers[kind, way, dist] = gather

    def x_arrive(dist, p):
        for way in (1, -1):
            source = place - way * dist
            ok = inside(source)
            region = xs.at[source, pl.ds(p * step, step)]
            links.take(("x", way, dist, p), region, ok)
            if dist < radius:
                links.send(("x", way, dist + 1, p), region, region, (batch, place + way), ok & inside(place + way))

    def stage(name, kind, dist):
        for way in (1, -1):
            getattr(gathers[kind, way, dist], name)()

    heads_own = rel_ref.shape[0] // 8 * 8
    heads = table.shape[0]
    span = table.shape[1]
    kinds = rel_ref.shape[1]

    def make_table():
        rel_all[place] = rel_ref[...]
        for d in range(1, count):
            for way in (1, -1):
                links.take(("r", way, d), rel_all.at[place - way * d], inside(place - way * d))
        per = heads // count
        joined = jnp.concatenate([rel_all[n, 0:per, :] for n in range(count)], axis=0)
        for at in range(0, span, 512):
            lanes = pl.ds(at, min(512, span - at))
            kind = kinds_ref[:, lanes]
            total = jnp.zeros((heads, kind.shape[1]), jnp.float32)
            for b in range(NB_MAX):
                if b < kinds:
                    total = total + jnp.where(kind == b, joined[:, b : b + 1], 0.0)
            table[:, lanes] = total

    strip_copies = []

    def make_strip(h):
        slot = h % 2
        if h >= 2:
            strip_copies[h - 2].wait()
        row = table[h : h + 1, :]
        strip_v[slot] = pltpu.roll(jnp.broadcast_to(row, (LANES, span)), 0, 1, stride=1, stride_axis=0)
        one = pltpu.make_async_copy(strip_v.at[slot], strips_out.at[h], local_sems.at[8 + slot])
        one.start()
        strip_copies.append(one)

    inner = was.shape[1] * was.shape[2] * rows_a

    def weight_tile(kind, n):
        return was[kind, n].reshape(2 * rows_a, width)

    def project(block, when):
        def go():
            x = xs[block]
            def one(n, _):
                at = pl.multiple_of(n * 2 * rows_a, 64)
                kt_v[pl.ds(at, 2 * rows_a), pl.ds(pl.multiple_of(block * own, LANES), own)] = dot_nt(weight_tile(1, n), x).astype(kt_v.dtype)
                vt_v[pl.ds(at, 2 * rows_a), pl.ds(pl.multiple_of(block * own, LANES), own)] = dot_nt(weight_tile(2, n), x).astype(vt_v.dtype)
                return 0
            lax.fori_loop(0, count, one, 0)
            rows = pl.ds(pl.multiple_of(block * own, LANES), own)
            tile = 256
            for at in range(0, inner, tile):
                wk = was[1].reshape(inner, width)[at : at + tile]
                wv = was[2].reshape(inner, width)[at : at + tile]
                k_v[rows, at : at + tile] = dot_nt(x, wk).astype(k_v.dtype)
                v_v[rows, at : at + tile] = dot_nt(x, wv).astype(v_v.dtype)
        if when is None:
            go()
        else:
            pl.when(when)(go)

    def project_q():
        x = xs[place]
        tile = 256
        for at in range(0, inner, tile):
            wq = was[0].reshape(inner, width)[at : at + tile]
            q_v[:, at : at + tile] = dot_nt(x, wq).astype(q_v.dtype)

    dists = range(1, count)
    make_table()
    for h in range(2):
        make_strip(h)
    for d in dists:
        weights_arrive("a", d)
    weights_arrive("f", 1)
    for h in range(2, 5):
        make_strip(h)
    for d in dists:
        stage("middle", "a", d)
    for p in range(PIECES):
        x_arrive(1, p)
        if p + 2 < count:
            weights_arrive("f", p + 2)
        if p == 1:
            stage("middle", "f", 1)
    for d in dists:
        stage("far", "a", d)
    for d in range(2, count):
        stage("middle", "f", d)
    for d in dists:
        stage("far", "f", d)
    for d in dists:
        stage("end", "a", d)
    own_a.wait()
    copy_local(was, was_out).start()
    project_q()
    copy_local(q_v, q_out).start()
    project(place, None)
    for h in range(5, heads):
        make_strip(h)
    for way in (1, -1):
        project(place + way, inside(place + way))
    for r in range(2, radius + 1):
        for p in range(PIECES):
            x_arrive(r, p)
        for way in (1, -1):
            project(place + way * r, inside(place + way * r))
    copy_local(xs, xs_out).start()
    for src, dst in ((k_v, k_out), (kt_v, kt_out), (v_v, v_out), (vt_v, vt_out)):
        copy_local(src, dst).start()
    for d in dists:
        stage("end", "f", d)
    links.drain()
    for one in local[1:] + strip_copies[-2:]:
        one.wait()


NB_MAX = 128


def gather(tokens, gain, wa, wf, rel, kinds, count, radius, heads):
    own, width = tokens.shape
    bf = jnp.bfloat16
    total = own * count
    inner = count * 2 * wa.shape[2]
    span = kinds.shape[1]
    vm = pl.BlockSpec(memory_space=pltpu.VMEM)
    hb = pl.BlockSpec(memory_space=pl.ANY)
    shapes = [
        ((count, own, width), bf),
        ((4, count, 2, wa.shape[2], width), bf),
        ((3, count, GROUP, wf.shape[2], width), bf),
        ((own, inner), bf), ((total, inner), bf), ((inner, total), bf), ((total, inner), bf), ((inner, total), bf),
        ((heads, LANES, span), jnp.float32),
    ]
    return pl.pallas_call(
        functools.partial(gather_kernel, count, radius),
        in_specs=[vm, vm, hb, hb, vm, vm],
        out_specs=[hb] * len(shapes),
        out_shape=[jax.ShapeDtypeStruct(*one) for one in shapes],
        scratch_shapes=[pltpu.VMEM(*shapes[n]) for n in (0, 1, 3, 4, 5, 6, 7)] + [
            pltpu.VMEM((count,) + rel.shape, jnp.float32),
            pltpu.VMEM((heads, span), jnp.float32),
            pltpu.VMEM((2, LANES, span), jnp.float32),
            pltpu.SemaphoreType.DMA((170,)),
            pltpu.SemaphoreType.DMA((170,)),
            pltpu.SemaphoreType.DMA((10,)),
        ],
        compiler_params=pltpu.CompilerParams(collective_id=1, has_side_effects=True, vmem_limit_bytes=60 * 2**20),
        name="gather",
    )(tokens, gain, wa, wf, rel, kinds)


def add_blocks(count, target, extra):
    def one(n, _):
        t, e = target(n), extra(n)
        t[...] = t[...] + e[...]
        return 0
    lax.fori_loop(0, count, one, 0)


def reduce_kernel(count, radius, scale, final, gx_ref, ga_ref, gg_ref, gu_ref, gd_ref, small_ref,
                  gn_ref, oa_ref, of_ref, side_ref, total_ref,
                  keep_a, got_a1, got_ax, got_ay, got_ay2, got_ax2, keep_f, got_f1, got_fx, got_fy, got_fy2, got_fx2,
                  from_a, from_f, full_a, full_f, got_x, tiny, tiny_z, side_z, send_sems, recv_sems, local_sems):
    batch, place = lax.axis_index("batch"), lax.axis_index("mp")
    sub = batch % GROUP
    core, xx, yy = sub % 2, (sub // 2) % 2, sub // 4
    links = Links(send_sems, recv_sems, batch, place)
    gf_refs = [gg_ref, gu_ref, gd_ref]
    rows_a, rows_f = keep_a.shape[3], keep_f.shape[4]
    ha, hf = rows_a // 2, rows_f // 2
    own = gn_ref.shape[0]
    step = own // PIECES

    def inside(n):
        return (n >= 0) & (n < count)

    sibling, x_near, y_near = [(flip(batch, bit), place) for bit in (1, 2, 4)]
    local_f = [pltpu.make_async_copy(gf_refs[t].at[:, :, :, core], keep_f.at[t], local_sems.at[t]) for t in range(3)]
    local_a = pltpu.make_async_copy(ga_ref.at[:, :, :, core], keep_a, local_sems.at[3])
    for one in local_f + [local_a]:
        one.start()
    greet(batch, place, count)
    for t in range(3):
        links.send(("f1", t), gf_refs[t].at[:, :, :, 1 - core], got_f1.at[t], sibling)
    links.send(("a1",), ga_ref.at[:, :, :, 1 - core], got_a1, sibling)
    for way in (1, -1):
        for p in range(PIECES):
            rows = pl.ds(p * step, step)
            dest = place + way * radius
            links.send(("x", way, radius, p), gx_ref.at[jnp.clip(dest, 0, count - 1), rows],
                       got_x.at[0 if way > 0 else 1, radius - 1, rows], (batch, place + way), inside(dest))
    links.send(("s", 0), small_ref, tiny.at[1], sibling)

    def start_a(t):
        if t == "a":
            links.send(("ax",), keep_a.at[:, 1 - xx, :, pl.ds(0, ha)], got_ax, x_near)
            links.send(("ay",), keep_a.at[1 - yy, :, :, pl.ds(ha, ha)], got_ay, y_near)
        else:
            links.send(("fx", t), keep_f.at[t, :, :, 1 - xx, pl.ds(0, hf)], got_fx.at[t], x_near)
            links.send(("fy", t), keep_f.at[t, :, 1 - yy, :, pl.ds(hf, hf)], got_fy.at[t], y_near)

    for t in range(3):
        local_f[t].wait()
        links.take(("f1", t), got_f1.at[t])
        def one(n, _):
            for i in range(2):
                for j in range(2):
                    keep_f[t, n, i, j] = keep_f[t, n, i, j] + got_f1[t, n, i, j]
            return 0
        lax.fori_loop(0, count, one, 0)
        start_a(t)
    local_a.wait()
    links.take(("a1",), got_a1)
    def one_a(n, _):
        for i in range(2):
            for j in range(2):
                keep_a[i, j, n] = keep_a[i, j, n] + got_a1[i, j, n]
        return 0
    lax.fori_loop(0, count, one_a, 0)
    start_a("a")

    def tiny_step(n):
        links.take(("s", n), tiny.at[2 * n + 1])
        before = small_ref if n == 0 else tiny.at[2 * n]
        tiny[2 * n + 2] = before[...] + tiny[2 * n + 1]
        if n < 2:
            links.send(("s", n + 1), tiny.at[2 * n + 2], tiny.at[2 * n + 3], (flip(batch, 2 << n), place))
        else:
            tiny_z[place] = tiny[6]
            for d in range(1, count):
                for way in (1, -1):
                    links.send(("sz", way, d), tiny.at[6], tiny_z.at[place], (batch, place + way * d), inside(place + way * d))

    tiny_step(0)

    def x_step(level, p):
        rows = pl.ds(p * step, step)
        for side, way in ((0, 1), (1, -1)):
            dest = place + way * (level - 1)
            ok = inside(place - way) & inside(dest)
            def add():
                got_x[side, level - 1, rows] = got_x[side, level - 1, rows] + gx_ref[dest, rows]
            links.take(("x", way, level, p), got_x.at[side, level - 1, rows], ok, add if level > 1 else None)
            if level > 1:
                ok2 = inside(place - way) & inside(dest)
                links.send(("x", way, level - 1, p), got_x.at[side, level - 1, rows], got_x.at[side, level - 2, rows],
                           (batch, place + way), ok2)
                links.send(("x0", way, level - 1, p), gx_ref.at[jnp.clip(dest, 0, count - 1), rows], got_x.at[side, level - 2, rows],
                           (batch, place + way), jnp.logical_not(inside(place - way)) & inside(dest))

    for level in range(radius, 1, -1):
        for p in range(PIECES):
            x_step(level, p)
    tiny_step(1)

    def middle(t):
        if t == "a":
            links.take(("ax",), got_ax)
            links.take(("ay",), got_ay)
            def one(n, _):
                for i in range(2):
                    keep_a[i, xx, n, pl.ds(0, ha)] = keep_a[i, xx, n, pl.ds(0, ha)] + got_ax[i, n]
                    keep_a[yy, i, n, pl.ds(ha, ha)] = keep_a[yy, i, n, pl.ds(ha, ha)] + got_ay[i, n]
                return 0
            lax.fori_loop(0, count, one, 0)
            links.send(("ay2",), keep_a.at[1 - yy, xx, :, pl.ds(0, ha)], got_ay2, y_near)
            links.send(("ax2",), keep_a.at[yy, 1 - xx, :, pl.ds(ha, ha)], got_ax2, x_near)
        else:
            links.take(("fx", t), got_fx.at[t])
            links.take(("fy", t), got_fy.at[t])
            def one(n, _):
                for i in range(2):
                    keep_f[t, n, i, xx, pl.ds(0, hf)] = keep_f[t, n, i, xx, pl.ds(0, hf)] + got_fx[t, n, i]
                    keep_f[t, n, yy, i, pl.ds(hf, hf)] = keep_f[t, n, yy, i, pl.ds(hf, hf)] + got_fy[t, n, i]
                return 0
            lax.fori_loop(0, count, one, 0)
            links.send(("fy2", t), keep_f.at[t, :, 1 - yy, xx, pl.ds(0, hf)], got_fy2.at[t], y_near)
            links.send(("fx2", t), keep_f.at[t, :, yy, 1 - xx, pl.ds(hf, hf)], got_fx2.at[t], x_near)

    def unit(t, n):
        return keep_a.at[yy, xx, n] if t == "a" else keep_f.at[t, n, yy, xx]

    def arrived(t, side, n):
        return from_a.at[side, n] if t == "a" else from_f.at[t, side, n]

    def last(t):
        if t == "a":
            links.take(("ay2",), got_ay2)
            links.take(("ax2",), got_ax2)
            def one(n, _):
                keep_a[yy, xx, n, pl.ds(0, ha)] = keep_a[yy, xx, n, pl.ds(0, ha)] + got_ay2[n]
                keep_a[yy, xx, n, pl.ds(ha, ha)] = keep_a[yy, xx, n, pl.ds(ha, ha)] + got_ax2[n]
                return 0
        else:
            links.take(("fy2", t), got_fy2.at[t])
            links.take(("fx2", t), got_fx2.at[t])
            def one(n, _):
                keep_f[t, n, yy, xx, pl.ds(0, hf)] = keep_f[t, n, yy, xx, pl.ds(0, hf)] + got_fy2[t, n]
                keep_f[t, n, yy, xx, pl.ds(hf, hf)] = keep_f[t, n, yy, xx, pl.ds(hf, hf)] + got_fx2[t, n]
                return 0
        lax.fori_loop(0, count, one, 0)

    def line(t, hop):
        for side, way in ((0, 1), (1, -1)):
            for n in (range(count - 1, 0, -1) if way > 0 else range(count - 1)):
                first = place == (0 if way > 0 else count - 1)
                beyond = (n > place) if way > 0 else (n < place)
                here = place == (hop if way > 0 else count - 1 - hop)
                if hop > 0:
                    def add():
                        ref, more = unit(t, n), arrived(t, side, n)
                        ref[...] = ref[...] + more[...]
                    links.take(("z", t, side, n, hop - 1), arrived(t, side, n), here & beyond, add)
                links.send(("z", t, side, n, hop), unit(t, n), arrived(t, side, n), (batch, place + way), here & beyond)

    def view_a(ref, s, half):
        return ref.at[s // 2, s % 2, half_rows(half, rows_a)]

    def view_f(t):
        return lambda ref, s, half: ref.at[t, s, half_rows(half, rows_f)]

    gathers = {}

    def finish(t):
        for side, way in ((0, 1), (1, -1)):
            for hop in range(count - 1):
                def add():
                    ref, more = unit(t, place), arrived(t, side, place)
                    ref[...] = ref[...] + more[...]
                for n in range(count):
                    here = (place == n) & (place == (hop + 1 if way > 0 else count - 2 - hop))
                    if (n == hop + 1) if way > 0 else (n == count - 2 - hop):
                        links.take(("z", t, side, n, hop), arrived(t, side, n), here, add)
        if t == "a":
            view, ref = view_a, full_a
            full_a[sub // 2, sub % 2] = keep_a[yy, xx, place]
        else:
            view, ref = view_f(t), full_f
            full_f[t, sub] = keep_f[t, place, yy, xx]
        gathers[t] = PlaneGather(links, ("g", t), view, ref, sub)
        gathers[t].start()

    order = [0, 1, 2, "a"]
    for t in order:
        middle(t)
    tiny_step(2)
    for t in order:
        last(t)
        line(t, 0)
    for p in range(PIECES):
        for side, way in ((0, 1), (1, -1)):
            rows = pl.ds(p * step, step)
            ok = inside(place - way)
            near = inside(place - 2 * way)
            if radius > 1:
                links.take(("x", way, 1, p), got_x.at[side, 0, rows], ok & near)
                links.take(("x0", way, 1, p), got_x.at[side, 0, rows], ok & jnp.logical_not(near))
            else:
                links.take(("x", way, 1, p), got_x.at[side, 0, rows], ok)
            def fill():
                got_x[side, 0, rows] = jnp.zeros((step, got_x.shape[3]), got_x.dtype)
            pl.when(jnp.logical_not(ok))(fill)
        rows = pl.ds(p * step, step)
        gn_ref[rows, :] = (gx_ref[place, rows].astype(jnp.float32) + got_x[0, 0, rows].astype(jnp.float32)
                           + got_x[1, 0, rows].astype(jnp.float32))
    for hop in range(1, count - 1):
        for t in order:
            line(t, hop)
    for t in order:
        finish(t)
    for d in range(1, count):
        for way in (1, -1):
            links.take(("sz", way, d), tiny_z.at[place - way * d], inside(place - way * d))
    summed = tiny_z[0]
    for n in range(1, count):
        summed = summed + tiny_z[n]
    total_ref[...] = summed
    for name in ("middle", "far", "end"):
        for t in order:
            getattr(gathers[t], name)()

    def scaled(value):
        return value.astype(jnp.float32) * scale if final else value.astype(jnp.float32)

    sums = []
    for s in range(4):
        acc = jnp.zeros((8, full_a.shape[3]), jnp.float32)
        for j in range(2):
            def one(r, acc):
                rows = pl.ds(pl.multiple_of(r * 32, 32), 32)
                value = scaled(full_a[s, j, rows])
                oa_ref[s, j, rows] = value
                sq = value * value
                return acc + sq[0:8] + sq[8:16] + sq[16:24] + sq[24:32]
            acc = lax.fori_loop(0, rows_a // 32, one, acc)
        sums.append(jnp.sum(acc, axis=0, keepdims=True))
    for t in range(3):
        def one(n, acc):
            for r in range(rows_f // 32):
                rows = pl.ds(r * 32, 32)
                value = scaled(full_f[t, n, rows])
                of_ref[t, n, rows] = value
                sq = value * value
                acc = acc + sq[0:8] + sq[8:16] + sq[16:24] + sq[24:32]
            return acc
        sums.append(jnp.sum(lax.fori_loop(0, GROUP, one, jnp.zeros((8, full_a.shape[3]), jnp.float32)), axis=0, keepdims=True))
    sums.append(jnp.zeros_like(sums[0]))
    side_z[place] = jnp.concatenate(sums, axis=0)
    for d in range(1, count):
        for way in (1, -1):
            links.send(("q", way, d), side_z.at[place], side_z.at[place], (batch, place + way * d), inside(place + way * d))
    for d in range(1, count):
        for way in (1, -1):
            links.take(("q", way, d), side_z.at[place - way * d], inside(place - way * d))
    summed = side_z[0]
    for n in range(1, count):
        summed = summed + side_z[n]
    side_ref[...] = summed
    links.drain()


def reduce(gx, ga, gfs, small, count, radius, scale, final):
    _, own, width = gx.shape
    bf = jnp.bfloat16
    ra, rf = ga.shape[4], gfs[0].shape[4]
    vm = pl.BlockSpec(memory_space=pltpu.VMEM)
    hb = pl.BlockSpec(memory_space=pl.ANY)
    V = lambda *s: pltpu.VMEM(s + (width,), bf)
    S = small.shape[0]
    return pl.pallas_call(
        functools.partial(reduce_kernel, count, radius, scale, final),
        in_specs=[vm, hb, hb, hb, hb, vm],
        out_specs=[vm] * 5,
        out_shape=[
            jax.ShapeDtypeStruct((own, width), jnp.float32),
            jax.ShapeDtypeStruct((4, 2, ra, width), jnp.float32),
            jax.ShapeDtypeStruct((3, GROUP, rf, width), jnp.float32),
            jax.ShapeDtypeStruct((8, width), jnp.float32),
            jax.ShapeDtypeStruct((S, width), jnp.float32),
        ],
        scratch_shapes=[
            V(2, 2, count, ra), V(2, 2, count, ra), V(2, count, ra // 2), V(2, count, ra // 2), V(count, ra // 2), V(count, ra // 2),
            V(3, count, 2, 2, rf), V(3, count, 2, 2, rf), V(3, count, 2, rf // 2), V(3, count, 2, rf // 2), V(3, count, rf // 2), V(3, count, rf // 2),
            V(2, count, ra), V(3, 2, count, rf), V(4, 2, ra), V(3, GROUP, rf), V(2, radius, own),
            pltpu.VMEM((7, S, width), jnp.float32), pltpu.VMEM((count, S, width), jnp.float32), pltpu.VMEM((count, 8, width), jnp.float32),
            pltpu.SemaphoreType.DMA((240,)), pltpu.SemaphoreType.DMA((240,)), pltpu.SemaphoreType.DMA((4,)),
        ],
        compiler_params=pltpu.CompilerParams(collective_id=2, has_side_effects=True, vmem_limit_bytes=56 * 2**20),
        name="reduce",
    )(gx, ga, *gfs, small)


TINY = 1e-30
HIGH = lax.Precision.HIGHEST


def norm_rows(values, gain_vec):
    return values * lax.rsqrt(jnp.mean(values * values, axis=-1, keepdims=True) + EPS) * gain_vec


def mm(a, b, ca, cb):
    return lax.dot_general(a, b, (((ca,), (cb,)), ((), ())), preferred_element_type=jnp.float32)


def on_device(tokens, cotangent, lengths, buckets, w_query, w_key, w_value, w_out, w_gate, w_up, w_down, rel_table, gain_one, gain_two):
    bf = jnp.bfloat16
    count = lax.axis_size("mp")
    batches = lax.axis_size("batch")
    own, width = tokens.shape
    total = own * count
    inner = w_query.shape[1]
    hidden_rows = w_gate.shape[1]
    limit = (buckets.shape[0] + 1) // 2
    radius = min(count - 1, -(-(limit - 1) // own))
    place = jnp.reshape(lax.axis_index("mp") * own, (1,)).astype(jnp.int32)
    kinds = rel_table.shape[0]
    heads = rel_table.shape[1] * count

    wa = jnp.concatenate([w_query.T, w_key.T, w_value.T, w_out], axis=0).reshape(4, 2, inner // 2, width)
    wf = jnp.stack([w_gate.T, w_up.T, w_down]).reshape(3, GROUP, hidden_rows // GROUP, width)
    inputs = tokens.astype(jnp.float32)
    kind_row = bucket_kinds(buckets, TQ)[None]
    hot = (kind_row[0][:, None] == jnp.arange(kinds, dtype=jnp.int32)[None, :]).astype(jnp.float32)
    rel_own = jnp.pad(rel_table.T, ((0, 8 - rel_table.shape[1]), (0, 0)))
    rows_one, wa_all, wf_all, q, k, kt, v, vt, strips = gather(
        tokens, gain_one[None], wa, wf, rel_own, kind_row, count, radius, heads
    )
    rows_one = rows_one.reshape(total, width)
    normed_one = lax.dynamic_slice_in_dim(rows_one, lax.axis_index("mp") * own, own, 0)
    wa_all = wa_all.reshape(4, count * inner, width)
    wf_all = wf_all.reshape(3, count * hidden_rows, width)
    wq, wk, wv, wo = [wa_all[n] for n in range(4)]
    wg, wu, wd = [wf_all[n] for n in range(3)]

    context, lse = attend(lengths, place, strips, q, k, vt, limit, TQ, TK, HP)

    middle = inputs + mm(context, wo, 1, 0)
    normed_two = norm_rows(middle, gain_two).astype(bf)
    gate_pre = mm(normed_two, wg, 1, 1)
    up_proj = mm(normed_two, wu, 1, 1)

    def gated_unit(gate_in, up_in):
        return jax.nn.gelu(gate_in, approximate=True) * up_in

    hidden, unit_back = jax.vjp(gated_unit, gate_pre, up_proj)
    hidden = hidden.astype(bf)
    layer_out = (middle + mm(hidden, wd, 1, 0)).astype(bf)
    grad_gate, grad_up = unit_back(mm(cotangent, wd, 1, 1))
    grad_gate = grad_gate.astype(bf)
    grad_up = grad_up.astype(bf)
    raw_down = mm(hidden, cotangent, 0, 0).astype(bf)
    raw_gate = mm(grad_gate, normed_two, 0, 0).astype(bf)
    raw_up = mm(grad_up, normed_two, 0, 0).astype(bf)
    grad_norm_two = mm(grad_gate, wg, 1, 0) + mm(grad_up, wu, 1, 0)
    grad_middle_part, gain_two_part = jax.vjp(norm_rows, middle, gain_two)[1](grad_norm_two)
    grad_middle = cotangent.astype(jnp.float32) + grad_middle_part
    grad_attn = grad_middle.astype(bf)
    grad_context = mm(grad_attn, wo, 1, 1).astype(bf)
    raw_out = mm(context, grad_attn, 0, 0).astype(bf)

    grad_q, grad_k, grad_v, grad_strips = attend_back(
        lengths, place, strips, q, k, kt, v, context, grad_context, lse, limit, TQ, TK, HP
    )
    grad_rel = jnp.dot(hot.T, sum_strips(grad_strips).T, precision=HIGH)
    raw_q = mm(grad_q, normed_one, 0, 0).astype(bf)
    raw_k = mm(grad_k, rows_one, 0, 0).astype(bf)
    raw_v = mm(grad_v, rows_one, 0, 0).astype(bf)
    grad_rows = (mm(grad_k, wk, 1, 0) + mm(grad_v, wv, 1, 0)).astype(bf)
    own_part = mm(grad_q, wq, 1, 0)
    gain_one_part = (
        jnp.sum(grad_rows.astype(jnp.float32) * rows_one.astype(jnp.float32), axis=0)
        + jnp.sum(own_part * normed_one.astype(jnp.float32), axis=0)
    ) / gain_one

    rel_rows = -(-(kinds * heads) // width)
    rel_flat = jnp.pad(grad_rel.reshape(-1), (0, rel_rows * width - kinds * heads)).reshape(rel_rows, width)
    small = jnp.concatenate([gain_one_part[None], gain_two_part[None], rel_flat], axis=0)
    small_rows = -(-small.shape[0] // 8) * 8
    small = jnp.pad(small, ((0, small_rows - small.shape[0]), (0, 0)))
    scale = (total * batches) ** -0.5
    one_group = batches == GROUP
    half = inner // 2
    part = hidden_rows // GROUP
    grads_a = jnp.stack([raw_q, raw_k, raw_v, raw_out]).reshape(2, 2, count, 2, half, width)
    grads_f = [one.reshape(count, 2, 2, 2, part, width) for one in (raw_gate, raw_up, raw_down)]
    grad_norm_one, full_a, full_f, side, summed = reduce(
        grad_rows.reshape(count, own, width), grads_a, grads_f, small, count, radius, scale, one_group
    )
    full_a = full_a.reshape(4, inner, width)
    full_f = full_f.reshape(3, hidden_rows, width)
    summed = summed * scale
    if not one_group:
        full_a, full_f, summed = lax.psum((full_a, full_f, summed), "batch")
        full_a, full_f, summed = full_a * (scale / GROUP), full_f * (scale / GROUP), summed / GROUP
        side = lax.psum(jnp.concatenate([jnp.sum(full_a * full_a, axis=1), jnp.sum(full_f * full_f, axis=1)]), "mp")
    grad_input_part = jax.vjp(lambda one: norm_rows(one, gain_one), inputs)[1](grad_norm_one + own_part)[0]
    grad_tokens = (grad_middle + grad_input_part).astype(bf)

    inner_total = float(inner * count)
    hidden_total = float(hidden_rows * count)
    stat_model = jnp.stack([side[0] / inner_total, side[1] / inner_total, side[2] / inner_total, side[3] / inner_total, side[6] / hidden_total]) + TINY
    stat_ffn_rows = side[4:6] / hidden_total + TINY
    stat_heads = jnp.mean(full_a * full_a, axis=2) + TINY
    stat_hidden = jnp.mean(full_f * full_f, axis=2) + TINY
    rel_sum = summed[2 : 2 + rel_rows].reshape(-1)[: kinds * heads].reshape(kinds, heads)
    rel_mine = lax.dynamic_slice_in_dim(rel_sum, lax.axis_index("mp") * rel_table.shape[1], rel_table.shape[1], 1)
    return (
        layer_out,
        grad_tokens,
        full_a[0].T,
        full_a[1].T,
        full_a[2].T,
        full_a[3],
        full_f[0].T,
        full_f[1].T,
        full_f[2],
        rel_mine,
        summed[0],
        summed[1],
        stat_model,
        stat_heads,
        stat_hidden,
        stat_ffn_rows,
    )


TQ = 512
TK = 256
HP = 2


def solution(mesh):
    in_specs = (
        P(("batch", "mp"), None),
        P(("batch", "mp"), None),
        P("batch", None),
        P(),
        P(None, "mp"),
        P(None, "mp"),
        P(None, "mp"),
        P("mp", None),
        P(None, "mp"),
        P(None, "mp"),
        P("mp", None),
        P(None, "mp"),
        P(),
        P(),
    )
    out_specs = (
        P(("batch", "mp"), None),
        P(("batch", "mp"), None),
        P(None, "mp"),
        P(None, "mp"),
        P(None, "mp"),
        P("mp", None),
        P(None, "mp"),
        P(None, "mp"),
        P("mp", None),
        P(None, "mp"),
        P(),
        P(),
        P(),
        P(None, "mp"),
        P(None, "mp"),
        P(),
    )
    return jax.shard_map(
        on_device, mesh=mesh, in_specs=in_specs, out_specs=out_specs, check_vma=False
    )
```

```python
import functools

import jax
import jax.numpy as jnp
from jax import lax
from jax.experimental import pallas as pl
from jax.experimental.pallas import tpu as pltpu
from jax.sharding import PartitionSpec as P

TINY = 1e-30

NEG = -1e9
LANES = 128

def strip_sizes(limit, tq):
    reach = -(-limit // LANES)
    nq = tq // LANES
    off = LANES * (reach + nq)
    return reach, off, off + LANES * reach + tq

def bucket_kinds(buckets, tq):
    limit = (buckets.shape[0] + 1) // 2
    _, off, width = strip_sizes(limit, tq)
    back = lax.rev(buckets, (0,))
    shift = off - (limit - 1)
    left = jnp.broadcast_to(back[:1], (shift,))
    right = jnp.broadcast_to(back[-1:], (width - shift - back.shape[0],))
    return jnp.concatenate([left, back, right])


def ends_list(lens_ref, rows_dev, count):
    total = jnp.int32(0)
    ends = []
    for r in range(rows_dev):
        for c in range(count):
            total = total + lens_ref[r, c]
            ends.append(total)
    return ends

def segment_of(place, ends, count):
    seg = jnp.zeros_like(place)
    pad = jnp.zeros_like(place)
    for n, end in enumerate(ends):
        past = place >= end
        seg = seg + jnp.where(past, 1, 0)
        if n % count == count - 2:
            pad = pad + jnp.where(past, 1, 0)
        if n % count == count - 1:
            pad = pad - jnp.where(past, 1, 0)
    return jnp.where(pad > 0, place + 4096, seg)

def key_range(first, last, ends, count, low_end, high_end, tk):
    low = jnp.int32(0)
    high = ends[-1]
    for n, end in enumerate(ends):
        is_pad_next = n % count == count - 2
        low = jnp.where(first >= end, jnp.maximum(low, first if is_pad_next else end), low)
    for n in range(len(ends) - 1, -1, -1):
        is_pad = n % count == count - 1
        high = jnp.where(last < ends[n], (last + 1) if is_pad else ends[n], high)
    low = (low // LANES) * LANES
    steps = (high - low + tk - 1) // tk
    low = jnp.minimum(low, high_end - steps * tk)
    return pl.multiple_of(low, LANES), steps

def window(place_ref, own, total, limit):
    first = place_ref[0]
    radius = -(-(limit - 1) // own)
    return jnp.maximum(first - radius * own, 0), jnp.minimum(first + (radius + 1) * own, total)

def fill_segments(kseg, ends, count, total):
    def one(n, _):
        at = pl.multiple_of(n * 256, 256)
        place = at + lax.broadcasted_iota(jnp.int32, (256, LANES), 0)
        kseg[pl.ds(at, 256), :] = segment_of(place, ends, count)
        return 0
    lax.fori_loop(0, total // 256, one, 0)

def tile_lanes(x, n):
    return x if n == 1 else jnp.concatenate([x] * n, axis=1)

def lane_start(ks, q_at, g, reach, off, nq):
    d = (ks - q_at) // LANES + g
    return pl.multiple_of(off - LANES * jnp.clip(d, -reach, reach + nq - 1), LANES)

def fwd_kernel(cfg, lens_ref, place_ref, strip, q_ref, k_ref, vt_ref, ctx_ref, lse_ref, kseg):
    tq, tk, limit, rows_dev, count, own, total, hp = cfg
    reach, off, width = strip_sizes(limit, tq)
    nq = tq // LANES
    ends = ends_list(lens_ref, rows_dev, count)
    @pl.when(pl.program_id(0) == 0)
    def _():
        fill_segments(kseg, ends, count, total)
    w_low, w_high = window(place_ref, own, total, limit)
    lane = lax.broadcasted_iota(jnp.int32, (tq, LANES), 1)
    for qt in range(own // tq):
        rows = slice(qt * tq, (qt + 1) * tq)
        q_at = place_ref[0] + qt * tq
        halves = []
        for h in range(hp):
            q2 = q_ref[rows, h // 2 * LANES : h // 2 * LANES + LANES]
            halves.append(jnp.where((lane < 64) == (h % 2 == 0), q2, jnp.zeros_like(q2)))
        qseg = segment_of(q_at + lax.broadcasted_iota(jnp.int32, (1, tq), 1), ends, count)
        low, steps = key_range(q_at, q_at + tq - 1, ends, count, w_low, w_high, tk)
        def step(c, carry):
            ks = pl.multiple_of(low + c * tk, LANES)
            same = tile_lanes(kseg[pl.ds(ks, tk), :], nq) == qseg
            starts = [lane_start(ks, q_at, g, reach, off, nq) for g in range(tk // LANES)]
            out = []
            for h in range(hp):
                top, tot, acc = carry[h]
                kc = k_ref[pl.ds(ks, tk), h // 2 * LANES : h // 2 * LANES + LANES]
                s = lax.dot_general(kc, halves[h], (((1,), (1,)), ((), ())), preferred_element_type=jnp.float32)
                bias = jnp.concatenate([strip[h, :, pl.ds(at, tq)] for at in starts], axis=0)
                s = jnp.where(same, s + bias, NEG)
                new = jnp.maximum(top, jnp.max(s, axis=0, keepdims=True))
                p = jnp.exp(s - new)
                fade = jnp.exp(top - new)
                tot = tot * fade + jnp.sum(p, axis=0, keepdims=True)
                acc = acc * fade + jnp.dot(vt_ref[h * 64 : h * 64 + 64, pl.ds(ks, tk)], p.astype(jnp.bfloat16), preferred_element_type=jnp.float32)
                out.append((new, tot, acc))
            return tuple(out)
        zero = (jnp.full((1, tq), 2 * NEG, jnp.float32), jnp.zeros((1, tq), jnp.float32), jnp.zeros((64, tq), jnp.float32))
        res = lax.fori_loop(0, steps, step, (zero,) * hp)
        for pair in range(hp // 2):
            both = jnp.concatenate([res[h][2] / res[h][1] for h in (2 * pair, 2 * pair + 1)], axis=0)
            ctx_ref[rows, pair * LANES : pair * LANES + LANES] = both.T.astype(jnp.bfloat16)
        for h in range(hp):
            lse_ref[0, h : h + 1, rows] = res[h][0] + jnp.log(res[h][1])


def attend(lengths, place, strips, q, k, vt, limit, tq, tk, hp):
    own, inner = q.shape
    total = k.shape[0]
    steps = inner // 64 // hp
    lanes = hp * 64
    rows_dev, count = lengths.shape
    width = strips.shape[2]
    cfg = (tq, tk, limit, rows_dev, count, own, total, hp)
    smem = pl.BlockSpec(memory_space=pltpu.SMEM)
    return pl.pallas_call(
        functools.partial(fwd_kernel, cfg),
        grid=(steps,),
        in_specs=[smem, smem,
            pl.BlockSpec((hp, LANES, width), lambda p: (p, 0, 0)),
            pl.BlockSpec((own, lanes), lambda p: (0, p)),
            pl.BlockSpec((total, lanes), lambda p: (0, p)),
            pl.BlockSpec((lanes, total), lambda p: (p, 0))],
        out_specs=[pl.BlockSpec((own, lanes), lambda p: (0, p)),
                   pl.BlockSpec((1, hp, own), lambda p: (p, 0, 0))],
        out_shape=[jax.ShapeDtypeStruct((own, inner), jnp.bfloat16), jax.ShapeDtypeStruct((steps, hp, own), jnp.float32)],
        scratch_shapes=[pltpu.VMEM((total, LANES), jnp.int32)],
        compiler_params=pltpu.CompilerParams(vmem_limit_bytes=56 * 2**20),
        name="attend",
    )(lengths, place, strips, q, k, vt)


def bwd_kernel(cfg, lens_ref, place_ref, strip, q_ref, k_ref, kt_ref, v_ref, ctx_ref, do_ref, lse_ref,
               dq_ref, dk_ref, dv_ref, dstrip, kseg, dk_acc, dv_acc):
    tq, tk, limit, rows_dev, count, own, total, hp = cfg
    reach, off, width = strip_sizes(limit, tq)
    nq = tq // LANES
    ends = ends_list(lens_ref, rows_dev, count)
    @pl.when(pl.program_id(0) == 0)
    def _():
        fill_segments(kseg, ends, count, total)
    dstrip[...] = jnp.zeros_like(dstrip)
    dk_acc[...] = jnp.zeros_like(dk_acc)
    dv_acc[...] = jnp.zeros_like(dv_acc)
    w_low, w_high = window(place_ref, own, total, limit)
    lane = lax.broadcasted_iota(jnp.int32, (tq, LANES), 1)
    for qt in range(own // tq):
        rows = slice(qt * tq, (qt + 1) * tq)
        q_at = place_ref[0] + qt * tq
        q_half, do_half, delta, lse = [], [], [], []
        for pair in range(hp // 2):
            lanes = slice(pair * LANES, pair * LANES + LANES)
            q2 = q_ref[rows, lanes]
            do2 = do_ref[rows, lanes]
            prod = (do2.astype(jnp.float32) * ctx_ref[rows, lanes].astype(jnp.float32)).T
            for hh in range(2):
                keep = (lane < 64) == (hh == 0)
                q_half.append(jnp.where(keep, q2, jnp.zeros_like(q2)))
                do_half.append(jnp.where(keep, do2, jnp.zeros_like(do2)))
                delta.append(jnp.sum(prod[hh * 64 : hh * 64 + 64], axis=0, keepdims=True))
                lse.append(lse_ref[0, 2 * pair + hh : 2 * pair + hh + 1, rows])
        qseg = segment_of(q_at + lax.broadcasted_iota(jnp.int32, (1, tq), 1), ends, count)
        low, steps = key_range(q_at, q_at + tq - 1, ends, count, w_low, w_high, tk)
        def step(c, carry):
            ks = pl.multiple_of(low + c * tk, LANES)
            same = tile_lanes(kseg[pl.ds(ks, tk), :], nq) == qseg
            starts = [lane_start(ks, q_at, g, reach, off, nq) for g in range(tk // LANES)]
            out = []
            for pair in range(hp // 2):
                lanes = slice(pair * LANES, pair * LANES + LANES)
                kc = k_ref[pl.ds(ks, tk), lanes]
                vc = v_ref[pl.ds(ks, tk), lanes]
                dk_part = dv_part = None
                for h in (2 * pair, 2 * pair + 1):
                    s = lax.dot_general(kc, q_half[h], (((1,), (1,)), ((), ())), preferred_element_type=jnp.float32)
                    bias = jnp.concatenate([strip[h, :, pl.ds(at, tq)] for at in starts], axis=0)
                    p = jnp.exp(jnp.where(same, s + (bias - lse[h]), NEG))
                    dp = lax.dot_general(vc, do_half[h], (((1,), (1,)), ((), ())), preferred_element_type=jnp.float32)
                    ds = p * (dp - delta[h])
                    for g, at in enumerate(starts):
                        dstrip[h, :, pl.ds(at, tq)] += ds[g * LANES : (g + 1) * LANES, :]
                    pb = p.astype(jnp.bfloat16)
                    dsb = ds.astype(jnp.bfloat16)
                    dv_one = jnp.dot(pb, do_half[h], preferred_element_type=jnp.float32)
                    dk_one = jnp.dot(dsb, q_half[h], preferred_element_type=jnp.float32)
                    dv_part = dv_one if dv_part is None else dv_part + dv_one
                    dk_part = dk_one if dk_part is None else dk_part + dk_one
                    out.append(carry[h] + jnp.dot(kt_ref[h * 64 : h * 64 + 64, pl.ds(ks, tk)], dsb, preferred_element_type=jnp.float32))
                dv_acc[pl.ds(ks, tk), lanes] += dv_part
                dk_acc[pl.ds(ks, tk), lanes] += dk_part
            return tuple(out)
        zero = jnp.zeros((64, tq), jnp.float32)
        res = lax.fori_loop(0, steps, step, (zero,) * hp)
        for pair in range(hp // 2):
            dq_ref[rows, pair * LANES : pair * LANES + LANES] = jnp.concatenate(res[2 * pair : 2 * pair + 2], axis=0).T.astype(jnp.bfloat16)
    dk_ref[...] = dk_acc[...].astype(jnp.bfloat16)
    dv_ref[...] = dv_acc[...].astype(jnp.bfloat16)


def attend_back(lengths, place, strips, q, k, kt, v, ctx, do, lse, limit, tq, tk, hp):
    own, inner = q.shape
    total = k.shape[0]
    steps = inner // 64 // hp
    lanes = hp * 64
    rows_dev, count = lengths.shape
    width = strips.shape[2]
    cfg = (tq, tk, limit, rows_dev, count, own, total, hp)
    smem = pl.BlockSpec(memory_space=pltpu.SMEM)
    tall = pl.BlockSpec((total, lanes), lambda p: (0, p))
    short = pl.BlockSpec((own, lanes), lambda p: (0, p))
    band = pl.BlockSpec((hp, LANES, width), lambda p: (p, 0, 0))
    return pl.pallas_call(
        functools.partial(bwd_kernel, cfg),
        grid=(steps,),
        in_specs=[smem, smem, band,
            short, tall, pl.BlockSpec((lanes, total), lambda p: (p, 0)), tall, short, short,
            pl.BlockSpec((1, hp, own), lambda p: (p, 0, 0))],
        out_specs=[short, tall, tall, band],
        out_shape=[jax.ShapeDtypeStruct((own, inner), jnp.bfloat16), jax.ShapeDtypeStruct((total, inner), jnp.bfloat16),
                   jax.ShapeDtypeStruct((total, inner), jnp.bfloat16), jax.ShapeDtypeStruct(strips.shape, jnp.float32)],
        scratch_shapes=[pltpu.VMEM((total, LANES), jnp.int32),
                        pltpu.VMEM((total, lanes), jnp.float32), pltpu.VMEM((total, lanes), jnp.float32)],
        compiler_params=pltpu.CompilerParams(vmem_limit_bytes=60 * 2**20),
        name="attend_back",
    )(lengths, place, strips, q, k, kt, v, ctx, do, lse)


MESH = pl.DeviceIdType.MESH
GROUP = 8


def flip(index, bit):
    return index + bit * (1 - 2 * ((index // bit) % 2))


class Links:
    def __init__(self, send_sems, recv_sems, batch, place):
        self.send_sems, self.recv_sems = send_sems, recv_sems
        self.batch, self.place = batch, place
        self.slots = {}
        self.sent = []

    def slot(self, key):
        return self.slots.setdefault(key, len(self.slots))

    def copy(self, key, src, dst, target):
        n = self.slot(key)
        return pltpu.make_async_remote_copy(
            src_ref=src, dst_ref=dst, send_sem=self.send_sems.at[n], recv_sem=self.recv_sems.at[n],
            device_id=target, device_id_type=MESH)

    def send(self, key, src, dst, target, when=None):
        def go():
            self.copy(key, src, dst, target).start()
        self.sent.append((key, src, dst, target, when))
        if when is None:
            go()
        else:
            pl.when(when)(go)

    def take(self, key, dst, when=None, then=None):
        def go():
            self.copy(key, dst, dst, (self.batch, self.place)).wait_recv()
            if then is not None:
                then()
        if when is None:
            go()
        else:
            pl.when(when)(go)

    def drain(self):
        for key, src, dst, target, when in self.sent:
            def go():
                self.copy(key, src, dst, target).wait_send()
            if when is None:
                go()
            else:
                pl.when(when)(go)


def greet(batch, place, count):
    bar = pltpu.get_barrier_semaphore()
    for bit in (1, 2, 4):
        pl.semaphore_signal(bar, inc=1, device_id=(flip(batch, bit), place), device_id_type=MESH)
    for way in range(1 - count, count):
        if way != 0:
            @pl.when((place + way >= 0) & (place + way < count))
            def _():
                pl.semaphore_signal(bar, inc=1, device_id=(batch, place + way), device_id_type=MESH)
    pl.semaphore_wait(bar, 3 + count - 1)


def both(a, b):
    return a if b is None else (b if a is None else a & b)


class PlaneGather:
    def __init__(self, links, key, view, ref, sub, when=None):
        self.l, self.key, self.view, self.ref, self.sub, self.when = links, key, view, ref, sub, when

    def put(self, path, sub, half, bit):
        region = self.view(self.ref, sub, half)
        self.l.send((self.key, path), region, region, (flip(self.l.batch, bit), self.l.place), self.when)

    def start(self):
        self.put("x", self.sub, None, 2)
        self.put("y", self.sub, None, 4)
        self.put("c", self.sub, None, 1)

    def middle(self):
        sub = self.sub
        self.l.take((self.key, "x"), self.view(self.ref, flip(sub, 2), None), self.when)
        self.put("xy", flip(sub, 2), 0, 4)
        self.put("xc", flip(sub, 2), None, 1)
        self.l.take((self.key, "y"), self.view(self.ref, flip(sub, 4), None), self.when)
        self.put("yx", flip(sub, 4), 1, 2)
        self.put("yc", flip(sub, 4), None, 1)

    def far(self):
        sub = self.sub
        diagonal = flip(flip(sub, 2), 4)
        self.l.take((self.key, "xy"), self.view(self.ref, diagonal, 0), self.when)
        self.put("0c", diagonal, 0, 1)
        self.l.take((self.key, "yx"), self.view(self.ref, diagonal, 1), self.when)
        self.put("1c", diagonal, 1, 1)

    def end(self):
        sub = flip(self.sub, 1)
        diagonal = flip(flip(sub, 2), 4)
        self.l.take((self.key, "c"), self.view(self.ref, sub, None), self.when)
        self.l.take((self.key, "xc"), self.view(self.ref, flip(sub, 2), None), self.when)
        self.l.take((self.key, "yc"), self.view(self.ref, flip(sub, 4), None), self.when)
        self.l.take((self.key, "0c"), self.view(self.ref, diagonal, 0), self.when)
        self.l.take((self.key, "1c"), self.view(self.ref, diagonal, 1), self.when)


def half_rows(half, rows):
    return pl.ds(0, rows) if half is None else pl.ds(half * (rows // 2), rows // 2)


PIECES = 4
EPS = 1e-06


def unit_norm(values):
    return lax.rsqrt(jnp.mean(values * values, axis=1, keepdims=True) + EPS)


def dot_nt(a, b):
    return lax.dot_general(a, b, (((1,), (1,)), ((), ())), preferred_element_type=jnp.float32)


def dot_nn(a, b):
    return jnp.dot(a, b, preferred_element_type=jnp.float32)


def gather_kernel(count, radius, tok_ref, gain_ref, wa_ref, wf_ref, rel_ref, kinds_ref,
                  xs_out, was_out, wfs_ref, q_out, k_out, kt_out, v_out, vt_out, strips_out,
                  xs, was, q_v, k_v, kt_v, v_v, vt_v, rel_all, table, strip_v, send_sems, recv_sems, local_sems):
    batch, place = lax.axis_index("batch"), lax.axis_index("mp")
    sub = batch % GROUP
    links = Links(send_sems, recv_sems, batch, place)
    own, width = tok_ref.shape
    rows_a = wa_ref.shape[2]
    rows_f = wf_ref.shape[2]
    step = own // PIECES
    local = []

    def copy_local(src, dst):
        one = pltpu.make_async_copy(src, dst, local_sems.at[len(local)])
        local.append(one)
        return one

    own_a = copy_local(wa_ref, was.at[:, place])
    own_a.start()
    copy_local(wf_ref, wfs_ref.at[:, place]).start()
    for p in range(PIECES):
        rows = pl.ds(p * step, step)
        values = tok_ref[rows, :].astype(jnp.float32)
        xs[place, rows] = (values * unit_norm(values) * gain_ref[...]).astype(xs.dtype)
    greet(batch, place, count)

    def view_a(mm):
        return lambda ref, s, half: ref.at[s // 2, mm, s % 2, half_rows(half, rows_a)]

    def view_f(mm):
        return lambda ref, s, half: ref.at[:, mm, s, half_rows(half, rows_f)]

    def inside(n):
        return (n >= 0) & (n < count)

    for way in (1, -1):
        ok = inside(place + way)
        target = (batch, place + way)
        links.send(("a", way, 1), wa_ref.at[sub // 2, sub % 2], view_a(place)(was, sub, None), target, ok)
        links.send(("f", way, 1), wf_ref.at[:, sub], view_f(place)(wfs_ref, sub, None), target, ok)
    for d in range(1, count):
        for way in (1, -1):
            links.send(("r", way, d), rel_ref, rel_all.at[place], (batch, place + way * d), inside(place + way * d))
    for way in (1, -1):
        ok = inside(place + way)
        target = (batch, place + way)
        for p in range(PIECES):
            rows = pl.ds(p * step, step)
            links.send(("x", way, 1, p), xs.at[place, rows], xs.at[place, rows], target, ok)
    for n in range(count):
        @pl.when((n - place > radius) | (place - n > radius))
        def _():
            def blank(p, _):
                xs[n, pl.ds(p * step, step)] = jnp.zeros((step, width), xs.dtype)
                return 0
            lax.fori_loop(0, PIECES, blank, 0)
            for ref in (k_v, v_v):
                ref[pl.ds(n * own, own)] = jnp.zeros((own, ref.shape[1]), ref.dtype)
            for ref in (kt_v, vt_v):
                ref[:, pl.ds(n * own, own)] = jnp.zeros((ref.shape[0], own), ref.dtype)

    gathers = {}

    def weights_arrive(kind, dist):
        for way in (1, -1):
            source = place - way * dist
            ok = inside(source)
            view, ref = (view_a(source), was) if kind == "a" else (view_f(source), wfs_ref)
            region = view(ref, sub, None)
            links.take((kind, way, dist), region, ok)
            if dist < count - 1:
                links.send((kind, way, dist + 1), region, region, (batch, place + way), ok & inside(place + way))
            gather = PlaneGather(links, ("g", kind, way, dist), view, ref, sub, ok)
            gather.start()
            gathers[kind, way, dist] = gather

    def x_arrive(dist, p):
        for way in (1, -1):
            source = place - way * dist
            ok = inside(source)
            region = xs.at[source, pl.ds(p * step, step)]
            links.take(("x", way, dist, p), region, ok)
            if dist < radius:
                links.send(("x", way, dist + 1, p), region, region, (batch, place + way), ok & inside(place + way))

    def stage(name, kind, dist):
        for way in (1, -1):
            getattr(gathers[kind, way, dist], name)()

    heads_own = rel_ref.shape[0] // 8 * 8
    heads = table.shape[0]
    span = table.shape[1]
    kinds = rel_ref.shape[1]

    def make_table():
        rel_all[place] = rel_ref[...]
        for d in range(1, count):
            for way in (1, -1):
                links.take(("r", way, d), rel_all.at[place - way * d], inside(place - way * d))
        per = heads // count
        joined = jnp.concatenate([rel_all[n, 0:per, :] for n in range(count)], axis=0)
        for at in range(0, span, 512):
            lanes = pl.ds(at, min(512, span - at))
            kind = kinds_ref[:, lanes]
            total = jnp.zeros((heads, kind.shape[1]), jnp.float32)
            for b in range(NB_MAX):
                if b < kinds:
                    total = total + jnp.where(kind == b, joined[:, b : b + 1], 0.0)
            table[:, lanes] = total

    strip_copies = []

    def make_strip(h):
        slot = h % 2
        if h >= 2:
            strip_copies[h - 2].wait()
        row = table[h : h + 1, :]
        strip_v[slot] = pltpu.roll(jnp.broadcast_to(row, (LANES, span)), 0, 1, stride=1, stride_axis=0)
        one = pltpu.make_async_copy(strip_v.at[slot], strips_out.at[h], local_sems.at[8 + slot])
        one.start()
        strip_copies.append(one)

    inner = was.shape[1] * was.shape[2] * rows_a

    def weight_tile(kind, n):
        return was[kind, n].reshape(2 * rows_a, width)

    def project(block, when):
        def go():
            x = xs[block]
            def one(n, _):
                at = pl.multiple_of(n * 2 * rows_a, 64)
                kt_v[pl.ds(at, 2 * rows_a), pl.ds(pl.multiple_of(block * own, LANES), own)] = dot_nt(weight_tile(1, n), x).astype(kt_v.dtype)
                vt_v[pl.ds(at, 2 * rows_a), pl.ds(pl.multiple_of(block * own, LANES), own)] = dot_nt(weight_tile(2, n), x).astype(vt_v.dtype)
                return 0
            lax.fori_loop(0, count, one, 0)
            rows = pl.ds(pl.multiple_of(block * own, LANES), own)
            tile = 256
            for at in range(0, inner, tile):
                wk = was[1].reshape(inner, width)[at : at + tile]
                wv = was[2].reshape(inner, width)[at : at + tile]
                k_v[rows, at : at + tile] = dot_nt(x, wk).astype(k_v.dtype)
                v_v[rows, at : at + tile] = dot_nt(x, wv).astype(v_v.dtype)
        if when is None:
            go()
        else:
            pl.when(when)(go)

    def project_q():
        x = xs[place]
        tile = 256
        for at in range(0, inner, tile):
            wq = was[0].reshape(inner, width)[at : at + tile]
            q_v[:, at : at + tile] = dot_nt(x, wq).astype(q_v.dtype)

    dists = range(1, count)
    make_table()
    for h in range(2):
        make_strip(h)
    for d in dists:
        weights_arrive("a", d)
    weights_arrive("f", 1)
    for h in range(2, 5):
        make_strip(h)
    for d in dists:
        stage("middle", "a", d)
    for p in range(PIECES):
        x_arrive(1, p)
        if p + 2 < count:
            weights_arrive("f", p + 2)
        if p == 1:
            stage("middle", "f", 1)
    for d in dists:
        stage("far", "a", d)
    for d in range(2, count):
        stage("middle", "f", d)
    for d in dists:
        stage("far", "f", d)
    for d in dists:
        stage("end", "a", d)
    own_a.wait()
    copy_local(was, was_out).start()
    project_q()
    copy_local(q_v, q_out).start()
    project(place, None)
    for h in range(5, heads):
        make_strip(h)
    for way in (1, -1):
        project(place + way, inside(place + way))
    for r in range(2, radius + 1):
        for p in range(PIECES):
            x_arrive(r, p)
        for way in (1, -1):
            project(place + way * r, inside(place + way * r))
    copy_local(xs, xs_out).start()
    for src, dst in ((k_v, k_out), (kt_v, kt_out), (v_v, v_out), (vt_v, vt_out)):
        copy_local(src, dst).start()
    for d in dists:
        stage("end", "f", d)
    links.drain()
    for one in local[1:] + strip_copies[-2:]:
        one.wait()


NB_MAX = 128


def gather(tokens, gain, wa, wf, rel, kinds, count, radius, heads):
    own, width = tokens.shape
    bf = jnp.bfloat16
    total = own * count
    inner = count * 2 * wa.shape[2]
    span = kinds.shape[1]
    vm = pl.BlockSpec(memory_space=pltpu.VMEM)
    hb = pl.BlockSpec(memory_space=pl.ANY)
    shapes = [
        ((count, own, width), bf),
        ((4, count, 2, wa.shape[2], width), bf),
        ((3, count, GROUP, wf.shape[2], width), bf),
        ((own, inner), bf), ((total, inner), bf), ((inner, total), bf), ((total, inner), bf), ((inner, total), bf),
        ((heads, LANES, span), jnp.float32),
    ]
    return pl.pallas_call(
        functools.partial(gather_kernel, count, radius),
        in_specs=[vm, vm, hb, hb, vm, vm],
        out_specs=[hb] * len(shapes),
        out_shape=[jax.ShapeDtypeStruct(*one) for one in shapes],
        scratch_shapes=[pltpu.VMEM(*shapes[n]) for n in (0, 1, 3, 4, 5, 6, 7)] + [
            pltpu.VMEM((count,) + rel.shape, jnp.float32),
            pltpu.VMEM((heads, span), jnp.float32),
            pltpu.VMEM((2, LANES, span), jnp.float32),
            pltpu.SemaphoreType.DMA((170,)),
            pltpu.SemaphoreType.DMA((170,)),
            pltpu.SemaphoreType.DMA((10,)),
        ],
        compiler_params=pltpu.CompilerParams(collective_id=1, has_side_effects=True, vmem_limit_bytes=60 * 2**20),
        name="gather",
    )(tokens, gain, wa, wf, rel, kinds)


def ffn_kernel(count, tok_ref, cot_ref, ctx_ref, gain_ref, was_ref, wfs_ref,
               out_ref, middle_ref, do_ref, raw_out_ref, gain_out, keep_out, fx_out, fy_out,
               wo, wf, normed, middle, acc_out, acc_back, raw, got, send_sems, recv_sems, local_sems):
    batch, place = lax.axis_index("batch"), lax.axis_index("mp")
    sub = batch % GROUP
    core, xx, yy = sub % 2, (sub // 2) % 2, sub // 4
    links = Links(send_sems, recv_sems, batch, place)
    sibling = (flip(batch, 1), place)
    own, width = tok_ref.shape
    hidden = wf.shape[1]
    per = hidden // count
    part = per // GROUP
    half = part // 2
    bf = jnp.bfloat16
    loads = [pltpu.make_async_copy(was_ref.at[3], wo, local_sems.at[0])]
    loads += [pltpu.make_async_copy(wfs_ref.at[t], wf.at[t], local_sems.at[1 + t]) for t in range(3)]
    for one in loads:
        one.start()
    bar = pltpu.get_barrier_semaphore()
    pl.semaphore_signal(bar, inc=1, device_id=sibling, device_id_type=MESH)
    loads[0].wait()
    tile = 256
    for at in range(0, own, tile):
        rows = slice(at, at + tile)
        mid = tok_ref[rows, :].astype(jnp.float32) + dot_nn(ctx_ref[rows, :], wo[...])
        middle[rows, :] = mid
        normed[rows, :] = (mid * unit_norm(mid) * gain_ref[...]).astype(bf)
    for one in loads[1:]:
        one.wait()
    pl.semaphore_wait(bar, 1)

    def units(n, _):
        for r in range(per // tile):
            at = pl.multiple_of(n * per + r * tile, tile)
            rows = pl.ds(at, tile)
            x, dy = normed[...], cot_ref[...]
            gate, up = dot_nt(x, wf[0, rows, :]), dot_nt(x, wf[1, rows, :])
            back = dot_nt(dy, wf[2, rows, :])
            cubed = 0.044715 * (gate * gate)
            t = jnp.tanh(0.7978845608028654 * gate * (1.0 + cubed))
            gelu = 0.5 * gate * (1.0 + t)
            slope = 0.5 * (1.0 + t) + 0.5 * gate * (1.0 - t * t) * (0.7978845608028654 * (1.0 + 3.0 * cubed))
            hid = (gelu * up).astype(bf)
            d_gate = (back * up * slope).astype(bf)
            d_up = (back * gelu).astype(bf)
            first = (n == 0) & (r == 0)
            part_out = dot_nn(hid, wf[2, rows, :])
            part_back = dot_nn(d_gate, wf[0, rows, :]) + dot_nn(d_up, wf[1, rows, :])
            acc_out[...] = jnp.where(first, part_out, acc_out[...] + part_out)
            acc_back[...] = jnp.where(first, part_back, acc_back[...] + part_back)
            for t_id, left, right in ((0, d_gate, x), (1, d_up, x), (2, hid, dy)):
                value = dot_nn(left.T, right).astype(bf)
                for s in range(tile // part):
                    unit = r * (tile // part) + s
                    raw[t_id, n, unit // 2, unit % 2] = value[s * part : (s + 1) * part]
        return 0

    for n in range(count):
        units(jnp.int32(n), 0)
        for t in range(3):
            links.send(("f1", t, n), raw.at[t, n, :, 1 - core], got.at[t, n], sibling)
    for at in range(0, own, tile):
        rows = slice(at, at + tile)
        mid = middle[rows, :]
        out_ref[rows, :] = (mid + acc_out[rows, :]).astype(bf)
        s = unit_norm(mid)
        n2 = mid * s
        gn = acc_back[rows, :]
        e = gn * gain_ref[...]
        grad = cot_ref[rows, :].astype(jnp.float32) + s * (e - n2 * jnp.mean(e * n2, axis=1, keepdims=True))
        middle_ref[rows, :] = grad
        normed[rows, :] = grad.astype(bf)
        gain = jnp.sum(gn * n2, axis=0, keepdims=True)
        gain_out[...] = gain if at == 0 else gain_out[...] + gain
    for at in range(0, width, tile):
        cols = slice(at, at + tile)
        do_ref[:, cols] = dot_nt(normed[...], wo[cols, :]).astype(bf)
        raw_out_ref[cols, :] = dot_nn(ctx_ref[:, cols].T, normed[...]).astype(bf)
    saves = []
    for t in range(3):
        for n in range(count):
            links.take(("f1", t, n), got.at[t, n])
            for s in range(GROUP // 2):
                got[t, n, s] = got[t, n, s] + raw[t, n, s, core]
        whole = got.at[t].reshape(count, 2, 2, part, width)
        for src, dst in ((whole, keep_out.at[t]), (whole.at[:, :, 1 - xx, pl.ds(0, half)], fx_out.at[t]),
                         (whole.at[:, 1 - yy, :, pl.ds(half, half)], fy_out.at[t])):
            one = pltpu.make_async_copy(src, dst, local_sems.at[4 + len(saves)])
            one.start()
            saves.append(one)
    links.drain()
    for one in saves:
        one.wait()


def ffn(tokens, cotangent, context, gain, was, wfs, count):
    own, width = tokens.shape
    hidden = wfs.shape[1]
    part = hidden // count // GROUP
    bf = jnp.bfloat16
    vm = pl.BlockSpec(memory_space=pltpu.VMEM)
    hb = pl.BlockSpec(memory_space=pl.ANY)
    return pl.pallas_call(
        functools.partial(ffn_kernel, count),
        in_specs=[vm, vm, vm, vm, hb, hb],
        out_specs=[vm] * 5 + [hb] * 3,
        out_shape=[
            jax.ShapeDtypeStruct((own, width), bf),
            jax.ShapeDtypeStruct((own, width), jnp.float32),
            jax.ShapeDtypeStruct(context.shape, bf),
            jax.ShapeDtypeStruct((context.shape[1], width), bf),
            jax.ShapeDtypeStruct((1, width), jnp.float32),
            jax.ShapeDtypeStruct((3, count, 2, 2, part, width), bf),
            jax.ShapeDtypeStruct((3, count, 2, part // 2, width), bf),
            jax.ShapeDtypeStruct((3, count, 2, part // 2, width), bf),
        ],
        scratch_shapes=[
            pltpu.VMEM((was.shape[1], width), bf),
            pltpu.VMEM((3, hidden, width), bf),
            pltpu.VMEM((own, width), bf),
            pltpu.VMEM((own, width), jnp.float32),
            pltpu.VMEM((own, width), jnp.float32),
            pltpu.VMEM((own, width), jnp.float32),
            pltpu.VMEM((3, count, GROUP // 2, 2, part, width), bf),
            pltpu.VMEM((3, count, GROUP // 2, part, width), bf),
            pltpu.SemaphoreType.DMA((3 * count,)),
            pltpu.SemaphoreType.DMA((3 * count,)),
            pltpu.SemaphoreType.DMA((16,)),
        ],
        compiler_params=pltpu.CompilerParams(collective_id=3, has_side_effects=True, vmem_limit_bytes=60 * 2**20),
        name="ffn",
    )(tokens, cotangent, context, gain, was, wfs)


def finish_kernel(count, radius, buckets, scale, final, tok_ref, gain_ref, mid_ref, tiny_ref, kinds_ref,
                  dq_ref, dk_ref, dv_ref, xs_ref, was_ref, raw_out_ref, keep_ref, fx_ref, fy_ref, strips_ref,
                  tokens_out, model_ref, rows_ref, heads_ref, units_ref, total_ref, gq_out, gk_out, gv_out, go_out, gg_out, gu_out, gd_out,
                  dq, dk, dv, xs, wq, wk, wv, ga, got_a1, got_ax, got_ay, got_ay2, got_ax2,
                  keep_f, got_fx, got_fy, got_fy2, got_fx2, from_a, from_f, full_a, full_f,
                  gx, own_acc, got_x, rows8, small, tiny, tiny_z, side_z, strip_v, send_sems, recv_sems, local_sems):
    batch, place = lax.axis_index("batch"), lax.axis_index("mp")
    sub = batch % GROUP
    core, xx, yy = sub % 2, (sub // 2) % 2, sub // 4
    links = Links(send_sems, recv_sems, batch, place)
    rows_a, rows_f = ga.shape[4], keep_f.shape[4]
    ha, hf = rows_a // 2, rows_f // 2
    own, width = tok_ref.shape
    step = own // PIECES
    bf = jnp.bfloat16
    f32 = jnp.float32
    sibling, x_near, y_near = [(flip(batch, bit), place) for bit in (1, 2, 4)]

    def inside(n):
        return (n >= 0) & (n < count)

    used = [0]

    def load(src, dst, start=True):
        one = pltpu.make_async_copy(src, dst, local_sems.at[used[0]])
        used[0] += 1
        if start:
            one.start()
        return one

    load_f = [(load(keep_ref.at[t], keep_f.at[t]), load(fx_ref.at[t], got_fx.at[t]), load(fy_ref.at[t], got_fy.at[t])) for t in range(3)]
    load_k = [load(dk_ref, dk), load(was_ref.at[1], wk), load(dv_ref, dv), load(was_ref.at[2], wv)]
    load_x = [load(xs_ref, xs), load(dq_ref, dq), load(was_ref.at[0], wq)]
    load_o = load(raw_out_ref, ga.at[1, 1])
    heads = strips_ref.shape[0]
    load_s = {}

    def load_strip(n):
        load_s[n] = pltpu.make_async_copy(strips_ref.at[n // 2, pl.ds(n % 2 * 64, 64)], strip_v.at[n % 2], local_sems.at[40 + n % 2])
        load_s[n].start()

    load_strip(0)
    load_strip(1)

    def one_f(t):
        def go(n, _):
            for i in range(2):
                keep_f[t, n, i, xx, pl.ds(0, hf)] = keep_f[t, n, i, xx, pl.ds(0, hf)] + got_fx[t, n, i]
                keep_f[t, n, yy, i, pl.ds(hf, hf)] = keep_f[t, n, yy, i, pl.ds(hf, hf)] + got_fy[t, n, i]
            return 0
        lax.fori_loop(0, count, go, 0)

    for t in range(3):
        for one in load_f[t]:
            one.wait()
        one_f(t)
        if t == 0:
            greet(batch, place, count)
        links.send(("fy2", t), keep_f.at[t, :, 1 - yy, xx, pl.ds(0, hf)], got_fy2.at[t], y_near)
        links.send(("fx2", t), keep_f.at[t, :, yy, 1 - xx, pl.ds(hf, hf)], got_fx2.at[t], x_near)

    for one in load_k + load_x:
        one.wait()
    rows8[...] = jnp.zeros_like(rows8)

    def block_part(block, local):
        tile = 256
        for at in range(0, own, tile):
            rows = pl.ds(pl.multiple_of(block * own + at, tile), tile)
            value = dot_nn(dk[rows, :], wk[...]) + dot_nn(dv[rows, :], wv[...])
            if local:
                value = value + dot_nn(dq[at : at + tile, :], wq[...])
                own_acc[at : at + tile, :] = value
            else:
                gx[block, at : at + tile] = value.astype(bf)
            prod = value * xs[block, at : at + tile].astype(f32)
            acc = prod[0:8]
            for r in range(8, tile, 8):
                acc = acc + prod[r : r + 8]
            rows8[...] = rows8[...] + acc

    def x_send(way, level):
        for p in range(PIECES):
            rows = pl.ds(p * step, step)
            links.send(("x", way, level, p), gx.at[place + way * level, rows], got_x.at[0 if way > 0 else 1, level - 1, rows],
                       (batch, place + way), inside(place + way * level))

    for level in range(radius, 0, -1):
        for way in (1, -1):
            @pl.when(inside(place + way * level))
            def _():
                block_part(place + way * level, False)
            if level == radius:
                x_send(way, level)

    def x_step(level, p):
        rows = pl.ds(p * step, step)
        for side, way in ((0, 1), (1, -1)):
            dest = place + way * (level - 1)
            behind = inside(place - way)
            def add():
                got_x[side, level - 1, rows] = got_x[side, level - 1, rows] + gx[dest, rows]
            links.take(("x", way, level, p), got_x.at[side, level - 1, rows], behind & inside(dest), add)
            links.send(("x", way, level - 1, p), got_x.at[side, level - 1, rows], got_x.at[side, level - 2, rows],
                       (batch, place + way), behind & inside(dest))

    def x_first(level, p):
        rows = pl.ds(p * step, step)
        for side, way in ((0, 1), (1, -1)):
            dest = place + way * (level - 1)
            links.send(("x0", way, level - 1, p), gx.at[jnp.clip(dest, 0, count - 1), rows], got_x.at[side, level - 2, rows],
                       (batch, place + way), jnp.logical_not(inside(place - way)) & inside(dest))

    for level in range(radius, 1, -1):
        for p in range(PIECES):
            x_first(level, p)

    inner = wq.shape[0]

    def raw_grad(kind, left, right):
        for c in range(0, inner, 256):
            value = dot_nn(left(c).T, right()).astype(bf)
            at = c
            while at < c + 256:
                n, r = at // (2 * rows_a), at % (2 * rows_a)
                h, r = r // rows_a, r % rows_a
                size = min(rows_a - r, c + 256 - at)
                ga[kind // 2, kind % 2, n, h, r : r + size] = value[at - c : at - c + size]
                at += size
        links.send(("a1", kind), ga.at[kind // 2, kind % 2, :, 1 - core], got_a1.at[kind // 2, kind % 2], sibling)

    load_o.wait()
    links.send(("a1", 3), ga.at[1, 1, :, 1 - core], got_a1.at[1, 1], sibling)
    raw_grad(1, lambda c: dk[:, c : c + 256], lambda: xs[...].reshape(count * own, width))
    raw_grad(2, lambda c: dv[:, c : c + 256], lambda: xs[...].reshape(count * own, width))
    raw_grad(0, lambda c: dq[:, c : c + 256], lambda: xs[place])
    for level in range(radius, 1, -1):
        for p in range(PIECES):
            x_step(level, p)
    block_part(place, True)

    def last_f(t):
        links.take(("fy2", t), got_fy2.at[t])
        links.take(("fx2", t), got_fx2.at[t])
        def one(n, _):
            keep_f[t, n, yy, xx, pl.ds(0, hf)] = keep_f[t, n, yy, xx, pl.ds(0, hf)] + got_fy2[t, n]
            keep_f[t, n, yy, xx, pl.ds(hf, hf)] = keep_f[t, n, yy, xx, pl.ds(hf, hf)] + got_fx2[t, n]
            return 0
        lax.fori_loop(0, count, one, 0)

    def unit(t, n):
        return ga.at[yy, xx, n, core] if t == "a" else keep_f.at[t, n, yy, xx]

    def arrived(t, side, n):
        return from_a.at[side, n] if t == "a" else from_f.at[t, side, n]

    def line(t, hop):
        for side, way in ((0, 1), (1, -1)):
            here = place == (hop if way > 0 else count - 1 - hop)
            for n in (range(count - 1, hop, -1) if way > 0 else range(count - 1 - hop)):
                if hop > 0:
                    def add():
                        ref, more = unit(t, n), arrived(t, side, n)
                        ref[...] = ref[...] + more[...]
                    links.take(("z", t, side, n, hop - 1), arrived(t, side, n), here, add)
                links.send(("z", t, side, n, hop), unit(t, n), arrived(t, side, n), (batch, place + way), here)

    def view_a(ref, s, half):
        return ref.at[s // 2, s % 2, half_rows(half, rows_a)]

    def view_f(t):
        return lambda ref, s, half: ref.at[t, s, half_rows(half, rows_f)]

    gathers = {}

    def finish(t):
        for side, way in ((0, 1), (1, -1)):
            for hop in range(count - 1):
                n = hop + 1 if way > 0 else count - 2 - hop
                def add():
                    ref, more = unit(t, n), arrived(t, side, n)
                    ref[...] = ref[...] + more[...]
                links.take(("z", t, side, n, hop), arrived(t, side, n), place == n, add)
        if t == "a":
            view, ref = view_a, full_a
            full_a[sub // 2, sub % 2] = ga[yy, xx, place, core]
        else:
            view, ref = view_f(t), full_f
            full_f[t, sub] = keep_f[t, place, yy, xx]
        gathers[t] = PlaneGather(links, ("g", t), view, ref, sub)
        gathers[t].start()

    for t in range(3):
        last_f(t)
        line(t, 0)

    def a_core(kind):
        i, j = kind // 2, kind % 2
        links.take(("a1", kind), got_a1.at[i, j])
        for n in range(count):
            ga[i, j, n, core] = ga[i, j, n, core] + got_a1[i, j, n]

    for kind in (3, 1, 2, 0):
        a_core(kind)
    links.send(("ax",), ga.at[:, 1 - xx, :, core, pl.ds(0, ha)], got_ax, x_near)
    links.send(("ay",), ga.at[1 - yy, :, :, core, pl.ds(ha, ha)], got_ay, y_near)

    sums = {}

    def strip_sum(h):
        span = strip_v.shape[2]
        eight = None
        for n in (2 * h, 2 * h + 1):
            load_s[n].wait()
            for g in range(8):
                shift = 8 * g + 64 * (n % 2)
                part = strip_v[n % 2, 8 * g : 8 * g + 8, :]
                part = part if shift == 0 else pltpu.roll(part, span - shift, 1)
                eight = part if eight is None else eight + part
            if n + 2 < 2 * heads:
                load_strip(n + 2)
        flat = eight[0:1, :]
        for r in range(1, 8):
            flat = flat + pltpu.roll(eight[r : r + 1, :], span - r, 1)
        sums[h] = flat

    for h in range(0, heads // 2):
        strip_sum(h)
    for hop in range(1, count - 1):
        for t in range(3):
            line(t, hop)
    links.take(("ax",), got_ax)
    links.take(("ay",), got_ay)
    for n in range(count):
        for i in range(2):
            ga[i, xx, n, core, pl.ds(0, ha)] = ga[i, xx, n, core, pl.ds(0, ha)] + got_ax[i, n]
            ga[yy, i, n, core, pl.ds(ha, ha)] = ga[yy, i, n, core, pl.ds(ha, ha)] + got_ay[i, n]
    links.send(("ay2",), ga.at[1 - yy, xx, :, core, pl.ds(0, ha)], got_ay2, y_near)
    links.send(("ax2",), ga.at[yy, 1 - xx, :, core, pl.ds(ha, ha)], got_ax2, x_near)
    for h in range(heads // 2, heads):
        strip_sum(h)

    diag = jnp.concatenate([sums[h] for h in range(heads)], axis=0)
    small[...] = jnp.zeros_like(small)
    small[0:1, :] = jnp.sum(rows8[...], axis=0, keepdims=True) / gain_ref[...]
    small[1:2, :] = tiny_ref[...]
    bucket_lane = lax.broadcasted_iota(jnp.int32, (heads, LANES), 1)
    rel = jnp.zeros((heads, LANES), f32)
    for b in range(buckets):
        rel = jnp.where(bucket_lane == b, jnp.sum(jnp.where(kinds_ref[...] == b, diag, 0.0), axis=1, keepdims=True), rel)
    per = width // LANES
    for h in range(heads):
        small[2 + h // per : 3 + h // per, h % per * LANES : (h % per + 1) * LANES] = rel[h : h + 1, :]
    links.send(("s", 0), small, tiny.at[1], sibling)

    for t in range(3):
        finish(t)
    links.take(("ay2",), got_ay2)
    links.take(("ax2",), got_ax2)
    for n in range(count):
        ga[yy, xx, n, core, pl.ds(0, ha)] = ga[yy, xx, n, core, pl.ds(0, ha)] + got_ay2[n]
        ga[yy, xx, n, core, pl.ds(ha, ha)] = ga[yy, xx, n, core, pl.ds(ha, ha)] + got_ax2[n]
    line("a", 0)

    def tiny_step(n):
        links.take(("s", n), tiny.at[2 * n + 1])
        before = small if n == 0 else tiny.at[2 * n]
        tiny[2 * n + 2] = before[...] + tiny[2 * n + 1]
        if n < 2:
            links.send(("s", n + 1), tiny.at[2 * n + 2], tiny.at[2 * n + 3], (flip(batch, 2 << n), place))
        else:
            tiny_z[place] = tiny[6]
            for d in range(1, count):
                for way in (1, -1):
                    links.send(("sz", way, d), tiny.at[6], tiny_z.at[place], (batch, place + way * d), inside(place + way * d))

    tiny_step(0)
    for t in range(3):
        gathers[t].middle()
    line("a", 1)
    tiny_step(1)
    for p in range(PIECES):
        rows = pl.ds(p * step, step)
        for side, way in ((0, 1), (1, -1)):
            ok = inside(place - way)
            near = inside(place - 2 * way)
            if radius > 1:
                links.take(("x", way, 1, p), got_x.at[side, 0, rows], ok & near)
                links.take(("x0", way, 1, p), got_x.at[side, 0, rows], ok & jnp.logical_not(near))
            else:
                links.take(("x", way, 1, p), got_x.at[side, 0, rows], ok)
            def blank():
                got_x[side, 0, rows] = jnp.zeros((step, width), bf)
            pl.when(jnp.logical_not(ok))(blank)
        grad = own_acc[rows, :] + got_x[0, 0, rows].astype(f32) + got_x[1, 0, rows].astype(f32)
        x = tok_ref[rows, :].astype(f32)
        s = unit_norm(x)
        n1 = x * s
        e = grad * gain_ref[...]
        tokens_out[rows, :] = (mid_ref[rows, :] + s * (e - n1 * jnp.mean(e * n1, axis=1, keepdims=True))).astype(bf)
    tiny_step(2)
    for hop in range(2, count - 1):
        line("a", hop)
    for t in range(3):
        gathers[t].far()
    finish("a")
    for d in range(1, count):
        for way in (1, -1):
            links.take(("sz", way, d), tiny_z.at[place - way * d], inside(place - way * d))
    summed = tiny_z[0]
    for n in range(1, count):
        summed = summed + tiny_z[n]
    total_ref[...] = summed * scale if final else summed

    for name in ("end",):
        for t in range(3):
            gathers[t].end()

    def scaled(value):
        value = value.astype(f32)
        return value * scale if final else value

    def block(value):
        turn = value.T
        sq = value * value
        acc = sq[0:8]
        for n in range(8, LANES, 8):
            acc = acc + sq[n : n + 8]
        return turn, acc, jnp.sum(turn * turn, axis=0, keepdims=True) * (1.0 / width) + TINY

    sums = []
    none = jnp.zeros((8, width), f32)
    per = full_f.shape[1] * rows_f
    f_sums = []
    for t, out in ((0, gg_out), (1, gu_out), (2, gd_out)):
        def one(n, acc):
            at = pl.multiple_of(n * LANES, LANES)
            blocks = LANES // rows_f
            value = scaled(jnp.concatenate([full_f[t, n * blocks + i] for i in range(blocks)], axis=0))
            turn, more, stat = block(value)
            units_ref[t : t + 1, pl.ds(at, LANES)] = stat
            if t < 2:
                out[:, pl.ds(at, LANES)] = turn
            else:
                out[pl.ds(at, LANES), :] = value
            return acc + more
        f_sums.append(jnp.sum(lax.fori_loop(0, per // LANES, one, none), axis=0, keepdims=True))
    gathers["a"].middle()
    gathers["a"].far()
    gathers["a"].end()
    a_sums = []
    for s, out in ((0, gq_out), (1, gk_out), (2, gv_out), (3, go_out)):
        value = scaled(jnp.concatenate([full_a[s, 0], full_a[s, 1]], axis=0))
        rows = value.shape[0]
        acc = none
        for at in range(0, rows, LANES):
            size = min(LANES, rows - at)
            one = value[at : at + size]
            if size < LANES:
                one = jnp.concatenate([one, jnp.zeros((LANES - size, width), f32)], axis=0)
            turn, more, stat = block(one)
            acc = acc + more
            heads_ref[s : s + 1, at : at + size] = stat[:, :size]
            if s < 3:
                out[:, at : at + size] = turn[:, :size]
        if s == 3:
            out[...] = value
        a_sums.append(jnp.sum(acc, axis=0, keepdims=True))
    side_z[place] = jnp.concatenate(a_sums + f_sums + [none[0:1]], axis=0)
    for d in range(1, count):
        for way in (1, -1):
            links.send(("q", way, d), side_z.at[place], side_z.at[place], (batch, place + way * d), inside(place + way * d))
    for d in range(1, count):
        for way in (1, -1):
            links.take(("q", way, d), side_z.at[place - way * d], inside(place - way * d))
    summed = side_z[0]
    for n in range(1, count):
        summed = summed + side_z[n]
    inner_part, hidden_part = 1.0 / inner, 1.0 / (per * count)
    model_ref[0:4, :] = summed[0:4] * inner_part + TINY
    model_ref[4:5, :] = summed[6:7] * hidden_part + TINY
    rows_ref[...] = summed[4:6] * hidden_part + TINY
    links.drain()


def finish(tokens, gain, middle, tiny, kinds, dq, dk, dv, xs, was, raw_out, keep, fx, fy, strips, count, radius, buckets, scale, final):
    own, width = tokens.shape
    total, inner = dk.shape
    heads, _, span = strips.shape
    part = keep.shape[4]
    half_a = inner // count // 2
    bf = jnp.bfloat16
    vm = pl.BlockSpec(memory_space=pltpu.VMEM)
    hb = pl.BlockSpec(memory_space=pl.ANY)
    V = lambda *s: pltpu.VMEM(s + (width,), bf)
    F = lambda *s: pltpu.VMEM(s, jnp.float32)
    O = lambda *s: jax.ShapeDtypeStruct(s, jnp.float32)
    shard, hidden = inner // count, part * GROUP
    return pl.pallas_call(
        functools.partial(finish_kernel, count, radius, buckets, scale, final),
        in_specs=[vm] * 5 + [hb] * 10,
        out_specs=[vm] * 13,
        out_shape=[
            jax.ShapeDtypeStruct((own, width), bf), O(5, width), O(2, width), O(4, shard), O(3, hidden), O(8, width),
            O(width, shard), O(width, shard), O(width, shard), O(shard, width), O(width, hidden), O(width, hidden), O(hidden, width),
        ],
        scratch_shapes=[
            pltpu.VMEM((own, inner), bf), pltpu.VMEM((total, inner), bf), pltpu.VMEM((total, inner), bf), V(count, own),
            V(inner), V(inner), V(inner),
            V(2, 2, count, 2, half_a), V(2, 2, count, half_a), V(2, count, half_a // 2), V(2, count, half_a // 2), V(count, half_a // 2), V(count, half_a // 2),
            V(3, count, 2, 2, part), V(3, count, 2, part // 2), V(3, count, 2, part // 2), V(3, count, part // 2), V(3, count, part // 2),
            V(2, count, half_a), V(3, 2, count, part), V(4, 2, half_a), V(3, GROUP, part),
            V(count, own), F(own, width), V(2, radius, own), F(8, width),
            F(8, width), F(7, 8, width), F(count, 8, width), F(count, 8, width), F(2, 64, span),
            pltpu.SemaphoreType.DMA((240,)), pltpu.SemaphoreType.DMA((240,)), pltpu.SemaphoreType.DMA((48,)),
        ],
        compiler_params=pltpu.CompilerParams(collective_id=2, has_side_effects=True, vmem_limit_bytes=63 * 2**20),
        name="finish",
    )(tokens, gain, middle, tiny, kinds, dq, dk, dv, xs, was, raw_out, keep, fx, fy, strips)


def on_device(tokens, cotangent, lengths, buckets, w_query, w_key, w_value, w_out, w_gate, w_up, w_down, rel_table, gain_one, gain_two):
    bf = jnp.bfloat16
    count = lax.axis_size("mp")
    batches = lax.axis_size("batch")
    own, width = tokens.shape
    total = own * count
    inner = w_query.shape[1]
    hidden_rows = w_gate.shape[1]
    limit = (buckets.shape[0] + 1) // 2
    radius = min(count - 1, -(-(limit - 1) // own))
    place = jnp.reshape(lax.axis_index("mp") * own, (1,)).astype(jnp.int32)
    kinds = rel_table.shape[0]
    heads = rel_table.shape[1] * count

    wa = jnp.concatenate([w_query.T, w_key.T, w_value.T, w_out], axis=0).reshape(4, 2, inner // 2, width)
    wf = jnp.stack([w_gate.T, w_up.T, w_down]).reshape(3, GROUP, hidden_rows // GROUP, width)
    kind_row = bucket_kinds(buckets, TQ)[None]
    rel_own = jnp.pad(rel_table.T, ((0, 8 - rel_table.shape[1]), (0, 0)))
    rows_one, wa_all, wf_all, q, k, kt, v, vt, strips = gather(
        tokens, gain_one[None], wa, wf, rel_own, kind_row, count, radius, heads
    )
    was = wa_all.reshape(4, count * inner, width)
    wfs = wf_all.reshape(3, count * hidden_rows, width)
    context, lse = attend(lengths, place, strips, q, k, vt, limit, TQ, TK, HP)

    layer_out, grad_middle, grad_context, raw_out, gain_two_part, keep, fx, fy = ffn(
        tokens, cotangent, context, gain_two[None], was, wfs, count
    )
    got_fx = lax.ppermute(fx, "batch", [(n, n ^ 2) for n in range(batches)])
    got_fy = lax.ppermute(fy, "batch", [(n, n ^ 4) for n in range(batches)])
    grad_q, grad_k, grad_v, grad_strips = attend_back(
        lengths, place, strips, q, k, kt, v, context, grad_context, lse, limit, TQ, TK, HP
    )
    scale = (total * batches) ** -0.5
    one_group = batches == GROUP
    grad_tokens, stat_model, stat_ffn_rows, stat_heads, stat_hidden, sums, *grads = finish(
        tokens, gain_one[None], grad_middle, gain_two_part, kind_row, grad_q, grad_k, grad_v, rows_one, was, raw_out.reshape(count, 2, inner // 2, width),
        keep, got_fx, got_fy, grad_strips, count, radius, kinds, scale, one_group
    )
    if not one_group:
        sums, *grads = [one * (scale / GROUP) for one in lax.psum((sums, *grads), "batch")]
        g_q, g_k, g_v, g_o, g_g, g_u, g_d = [one * one for one in grads]
        over_rows = [jnp.sum(one, axis=1) for one in (g_q, g_k, g_v)] + [jnp.sum(g_o, axis=0)]
        over_rows += [jnp.sum(g_g, axis=1), jnp.sum(g_u, axis=1), jnp.sum(g_d, axis=0)]
        side = lax.psum(jnp.stack(over_rows), "mp")
        stat_model = jnp.concatenate([side[:4] / (inner * count), side[6:] / (hidden_rows * count)]) + TINY
        stat_ffn_rows = side[4:6] / (hidden_rows * count) + TINY
        stat_heads = jnp.stack([jnp.mean(one, axis=0) for one in (g_q, g_k, g_v)] + [jnp.mean(g_o, axis=1)]) + TINY
        stat_hidden = jnp.stack([jnp.mean(g_g, axis=0), jnp.mean(g_u, axis=0), jnp.mean(g_d, axis=1)]) + TINY
    per = heads // count
    rel_rows = -(-heads * LANES // width)
    rel_sums = sums[2 : 2 + rel_rows].reshape(-1, LANES)[:heads, :kinds]
    rel_mine = lax.dynamic_slice_in_dim(rel_sums, lax.axis_index("mp") * per, per, 0).T
    return (
        layer_out,
        grad_tokens,
        *grads,
        rel_mine,
        sums[0],
        sums[1],
        stat_model,
        stat_heads,
        stat_hidden,
        stat_ffn_rows,
    )


TQ = 512
TK = 256
HP = 2


def solution(mesh):
    in_specs = (
        P(("batch", "mp"), None),
        P(("batch", "mp"), None),
        P("batch", None),
        P(),
        P(None, "mp"),
        P(None, "mp"),
        P(None, "mp"),
        P("mp", None),
        P(None, "mp"),
        P(None, "mp"),
        P("mp", None),
        P(None, "mp"),
        P(),
        P(),
    )
    out_specs = (
        P(("batch", "mp"), None),
        P(("batch", "mp"), None),
        P(None, "mp"),
        P(None, "mp"),
        P(None, "mp"),
        P("mp", None),
        P(None, "mp"),
        P(None, "mp"),
        P("mp", None),
        P(None, "mp"),
        P(),
        P(),
        P(),
        P(None, "mp"),
        P(None, "mp"),
        P(),
    )
    return jax.shard_map(
        on_device, mesh=mesh, in_specs=in_specs, out_specs=out_specs, check_vma=False
    )
```

```python
import functools

import jax
import jax.numpy as jnp
from jax import lax
from jax.experimental import pallas as pl
from jax.experimental.pallas import tpu as pltpu
from jax.sharding import PartitionSpec as P

TINY = 1e-30

NEG = -1e9
LANES = 128

def strip_sizes(limit, tq):
    reach = -(-limit // LANES)
    nq = tq // LANES
    off = LANES * (reach + nq)
    return reach, off, off + LANES * reach + tq

def bucket_kinds(buckets, tq):
    limit = (buckets.shape[0] + 1) // 2
    _, off, width = strip_sizes(limit, tq)
    back = lax.rev(buckets, (0,))
    shift = off - (limit - 1)
    left = jnp.broadcast_to(back[:1], (shift,))
    right = jnp.broadcast_to(back[-1:], (width - shift - back.shape[0],))
    return jnp.concatenate([left, back, right])


def ends_list(lens_ref, rows_dev, count):
    total = jnp.int32(0)
    ends = []
    for r in range(rows_dev):
        for c in range(count):
            total = total + lens_ref[r, c]
            ends.append(total)
    return ends

def segment_of(place, ends, count):
    seg = jnp.zeros_like(place)
    pad = jnp.zeros_like(place)
    for n, end in enumerate(ends):
        past = place >= end
        seg = seg + jnp.where(past, 1, 0)
        if n % count == count - 2:
            pad = pad + jnp.where(past, 1, 0)
        if n % count == count - 1:
            pad = pad - jnp.where(past, 1, 0)
    return jnp.where(pad > 0, place + 4096, seg)

def key_range(first, last, ends, count):
    low = jnp.int32(0)
    high = ends[-1]
    for n, end in enumerate(ends):
        is_pad_next = n % count == count - 2
        low = jnp.where(first >= end, jnp.maximum(low, first if is_pad_next else end), low)
    for n in range(len(ends) - 1, -1, -1):
        is_pad = n % count == count - 1
        high = jnp.where(last < ends[n], (last + 1) if is_pad else ends[n], high)
    return (low // LANES) * LANES, high


def for_chunks(body, q_at, tq, tk, half, ends, count, w_high):
    ranges = [key_range(q_at + at, q_at + at + half - 1, ends, count) for at in range(0, tq, half)]
    low, high = ranges[0][0], ranges[-1][1]
    steps = (high - low + tk - 1) // tk
    low = jnp.minimum(low, w_high - steps * tk)

    def step(c, _):
        ks = pl.multiple_of(low + c * tk, LANES)
        if len(ranges) == 1:
            body(ks, 0, tq)
            return 0
        one, two = [(ks < end) & (ks + tk > start) for start, end in ranges]
        pl.when(one & two)(lambda: body(ks, 0, tq))
        pl.when(one & jnp.logical_not(two))(lambda: body(ks, 0, half))
        pl.when(two & jnp.logical_not(one))(lambda: body(ks, half, half))
        return 0

    lax.fori_loop(0, steps, step, 0)


def window(place_ref, own, total, limit):
    first = place_ref[0]
    radius = -(-(limit - 1) // own)
    return jnp.maximum(first - radius * own, 0), jnp.minimum(first + (radius + 1) * own, total)

def fill_segments(kseg, ends, count, total):
    def one(n, _):
        at = pl.multiple_of(n * 256, 256)
        place = at + lax.broadcasted_iota(jnp.int32, (256, LANES), 0)
        kseg[pl.ds(at, 256), :] = segment_of(place, ends, count)
        return 0
    lax.fori_loop(0, total // 256, one, 0)

def tile_lanes(x, n):
    return x if n == 1 else jnp.concatenate([x] * n, axis=1)

def lane_start(ks, q_at, g, reach, off, nq):
    d = (ks - q_at) // LANES + g
    return pl.multiple_of(off - LANES * jnp.clip(d, -reach, reach + nq - 1), LANES)

def fwd_kernel(cfg, lens_ref, place_ref, strip, q_ref, k_ref, vt_ref, ctx_ref, lse_ref, kseg, top, tot, acc):
    tq, tk, limit, rows_dev, count, own, total, hp = cfg
    reach, off, width = strip_sizes(limit, tq)
    ends = ends_list(lens_ref, rows_dev, count)
    @pl.when(pl.program_id(0) == 0)
    def _():
        fill_segments(kseg, ends, count, total)
    w_high = window(place_ref, own, total, limit)[1]
    lane = lax.broadcasted_iota(jnp.int32, (tq, LANES), 1)
    for qt in range(own // tq):
        rows = slice(qt * tq, (qt + 1) * tq)
        q_at = place_ref[0] + qt * tq
        halves = []
        for h in range(hp):
            q2 = q_ref[rows, h // 2 * LANES : h // 2 * LANES + LANES]
            halves.append(jnp.where((lane < 64) == (h % 2 == 0), q2, jnp.zeros_like(q2)))
        qseg = segment_of(q_at + lax.broadcasted_iota(jnp.int32, (1, tq), 1), ends, count)
        top[...] = jnp.full(top.shape, 2 * NEG, jnp.float32)
        tot[...] = jnp.zeros_like(tot)
        acc[...] = jnp.zeros_like(acc)

        def body(ks, first, lanes):
            nq = lanes // LANES
            at = slice(first, first + lanes)
            same = tile_lanes(kseg[pl.ds(ks, tk), :], nq) == qseg[:, at]
            starts = [lane_start(ks, q_at + first, g, reach, off, nq) for g in range(tk // LANES)]
            raws, news, fades, lows = [], [], [], []
            for h in range(hp):
                kc = k_ref[pl.ds(ks, tk), h // 2 * LANES : h // 2 * LANES + LANES]
                raws.append(lax.dot_general(kc, halves[h][at], (((1,), (1,)), ((), ())), preferred_element_type=jnp.float32))
            for h in range(hp):
                bias = jnp.concatenate([strip[h, :, pl.ds(one, lanes)] for one in starts], axis=0)
                raws[h] = jnp.where(same, raws[h] + bias, NEG)
                old = top[h : h + 1, at]
                new = jnp.maximum(old, jnp.max(raws[h], axis=0, keepdims=True))
                top[h : h + 1, at] = new
                news.append(new)
                fades.append(jnp.exp(old - new))
            for h in range(hp):
                p = jnp.exp(raws[h] - news[h])
                tot[h : h + 1, at] = tot[h : h + 1, at] * fades[h] + jnp.sum(p, axis=0, keepdims=True)
                lows.append(p.astype(jnp.bfloat16))
            for h in range(hp):
                acc[h, :, at] = acc[h, :, at] * fades[h] + jnp.dot(
                    vt_ref[h * 64 : h * 64 + 64, pl.ds(ks, tk)], lows[h], preferred_element_type=jnp.float32
                )

        for_chunks(body, q_at, tq, tk, min(256, tq), ends, count, w_high)
        for pair in range(hp // 2):
            both = jnp.concatenate([acc[h] / tot[h : h + 1, :] for h in (2 * pair, 2 * pair + 1)], axis=0)
            ctx_ref[rows, pair * LANES : pair * LANES + LANES] = both.T.astype(jnp.bfloat16)
        for h in range(hp):
            lse_ref[0, h : h + 1, rows] = top[h : h + 1, :] + jnp.log(tot[h : h + 1, :])


def attend(lengths, place, strips, q, k, vt, limit, tq, tk, hp):
    own, inner = q.shape
    total = k.shape[0]
    steps = inner // 64 // hp
    lanes = hp * 64
    rows_dev, count = lengths.shape
    width = strips.shape[2]
    cfg = (tq, tk, limit, rows_dev, count, own, total, hp)
    smem = pl.BlockSpec(memory_space=pltpu.SMEM)
    return pl.pallas_call(
        functools.partial(fwd_kernel, cfg),
        grid=(steps,),
        in_specs=[smem, smem,
            pl.BlockSpec((hp, LANES, width), lambda p: (p, 0, 0)),
            pl.BlockSpec((own, lanes), lambda p: (0, p)),
            pl.BlockSpec((total, lanes), lambda p: (0, p)),
            pl.BlockSpec((lanes, total), lambda p: (p, 0))],
        out_specs=[pl.BlockSpec((own, lanes), lambda p: (0, p)),
                   pl.BlockSpec((1, hp, own), lambda p: (p, 0, 0))],
        out_shape=[jax.ShapeDtypeStruct((own, inner), jnp.bfloat16), jax.ShapeDtypeStruct((steps, hp, own), jnp.float32)],
        scratch_shapes=[pltpu.VMEM((total, LANES), jnp.int32), pltpu.VMEM((hp, tq), jnp.float32), pltpu.VMEM((hp, tq), jnp.float32),
                        pltpu.VMEM((hp, 64, tq), jnp.float32)],
        compiler_params=pltpu.CompilerParams(vmem_limit_bytes=56 * 2**20),
        name="attend",
    )(lengths, place, strips, q, k, vt)


def bwd_kernel(cfg, lens_ref, place_ref, strip, q_ref, k_ref, kt_ref, v_ref, ctx_ref, do_ref, lse_ref,
               dq_ref, dk_ref, dv_ref, dstrip, kseg, dk_acc, dv_acc, dq_acc):
    tq, tk, limit, rows_dev, count, own, total, hp = cfg
    reach, off, width = strip_sizes(limit, tq)
    nq = tq // LANES
    ends = ends_list(lens_ref, rows_dev, count)
    @pl.when(pl.program_id(0) == 0)
    def _():
        fill_segments(kseg, ends, count, total)
    dstrip[...] = jnp.zeros_like(dstrip)
    dk_acc[...] = jnp.zeros_like(dk_acc)
    dv_acc[...] = jnp.zeros_like(dv_acc)
    w_high = window(place_ref, own, total, limit)[1]
    lane = lax.broadcasted_iota(jnp.int32, (tq, LANES), 1)
    for qt in range(own // tq):
        rows = slice(qt * tq, (qt + 1) * tq)
        q_at = place_ref[0] + qt * tq
        q_half, do_half, delta, lse = [], [], [], []
        for pair in range(hp // 2):
            lanes = slice(pair * LANES, pair * LANES + LANES)
            q2 = q_ref[rows, lanes]
            do2 = do_ref[rows, lanes]
            prod = (do2.astype(jnp.float32) * ctx_ref[rows, lanes].astype(jnp.float32)).T
            for hh in range(2):
                keep = (lane < 64) == (hh == 0)
                q_half.append(jnp.where(keep, q2, jnp.zeros_like(q2)))
                do_half.append(jnp.where(keep, do2, jnp.zeros_like(do2)))
                delta.append(jnp.sum(prod[hh * 64 : hh * 64 + 64], axis=0, keepdims=True))
                lse.append(lse_ref[0, 2 * pair + hh : 2 * pair + hh + 1, rows])
        qseg = segment_of(q_at + lax.broadcasted_iota(jnp.int32, (1, tq), 1), ends, count)
        dq_acc[...] = jnp.zeros_like(dq_acc)

        def body(ks, first, span):
            nq = span // LANES
            at = slice(first, first + span)
            same = tile_lanes(kseg[pl.ds(ks, tk), :], nq) == qseg[:, at]
            starts = [lane_start(ks, q_at + first, g, reach, off, nq) for g in range(tk // LANES)]
            for pair in range(hp // 2):
                lanes = slice(pair * LANES, pair * LANES + LANES)
                kc = k_ref[pl.ds(ks, tk), lanes]
                vc = v_ref[pl.ds(ks, tk), lanes]
                dk_part = dv_part = None
                for h in (2 * pair, 2 * pair + 1):
                    s = lax.dot_general(kc, q_half[h][at], (((1,), (1,)), ((), ())), preferred_element_type=jnp.float32)
                    bias = jnp.concatenate([strip[h, :, pl.ds(one, span)] for one in starts], axis=0)
                    p = jnp.exp(jnp.where(same, s + (bias - lse[h][:, at]), NEG))
                    dp = lax.dot_general(vc, do_half[h][at], (((1,), (1,)), ((), ())), preferred_element_type=jnp.float32)
                    ds = p * (dp - delta[h][:, at])
                    for g, one in enumerate(starts):
                        dstrip[h, :, pl.ds(one, span)] += ds[g * LANES : (g + 1) * LANES, :]
                    pb = p.astype(jnp.bfloat16)
                    dsb = ds.astype(jnp.bfloat16)
                    dv_one = jnp.dot(pb, do_half[h][at], preferred_element_type=jnp.float32)
                    dk_one = jnp.dot(dsb, q_half[h][at], preferred_element_type=jnp.float32)
                    dv_part = dv_one if dv_part is None else dv_part + dv_one
                    dk_part = dk_one if dk_part is None else dk_part + dk_one
                    dq_acc[h, :, at] += jnp.dot(kt_ref[h * 64 : h * 64 + 64, pl.ds(ks, tk)], dsb, preferred_element_type=jnp.float32)
                dv_acc[pl.ds(ks, tk), lanes] += dv_part
                dk_acc[pl.ds(ks, tk), lanes] += dk_part

        for_chunks(body, q_at, tq, tk, min(256, tq), ends, count, w_high)
        for pair in range(hp // 2):
            dq_ref[rows, pair * LANES : pair * LANES + LANES] = jnp.concatenate([dq_acc[2 * pair], dq_acc[2 * pair + 1]], axis=0).T.astype(jnp.bfloat16)
    dk_ref[...] = dk_acc[...].astype(jnp.bfloat16)
    dv_ref[...] = dv_acc[...].astype(jnp.bfloat16)


def attend_back(lengths, place, strips, q, k, kt, v, ctx, do, lse, limit, tq, tk, hp):
    own, inner = q.shape
    total = k.shape[0]
    steps = inner // 64 // hp
    lanes = hp * 64
    rows_dev, count = lengths.shape
    width = strips.shape[2]
    cfg = (tq, tk, limit, rows_dev, count, own, total, hp)
    smem = pl.BlockSpec(memory_space=pltpu.SMEM)
    tall = pl.BlockSpec((total, lanes), lambda p: (0, p))
    short = pl.BlockSpec((own, lanes), lambda p: (0, p))
    band = pl.BlockSpec((hp, LANES, width), lambda p: (p, 0, 0))
    return pl.pallas_call(
        functools.partial(bwd_kernel, cfg),
        grid=(steps,),
        in_specs=[smem, smem, band,
            short, tall, pl.BlockSpec((lanes, total), lambda p: (p, 0)), tall, short, short,
            pl.BlockSpec((1, hp, own), lambda p: (p, 0, 0))],
        out_specs=[short, tall, tall, band],
        out_shape=[jax.ShapeDtypeStruct((own, inner), jnp.bfloat16), jax.ShapeDtypeStruct((total, inner), jnp.bfloat16),
                   jax.ShapeDtypeStruct((total, inner), jnp.bfloat16), jax.ShapeDtypeStruct(strips.shape, jnp.float32)],
        scratch_shapes=[pltpu.VMEM((total, LANES), jnp.int32),
                        pltpu.VMEM((total, lanes), jnp.float32), pltpu.VMEM((total, lanes), jnp.float32),
                        pltpu.VMEM((hp, 64, tq), jnp.float32)],
        compiler_params=pltpu.CompilerParams(vmem_limit_bytes=60 * 2**20),
        name="attend_back",
    )(lengths, place, strips, q, k, kt, v, ctx, do, lse)


MESH = pl.DeviceIdType.MESH
GROUP = 8


def flip(index, bit):
    return index + bit * (1 - 2 * ((index // bit) % 2))


class Links:
    def __init__(self, send_sems, recv_sems, batch, place):
        self.send_sems, self.recv_sems = send_sems, recv_sems
        self.batch, self.place = batch, place
        self.slots = {}
        self.sent = []

    def slot(self, key):
        return self.slots.setdefault(key, len(self.slots))

    def copy(self, key, src, dst, target):
        n = self.slot(key)
        return pltpu.make_async_remote_copy(
            src_ref=src, dst_ref=dst, send_sem=self.send_sems.at[n], recv_sem=self.recv_sems.at[n],
            device_id=target, device_id_type=MESH)

    def send(self, key, src, dst, target, when=None):
        def go():
            self.copy(key, src, dst, target).start()
        self.sent.append((key, src, dst, target, when))
        if when is None:
            go()
        else:
            pl.when(when)(go)

    def take(self, key, dst, when=None, then=None):
        def go():
            self.copy(key, dst, dst, (self.batch, self.place)).wait_recv()
            if then is not None:
                then()
        if when is None:
            go()
        else:
            pl.when(when)(go)

    def drain(self):
        for key, src, dst, target, when in self.sent:
            def go():
                self.copy(key, src, dst, target).wait_send()
            if when is None:
                go()
            else:
                pl.when(when)(go)


def greet(batch, place, count):
    bar = pltpu.get_barrier_semaphore()
    for bit in (1, 2, 4):
        pl.semaphore_signal(bar, inc=1, device_id=(flip(batch, bit), place), device_id_type=MESH)
    for way in range(1 - count, count):
        if way != 0:
            @pl.when((place + way >= 0) & (place + way < count))
            def _():
                pl.semaphore_signal(bar, inc=1, device_id=(batch, place + way), device_id_type=MESH)
    pl.semaphore_wait(bar, 3 + count - 1)


def both(a, b):
    return a if b is None else (b if a is None else a & b)


class PlaneGather:
    def __init__(self, links, key, view, ref, sub, when=None):
        self.l, self.key, self.view, self.ref, self.sub, self.when = links, key, view, ref, sub, when

    def put(self, path, sub, half, bit):
        region = self.view(self.ref, sub, half)
        self.l.send((self.key, path), region, region, (flip(self.l.batch, bit), self.l.place), self.when)

    def start(self):
        self.put("x", self.sub, None, 2)
        self.put("y", self.sub, None, 4)
        self.put("c", self.sub, None, 1)

    def middle(self):
        sub = self.sub
        self.l.take((self.key, "x"), self.view(self.ref, flip(sub, 2), None), self.when)
        self.put("xy", flip(sub, 2), 0, 4)
        self.put("xc", flip(sub, 2), None, 1)
        self.l.take((self.key, "y"), self.view(self.ref, flip(sub, 4), None), self.when)
        self.put("yx", flip(sub, 4), 1, 2)
        self.put("yc", flip(sub, 4), None, 1)

    def far(self):
        sub = self.sub
        diagonal = flip(flip(sub, 2), 4)
        self.l.take((self.key, "xy"), self.view(self.ref, diagonal, 0), self.when)
        self.put("0c", diagonal, 0, 1)
        self.l.take((self.key, "yx"), self.view(self.ref, diagonal, 1), self.when)
        self.put("1c", diagonal, 1, 1)

    def end(self):
        sub = flip(self.sub, 1)
        diagonal = flip(flip(sub, 2), 4)
        self.l.take((self.key, "c"), self.view(self.ref, sub, None), self.when)
        self.l.take((self.key, "xc"), self.view(self.ref, flip(sub, 2), None), self.when)
        self.l.take((self.key, "yc"), self.view(self.ref, flip(sub, 4), None), self.when)
        self.l.take((self.key, "0c"), self.view(self.ref, diagonal, 0), self.when)
        self.l.take((self.key, "1c"), self.view(self.ref, diagonal, 1), self.when)


def half_rows(half, rows):
    return pl.ds(0, rows) if half is None else pl.ds(half * (rows // 2), rows // 2)


PIECES = 4
EPS = 1e-06


def unit_norm(values):
    return lax.rsqrt(jnp.mean(values * values, axis=1, keepdims=True) + EPS)


def dot_nt(a, b):
    return lax.dot_general(a, b, (((1,), (1,)), ((), ())), preferred_element_type=jnp.float32)


def dot_nn(a, b):
    return jnp.dot(a, b, preferred_element_type=jnp.float32)


def gather_kernel(count, radius, tok_ref, gain_ref, wa_ref, wf_ref, rel_ref, kinds_ref,
                  xs_out, was_out, wfs_ref, q_out, k_out, kt_out, v_out, vt_out, strips_out,
                  xs, was, q_v, k_v, kt_v, v_v, vt_v, rel_all, table, strip_v, send_sems, recv_sems, local_sems):
    batch, place = lax.axis_index("batch"), lax.axis_index("mp")
    sub = batch % GROUP
    links = Links(send_sems, recv_sems, batch, place)
    own, width = tok_ref.shape
    rows_a = wa_ref.shape[2]
    rows_f = wf_ref.shape[2]
    step = own // PIECES
    local = []

    def copy_local(src, dst):
        one = pltpu.make_async_copy(src, dst, local_sems.at[len(local)])
        local.append(one)
        return one

    own_a = copy_local(wa_ref, was.at[:, place])
    own_a.start()
    copy_local(wf_ref, wfs_ref.at[:, place]).start()
    for p in range(PIECES):
        rows = pl.ds(p * step, step)
        values = tok_ref[rows, :].astype(jnp.float32)
        xs[place, rows] = (values * unit_norm(values) * gain_ref[...]).astype(xs.dtype)
    greet(batch, place, count)

    def view_a(mm):
        return lambda ref, s, half: ref.at[s // 2, mm, s % 2, half_rows(half, rows_a)]

    def view_f(mm):
        return lambda ref, s, half: ref.at[:, mm, s, half_rows(half, rows_f)]

    def inside(n):
        return (n >= 0) & (n < count)

    for way in (1, -1):
        ok = inside(place + way)
        target = (batch, place + way)
        links.send(("a", way, 1), wa_ref.at[sub // 2, sub % 2], view_a(place)(was, sub, None), target, ok)
        links.send(("f", way, 1), wf_ref.at[:, sub], view_f(place)(wfs_ref, sub, None), target, ok)
    for d in range(1, count):
        for way in (1, -1):
            links.send(("r", way, d), rel_ref, rel_all.at[place], (batch, place + way * d), inside(place + way * d))
    for way in (1, -1):
        ok = inside(place + way)
        target = (batch, place + way)
        for p in range(PIECES):
            rows = pl.ds(p * step, step)
            links.send(("x", way, 1, p), xs.at[place, rows], xs.at[place, rows], target, ok)
    for n in range(count):
        @pl.when((n - place > radius) | (place - n > radius))
        def _():
            def blank(p, _):
                xs[n, pl.ds(p * step, step)] = jnp.zeros((step, width), xs.dtype)
                return 0
            lax.fori_loop(0, PIECES, blank, 0)
            for ref in (k_v, v_v):
                ref[pl.ds(n * own, own)] = jnp.zeros((own, ref.shape[1]), ref.dtype)
            for ref in (kt_v, vt_v):
                ref[:, pl.ds(n * own, own)] = jnp.zeros((ref.shape[0], own), ref.dtype)

    gathers = {}

    def weights_arrive(kind, dist):
        for way in (1, -1):
            source = place - way * dist
            ok = inside(source)
            view, ref = (view_a(source), was) if kind == "a" else (view_f(source), wfs_ref)
            region = view(ref, sub, None)
            links.take((kind, way, dist), region, ok)
            if dist < count - 1:
                links.send((kind, way, dist + 1), region, region, (batch, place + way), ok & inside(place + way))
            gather = PlaneGather(links, ("g", kind, way, dist), view, ref, sub, ok)
            gather.start()
            gathers[kind, way, dist] = gather

    def x_arrive(dist, p):
        for way in (1, -1):
            source = place - way * dist
            ok = inside(source)
            region = xs.at[source, pl.ds(p * step, step)]
            links.take(("x", way, dist, p), region, ok)
            if dist < radius:
                links.send(("x", way, dist + 1, p), region, region, (batch, place + way), ok & inside(place + way))

    def stage(name, kind, dist):
        for way in (1, -1):
            getattr(gathers[kind, way, dist], name)()

    heads_own = rel_ref.shape[0] // 8 * 8
    heads = table.shape[0]
    span = table.shape[1]
    kinds = rel_ref.shape[1]

    def make_table():
        rel_all[place] = rel_ref[...]
        for d in range(1, count):
            for way in (1, -1):
                links.take(("r", way, d), rel_all.at[place - way * d], inside(place - way * d))
        per = heads // count
        joined = jnp.concatenate([rel_all[n, 0:per, :] for n in range(count)], axis=0)
        for at in range(0, span, 512):
            lanes = pl.ds(at, min(512, span - at))
            kind = kinds_ref[:, lanes]
            total = jnp.zeros((heads, kind.shape[1]), jnp.float32)
            for b in range(NB_MAX):
                if b < kinds:
                    total = total + jnp.where(kind == b, joined[:, b : b + 1], 0.0)
            table[:, lanes] = total

    strip_copies = []

    def make_strip(h):
        slot = h % 2
        if h >= 2:
            strip_copies[h - 2].wait()
        row = table[h : h + 1, :]
        strip_v[slot] = pltpu.roll(jnp.broadcast_to(row, (LANES, span)), 0, 1, stride=1, stride_axis=0)
        one = pltpu.make_async_copy(strip_v.at[slot], strips_out.at[h], local_sems.at[8 + slot])
        one.start()
        strip_copies.append(one)

    inner = was.shape[1] * was.shape[2] * rows_a

    def weight_tile(kind, n):
        return was[kind, n].reshape(2 * rows_a, width)

    def project(block, when):
        def go():
            x = xs[block]
            def one(n, _):
                at = pl.multiple_of(n * 2 * rows_a, 64)
                kt_v[pl.ds(at, 2 * rows_a), pl.ds(pl.multiple_of(block * own, LANES), own)] = dot_nt(weight_tile(1, n), x).astype(kt_v.dtype)
                vt_v[pl.ds(at, 2 * rows_a), pl.ds(pl.multiple_of(block * own, LANES), own)] = dot_nt(weight_tile(2, n), x).astype(vt_v.dtype)
                return 0
            lax.fori_loop(0, count, one, 0)
            rows = pl.ds(pl.multiple_of(block * own, LANES), own)
            tile = 256
            for at in range(0, inner, tile):
                wk = was[1].reshape(inner, width)[at : at + tile]
                wv = was[2].reshape(inner, width)[at : at + tile]
                k_v[rows, at : at + tile] = dot_nt(x, wk).astype(k_v.dtype)
                v_v[rows, at : at + tile] = dot_nt(x, wv).astype(v_v.dtype)
        if when is None:
            go()
        else:
            pl.when(when)(go)

    def project_q():
        x = xs[place]
        tile = 256
        for at in range(0, inner, tile):
            wq = was[0].reshape(inner, width)[at : at + tile]
            q_v[:, at : at + tile] = dot_nt(x, wq).astype(q_v.dtype)

    saves = []

    def save_block(block, when):
        rows = pl.ds(pl.multiple_of(block * own, LANES), own)
        for src, dst in ((k_v, k_out), (v_v, v_out)):
            saves.append((pltpu.make_async_copy(src.at[rows], dst.at[rows], local_sems.at[10 + len(saves)]), when))
        for src, dst in ((kt_v, kt_out), (vt_v, vt_out)):
            saves.append((pltpu.make_async_copy(src.at[:, rows], dst.at[:, rows], local_sems.at[10 + len(saves)]), when))
        for one, ok in saves[-4:]:
            one.start() if ok is None else pl.when(ok)(one.start)

    dists = range(1, count)
    make_table()
    for h in range(2):
        make_strip(h)
    for d in dists:
        weights_arrive("a", d)
    weights_arrive("f", 1)
    for h in range(2, 4):
        make_strip(h)
    for d in dists:
        stage("middle", "a", d)
    if count > 2:
        weights_arrive("f", 2)
    for h in range(4, 6):
        make_strip(h)
    for d in dists:
        stage("far", "a", d)
    for d in range(3, count):
        weights_arrive("f", d)
    stage("middle", "f", 1)
    for p in range(PIECES):
        x_arrive(1, p)
    for d in dists:
        stage("end", "a", d)
    own_a.wait()
    copy_local(was, was_out).start()
    project_q()
    copy_local(q_v, q_out).start()
    project(place, None)
    save_block(place, None)
    for d in range(2, count):
        stage("middle", "f", d)
    for way in (1, -1):
        project(place + way, inside(place + way))
        save_block(place + way, inside(place + way))
    for d in dists:
        stage("far", "f", d)
    for h in range(6, heads):
        make_strip(h)
    for r in range(2, radius + 1):
        for p in range(PIECES):
            x_arrive(r, p)
        for way in (1, -1):
            project(place + way * r, inside(place + way * r))
            save_block(place + way * r, inside(place + way * r))
    copy_local(xs, xs_out).start()
    for n in range(count):
        save_block(n, (n - place > radius) | (place - n > radius))
    for d in dists:
        stage("end", "f", d)
    links.drain()
    for one in local[1:] + strip_copies[-2:]:
        one.wait()
    for one, ok in saves:
        one.wait() if ok is None else pl.when(ok)(one.wait)


NB_MAX = 128


def gather(tokens, gain, wa, wf, rel, kinds, count, radius, heads):
    own, width = tokens.shape
    bf = jnp.bfloat16
    total = own * count
    inner = count * 2 * wa.shape[2]
    span = kinds.shape[1]
    vm = pl.BlockSpec(memory_space=pltpu.VMEM)
    hb = pl.BlockSpec(memory_space=pl.ANY)
    shapes = [
        ((count, own, width), bf),
        ((4, count, 2, wa.shape[2], width), bf),
        ((3, count, GROUP, wf.shape[2], width), bf),
        ((own, inner), bf), ((total, inner), bf), ((inner, total), bf), ((total, inner), bf), ((inner, total), bf),
        ((heads, LANES, span), jnp.float32),
    ]
    return pl.pallas_call(
        functools.partial(gather_kernel, count, radius),
        in_specs=[vm, vm, hb, hb, vm, vm],
        out_specs=[hb] * len(shapes),
        out_shape=[jax.ShapeDtypeStruct(*one) for one in shapes],
        scratch_shapes=[pltpu.VMEM(*shapes[n]) for n in (0, 1, 3, 4, 5, 6, 7)] + [
            pltpu.VMEM((count,) + rel.shape, jnp.float32),
            pltpu.VMEM((heads, span), jnp.float32),
            pltpu.VMEM((2, LANES, span), jnp.float32),
            pltpu.SemaphoreType.DMA((170,)),
            pltpu.SemaphoreType.DMA((170,)),
            pltpu.SemaphoreType.DMA((64,)),
        ],
        compiler_params=pltpu.CompilerParams(collective_id=1, has_side_effects=True, vmem_limit_bytes=60 * 2**20),
        name="gather",
    )(tokens, gain, wa, wf, rel, kinds)


def ffn_kernel(count, tok_ref, cot_ref, ctx_ref, gain_ref, was_ref, wfs_ref,
               out_ref, middle_ref, do_ref, raw_out_ref, gain_out, keep_out, fx_out, fy_out,
               wo, wf, normed, middle, acc_out, acc_back, raw, got, send_sems, recv_sems, local_sems):
    batch, place = lax.axis_index("batch"), lax.axis_index("mp")
    sub = batch % GROUP
    core, xx, yy = sub % 2, (sub // 2) % 2, sub // 4
    links = Links(send_sems, recv_sems, batch, place)
    sibling = (flip(batch, 1), place)
    own, width = tok_ref.shape
    hidden = wf.shape[1]
    per = hidden // count
    part = per // GROUP
    half = part // 2
    bf = jnp.bfloat16
    loads = [pltpu.make_async_copy(was_ref.at[3], wo, local_sems.at[0])]
    loads += [pltpu.make_async_copy(wfs_ref.at[t], wf.at[t], local_sems.at[1 + t]) for t in range(3)]
    for one in loads:
        one.start()
    bar = pltpu.get_barrier_semaphore()
    pl.semaphore_signal(bar, inc=1, device_id=sibling, device_id_type=MESH)
    loads[0].wait()
    tile = 256
    for at in range(0, own, tile):
        rows = slice(at, at + tile)
        mid = tok_ref[rows, :].astype(jnp.float32) + dot_nn(ctx_ref[rows, :], wo[...])
        middle[rows, :] = mid
        normed[rows, :] = (mid * unit_norm(mid) * gain_ref[...]).astype(bf)
    for one in loads[1:]:
        one.wait()
    pl.semaphore_wait(bar, 1)

    def units(n, _):
        for r in range(per // tile):
            at = pl.multiple_of(n * per + r * tile, tile)
            rows = pl.ds(at, tile)
            x, dy = normed[...], cot_ref[...]
            gate, up = dot_nt(x, wf[0, rows, :]), dot_nt(x, wf[1, rows, :])
            back = dot_nt(dy, wf[2, rows, :])
            cubed = 0.044715 * (gate * gate)
            t = jnp.tanh(0.7978845608028654 * gate * (1.0 + cubed))
            gelu = 0.5 * gate * (1.0 + t)
            slope = 0.5 * (1.0 + t) + 0.5 * gate * (1.0 - t * t) * (0.7978845608028654 * (1.0 + 3.0 * cubed))
            hid = (gelu * up).astype(bf)
            d_gate = (back * up * slope).astype(bf)
            d_up = (back * gelu).astype(bf)
            first = (n == 0) & (r == 0)
            part_out = dot_nn(hid, wf[2, rows, :])
            part_back = dot_nn(d_gate, wf[0, rows, :]) + dot_nn(d_up, wf[1, rows, :])
            acc_out[...] = jnp.where(first, part_out, acc_out[...] + part_out)
            acc_back[...] = jnp.where(first, part_back, acc_back[...] + part_back)
            for t_id, left, right in ((0, d_gate, x), (1, d_up, x), (2, hid, dy)):
                value = dot_nn(left.T, right).astype(bf)
                for s in range(tile // part):
                    unit = r * (tile // part) + s
                    raw[t_id, n, unit // 2, unit % 2] = value[s * part : (s + 1) * part]
        return 0

    for n in range(count):
        units(jnp.int32(n), 0)
        for t in range(3):
            links.send(("f1", t, n), raw.at[t, n, :, 1 - core], got.at[t, n], sibling)
    for at in range(0, own, tile):
        rows = slice(at, at + tile)
        mid = middle[rows, :]
        out_ref[rows, :] = (mid + acc_out[rows, :]).astype(bf)
        s = unit_norm(mid)
        n2 = mid * s
        gn = acc_back[rows, :]
        e = gn * gain_ref[...]
        grad = cot_ref[rows, :].astype(jnp.float32) + s * (e - n2 * jnp.mean(e * n2, axis=1, keepdims=True))
        middle_ref[rows, :] = grad
        normed[rows, :] = grad.astype(bf)
        gain = jnp.sum(gn * n2, axis=0, keepdims=True)
        gain_out[...] = gain if at == 0 else gain_out[...] + gain
    for at in range(0, width, tile):
        cols = slice(at, at + tile)
        do_ref[:, cols] = dot_nt(normed[...], wo[cols, :]).astype(bf)
        raw_out_ref[cols, :] = dot_nn(ctx_ref[:, cols].T, normed[...]).astype(bf)
    saves = []
    for t in range(3):
        for n in range(count):
            links.take(("f1", t, n), got.at[t, n])
            for s in range(GROUP // 2):
                got[t, n, s] = got[t, n, s] + raw[t, n, s, core]
        whole = got.at[t].reshape(count, 2, 2, part, width)
        for src, dst in ((whole, keep_out.at[t]), (whole.at[:, :, 1 - xx, pl.ds(0, half)], fx_out.at[t]),
                         (whole.at[:, 1 - yy, :, pl.ds(half, half)], fy_out.at[t])):
            one = pltpu.make_async_copy(src, dst, local_sems.at[4 + len(saves)])
            one.start()
            saves.append(one)
    links.drain()
    for one in saves:
        one.wait()


def ffn(tokens, cotangent, context, gain, was, wfs, count):
    own, width = tokens.shape
    hidden = wfs.shape[1]
    part = hidden // count // GROUP
    bf = jnp.bfloat16
    vm = pl.BlockSpec(memory_space=pltpu.VMEM)
    hb = pl.BlockSpec(memory_space=pl.ANY)
    return pl.pallas_call(
        functools.partial(ffn_kernel, count),
        in_specs=[vm, vm, vm, vm, hb, hb],
        out_specs=[vm] * 5 + [hb] * 3,
        out_shape=[
            jax.ShapeDtypeStruct((own, width), bf),
            jax.ShapeDtypeStruct((own, width), jnp.float32),
            jax.ShapeDtypeStruct(context.shape, bf),
            jax.ShapeDtypeStruct((context.shape[1], width), bf),
            jax.ShapeDtypeStruct((1, width), jnp.float32),
            jax.ShapeDtypeStruct((3, count, 2, 2, part, width), bf),
            jax.ShapeDtypeStruct((3, count, 2, part // 2, width), bf),
            jax.ShapeDtypeStruct((3, count, 2, part // 2, width), bf),
        ],
        scratch_shapes=[
            pltpu.VMEM((was.shape[1], width), bf),
            pltpu.VMEM((3, hidden, width), bf),
            pltpu.VMEM((own, width), bf),
            pltpu.VMEM((own, width), jnp.float32),
            pltpu.VMEM((own, width), jnp.float32),
            pltpu.VMEM((own, width), jnp.float32),
            pltpu.VMEM((3, count, GROUP // 2, 2, part, width), bf),
            pltpu.VMEM((3, count, GROUP // 2, part, width), bf),
            pltpu.SemaphoreType.DMA((3 * count,)),
            pltpu.SemaphoreType.DMA((3 * count,)),
            pltpu.SemaphoreType.DMA((16,)),
        ],
        compiler_params=pltpu.CompilerParams(collective_id=3, has_side_effects=True, vmem_limit_bytes=60 * 2**20),
        name="ffn",
    )(tokens, cotangent, context, gain, was, wfs)


def finish_kernel(count, radius, buckets, scale, gain_ref, tiny_ref, kinds_ref,
                  dq_ref, dk_ref, dv_ref, xs_ref, was_ref, raw_out_ref, keep_ref, fx_ref, fy_ref, strips_ref,
                  full_a, full_f, gn_out, side_ref, total_ref,
                  dq, dk, dv, xs, wq, wk, wv, ga, got_a1, got_ax, got_ay, got_ay2, got_ax2,
                  keep_f, got_fx, got_fy, got_fy2, got_fx2, from_a, from_f,
                  gx, own_acc, got_x, rows8, small, tiny, tiny_z, side_z, strip_v, send_sems, recv_sems, local_sems):
    batch, place = lax.axis_index("batch"), lax.axis_index("mp")
    sub = batch % GROUP
    core, xx, yy = sub % 2, (sub // 2) % 2, sub // 4
    links = Links(send_sems, recv_sems, batch, place)
    rows_a, rows_f = ga.shape[4], keep_f.shape[4]
    ha, hf = rows_a // 2, rows_f // 2
    own, width = gn_out.shape
    step = own // PIECES
    bf = jnp.bfloat16
    f32 = jnp.float32
    sibling, x_near, y_near = [(flip(batch, bit), place) for bit in (1, 2, 4)]

    def inside(n):
        return (n >= 0) & (n < count)

    used = [0]

    def load(src, dst, start=True):
        one = pltpu.make_async_copy(src, dst, local_sems.at[used[0]])
        used[0] += 1
        if start:
            one.start()
        return one

    load_f = [(load(keep_ref.at[t], keep_f.at[t]), load(fx_ref.at[t], got_fx.at[t]), load(fy_ref.at[t], got_fy.at[t])) for t in range(3)]
    load_k = [load(dk_ref, dk), load(was_ref.at[1], wk), load(dv_ref, dv), load(was_ref.at[2], wv)]
    load_x = [load(xs_ref, xs), load(dq_ref, dq), load(was_ref.at[0], wq)]
    load_o = load(raw_out_ref, ga.at[1, 1])
    heads = strips_ref.shape[0]
    load_s = {}

    def load_strip(n):
        load_s[n] = pltpu.make_async_copy(strips_ref.at[n // 2, pl.ds(n % 2 * 64, 64)], strip_v.at[n % 2], local_sems.at[40 + n % 2])
        load_s[n].start()

    load_strip(0)
    load_strip(1)

    def one_f(t):
        def go(n, _):
            for i in range(2):
                keep_f[t, n, i, xx, pl.ds(0, hf)] = keep_f[t, n, i, xx, pl.ds(0, hf)] + got_fx[t, n, i]
                keep_f[t, n, yy, i, pl.ds(hf, hf)] = keep_f[t, n, yy, i, pl.ds(hf, hf)] + got_fy[t, n, i]
            return 0
        lax.fori_loop(0, count, go, 0)

    for t in range(3):
        for one in load_f[t]:
            one.wait()
        one_f(t)
        if t == 0:
            greet(batch, place, count)
        links.send(("fy2", t), keep_f.at[t, :, 1 - yy, xx, pl.ds(0, hf)], got_fy2.at[t], y_near)
        links.send(("fx2", t), keep_f.at[t, :, yy, 1 - xx, pl.ds(hf, hf)], got_fx2.at[t], x_near)

    for one in load_k + load_x:
        one.wait()
    rows8[...] = jnp.zeros_like(rows8)

    def block_part(block, local):
        tile = 256
        for at in range(0, own, tile):
            rows = pl.ds(pl.multiple_of(block * own + at, tile), tile)
            value = dot_nn(dk[rows, :], wk[...]) + dot_nn(dv[rows, :], wv[...])
            if local:
                value = value + dot_nn(dq[at : at + tile, :], wq[...])
                own_acc[at : at + tile, :] = value
            else:
                gx[block, at : at + tile] = value.astype(bf)
            prod = value * xs[block, at : at + tile].astype(f32)
            acc = prod[0:8]
            for r in range(8, tile, 8):
                acc = acc + prod[r : r + 8]
            rows8[...] = rows8[...] + acc

    def x_send(way, level):
        for p in range(PIECES):
            rows = pl.ds(p * step, step)
            links.send(("x", way, level, p), gx.at[place + way * level, rows], got_x.at[0 if way > 0 else 1, level - 1, rows],
                       (batch, place + way), inside(place + way * level))

    def x_step(level, p):
        rows = pl.ds(p * step, step)
        for side, way in ((0, 1), (1, -1)):
            dest = place + way * (level - 1)
            behind = inside(place - way)
            def add():
                got_x[side, level - 1, rows] = got_x[side, level - 1, rows] + gx[dest, rows]
            links.take(("x", way, level, p), got_x.at[side, level - 1, rows], behind & inside(dest), add)
            links.send(("x", way, level - 1, p), got_x.at[side, level - 1, rows], got_x.at[side, level - 2, rows],
                       (batch, place + way), behind & inside(dest))

    def x_first(level, p):
        rows = pl.ds(p * step, step)
        for side, way in ((0, 1), (1, -1)):
            dest = place + way * (level - 1)
            links.send(("x0", way, level - 1, p), gx.at[jnp.clip(dest, 0, count - 1), rows], got_x.at[side, level - 2, rows],
                       (batch, place + way), jnp.logical_not(inside(place - way)) & inside(dest))

    inner = wq.shape[0]

    def raw_grad(kind, left, right):
        for c in range(0, inner, 256):
            value = dot_nn(left(c).T, right()).astype(bf)
            at = c
            while at < c + 256:
                n, r = at // (2 * rows_a), at % (2 * rows_a)
                h, r = r // rows_a, r % rows_a
                size = min(rows_a - r, c + 256 - at)
                ga[kind // 2, kind % 2, n, h, r : r + size] = value[at - c : at - c + size]
                at += size
        links.send(("a1", kind), ga.at[kind // 2, kind % 2, :, 1 - core], got_a1.at[kind // 2, kind % 2], sibling)

    def last_f(t):
        links.take(("fy2", t), got_fy2.at[t])
        links.take(("fx2", t), got_fx2.at[t])
        def one(n, _):
            keep_f[t, n, yy, xx, pl.ds(0, hf)] = keep_f[t, n, yy, xx, pl.ds(0, hf)] + got_fy2[t, n]
            keep_f[t, n, yy, xx, pl.ds(hf, hf)] = keep_f[t, n, yy, xx, pl.ds(hf, hf)] + got_fx2[t, n]
            return 0
        lax.fori_loop(0, count, one, 0)

    def unit(t, n):
        return keep_f.at[t, n, yy, xx]

    def line(t, hop):
        for side, way in ((0, 1), (1, -1)):
            here = place == (hop if way > 0 else count - 1 - hop)
            for n in (range(count - 1, hop, -1) if way > 0 else range(count - 1 - hop)):
                if hop > 0:
                    def add():
                        ref, more = unit(t, n), from_f.at[t, side, n]
                        ref[...] = ref[...] + more[...]
                    links.take(("z", t, side, n, hop - 1), from_f.at[t, side, n], here, add)
                links.send(("z", t, side, n, hop), unit(t, n), from_f.at[t, side, n], (batch, place + way), here)

    def line_a():
        for d in range(count - 1, 0, -1):
            for way in (1, -1):
                dest = place + way * d
                links.send(("za", way, d), ga.at[yy, xx, jnp.clip(dest, 0, count - 1), core], from_a.at[place], (batch, dest), inside(dest))

    def view_a(ref, s, half):
        return ref.at[s // 2, s % 2, half_rows(half, rows_a)]

    def view_f(t):
        return lambda ref, s, half: ref.at[t, s, half_rows(half, rows_f)]

    gathers = {}

    def finish(t):
        for side, way in ((0, 1), (1, -1)):
            for hop in range(count - 1):
                n = hop + 1 if way > 0 else count - 2 - hop
                def add():
                    ref, more = unit(t, n), from_f.at[t, side, n]
                    ref[...] = ref[...] + more[...]
                links.take(("z", t, side, n, hop), from_f.at[t, side, n], place == n, add)
        full_f[t, sub] = keep_f[t, place, yy, xx]
        gathers[t] = PlaneGather(links, ("g", t), view_f(t), full_f, sub)
        gathers[t].start()

    def finish_a():
        from_a[place] = ga[yy, xx, place, core]
        for d in range(1, count):
            for way in (1, -1):
                links.take(("za", way, d), from_a.at[place - way * d], inside(place - way * d))
        total = from_a[0].astype(f32)
        for n in range(1, count):
            total = total + from_a[n].astype(f32)
        full_a[sub // 2, sub % 2] = total.astype(bf)
        gathers["a"] = PlaneGather(links, ("g", "a"), view_a, full_a, sub)
        gathers["a"].start()

    def a_core(kind):
        i, j = kind // 2, kind % 2
        links.take(("a1", kind), got_a1.at[i, j])
        for n in range(count):
            ga[i, j, n, core] = ga[i, j, n, core] + got_a1[i, j, n]

    def a_middle():
        links.take(("ax",), got_ax)
        links.take(("ay",), got_ay)
        for n in range(count):
            for i in range(2):
                ga[i, xx, n, core, pl.ds(0, ha)] = ga[i, xx, n, core, pl.ds(0, ha)] + got_ax[i, n]
                ga[yy, i, n, core, pl.ds(ha, ha)] = ga[yy, i, n, core, pl.ds(ha, ha)] + got_ay[i, n]
        links.send(("ay2",), ga.at[1 - yy, xx, :, core, pl.ds(0, ha)], got_ay2, y_near)
        links.send(("ax2",), ga.at[yy, 1 - xx, :, core, pl.ds(ha, ha)], got_ax2, x_near)

    def a_last():
        links.take(("ay2",), got_ay2)
        links.take(("ax2",), got_ax2)
        for n in range(count):
            ga[yy, xx, n, core, pl.ds(0, ha)] = ga[yy, xx, n, core, pl.ds(0, ha)] + got_ay2[n]
            ga[yy, xx, n, core, pl.ds(ha, ha)] = ga[yy, xx, n, core, pl.ds(ha, ha)] + got_ax2[n]

    sums = {}

    def strip_sum(h):
        span = strip_v.shape[2]
        eight = None
        for n in (2 * h, 2 * h + 1):
            load_s[n].wait()
            for g in range(8):
                shift = 8 * g + 64 * (n % 2)
                part = strip_v[n % 2, 8 * g : 8 * g + 8, :]
                part = part if shift == 0 else pltpu.roll(part, span - shift, 1)
                eight = part if eight is None else eight + part
            if n + 2 < 2 * heads:
                load_strip(n + 2)
        flat = eight[0:1, :]
        for r in range(1, 8):
            flat = flat + pltpu.roll(eight[r : r + 1, :], span - r, 1)
        sums[h] = flat

    def tiny_step(n):
        links.take(("s", n), tiny.at[2 * n + 1])
        before = small if n == 0 else tiny.at[2 * n]
        tiny[2 * n + 2] = before[...] + tiny[2 * n + 1]
        if n < 2:
            links.send(("s", n + 1), tiny.at[2 * n + 2], tiny.at[2 * n + 3], (flip(batch, 2 << n), place))
        else:
            tiny_z[place] = tiny[6]
            for d in range(1, count):
                for way in (1, -1):
                    links.send(("sz", way, d), tiny.at[6], tiny_z.at[place], (batch, place + way * d), inside(place + way * d))

    def parts(level):
        for way in (1, -1):
            @pl.when(inside(place + way * level))
            def _():
                block_part(place + way * level, False)

    for way in (1, -1):
        @pl.when(inside(place + way * radius))
        def _():
            block_part(place + way * radius, False)
        x_send(way, radius)
    load_o.wait()
    links.send(("a1", 3), ga.at[1, 1, :, 1 - core], got_a1.at[1, 1], sibling)
    raw_grad(1, lambda c: dk[:, c : c + 256], lambda: xs[...].reshape(count * own, width))
    raw_grad(2, lambda c: dv[:, c : c + 256], lambda: xs[...].reshape(count * own, width))
    raw_grad(0, lambda c: dq[:, c : c + 256], lambda: xs[place])
    for level in range(radius - 1, 0, -1):
        parts(level)
    for t in range(3):
        last_f(t)
        line(t, 0)
    for kind in (3, 1, 2, 0):
        a_core(kind)
    links.send(("ax",), ga.at[:, 1 - xx, :, core, pl.ds(0, ha)], got_ax, x_near)
    links.send(("ay",), ga.at[1 - yy, :, :, core, pl.ds(ha, ha)], got_ay, y_near)
    for level in range(radius, 1, -1):
        for p in range(PIECES):
            x_step(level, p)
    for level in range(radius, 1, -1):
        for p in range(PIECES):
            x_first(level, p)
    block_part(place, True)
    for h in range(0, heads // 2):
        strip_sum(h)
    a_middle()
    for hop in range(1, count - 1):
        for t in range(3):
            line(t, hop)
        if hop == 1:
            for h in range(heads // 2, heads):
                strip_sum(h)
            a_last()
            line_a()

    diag = jnp.concatenate([sums[h] for h in range(heads)], axis=0)
    small[...] = jnp.zeros_like(small)
    small[0:1, :] = jnp.sum(rows8[...], axis=0, keepdims=True) / gain_ref[...]
    small[1:2, :] = tiny_ref[...]
    bucket_lane = lax.broadcasted_iota(jnp.int32, (heads, LANES), 1)
    rel = jnp.zeros((heads, LANES), f32)
    for b in range(buckets):
        rel = jnp.where(bucket_lane == b, jnp.sum(jnp.where(kinds_ref[...] == b, diag, 0.0), axis=1, keepdims=True), rel)
    per = width // LANES
    for h in range(heads):
        small[2 + h // per : 3 + h // per, h % per * LANES : (h % per + 1) * LANES] = rel[h : h + 1, :]
    links.send(("s", 0), small, tiny.at[1], sibling)
    for t in range(3):
        finish(t)
    tiny_step(0)
    for t in range(3):
        gathers[t].middle()
    tiny_step(1)
    finish_a()
    for p in range(PIECES):
        rows = pl.ds(p * step, step)
        for side, way in ((0, 1), (1, -1)):
            ok = inside(place - way)
            near = inside(place - 2 * way)
            if radius > 1:
                links.take(("x", way, 1, p), got_x.at[side, 0, rows], ok & near)
                links.take(("x0", way, 1, p), got_x.at[side, 0, rows], ok & jnp.logical_not(near))
            else:
                links.take(("x", way, 1, p), got_x.at[side, 0, rows], ok)
            def blank():
                got_x[side, 0, rows] = jnp.zeros((step, width), bf)
            pl.when(jnp.logical_not(ok))(blank)
        gn_out[rows, :] = own_acc[rows, :] + got_x[0, 0, rows].astype(f32) + got_x[1, 0, rows].astype(f32)
    tiny_step(2)
    for t in range(3):
        gathers[t].far()
    gathers["a"].middle()
    for t in range(3):
        gathers[t].end()

    def squares(read, blocks):
        def one(n, acc):
            value = read(n).astype(f32) * scale
            for r in range(0, value.shape[0], 8):
                acc = acc + value[r : r + 8] * value[r : r + 8]
            return acc
        return jnp.sum(lax.fori_loop(0, blocks, one, jnp.zeros((8, width), f32)), axis=0, keepdims=True)

    f_sums = [squares(lambda n: full_f[t, n], GROUP) for t in range(3)]
    gathers["a"].far()
    for d in range(1, count):
        for way in (1, -1):
            links.take(("sz", way, d), tiny_z.at[place - way * d], inside(place - way * d))
    summed = tiny_z[0]
    for n in range(1, count):
        summed = summed + tiny_z[n]
    total_ref[...] = summed
    gathers["a"].end()
    a_sums = [squares(lambda n: full_a[s, n], 2) for s in range(4)]
    side_z[place] = jnp.concatenate(a_sums + f_sums + [jnp.zeros((1, width), f32)], axis=0)
    for d in range(1, count):
        for way in (1, -1):
            links.send(("q", way, d), side_z.at[place], side_z.at[place], (batch, place + way * d), inside(place + way * d))
    for d in range(1, count):
        for way in (1, -1):
            links.take(("q", way, d), side_z.at[place - way * d], inside(place - way * d))
    summed = side_z[0]
    for n in range(1, count):
        summed = summed + side_z[n]
    side_ref[...] = summed
    links.drain()


def finish(gain, tiny, kinds, dq, dk, dv, xs, was, raw_out, keep, fx, fy, strips, count, radius, buckets, scale):
    own = dq.shape[0]
    width = gain.shape[1]
    total, inner = dk.shape
    heads, _, span = strips.shape
    part = keep.shape[4]
    half_a = inner // count // 2
    bf = jnp.bfloat16
    vm = pl.BlockSpec(memory_space=pltpu.VMEM)
    hb = pl.BlockSpec(memory_space=pl.ANY)
    V = lambda *s: pltpu.VMEM(s + (width,), bf)
    F = lambda *s: pltpu.VMEM(s, jnp.float32)
    O = lambda *s: jax.ShapeDtypeStruct(s, jnp.float32)
    return pl.pallas_call(
        functools.partial(finish_kernel, count, radius, buckets, scale),
        in_specs=[vm] * 3 + [hb] * 10,
        out_specs=[vm] * 5,
        out_shape=[
            jax.ShapeDtypeStruct((4, 2, half_a, width), bf), jax.ShapeDtypeStruct((3, GROUP, part, width), bf),
            O(own, width), O(8, width), O(8, width),
        ],
        scratch_shapes=[
            pltpu.VMEM((own, inner), bf), pltpu.VMEM((total, inner), bf), pltpu.VMEM((total, inner), bf), V(count, own),
            V(inner), V(inner), V(inner),
            V(2, 2, count, 2, half_a), V(2, 2, count, half_a), V(2, count, half_a // 2), V(2, count, half_a // 2), V(count, half_a // 2), V(count, half_a // 2),
            V(3, count, 2, 2, part), V(3, count, 2, part // 2), V(3, count, 2, part // 2), V(3, count, part // 2), V(3, count, part // 2),
            V(count, half_a), V(3, 2, count, part),
            V(count, own), F(own, width), V(2, radius, own), F(8, width),
            F(8, width), F(7, 8, width), F(count, 8, width), F(count, 8, width), F(2, 64, span),
            pltpu.SemaphoreType.DMA((240,)), pltpu.SemaphoreType.DMA((240,)), pltpu.SemaphoreType.DMA((48,)),
        ],
        compiler_params=pltpu.CompilerParams(collective_id=2, has_side_effects=True, vmem_limit_bytes=63 * 2**20),
        name="finish",
    )(gain, tiny, kinds, dq, dk, dv, xs, was, raw_out, keep, fx, fy, strips)


def emit_kernel(heads, kinds, scale, totals, place_ref, tok_ref, mid_ref, gn_ref, layer_ref, gain_ref, a_ref, f_ref, side_ref, sums_ref,
                layer_out, tokens_out, gq, gk, gv, go, gg, gu, gd, rel_out, g1_out, g2_out, model_out, heads_out, units_out, rows_out):
    n = pl.program_id(0)
    f32 = jnp.float32
    layer_out[...] = layer_ref[...]
    x = tok_ref[...].astype(f32)
    s = unit_norm(x)
    n1 = x * s
    e = gn_ref[...] * gain_ref[...]
    tokens_out[...] = (mid_ref[...] + s * (e - n1 * jnp.mean(e * n1, axis=1, keepdims=True))).astype(tokens_out.dtype)
    inner_total, hidden_total, width = totals
    shard = a_ref.shape[0] // 4
    hidden = f_ref.shape[0] // 3

    def part(ref, at, size, straight, turned, stat, row):
        for c in range(0, size, LANES):
            rows = min(LANES, size - c)
            value = ref[at + c : at + c + rows, :].astype(f32) * scale
            if rows < LANES:
                value = jnp.concatenate([value, jnp.zeros((LANES - rows, LANES), f32)], axis=0)
            turn = value.T
            if straight is not None:
                straight[c : c + rows, :] = value[:rows]
            if turned is not None:
                turned[:, c : c + rows] = turn[:, :rows]
            more = jnp.sum(turn * turn, axis=0, keepdims=True)[:, :rows] * (1.0 / width)
            old = stat[row : row + 1, c : c + rows]
            stat[row : row + 1, c : c + rows] = jnp.where(n == 0, TINY, old) + more

    for row, (straight, turned) in enumerate(((None, gq), (None, gk), (None, gv), (go, None))):
        part(a_ref, row * shard, shard, straight, turned, heads_out, row)
    for row, (straight, turned) in enumerate(((None, gg), (None, gu), (gd, None))):
        part(f_ref, row * hidden, hidden, straight, turned, units_out, row)

    @pl.when(n == 0)
    def _():
        model_out[0:4, :] = side_ref[0:4, :] * (1.0 / inner_total) + TINY
        model_out[4:5, :] = side_ref[6:7, :] * (1.0 / hidden_total) + TINY
        rows_out[...] = side_ref[4:6, :] * (1.0 / hidden_total) + TINY
        g1_out[...] = sums_ref[0:1, :] * scale
        g2_out[...] = sums_ref[1:2, :] * scale
        per = width // LANES
        rel = jnp.concatenate([sums_ref[2 + h // per : 3 + h // per, h % per * LANES : (h % per + 1) * LANES] for h in range(heads)], axis=0)
        own_heads = rel_out.shape[1]
        mine = jnp.zeros((8, LANES), f32)
        for m in range(heads // own_heads):
            block = jnp.concatenate([rel[m * own_heads : (m + 1) * own_heads], jnp.zeros((8 - own_heads, LANES), f32)], axis=0)
            mine = jnp.where(place_ref[0] == m, block, mine)
        mine = jnp.concatenate([mine * scale, jnp.zeros((LANES - 8, LANES), f32)], axis=0).T
        rel_out[...] = mine[:kinds, :own_heads]


def emit(place, tokens, middle, gn, layer, gain, full_a, full_f, side, sums, heads, own_heads, kinds, scale, count):
    own, width = tokens.shape
    inner, hidden = full_a.shape[0] // 4, full_f.shape[0] // 3
    steps = width // LANES
    pieces = max(n for n in range(1, steps + 1) if own % n == 0 and own // n % 16 == 0)
    rows = pl.BlockSpec((own // pieces, width), lambda n: (jnp.minimum(n, pieces - 1), 0))
    whole = lambda *s: pl.BlockSpec(s, lambda n: (0,) * len(s))
    down = lambda r: pl.BlockSpec((LANES, r), lambda n: (n, 0))
    across = lambda r: pl.BlockSpec((r, LANES), lambda n: (0, n))
    O = lambda *s: jax.ShapeDtypeStruct(s, jnp.float32)
    totals = (float(inner * count), float(hidden * count), width)
    return pl.pallas_call(
        functools.partial(emit_kernel, heads, kinds, scale, totals),
        grid=(steps,),
        in_specs=[pl.BlockSpec(memory_space=pltpu.SMEM), rows, rows, rows, rows, whole(1, width), across(4 * inner), across(3 * hidden),
                  whole(8, width), whole(8, width)],
        out_specs=[rows, rows, down(inner), down(inner), down(inner), across(inner), down(hidden), down(hidden), across(hidden),
                   whole(kinds, own_heads), whole(1, width), whole(1, width), whole(5, width), whole(4, inner), whole(3, hidden), whole(2, width)],
        out_shape=[
            jax.ShapeDtypeStruct((own, width), jnp.bfloat16), jax.ShapeDtypeStruct((own, width), jnp.bfloat16),
            O(width, inner), O(width, inner), O(width, inner), O(inner, width), O(width, hidden), O(width, hidden), O(hidden, width),
            O(kinds, own_heads), O(1, width), O(1, width), O(5, width), O(4, inner), O(3, hidden), O(2, width),
        ],
        compiler_params=pltpu.CompilerParams(vmem_limit_bytes=40 * 2**20),
        name="emit",
    )(place, tokens, middle, gn, layer, gain, full_a, full_f, side, sums)


def on_device(tokens, cotangent, lengths, buckets, w_query, w_key, w_value, w_out, w_gate, w_up, w_down, rel_table, gain_one, gain_two):
    bf = jnp.bfloat16
    count = lax.axis_size("mp")
    batches = lax.axis_size("batch")
    own, width = tokens.shape
    total = own * count
    inner = w_query.shape[1]
    hidden_rows = w_gate.shape[1]
    limit = (buckets.shape[0] + 1) // 2
    radius = min(count - 1, -(-(limit - 1) // own))
    place = jnp.reshape(lax.axis_index("mp") * own, (1,)).astype(jnp.int32)
    kinds = rel_table.shape[0]
    heads = rel_table.shape[1] * count

    wa = jnp.concatenate([w_query.T, w_key.T, w_value.T, w_out], axis=0).reshape(4, 2, inner // 2, width)
    wf = jnp.stack([w_gate.T, w_up.T, w_down]).reshape(3, GROUP, hidden_rows // GROUP, width)
    kind_row = bucket_kinds(buckets, TQ)[None]
    rel_own = jnp.pad(rel_table.T, ((0, 8 - rel_table.shape[1]), (0, 0)))
    rows_one, wa_all, wf_all, q, k, kt, v, vt, strips = gather(
        tokens, gain_one[None], wa, wf, rel_own, kind_row, count, radius, heads
    )
    was = wa_all.reshape(4, count * inner, width)
    wfs = wf_all.reshape(3, count * hidden_rows, width)
    context, lse = attend(lengths, place, strips, q, k, vt, limit, TQ, TK, HP_F)

    layer_out, grad_middle, grad_context, raw_out, gain_two_part, keep, fx, fy = ffn(
        tokens, cotangent, context, gain_two[None], was, wfs, count
    )
    got_fx = lax.ppermute(fx, "batch", [(n, n ^ 2) for n in range(batches)])
    got_fy = lax.ppermute(fy, "batch", [(n, n ^ 4) for n in range(batches)])
    grad_q, grad_k, grad_v, grad_strips = attend_back(
        lengths, place, strips, q, k, kt, v, context, grad_context, lse.reshape(heads // HP_B, HP_B, own), limit, TQ, TK, HP_B
    )
    scale = (total * batches) ** -0.5
    one_group = batches == GROUP
    full_a, full_f, grad_norm_one, side, sums = finish(
        gain_one[None], gain_two_part, kind_row, grad_q, grad_k, grad_v, rows_one, was,
        raw_out.reshape(count, 2, inner // 2, width), keep, got_fx, got_fy, grad_strips, count, radius, kinds, scale
    )
    full_a = full_a.reshape(4 * inner, width)
    full_f = full_f.reshape(3 * hidden_rows, width)
    if not one_group:
        full_a, full_f, sums = [one / GROUP for one in lax.psum((full_a.astype(jnp.float32), full_f.astype(jnp.float32), sums), "batch")]
        squares = [jnp.sum((one * scale) ** 2, axis=0) for one in (*jnp.split(full_a, 4), *jnp.split(full_f, 3))]
        side = lax.psum(jnp.stack(squares + [squares[0]]), "mp")
    outs = emit(
        lax.axis_index("mp").astype(jnp.int32).reshape(1), tokens, grad_middle, grad_norm_one, layer_out, gain_one[None], full_a, full_f, side, sums,
        heads, rel_table.shape[1], kinds, scale, count
    )
    return (*outs[:10], outs[10][0], outs[11][0], *outs[12:])


TQ = 512
TK = 256
HP_F = 4
HP_B = 2


def solution(mesh):
    in_specs = (
        P(("batch", "mp"), None),
        P(("batch", "mp"), None),
        P("batch", None),
        P(),
        P(None, "mp"),
        P(None, "mp"),
        P(None, "mp"),
        P("mp", None),
        P(None, "mp"),
        P(None, "mp"),
        P("mp", None),
        P(None, "mp"),
        P(),
        P(),
    )
    out_specs = (
        P(("batch", "mp"), None),
        P(("batch", "mp"), None),
        P(None, "mp"),
        P(None, "mp"),
        P(None, "mp"),
        P("mp", None),
        P(None, "mp"),
        P(None, "mp"),
        P("mp", None),
        P(None, "mp"),
        P(),
        P(),
        P(),
        P(None, "mp"),
        P(None, "mp"),
        P(),
    )
    return jax.shard_map(
        on_device, mesh=mesh, in_specs=in_specs, out_specs=out_specs, check_vma=False
    )
```

```python
import functools

import jax
import jax.numpy as jnp
from jax import lax
from jax.experimental import pallas as pl
from jax.experimental.pallas import tpu as pltpu
from jax.sharding import PartitionSpec as P

TINY = 1e-30

NEG = -1e9
LANES = 128

def strip_sizes(limit, tq):
    reach = -(-limit // LANES)
    nq = tq // LANES
    off = LANES * (reach + nq)
    return reach, off, off + LANES * reach + tq

def bucket_kinds(buckets, tq):
    limit = (buckets.shape[0] + 1) // 2
    _, off, width = strip_sizes(limit, tq)
    shift = off - (limit - 1)
    return jnp.pad(lax.rev(buckets, (0,)), (shift, width - shift - buckets.shape[0]))


def ends_list(lens_ref, rows_dev, count):
    total = jnp.int32(0)
    ends = []
    for r in range(rows_dev):
        for c in range(count):
            total = total + lens_ref[r, c]
            ends.append(total)
    return ends

def segment_of(place, ends, count):
    seg = jnp.zeros_like(place)
    pad = jnp.zeros_like(place)
    for n, end in enumerate(ends):
        past = place >= end
        seg = seg + jnp.where(past, 1, 0)
        if n % count == count - 2:
            pad = pad + jnp.where(past, 1, 0)
        if n % count == count - 1:
            pad = pad - jnp.where(past, 1, 0)
    return jnp.where(pad > 0, place + 4096, seg)

def key_range(first, last, ends, count):
    low = jnp.int32(0)
    high = ends[-1]
    for n, end in enumerate(ends):
        is_pad_next = n % count == count - 2
        low = jnp.where(first >= end, jnp.maximum(low, first if is_pad_next else end), low)
    for n in range(len(ends) - 1, -1, -1):
        is_pad = n % count == count - 1
        high = jnp.where(last < ends[n], (last + 1) if is_pad else ends[n], high)
    return (low // LANES) * LANES, high


def for_chunks(body, q_at, tq, tk, half, ends, count, w_high):
    ranges = [key_range(q_at + at, q_at + at + half - 1, ends, count) for at in range(0, tq, half)]
    low, high = ranges[0][0], ranges[-1][1]
    steps = (high - low + tk - 1) // tk
    low = jnp.minimum(low, w_high - steps * tk)

    def step(c, _):
        ks = pl.multiple_of(low + c * tk, LANES)
        if len(ranges) == 1:
            body(ks, 0, tq)
            return 0
        one, two = [(ks < end) & (ks + tk > start) for start, end in ranges]
        pl.when(one & two)(lambda: body(ks, 0, tq))
        pl.when(one & jnp.logical_not(two))(lambda: body(ks, 0, half))
        pl.when(two & jnp.logical_not(one))(lambda: body(ks, half, half))
        return 0

    lax.fori_loop(0, steps, step, 0)


def window(own, total, limit):
    first = lax.axis_index("mp") * own
    radius = -(-(limit - 1) // own)
    return jnp.maximum(first - radius * own, 0), jnp.minimum(first + (radius + 1) * own, total)

def fill_segments(kseg, ends, count, total):
    def one(n, _):
        at = pl.multiple_of(n * 256, 256)
        place = at + lax.broadcasted_iota(jnp.int32, (256, LANES), 0)
        kseg[pl.ds(at, 256), :] = segment_of(place, ends, count)
        return 0
    lax.fori_loop(0, total // 256, one, 0)

def tile_lanes(x, n):
    return x if n == 1 else jnp.concatenate([x] * n, axis=1)

def lane_start(ks, q_at, g, reach, off, nq):
    d = (ks - q_at) // LANES + g
    return pl.multiple_of(off - LANES * jnp.clip(d, -reach, reach + nq - 1), LANES)

def fwd_kernel(cfg, lens_ref, strip, q_ref, k_ref, vt_ref, ctx_ref, lse_ref, kseg, top, tot, acc):
    tq, tk, limit, rows_dev, count, own, total, hp = cfg
    reach, off, width = strip_sizes(limit, tq)
    ends = ends_list(lens_ref, rows_dev, count)
    @pl.when(pl.program_id(0) == 0)
    def _():
        fill_segments(kseg, ends, count, total)
    first = lax.axis_index("mp") * own
    w_high = window(own, total, limit)[1]
    lane = lax.broadcasted_iota(jnp.int32, (tq, LANES), 1)
    for qt in range(own // tq):
        rows = slice(qt * tq, (qt + 1) * tq)
        q_at = first + qt * tq
        halves = []
        for h in range(hp):
            q2 = q_ref[rows, h // 2 * LANES : h // 2 * LANES + LANES]
            halves.append(jnp.where((lane < 64) == (h % 2 == 0), q2, jnp.zeros_like(q2)))
        qseg = segment_of(q_at + lax.broadcasted_iota(jnp.int32, (1, tq), 1), ends, count)
        top[...] = jnp.full(top.shape, 2 * NEG, jnp.float32)
        tot[...] = jnp.zeros_like(tot)
        acc[...] = jnp.zeros_like(acc)

        def body(ks, skip, lanes):
            nq = lanes // LANES
            at = slice(skip, skip + lanes)
            same = tile_lanes(kseg[pl.ds(ks, tk), :], nq) == qseg[:, at]
            starts = [lane_start(ks, q_at + skip, g, reach, off, nq) for g in range(tk // LANES)]
            raws, news, fades, lows = [], [], [], []
            for h in range(hp):
                kc = k_ref[pl.ds(ks, tk), h // 2 * LANES : h // 2 * LANES + LANES]
                raws.append(lax.dot_general(kc, halves[h][at], (((1,), (1,)), ((), ())), preferred_element_type=jnp.float32))
            for h in range(hp):
                bias = jnp.concatenate([strip[h, :, pl.ds(one, lanes)] for one in starts], axis=0)
                raws[h] = jnp.where(same, raws[h] + bias, NEG)
                old = top[h : h + 1, at]
                new = jnp.maximum(old, jnp.max(raws[h], axis=0, keepdims=True))
                top[h : h + 1, at] = new
                news.append(new)
                fades.append(jnp.exp(old - new))
            for h in range(hp):
                p = jnp.exp(raws[h] - news[h])
                tot[h : h + 1, at] = tot[h : h + 1, at] * fades[h] + jnp.sum(p, axis=0, keepdims=True)
                lows.append(p.astype(jnp.bfloat16))
            for h in range(hp):
                acc[h, :, at] = acc[h, :, at] * fades[h] + jnp.dot(
                    vt_ref[h * 64 : h * 64 + 64, pl.ds(ks, tk)], lows[h], preferred_element_type=jnp.float32
                )

        for_chunks(body, q_at, tq, tk, min(256, tq), ends, count, w_high)
        for pair in range(hp // 2):
            both = jnp.concatenate([acc[h] / tot[h : h + 1, :] for h in (2 * pair, 2 * pair + 1)], axis=0)
            ctx_ref[rows, pair * LANES : pair * LANES + LANES] = both.T.astype(jnp.bfloat16)
        for h in range(hp):
            lse_ref[0, h : h + 1, rows] = top[h : h + 1, :] + jnp.log(tot[h : h + 1, :])


def attend(lengths, strips, q, k, vt, limit, tq, tk, hp):
    own, inner = q.shape
    total = k.shape[0]
    steps = inner // 64 // hp
    lanes = hp * 64
    rows_dev, count = lengths.shape
    width = strips.shape[2]
    cfg = (tq, tk, limit, rows_dev, count, own, total, hp)
    smem = pl.BlockSpec(memory_space=pltpu.SMEM)
    return pl.pallas_call(
        functools.partial(fwd_kernel, cfg),
        grid=(steps,),
        in_specs=[smem,
            pl.BlockSpec((hp, LANES, width), lambda p: (p, 0, 0)),
            pl.BlockSpec((own, lanes), lambda p: (0, p)),
            pl.BlockSpec((total, lanes), lambda p: (0, p)),
            pl.BlockSpec((lanes, total), lambda p: (p, 0))],
        out_specs=[pl.BlockSpec((own, lanes), lambda p: (0, p)),
                   pl.BlockSpec((1, hp, own), lambda p: (p, 0, 0))],
        out_shape=[jax.ShapeDtypeStruct((own, inner), jnp.bfloat16), jax.ShapeDtypeStruct((steps, hp, own), jnp.float32)],
        scratch_shapes=[pltpu.VMEM((total, LANES), jnp.int32), pltpu.VMEM((hp, tq), jnp.float32), pltpu.VMEM((hp, tq), jnp.float32),
                        pltpu.VMEM((hp, 64, tq), jnp.float32)],
        compiler_params=pltpu.CompilerParams(vmem_limit_bytes=56 * 2**20),
        name="attend",
    )(lengths, strips, q, k, vt)


def bwd_kernel(cfg, lens_ref, strip, q_ref, k_ref, kt_ref, v_ref, ctx_ref, do_ref, lse_ref,
               dq_ref, dk_ref, dv_ref, dstrip, kseg, dk_acc, dv_acc, dq_acc):
    tq, tk, limit, rows_dev, count, own, total, hp = cfg
    reach, off, width = strip_sizes(limit, tq)
    nq = tq // LANES
    ends = ends_list(lens_ref, rows_dev, count)
    @pl.when(pl.program_id(0) == 0)
    def _():
        fill_segments(kseg, ends, count, total)
    dstrip[...] = jnp.zeros_like(dstrip)
    dk_acc[...] = jnp.zeros_like(dk_acc)
    dv_acc[...] = jnp.zeros_like(dv_acc)
    first = lax.axis_index("mp") * own
    w_high = window(own, total, limit)[1]
    lane = lax.broadcasted_iota(jnp.int32, (tq, LANES), 1)
    for qt in range(own // tq):
        rows = slice(qt * tq, (qt + 1) * tq)
        q_at = first + qt * tq
        q_half, do_half, delta, lse = [], [], [], []
        for pair in range(hp // 2):
            lanes = slice(pair * LANES, pair * LANES + LANES)
            q2 = q_ref[rows, lanes]
            do2 = do_ref[rows, lanes]
            prod = (do2.astype(jnp.float32) * ctx_ref[rows, lanes].astype(jnp.float32)).T
            for hh in range(2):
                keep = (lane < 64) == (hh == 0)
                q_half.append(jnp.where(keep, q2, jnp.zeros_like(q2)))
                do_half.append(jnp.where(keep, do2, jnp.zeros_like(do2)))
                delta.append(jnp.sum(prod[hh * 64 : hh * 64 + 64], axis=0, keepdims=True))
                lse.append(lse_ref[0, 2 * pair + hh : 2 * pair + hh + 1, rows])
        qseg = segment_of(q_at + lax.broadcasted_iota(jnp.int32, (1, tq), 1), ends, count)
        dq_acc[...] = jnp.zeros_like(dq_acc)

        def body(ks, skip, span):
            nq = span // LANES
            at = slice(skip, skip + span)
            same = tile_lanes(kseg[pl.ds(ks, tk), :], nq) == qseg[:, at]
            starts = [lane_start(ks, q_at + skip, g, reach, off, nq) for g in range(tk // LANES)]
            for pair in range(hp // 2):
                lanes = slice(pair * LANES, pair * LANES + LANES)
                kc = k_ref[pl.ds(ks, tk), lanes]
                vc = v_ref[pl.ds(ks, tk), lanes]
                dk_part = dv_part = None
                for h in (2 * pair, 2 * pair + 1):
                    s = lax.dot_general(kc, q_half[h][at], (((1,), (1,)), ((), ())), preferred_element_type=jnp.float32)
                    bias = jnp.concatenate([strip[h, :, pl.ds(one, span)] for one in starts], axis=0)
                    p = jnp.exp(jnp.where(same, s + (bias - lse[h][:, at]), NEG))
                    dp = lax.dot_general(vc, do_half[h][at], (((1,), (1,)), ((), ())), preferred_element_type=jnp.float32)
                    ds = p * (dp - delta[h][:, at])
                    for g, one in enumerate(starts):
                        dstrip[h, :, pl.ds(one, span)] += ds[g * LANES : (g + 1) * LANES, :]
                    pb = p.astype(jnp.bfloat16)
                    dsb = ds.astype(jnp.bfloat16)
                    dv_one = jnp.dot(pb, do_half[h][at], preferred_element_type=jnp.float32)
                    dk_one = jnp.dot(dsb, q_half[h][at], preferred_element_type=jnp.float32)
                    dv_part = dv_one if dv_part is None else dv_part + dv_one
                    dk_part = dk_one if dk_part is None else dk_part + dk_one
                    dq_acc[h, :, at] += jnp.dot(kt_ref[h * 64 : h * 64 + 64, pl.ds(ks, tk)], dsb, preferred_element_type=jnp.float32)
                dv_acc[pl.ds(ks, tk), lanes] += dv_part
                dk_acc[pl.ds(ks, tk), lanes] += dk_part

        for_chunks(body, q_at, tq, tk, min(256, tq), ends, count, w_high)
        for pair in range(hp // 2):
            dq_ref[rows, pair * LANES : pair * LANES + LANES] = jnp.concatenate([dq_acc[2 * pair], dq_acc[2 * pair + 1]], axis=0).T.astype(jnp.bfloat16)
    dk_ref[...] = dk_acc[...].astype(jnp.bfloat16)
    dv_ref[...] = dv_acc[...].astype(jnp.bfloat16)


def attend_back(lengths, strips, q, k, kt, v, ctx, do, lse, limit, tq, tk, hp):
    own, inner = q.shape
    total = k.shape[0]
    steps = inner // 64 // hp
    lanes = hp * 64
    rows_dev, count = lengths.shape
    width = strips.shape[2]
    cfg = (tq, tk, limit, rows_dev, count, own, total, hp)
    smem = pl.BlockSpec(memory_space=pltpu.SMEM)
    tall = pl.BlockSpec((total, lanes), lambda p: (0, p))
    short = pl.BlockSpec((own, lanes), lambda p: (0, p))
    band = pl.BlockSpec((hp, LANES, width), lambda p: (p, 0, 0))
    return pl.pallas_call(
        functools.partial(bwd_kernel, cfg),
        grid=(steps,),
        in_specs=[smem, band,
            short, tall, pl.BlockSpec((lanes, total), lambda p: (p, 0)), tall, short, short,
            pl.BlockSpec((1, hp, own), lambda p: (p, 0, 0))],
        out_specs=[short, tall, tall, band],
        out_shape=[jax.ShapeDtypeStruct((own, inner), jnp.bfloat16), jax.ShapeDtypeStruct((total, inner), jnp.bfloat16),
                   jax.ShapeDtypeStruct((total, inner), jnp.bfloat16), jax.ShapeDtypeStruct(strips.shape, jnp.float32)],
        scratch_shapes=[pltpu.VMEM((total, LANES), jnp.int32),
                        pltpu.VMEM((total, lanes), jnp.float32), pltpu.VMEM((total, lanes), jnp.float32),
                        pltpu.VMEM((hp, 64, tq), jnp.float32)],
        compiler_params=pltpu.CompilerParams(vmem_limit_bytes=60 * 2**20),
        name="attend_back",
    )(lengths, strips, q, k, kt, v, ctx, do, lse)


MESH = pl.DeviceIdType.MESH
GROUP = 8


def flip(index, bit):
    return index + bit * (1 - 2 * ((index // bit) % 2))


class Links:
    def __init__(self, send_sems, recv_sems, batch, place):
        self.send_sems, self.recv_sems = send_sems, recv_sems
        self.batch, self.place = batch, place
        self.slots = {}
        self.sent = []

    def slot(self, key):
        return self.slots.setdefault(key, len(self.slots))

    def copy(self, key, src, dst, target):
        n = self.slot(key)
        return pltpu.make_async_remote_copy(
            src_ref=src, dst_ref=dst, send_sem=self.send_sems.at[n], recv_sem=self.recv_sems.at[n],
            device_id=target, device_id_type=MESH)

    def send(self, key, src, dst, target, when=None):
        def go():
            self.copy(key, src, dst, target).start()
        self.sent.append((key, src, dst, target, when))
        if when is None:
            go()
        else:
            pl.when(when)(go)

    def take(self, key, dst, when=None, then=None):
        def go():
            self.copy(key, dst, dst, (self.batch, self.place)).wait_recv()
            if then is not None:
                then()
        if when is None:
            go()
        else:
            pl.when(when)(go)

    def drain(self):
        for key, src, dst, target, when in self.sent:
            def go():
                self.copy(key, src, dst, target).wait_send()
            if when is None:
                go()
            else:
                pl.when(when)(go)


def greet(batch, place, count):
    bar = pltpu.get_barrier_semaphore()
    for bit in (1, 2, 4):
        pl.semaphore_signal(bar, inc=1, device_id=(flip(batch, bit), place), device_id_type=MESH)
    for way in range(1 - count, count):
        if way != 0:
            @pl.when((place + way >= 0) & (place + way < count))
            def _():
                pl.semaphore_signal(bar, inc=1, device_id=(batch, place + way), device_id_type=MESH)
    pl.semaphore_wait(bar, 3 + count - 1)


def both(a, b):
    return a if b is None else (b if a is None else a & b)


class PlaneGather:
    def __init__(self, links, key, view, ref, sub, when=None):
        self.l, self.key, self.view, self.ref, self.sub, self.when = links, key, view, ref, sub, when

    def put(self, path, sub, half, bit):
        region = self.view(self.ref, sub, half)
        self.l.send((self.key, path), region, region, (flip(self.l.batch, bit), self.l.place), self.when)

    def start(self):
        self.put("x", self.sub, None, 2)
        self.put("y", self.sub, None, 4)
        self.put("c", self.sub, None, 1)

    def middle(self):
        sub = self.sub
        self.l.take((self.key, "x"), self.view(self.ref, flip(sub, 2), None), self.when)
        self.put("xy", flip(sub, 2), 0, 4)
        self.put("xc", flip(sub, 2), None, 1)
        self.l.take((self.key, "y"), self.view(self.ref, flip(sub, 4), None), self.when)
        self.put("yx", flip(sub, 4), 1, 2)
        self.put("yc", flip(sub, 4), None, 1)

    def far(self):
        sub = self.sub
        diagonal = flip(flip(sub, 2), 4)
        self.l.take((self.key, "xy"), self.view(self.ref, diagonal, 0), self.when)
        self.put("0c", diagonal, 0, 1)
        self.l.take((self.key, "yx"), self.view(self.ref, diagonal, 1), self.when)
        self.put("1c", diagonal, 1, 1)

    def end(self):
        sub = flip(self.sub, 1)
        diagonal = flip(flip(sub, 2), 4)
        self.l.take((self.key, "c"), self.view(self.ref, sub, None), self.when)
        self.l.take((self.key, "xc"), self.view(self.ref, flip(sub, 2), None), self.when)
        self.l.take((self.key, "yc"), self.view(self.ref, flip(sub, 4), None), self.when)
        self.l.take((self.key, "0c"), self.view(self.ref, diagonal, 0), self.when)
        self.l.take((self.key, "1c"), self.view(self.ref, diagonal, 1), self.when)


def half_rows(half, rows):
    return pl.ds(0, rows) if half is None else pl.ds(half * (rows // 2), rows // 2)


PIECES = 4
EPS = 1e-06


def unit_norm(values):
    return lax.rsqrt(jnp.mean(values * values, axis=1, keepdims=True) + EPS)


def dot_nt(a, b):
    return lax.dot_general(a, b, (((1,), (1,)), ((), ())), preferred_element_type=jnp.float32)


def dot_nn(a, b):
    return jnp.dot(a, b, preferred_element_type=jnp.float32)


def gather_kernel(count, radius, tok_ref, gain_ref, wq_ref, wk_ref, wv_ref, wo_ref, wg_ref, wu_ref, wd_ref, rel_ref, kinds_ref,
                  xs_out, was_out, wfs_ref, q_out, k_out, kt_out, v_out, vt_out, strips_out,
                  xs, was, q_v, k_v, kt_v, v_v, vt_v, wf, rel_all, table, strip_v, send_sems, recv_sems, local_sems):
    batch, place = lax.axis_index("batch"), lax.axis_index("mp")
    sub = batch % GROUP
    links = Links(send_sems, recv_sems, batch, place)
    own, width = tok_ref.shape
    rows_a = was.shape[3]
    rows_f = wf.shape[2]
    step = own // PIECES
    local = []

    def copy_local(src, dst):
        one = pltpu.make_async_copy(src, dst, local_sems.at[len(local)])
        local.append(one)
        return one

    own_a = [copy_local(ref, was.at[n, place]) for n, ref in enumerate((wq_ref, wk_ref, wv_ref, wo_ref))]
    own_d = copy_local(wd_ref, wf.at[2])
    for one in own_a + [own_d]:
        one.start()
    gain = gain_ref[...].reshape(1, width)
    for p in range(PIECES):
        rows = pl.ds(p * step, step)
        values = tok_ref[rows, :].astype(jnp.float32)
        xs[place, rows] = (values * unit_norm(values) * gain).astype(xs.dtype)
    for n, ref in enumerate((wg_ref, wu_ref)):
        turn = ref[...].T
        for g in range(GROUP):
            wf[n, g] = turn[g * rows_f : (g + 1) * rows_f]
    for one in own_a + [own_d]:
        one.wait()
    copy_local(wf, wfs_ref.at[:, place]).start()
    greet(batch, place, count)

    def view_a(mm):
        return lambda ref, s, half: ref.at[s // 2, mm, s % 2, half_rows(half, rows_a)]

    def view_f(mm):
        return lambda ref, s, half: ref.at[:, mm, s, half_rows(half, rows_f)]

    def inside(n):
        return (n >= 0) & (n < count)

    for way in (1, -1):
        ok = inside(place + way)
        target = (batch, place + way)
        links.send(("a", way, 1), view_a(place)(was, sub, None), view_a(place)(was, sub, None), target, ok)
        links.send(("f", way, 1), wf.at[:, sub], view_f(place)(wfs_ref, sub, None), target, ok)
    rel_all[place, 0 : rel_ref.shape[0], :] = rel_ref[...]
    for d in range(1, count):
        for way in (1, -1):
            links.send(("r", way, d), rel_all.at[place], rel_all.at[place], (batch, place + way * d), inside(place + way * d))
    for way in (1, -1):
        ok = inside(place + way)
        target = (batch, place + way)
        for p in range(PIECES):
            rows = pl.ds(p * step, step)
            links.send(("x", way, 1, p), xs.at[place, rows], xs.at[place, rows], target, ok)
    for n in range(count):
        @pl.when((n - place > radius) | (place - n > radius))
        def _():
            def blank(p, _):
                xs[n, pl.ds(p * step, step)] = jnp.zeros((step, width), xs.dtype)
                return 0
            lax.fori_loop(0, PIECES, blank, 0)
            for ref in (k_v, v_v):
                ref[pl.ds(n * own, own)] = jnp.zeros((own, ref.shape[1]), ref.dtype)
            for ref in (kt_v, vt_v):
                ref[:, pl.ds(n * own, own)] = jnp.zeros((ref.shape[0], own), ref.dtype)

    gathers = {}

    def weights_arrive(kind, dist):
        for way in (1, -1):
            source = place - way * dist
            ok = inside(source)
            view, ref = (view_a(source), was) if kind == "a" else (view_f(source), wfs_ref)
            region = view(ref, sub, None)
            links.take((kind, way, dist), region, ok)
            if dist < count - 1:
                links.send((kind, way, dist + 1), region, region, (batch, place + way), ok & inside(place + way))
            gather = PlaneGather(links, ("g", kind, way, dist), view, ref, sub, ok)
            gather.start()
            gathers[kind, way, dist] = gather

    def x_arrive(dist, p):
        for way in (1, -1):
            source = place - way * dist
            ok = inside(source)
            region = xs.at[source, pl.ds(p * step, step)]
            links.take(("x", way, dist, p), region, ok)
            if dist < radius:
                links.send(("x", way, dist + 1, p), region, region, (batch, place + way), ok & inside(place + way))

    def stage(name, kind, dist):
        for way in (1, -1):
            getattr(gathers[kind, way, dist], name)()

    heads = table.shape[0]
    span = table.shape[1]
    kinds = rel_ref.shape[1]

    def make_table():
        for d in range(1, count):
            for way in (1, -1):
                links.take(("r", way, d), rel_all.at[place - way * d], inside(place - way * d))
        per = heads // count
        joined = jnp.concatenate([rel_all[n, 0:per, :] for n in range(count)], axis=0)
        for at in range(0, span, 512):
            lanes = pl.ds(at, min(512, span - at))
            kind = kinds_ref[:, lanes]
            total = jnp.zeros((heads, kind.shape[1]), jnp.float32)
            for b in range(NB_MAX):
                if b < kinds:
                    total = total + jnp.where(kind == b, joined[:, b : b + 1], 0.0)
            table[:, lanes] = total

    strip_copies = []

    def make_strip(h):
        slot = h % 2
        if h >= 2:
            strip_copies[h - 2].wait()
        row = table[h : h + 1, :]
        strip_v[slot] = pltpu.roll(jnp.broadcast_to(row, (LANES, span)), 0, 1, stride=1, stride_axis=0)
        one = pltpu.make_async_copy(strip_v.at[slot], strips_out.at[h], local_sems.at[8 + slot])
        one.start()
        strip_copies.append(one)

    inner = was.shape[1] * was.shape[2] * rows_a

    def weight_tile(kind, n):
        return was[kind, n].reshape(2 * rows_a, width)

    def project(block, when):
        def go():
            x = xs[block]
            def one(n, _):
                at = pl.multiple_of(n * 2 * rows_a, 64)
                kt_v[pl.ds(at, 2 * rows_a), pl.ds(pl.multiple_of(block * own, LANES), own)] = dot_nt(weight_tile(1, n), x).astype(kt_v.dtype)
                vt_v[pl.ds(at, 2 * rows_a), pl.ds(pl.multiple_of(block * own, LANES), own)] = dot_nt(weight_tile(2, n), x).astype(vt_v.dtype)
                return 0
            lax.fori_loop(0, count, one, 0)
            rows = pl.ds(pl.multiple_of(block * own, LANES), own)
            tile = 256
            for at in range(0, inner, tile):
                wk = was[1].reshape(inner, width)[at : at + tile]
                wv = was[2].reshape(inner, width)[at : at + tile]
                k_v[rows, at : at + tile] = dot_nt(x, wk).astype(k_v.dtype)
                v_v[rows, at : at + tile] = dot_nt(x, wv).astype(v_v.dtype)
        if when is None:
            go()
        else:
            pl.when(when)(go)

    def project_q():
        x = xs[place]
        tile = 256
        for at in range(0, inner, tile):
            wq = was[0].reshape(inner, width)[at : at + tile]
            q_v[:, at : at + tile] = dot_nt(x, wq).astype(q_v.dtype)

    saves = []

    def save_block(block, when):
        rows = pl.ds(pl.multiple_of(block * own, LANES), own)
        for src, dst in ((k_v, k_out), (v_v, v_out)):
            saves.append((pltpu.make_async_copy(src.at[rows], dst.at[rows], local_sems.at[10 + len(saves)]), when))
        for src, dst in ((kt_v, kt_out), (vt_v, vt_out)):
            saves.append((pltpu.make_async_copy(src.at[:, rows], dst.at[:, rows], local_sems.at[10 + len(saves)]), when))
        for one, ok in saves[-4:]:
            one.start() if ok is None else pl.when(ok)(one.start)

    dists = range(1, count)
    make_table()
    for h in range(2):
        make_strip(h)
    for d in dists:
        weights_arrive("a", d)
    weights_arrive("f", 1)
    for h in range(2, 4):
        make_strip(h)
    for d in dists:
        stage("middle", "a", d)
    if count > 2:
        weights_arrive("f", 2)
    for h in range(4, 6):
        make_strip(h)
    for d in dists:
        stage("far", "a", d)
    for d in range(3, count):
        weights_arrive("f", d)
    stage("middle", "f", 1)
    for p in range(PIECES):
        x_arrive(1, p)
    for d in dists:
        stage("end", "a", d)
    copy_local(was, was_out).start()
    project_q()
    copy_local(q_v, q_out).start()
    project(place, None)
    save_block(place, None)
    for d in range(2, count):
        stage("middle", "f", d)
    for way in (1, -1):
        project(place + way, inside(place + way))
        save_block(place + way, inside(place + way))
    for d in dists:
        stage("far", "f", d)
    for h in range(6, heads):
        make_strip(h)
    for r in range(2, radius + 1):
        for p in range(PIECES):
            x_arrive(r, p)
        for way in (1, -1):
            project(place + way * r, inside(place + way * r))
            save_block(place + way * r, inside(place + way * r))
    copy_local(xs, xs_out).start()
    for n in range(count):
        save_block(n, (n - place > radius) | (place - n > radius))
    for d in dists:
        stage("end", "f", d)
    links.drain()
    for one in local[5:] + strip_copies[-2:]:
        one.wait()
    for one, ok in saves:
        one.wait() if ok is None else pl.when(ok)(one.wait)


NB_MAX = 128


def gather(tokens, gain, w_heads, w_hidden, rel, kinds, count, radius, heads):
    own, width = tokens.shape
    bf = jnp.bfloat16
    total = own * count
    half_a = w_heads[0].shape[0] // 2
    part = w_hidden[2].shape[0] // GROUP
    inner = count * 2 * half_a
    span = kinds.shape[1]
    vm = pl.BlockSpec(memory_space=pltpu.VMEM)
    hb = pl.BlockSpec(memory_space=pl.ANY)
    shapes = [
        ((count, own, width), bf),
        ((4, count, 2, half_a, width), bf),
        ((3, count, GROUP, part, width), bf),
        ((own, inner), bf), ((total, inner), bf), ((inner, total), bf), ((total, inner), bf), ((inner, total), bf),
        ((heads, LANES, span), jnp.float32),
    ]
    return pl.pallas_call(
        functools.partial(gather_kernel, count, radius),
        in_specs=[vm, vm] + [hb] * 4 + [vm, vm, hb, vm, vm],
        out_specs=[hb] * len(shapes),
        out_shape=[jax.ShapeDtypeStruct(*one) for one in shapes],
        scratch_shapes=[pltpu.VMEM(*shapes[n]) for n in (0, 1, 3, 4, 5, 6, 7)] + [
            pltpu.VMEM((3, GROUP, part, width), bf),
            pltpu.VMEM((count, 8, rel.shape[1]), jnp.float32),
            pltpu.VMEM((heads, span), jnp.float32),
            pltpu.VMEM((2, LANES, span), jnp.float32),
            pltpu.SemaphoreType.DMA((170,)),
            pltpu.SemaphoreType.DMA((170,)),
            pltpu.SemaphoreType.DMA((64,)),
        ],
        compiler_params=pltpu.CompilerParams(collective_id=1, has_side_effects=True, vmem_limit_bytes=60 * 2**20),
        name="gather",
    )(tokens, gain, *[one.reshape(2, half_a, width) for one in w_heads], *w_hidden[:2], w_hidden[2].reshape(GROUP, part, width), rel, kinds)


def ffn_kernel(count, tok_ref, cot_ref, ctx_ref, gain_ref, was_ref, wfs_ref,
               out_ref, middle_ref, do_ref, raw_out_ref, gain_out, keep_out, fx_out, fy_out,
               wo, wf, normed, middle, act, raw, got, send_sems, recv_sems, local_sems):
    batch, place = lax.axis_index("batch"), lax.axis_index("mp")
    sub = batch % GROUP
    core, xx, yy = sub % 2, (sub // 2) % 2, sub // 4
    links = Links(send_sems, recv_sems, batch, place)
    sibling = (flip(batch, 1), place)
    own, width = tok_ref.shape
    gain_two = gain_ref[...].reshape(1, width)
    hidden = wf.shape[1]
    per = hidden // count
    part = per // GROUP
    half = part // 2
    bf = jnp.bfloat16
    loads = [pltpu.make_async_copy(was_ref.at[3], wo, local_sems.at[0])]
    loads += [pltpu.make_async_copy(wfs_ref.at[t], wf.at[t], local_sems.at[1 + t]) for t in range(3)]
    for one in loads:
        one.start()
    bar = pltpu.get_barrier_semaphore()
    pl.semaphore_signal(bar, inc=1, device_id=sibling, device_id_type=MESH)
    loads[0].wait()
    tile = 256
    for at in range(0, own, tile):
        rows = slice(at, at + tile)
        mid = tok_ref[rows, :].astype(jnp.float32) + dot_nn(ctx_ref[rows, :], wo[...])
        middle[rows, :] = mid
        normed[rows, :] = (mid * unit_norm(mid) * gain_two).astype(bf)
    for one in loads[1:]:
        one.wait()
    pl.semaphore_wait(bar, 1)

    def products(j):
        rows = slice(j * tile, (j + 1) * tile)
        return dot_nt(normed[...], wf[0, rows, :]), dot_nt(normed[...], wf[1, rows, :]), dot_nt(cot_ref[...], wf[2, rows, :])

    ahead = products(0)
    tiles = hidden // tile
    for j in range(tiles):
        gate, up, back = ahead
        if j + 1 < tiles:
            ahead = products(j + 1)
        cols = slice(j * tile, (j + 1) * tile)
        squared = 0.044715 * (gate * gate)
        t = jnp.tanh(0.7978845608028654 * gate * (1.0 + squared))
        half_up = 0.5 * (1.0 + t)
        gelu = gate * half_up
        slope = half_up + 0.5 * gate * (1.0 - t * t) * (0.7978845608028654 * (1.0 + 3.0 * squared))
        act[0, :, cols] = (back * up * slope).astype(bf)
        act[1, :, cols] = (back * gelu).astype(bf)
        act[2, :, cols] = (gelu * up).astype(bf)
        n, r = j * tile // per, j * tile % per // part
        for t_id in range(3):
            value = dot_nn(act[t_id, :, cols].T, cot_ref[...] if t_id == 2 else normed[...]).astype(bf)
            for s in range(tile // part):
                raw[t_id, n, (r + s) // 2, (r + s) % 2] = value[s * part : (s + 1) * part]
        if (j + 1) * tile % per == 0:
            for t_id in range(3):
                links.send(("f1", t_id, n), raw.at[t_id, n, :, 1 - core], got.at[t_id, n], sibling)
    for at in range(0, own, tile):
        rows = slice(at, at + tile)
        mid = middle[rows, :]
        out_ref[rows, :] = (mid + dot_nn(act[2, rows, :], wf[2])).astype(bf)
        s = unit_norm(mid)
        n2 = mid * s
        gn = dot_nn(act[0, rows, :], wf[0]) + dot_nn(act[1, rows, :], wf[1])
        e = gn * gain_two
        grad = cot_ref[rows, :].astype(jnp.float32) + s * (e - n2 * jnp.mean(e * n2, axis=1, keepdims=True))
        middle_ref[rows, :] = grad
        normed[rows, :] = grad.astype(bf)
        gain = jnp.sum(gn * n2, axis=0, keepdims=True)
        gain_out[...] = gain if at == 0 else gain_out[...] + gain
    for at in range(0, width, tile):
        cols = slice(at, at + tile)
        do_ref[:, cols] = dot_nt(normed[...], wo[cols, :]).astype(bf)
        raw_out_ref[cols, :] = dot_nn(ctx_ref[:, cols].T, normed[...]).astype(bf)
    saves = []
    for t in range(3):
        for n in range(count):
            links.take(("f1", t, n), got.at[t, n])
            for s in range(GROUP // 2):
                got[t, n, s] = got[t, n, s] + raw[t, n, s, core]
        whole = got.at[t].reshape(count, 2, 2, part, width)
        for src, dst in ((whole, keep_out.at[t]), (whole.at[:, :, 1 - xx, pl.ds(0, half)], fx_out.at[t]),
                         (whole.at[:, 1 - yy, :, pl.ds(half, half)], fy_out.at[t])):
            one = pltpu.make_async_copy(src, dst, local_sems.at[4 + len(saves)])
            one.start()
            saves.append(one)
    links.drain()
    for one in saves:
        one.wait()


def ffn(tokens, cotangent, context, gain, was, wfs, count):
    own, width = tokens.shape
    hidden = wfs.shape[1]
    part = hidden // count // GROUP
    bf = jnp.bfloat16
    vm = pl.BlockSpec(memory_space=pltpu.VMEM)
    hb = pl.BlockSpec(memory_space=pl.ANY)
    return pl.pallas_call(
        functools.partial(ffn_kernel, count),
        in_specs=[vm, vm, vm, vm, hb, hb],
        out_specs=[vm] * 5 + [hb] * 3,
        out_shape=[
            jax.ShapeDtypeStruct((own, width), bf),
            jax.ShapeDtypeStruct((own, width), jnp.float32),
            jax.ShapeDtypeStruct(context.shape, bf),
            jax.ShapeDtypeStruct((context.shape[1], width), bf),
            jax.ShapeDtypeStruct((1, width), jnp.float32),
            jax.ShapeDtypeStruct((3, count, 2, 2, part, width), bf),
            jax.ShapeDtypeStruct((3, count, 2, part // 2, width), bf),
            jax.ShapeDtypeStruct((3, count, 2, part // 2, width), bf),
        ],
        scratch_shapes=[
            pltpu.VMEM((was.shape[1], width), bf),
            pltpu.VMEM((3, hidden, width), bf),
            pltpu.VMEM((own, width), bf),
            pltpu.VMEM((own, width), jnp.float32),
            pltpu.VMEM((3, own, hidden), bf),
            pltpu.VMEM((3, count, GROUP // 2, 2, part, width), bf),
            pltpu.VMEM((3, count, GROUP // 2, part, width), bf),
            pltpu.SemaphoreType.DMA((3 * count,)),
            pltpu.SemaphoreType.DMA((3 * count,)),
            pltpu.SemaphoreType.DMA((16,)),
        ],
        compiler_params=pltpu.CompilerParams(collective_id=3, has_side_effects=True, vmem_limit_bytes=60 * 2**20),
        name="ffn",
    )(tokens, cotangent, context, gain, was, wfs)


def finish_kernel(count, radius, buckets, scale, gain_ref, tiny_ref, kinds_ref,
                  dq_ref, dk_ref, dv_ref, xs_ref, was_ref, raw_out_ref, keep_ref, fx_ref, fy_ref, strips_ref,
                  full_a, full_f, gn_out, side_ref, total_ref,
                  dq, dk, dv, xs, wq, wk, wv, ga, got_a1, got_ax, got_ay, got_ay2, got_ax2,
                  keep_f, got_fx, got_fy, got_fy2, got_fx2, from_a, from_f,
                  gx, own_acc, got_x, rows8, small, tiny, tiny_z, side_z, strip_v, send_sems, recv_sems, local_sems):
    batch, place = lax.axis_index("batch"), lax.axis_index("mp")
    sub = batch % GROUP
    core, xx, yy = sub % 2, (sub // 2) % 2, sub // 4
    links = Links(send_sems, recv_sems, batch, place)
    rows_a, rows_f = ga.shape[4], keep_f.shape[4]
    ha, hf = rows_a // 2, rows_f // 2
    own, width = gn_out.shape
    step = own // PIECES
    bf = jnp.bfloat16
    f32 = jnp.float32
    sibling, x_near, y_near = [(flip(batch, bit), place) for bit in (1, 2, 4)]

    def inside(n):
        return (n >= 0) & (n < count)

    used = [0]

    def load(src, dst, start=True):
        one = pltpu.make_async_copy(src, dst, local_sems.at[used[0]])
        used[0] += 1
        if start:
            one.start()
        return one

    load_f = [(load(keep_ref.at[t], keep_f.at[t]), load(fx_ref.at[t], got_fx.at[t]), load(fy_ref.at[t], got_fy.at[t])) for t in range(3)]
    load_k = [load(dk_ref, dk), load(was_ref.at[1], wk), load(dv_ref, dv), load(was_ref.at[2], wv)]
    load_x = [load(xs_ref, xs), load(dq_ref, dq), load(was_ref.at[0], wq)]
    load_o = load(raw_out_ref, ga.at[1, 1])
    heads = strips_ref.shape[0]
    load_s = {}

    def load_strip(n):
        load_s[n] = pltpu.make_async_copy(strips_ref.at[n // 2, pl.ds(n % 2 * 64, 64)], strip_v.at[n % 2], local_sems.at[40 + n % 2])
        load_s[n].start()

    load_strip(0)
    load_strip(1)

    def one_f(t):
        def go(n, _):
            for i in range(2):
                keep_f[t, n, i, xx, pl.ds(0, hf)] = keep_f[t, n, i, xx, pl.ds(0, hf)] + got_fx[t, n, i]
                keep_f[t, n, yy, i, pl.ds(hf, hf)] = keep_f[t, n, yy, i, pl.ds(hf, hf)] + got_fy[t, n, i]
            return 0
        lax.fori_loop(0, count, go, 0)

    def first_f():
        for t in range(3):
            for one in load_f[t]:
                one.wait()
            one_f(t)
            if t == 0:
                greet(batch, place, count)
            links.send(("fy2", t), keep_f.at[t, :, 1 - yy, xx, pl.ds(0, hf)], got_fy2.at[t], y_near)
            links.send(("fx2", t), keep_f.at[t, :, yy, 1 - xx, pl.ds(hf, hf)], got_fx2.at[t], x_near)

    rows8[...] = jnp.zeros_like(rows8)

    def block_part(block, local):
        tile = 256
        for at in range(0, own, tile):
            rows = pl.ds(pl.multiple_of(block * own + at, tile), tile)
            value = dot_nn(dk[rows, :], wk[...]) + dot_nn(dv[rows, :], wv[...])
            if local:
                value = value + dot_nn(dq[at : at + tile, :], wq[...])
                own_acc[at : at + tile, :] = value
            else:
                gx[block, at : at + tile] = value.astype(bf)
            prod = value * xs[block, at : at + tile].astype(f32)
            acc = prod[0:8]
            for r in range(8, tile, 8):
                acc = acc + prod[r : r + 8]
            rows8[...] = rows8[...] + acc

    def x_send(way, level):
        for p in range(PIECES):
            rows = pl.ds(p * step, step)
            links.send(("x", way, level, p), gx.at[place + way * level, rows], got_x.at[0 if way > 0 else 1, level - 1, rows],
                       (batch, place + way), inside(place + way * level))

    def x_step(level, p):
        rows = pl.ds(p * step, step)
        for side, way in ((0, 1), (1, -1)):
            dest = place + way * (level - 1)
            behind = inside(place - way)
            def add():
                got_x[side, level - 1, rows] = got_x[side, level - 1, rows] + gx[dest, rows]
            links.take(("x", way, level, p), got_x.at[side, level - 1, rows], behind & inside(dest), add)
            links.send(("x", way, level - 1, p), got_x.at[side, level - 1, rows], got_x.at[side, level - 2, rows],
                       (batch, place + way), behind & inside(dest))

    def x_first(level, p):
        rows = pl.ds(p * step, step)
        for side, way in ((0, 1), (1, -1)):
            dest = place + way * (level - 1)
            links.send(("x0", way, level - 1, p), gx.at[jnp.clip(dest, 0, count - 1), rows], got_x.at[side, level - 2, rows],
                       (batch, place + way), jnp.logical_not(inside(place - way)) & inside(dest))

    inner = wq.shape[0]

    def raw_grad(kind, left, right):
        for c in range(0, inner, 256):
            value = dot_nn(left(c).T, right()).astype(bf)
            at = c
            while at < c + 256:
                n, r = at // (2 * rows_a), at % (2 * rows_a)
                h, r = r // rows_a, r % rows_a
                size = min(rows_a - r, c + 256 - at)
                ga[kind // 2, kind % 2, n, h, r : r + size] = value[at - c : at - c + size]
                at += size
        links.send(("a1", kind), ga.at[kind // 2, kind % 2, :, 1 - core], got_a1.at[kind // 2, kind % 2], sibling)

    def last_f(t):
        links.take(("fy2", t), got_fy2.at[t])
        links.take(("fx2", t), got_fx2.at[t])
        def one(n, _):
            keep_f[t, n, yy, xx, pl.ds(0, hf)] = keep_f[t, n, yy, xx, pl.ds(0, hf)] + got_fy2[t, n]
            keep_f[t, n, yy, xx, pl.ds(hf, hf)] = keep_f[t, n, yy, xx, pl.ds(hf, hf)] + got_fx2[t, n]
            return 0
        lax.fori_loop(0, count, one, 0)

    def unit(t, n):
        return keep_f.at[t, n, yy, xx]

    def line(t, hop, rank):
        for side, way in ((0, 1), (1, -1)):
            here = place == (hop if way > 0 else count - 1 - hop)
            n = count - 1 - rank if way > 0 else rank
            if hop > 0:
                def add():
                    ref, more = unit(t, n), from_f.at[t, side, n]
                    ref[...] = ref[...] + more[...]
                links.take(("z", t, side, n, hop - 1), from_f.at[t, side, n], here, add)
            links.send(("z", t, side, n, hop), unit(t, n), from_f.at[t, side, n], (batch, place + way), here)

    def line_a():
        for d in range(count - 1, 0, -1):
            for way in (1, -1):
                dest = place + way * d
                links.send(("za", way, d), ga.at[yy, xx, jnp.clip(dest, 0, count - 1), core], from_a.at[place], (batch, dest), inside(dest))

    def view_a(ref, s, half):
        return ref.at[s // 2, s % 2, half_rows(half, rows_a)]

    def view_f(t):
        return lambda ref, s, half: ref.at[t, s, half_rows(half, rows_f)]

    gathers = {}

    def finish(t):
        for side, way in ((0, 1), (1, -1)):
            for hop in range(count - 1):
                n = hop + 1 if way > 0 else count - 2 - hop
                def add():
                    ref, more = unit(t, n), from_f.at[t, side, n]
                    ref[...] = ref[...] + more[...]
                links.take(("z", t, side, n, hop), from_f.at[t, side, n], place == n, add)
        full_f[t, sub] = keep_f[t, place, yy, xx]
        gathers[t] = PlaneGather(links, ("g", t), view_f(t), full_f, sub)
        gathers[t].start()

    def finish_a():
        from_a[place] = ga[yy, xx, place, core]
        for d in range(1, count):
            for way in (1, -1):
                links.take(("za", way, d), from_a.at[place - way * d], inside(place - way * d))
        total = from_a[0].astype(f32)
        for n in range(1, count):
            total = total + from_a[n].astype(f32)
        full_a[sub // 2, sub % 2] = total.astype(bf)
        gathers["a"] = PlaneGather(links, ("g", "a"), view_a, full_a, sub)
        gathers["a"].start()

    def a_core(kind):
        i, j = kind // 2, kind % 2
        links.take(("a1", kind), got_a1.at[i, j])
        for n in range(count):
            ga[i, j, n, core] = ga[i, j, n, core] + got_a1[i, j, n]

    def a_middle():
        links.take(("ax",), got_ax)
        links.take(("ay",), got_ay)
        for n in range(count):
            for i in range(2):
                ga[i, xx, n, core, pl.ds(0, ha)] = ga[i, xx, n, core, pl.ds(0, ha)] + got_ax[i, n]
                ga[yy, i, n, core, pl.ds(ha, ha)] = ga[yy, i, n, core, pl.ds(ha, ha)] + got_ay[i, n]
        links.send(("ay2",), ga.at[1 - yy, xx, :, core, pl.ds(0, ha)], got_ay2, y_near)
        links.send(("ax2",), ga.at[yy, 1 - xx, :, core, pl.ds(ha, ha)], got_ax2, x_near)

    def a_last():
        links.take(("ay2",), got_ay2)
        links.take(("ax2",), got_ax2)
        for n in range(count):
            ga[yy, xx, n, core, pl.ds(0, ha)] = ga[yy, xx, n, core, pl.ds(0, ha)] + got_ay2[n]
            ga[yy, xx, n, core, pl.ds(ha, ha)] = ga[yy, xx, n, core, pl.ds(ha, ha)] + got_ax2[n]

    sums = {}

    def strip_sum(h):
        span = strip_v.shape[2]
        eight = None
        for n in (2 * h, 2 * h + 1):
            load_s[n].wait()
            for g in range(8):
                shift = 8 * g + 64 * (n % 2)
                part = strip_v[n % 2, 8 * g : 8 * g + 8, :]
                part = part if shift == 0 else pltpu.roll(part, span - shift, 1)
                eight = part if eight is None else eight + part
            if n + 2 < 2 * heads:
                load_strip(n + 2)
        flat = eight[0:1, :]
        for r in range(1, 8):
            flat = flat + pltpu.roll(eight[r : r + 1, :], span - r, 1)
        sums[h] = flat

    def tiny_step(n):
        links.take(("s", n), tiny.at[2 * n + 1])
        before = small if n == 0 else tiny.at[2 * n]
        tiny[2 * n + 2] = before[...] + tiny[2 * n + 1]
        if n < 2:
            links.send(("s", n + 1), tiny.at[2 * n + 2], tiny.at[2 * n + 3], (flip(batch, 2 << n), place))
        else:
            tiny_z[place] = tiny[6]
            for d in range(1, count):
                for way in (1, -1):
                    links.send(("sz", way, d), tiny.at[6], tiny_z.at[place], (batch, place + way * d), inside(place + way * d))

    def parts(level):
        for way in (1, -1):
            @pl.when(inside(place + way * level))
            def _():
                block_part(place + way * level, False)

    def wave(n):
        for hop in range(count - 2, -1, -1):
            rank = n - 2 * hop
            if 0 <= rank < count - 1 - hop:
                for t in range(3):
                    line(t, hop, rank)

    first_f()
    for one in load_k + load_x:
        one.wait()
    for way in (1, -1):
        @pl.when(inside(place + way * radius))
        def _():
            block_part(place + way * radius, False)
        x_send(way, radius)
    load_o.wait()
    links.send(("a1", 3), ga.at[1, 1, :, 1 - core], got_a1.at[1, 1], sibling)
    raw_grad(1, lambda c: dk[:, c : c + 256], lambda: xs[...].reshape(count * own, width))
    raw_grad(2, lambda c: dv[:, c : c + 256], lambda: xs[...].reshape(count * own, width))
    raw_grad(0, lambda c: dq[:, c : c + 256], lambda: xs[place])
    for t in range(3):
        last_f(t)
    wave(0)
    for level in range(radius - 1, 0, -1):
        parts(level)
    for kind in (3, 1, 2, 0):
        a_core(kind)
    links.send(("ax",), ga.at[:, 1 - xx, :, core, pl.ds(0, ha)], got_ax, x_near)
    links.send(("ay",), ga.at[1 - yy, :, :, core, pl.ds(ha, ha)], got_ay, y_near)
    wave(1)
    for level in range(radius, 1, -1):
        for p in range(PIECES):
            x_step(level, p)
    block_part(place, True)
    wave(2)
    for level in range(radius, 1, -1):
        for p in range(PIECES):
            x_first(level, p)
    for h in range(0, heads // 2):
        strip_sum(h)
    a_middle()
    wave(3)
    for h in range(heads // 2, heads * 3 // 4):
        strip_sum(h)
    a_last()
    line_a()
    for n in range(4, 2 * count - 3):
        wave(n)
    for h in range(heads * 3 // 4, heads):
        strip_sum(h)

    diag = jnp.concatenate([sums[h] for h in range(heads)], axis=0)
    small[...] = jnp.zeros_like(small)
    small[0:1, :] = jnp.sum(rows8[...], axis=0, keepdims=True) / gain_ref[...].reshape(1, width)
    small[1:2, :] = tiny_ref[...]
    bucket_lane = lax.broadcasted_iota(jnp.int32, (heads, LANES), 1)
    rel = jnp.zeros((heads, LANES), f32)
    for b in range(buckets):
        rel = jnp.where(bucket_lane == b, jnp.sum(jnp.where(kinds_ref[...] == b, diag, 0.0), axis=1, keepdims=True), rel)
    per = width // LANES
    for h in range(heads):
        small[2 + h // per : 3 + h // per, h % per * LANES : (h % per + 1) * LANES] = rel[h : h + 1, :]
    links.send(("s", 0), small, tiny.at[1], sibling)
    for t in range(3):
        finish(t)
    tiny_step(0)
    for t in range(3):
        gathers[t].middle()
    tiny_step(1)
    finish_a()
    for p in range(PIECES):
        rows = pl.ds(p * step, step)
        for side, way in ((0, 1), (1, -1)):
            ok = inside(place - way)
            near = inside(place - 2 * way)
            if radius > 1:
                links.take(("x", way, 1, p), got_x.at[side, 0, rows], ok & near)
                links.take(("x0", way, 1, p), got_x.at[side, 0, rows], ok & jnp.logical_not(near))
            else:
                links.take(("x", way, 1, p), got_x.at[side, 0, rows], ok)
            def blank():
                got_x[side, 0, rows] = jnp.zeros((step, width), bf)
            pl.when(jnp.logical_not(ok))(blank)
        gn_out[rows, :] = own_acc[rows, :] + got_x[0, 0, rows].astype(f32) + got_x[1, 0, rows].astype(f32)
    tiny_step(2)
    for t in range(3):
        gathers[t].far()
    gathers["a"].middle()
    for t in range(3):
        gathers[t].end()

    def squares(read, blocks):
        def one(n, acc):
            value = read(n).astype(f32) * scale
            for r in range(0, value.shape[0], 8):
                acc = acc + value[r : r + 8] * value[r : r + 8]
            return acc
        return jnp.sum(lax.fori_loop(0, blocks, one, jnp.zeros((8, width), f32)), axis=0, keepdims=True)

    f_sums = [squares(lambda n: full_f[t, n], GROUP) for t in range(3)]
    gathers["a"].far()
    for d in range(1, count):
        for way in (1, -1):
            links.take(("sz", way, d), tiny_z.at[place - way * d], inside(place - way * d))
    summed = tiny_z[0]
    for n in range(1, count):
        summed = summed + tiny_z[n]
    total_ref[...] = summed
    gathers["a"].end()
    a_sums = [squares(lambda n: full_a[s, n], 2) for s in range(4)]
    side_z[place] = jnp.concatenate(a_sums + f_sums + [jnp.zeros((1, width), f32)], axis=0)
    for d in range(1, count):
        for way in (1, -1):
            links.send(("q", way, d), side_z.at[place], side_z.at[place], (batch, place + way * d), inside(place + way * d))
    for d in range(1, count):
        for way in (1, -1):
            links.take(("q", way, d), side_z.at[place - way * d], inside(place - way * d))
    summed = side_z[0]
    for n in range(1, count):
        summed = summed + side_z[n]
    side_ref[...] = summed
    links.drain()


def finish(gain, tiny, kinds, dq, dk, dv, xs, was, raw_out, keep, fx, fy, strips, count, radius, buckets, scale):
    own = dq.shape[0]
    width = gain.shape[0]
    total, inner = dk.shape
    heads, _, span = strips.shape
    part = keep.shape[4]
    half_a = inner // count // 2
    bf = jnp.bfloat16
    vm = pl.BlockSpec(memory_space=pltpu.VMEM)
    hb = pl.BlockSpec(memory_space=pl.ANY)
    V = lambda *s: pltpu.VMEM(s + (width,), bf)
    F = lambda *s: pltpu.VMEM(s, jnp.float32)
    O = lambda *s: jax.ShapeDtypeStruct(s, jnp.float32)
    return pl.pallas_call(
        functools.partial(finish_kernel, count, radius, buckets, scale),
        in_specs=[vm] * 3 + [hb] * 10,
        out_specs=[vm] * 5,
        out_shape=[
            jax.ShapeDtypeStruct((4, 2, half_a, width), bf), jax.ShapeDtypeStruct((3, GROUP, part, width), bf),
            O(own, width), O(8, width), O(8, width),
        ],
        scratch_shapes=[
            pltpu.VMEM((own, inner), bf), pltpu.VMEM((total, inner), bf), pltpu.VMEM((total, inner), bf), V(count, own),
            V(inner), V(inner), V(inner),
            V(2, 2, count, 2, half_a), V(2, 2, count, half_a), V(2, count, half_a // 2), V(2, count, half_a // 2), V(count, half_a // 2), V(count, half_a // 2),
            V(3, count, 2, 2, part), V(3, count, 2, part // 2), V(3, count, 2, part // 2), V(3, count, part // 2), V(3, count, part // 2),
            V(count, half_a), V(3, 2, count, part),
            V(count, own), F(own, width), V(2, radius, own), F(8, width),
            F(8, width), F(7, 8, width), F(count, 8, width), F(count, 8, width), F(2, 64, span),
            pltpu.SemaphoreType.DMA((240,)), pltpu.SemaphoreType.DMA((240,)), pltpu.SemaphoreType.DMA((48,)),
        ],
        compiler_params=pltpu.CompilerParams(collective_id=2, has_side_effects=True, vmem_limit_bytes=63 * 2**20),
        name="finish",
    )(gain, tiny, kinds, dq, dk, dv, xs, was, raw_out, keep, fx, fy, strips)


def emit_kernel(heads, kinds, scale, totals, tok_ref, mid_ref, gn_ref, layer_ref, gain_ref, a_ref, f_ref, side_ref, sums_ref,
                layer_out, tokens_out, gq, gk, gv, go, gg, gu, gd, rel_out, g1_out, g2_out, model_out, heads_out, units_out, rows_out):
    n = pl.program_id(0)
    f32 = jnp.float32
    layer_out[...] = layer_ref[...]
    x = tok_ref[...].astype(f32)
    s = unit_norm(x)
    n1 = x * s
    e = gn_ref[...] * gain_ref[...].reshape(1, gain_ref.shape[0])
    tokens_out[...] = (mid_ref[...] + s * (e - n1 * jnp.mean(e * n1, axis=1, keepdims=True))).astype(tokens_out.dtype)
    inner_total, hidden_total, width = totals
    shard = a_ref.shape[0] // 4
    hidden = f_ref.shape[0] // 3

    def part(ref, at, size, straight, turned, stat, row):
        for c in range(0, size, LANES):
            rows = min(LANES, size - c)
            value = ref[at + c : at + c + rows, :].astype(f32) * scale
            if rows < LANES:
                value = jnp.concatenate([value, jnp.zeros((LANES - rows, LANES), f32)], axis=0)
            turn = value.T
            if straight is not None:
                straight[c : c + rows, :] = value[:rows]
            if turned is not None:
                turned[:, c : c + rows] = turn[:, :rows]
            more = jnp.sum(turn * turn, axis=0, keepdims=True)[:, :rows] * (1.0 / width)
            old = stat[row : row + 1, c : c + rows]
            stat[row : row + 1, c : c + rows] = jnp.where(n == 0, TINY, old) + more

    for row, (straight, turned) in enumerate(((gq, None), (gk, None), (gv, None), (go, None))):
        part(a_ref, row * shard, shard, straight, turned, heads_out, row)
    for row, (straight, turned) in enumerate(((None, gg), (None, gu), (gd, None))):
        part(f_ref, row * hidden, hidden, straight, turned, units_out, row)

    @pl.when(n == 0)
    def _():
        model_out[0:4, :] = side_ref[0:4, :] * (1.0 / inner_total) + TINY
        model_out[4:5, :] = side_ref[6:7, :] * (1.0 / hidden_total) + TINY
        rows_out[...] = side_ref[4:6, :] * (1.0 / hidden_total) + TINY
        g1_out[...] = (sums_ref[0:1, :] * scale).reshape(g1_out.shape)
        g2_out[...] = (sums_ref[1:2, :] * scale).reshape(g2_out.shape)
        place = lax.axis_index("mp")
        per = width // LANES
        rel = jnp.concatenate([sums_ref[2 + h // per : 3 + h // per, h % per * LANES : (h % per + 1) * LANES] for h in range(heads)], axis=0)
        own_heads = rel_out.shape[0]
        mine = jnp.zeros((8, LANES), f32)
        for m in range(heads // own_heads):
            block = jnp.concatenate([rel[m * own_heads : (m + 1) * own_heads], jnp.zeros((8 - own_heads, LANES), f32)], axis=0)
            mine = jnp.where(place == m, block, mine)
        rel_out[...] = mine[:own_heads, :kinds] * scale


def emit(tokens, middle, gn, layer, gain, full_a, full_f, side, sums, heads, own_heads, kinds, scale, count):
    own, width = tokens.shape
    inner, hidden = full_a.shape[0] // 4, full_f.shape[0] // 3
    steps = width // LANES
    pieces = max(n for n in range(1, steps + 1) if own % n == 0 and own // n % 16 == 0)
    rows = pl.BlockSpec((own // pieces, width), lambda n: (jnp.minimum(n, pieces - 1), 0))
    whole = lambda *s: pl.BlockSpec(s, lambda n: (0,) * len(s))
    down = lambda r: pl.BlockSpec((LANES, r), lambda n: (n, 0))
    across = lambda r: pl.BlockSpec((r, LANES), lambda n: (0, n))
    O = lambda *s: jax.ShapeDtypeStruct(s, jnp.float32)
    totals = (float(inner * count), float(hidden * count), width)
    return pl.pallas_call(
        functools.partial(emit_kernel, heads, kinds, scale, totals),
        grid=(steps,),
        in_specs=[rows, rows, rows, rows, whole(width), across(4 * inner), across(3 * hidden),
                  whole(8, width), whole(8, width)],
        out_specs=[rows, rows, across(inner), across(inner), across(inner), across(inner), down(hidden), down(hidden), across(hidden),
                   whole(own_heads, kinds), whole(width), whole(width), whole(5, width), whole(4, inner), whole(3, hidden), whole(2, width)],
        out_shape=[
            jax.ShapeDtypeStruct((own, width), jnp.bfloat16), jax.ShapeDtypeStruct((own, width), jnp.bfloat16),
            O(inner, width), O(inner, width), O(inner, width), O(inner, width), O(width, hidden), O(width, hidden), O(hidden, width),
            O(own_heads, kinds), O(width), O(width), O(5, width), O(4, inner), O(3, hidden), O(2, width),
        ],
        compiler_params=pltpu.CompilerParams(vmem_limit_bytes=60 * 2**20),
        name="emit",
    )(tokens, middle, gn, layer, gain, full_a, full_f, side, sums)


def on_device(tokens, cotangent, lengths, buckets, w_query, w_key, w_value, w_out, w_gate, w_up, w_down, rel_table, gain_one, gain_two):
    bf = jnp.bfloat16
    count = lax.axis_size("mp")
    batches = lax.axis_size("batch")
    own, width = tokens.shape
    total = own * count
    inner = w_query.shape[1]
    hidden_rows = w_gate.shape[1]
    limit = (buckets.shape[0] + 1) // 2
    radius = min(count - 1, -(-(limit - 1) // own))
    kinds = rel_table.shape[0]
    heads = rel_table.shape[1] * count

    kind_row = bucket_kinds(buckets, TQ)[None]
    rows_one, wa_all, wf_all, q, k, kt, v, vt, strips = gather(
        tokens, gain_one, (w_query.T, w_key.T, w_value.T, w_out), (w_gate, w_up, w_down), rel_table.T, kind_row, count, radius, heads
    )
    was = wa_all.reshape(4, count * inner, width)
    wfs = wf_all.reshape(3, count * hidden_rows, width)
    context, lse = attend(lengths, strips, q, k, vt, limit, TQ, TK, HP_F)

    layer_out, grad_middle, grad_context, raw_out, gain_two_part, keep, fx, fy = ffn(
        tokens, cotangent, context, gain_two, was, wfs, count
    )
    got_fx = lax.ppermute(fx, "batch", [(n, n ^ 2) for n in range(batches)])
    got_fy = lax.ppermute(fy, "batch", [(n, n ^ 4) for n in range(batches)])
    grad_q, grad_k, grad_v, grad_strips = attend_back(
        lengths, strips, q, k, kt, v, context, grad_context, lse.reshape(heads // HP_B, HP_B, own), limit, TQ, TK, HP_B
    )
    scale = (total * batches) ** -0.5
    one_group = batches == GROUP
    full_a, full_f, grad_norm_one, side, sums = finish(
        gain_one, gain_two_part, kind_row, grad_q, grad_k, grad_v, rows_one, was,
        raw_out.reshape(count, 2, inner // 2, width), keep, got_fx, got_fy, grad_strips, count, radius, kinds, scale
    )
    full_a = full_a.reshape(4 * inner, width)
    full_f = full_f.reshape(3 * hidden_rows, width)
    if not one_group:
        full_a, full_f, sums = [one / GROUP for one in lax.psum((full_a.astype(jnp.float32), full_f.astype(jnp.float32), sums), "batch")]
        squares = [jnp.sum((one * scale) ** 2, axis=0) for one in (*jnp.split(full_a, 4), *jnp.split(full_f, 3))]
        side = lax.psum(jnp.stack(squares + [squares[0]]), "mp")
    outs = emit(
        tokens, grad_middle, grad_norm_one, layer_out, gain_one, full_a, full_f, side, sums,
        heads, rel_table.shape[1], kinds, scale, count
    )
    return (*outs[:2], *[one.T for one in outs[2:5]], *outs[5:9], outs[9].T, *outs[10:])


TQ = 512
TK = 256
HP_F = 4
HP_B = 2


def solution(mesh):
    in_specs = (
        P(("batch", "mp"), None),
        P(("batch", "mp"), None),
        P("batch", None),
        P(),
        P(None, "mp"),
        P(None, "mp"),
        P(None, "mp"),
        P("mp", None),
        P(None, "mp"),
        P(None, "mp"),
        P("mp", None),
        P(None, "mp"),
        P(),
        P(),
    )
    out_specs = (
        P(("batch", "mp"), None),
        P(("batch", "mp"), None),
        P(None, "mp"),
        P(None, "mp"),
        P(None, "mp"),
        P("mp", None),
        P(None, "mp"),
        P(None, "mp"),
        P("mp", None),
        P(None, "mp"),
        P(),
        P(),
        P(),
        P(None, "mp"),
        P(None, "mp"),
        P(),
    )
    return jax.shard_map(
        on_device, mesh=mesh, in_specs=in_specs, out_specs=out_specs, check_vma=False
    )
```

```python
import functools

import jax
import jax.numpy as jnp
from jax import lax
from jax.experimental import pallas as pl
from jax.experimental.pallas import tpu as pltpu
from jax.sharding import PartitionSpec as P

TINY = 1e-30

NEG = -1e9
LANES = 128

def strip_sizes(limit, tq):
    reach = -(-limit // LANES)
    nq = tq // LANES
    off = LANES * (reach + nq)
    return reach, off, off + LANES * reach + tq

def bucket_kinds(buckets, tq):
    limit = (buckets.shape[0] + 1) // 2
    _, off, width = strip_sizes(limit, tq)
    shift = off - (limit - 1)
    return jnp.pad(lax.rev(buckets, (0,)), (shift, width - shift - buckets.shape[0]))


def ends_list(lens_ref, rows_dev, count):
    total = jnp.int32(0)
    ends = []
    for r in range(rows_dev):
        for c in range(count):
            total = total + lens_ref[r, c]
            ends.append(total)
    return ends

def segment_of(place, ends, count):
    seg = jnp.zeros_like(place)
    pad = jnp.zeros_like(place)
    for n, end in enumerate(ends):
        past = place >= end
        seg = seg + jnp.where(past, 1, 0)
        if n % count == count - 2:
            pad = pad + jnp.where(past, 1, 0)
        if n % count == count - 1:
            pad = pad - jnp.where(past, 1, 0)
    return jnp.where(pad > 0, place + 4096, seg)

def key_range(first, last, ends, count):
    low = jnp.int32(0)
    high = ends[-1]
    for n, end in enumerate(ends):
        is_pad_next = n % count == count - 2
        low = jnp.where(first >= end, jnp.maximum(low, first if is_pad_next else end), low)
    for n in range(len(ends) - 1, -1, -1):
        is_pad = n % count == count - 1
        high = jnp.where(last < ends[n], (last + 1) if is_pad else ends[n], high)
    return low, high


def for_chunks(body, q_at, tq, tk, half, ends, count, w_high):
    ranges = [key_range(q_at + at, q_at + at + half - 1, ends, count) for at in range(0, tq, half)]
    start, high = ranges[0][0], ranges[-1][1]
    alike = start == key_range(q_at + tq - 1, q_at + tq - 1, ends, count)[0]
    low = (start // LANES) * LANES
    steps = (high - low + tk - 1) // tk
    low = jnp.minimum(low, w_high - steps * tk)

    def step(c, _):
        ks = pl.multiple_of(low + c * tk, LANES)
        if len(ranges) == 1:
            body(ks, 0, tq)
            return 0
        one, two = [(ks < stop) & (ks + tk > begin) for begin, stop in ranges]
        plain = alike & (ks >= start) & (ks + tk <= high)
        pl.when(plain)(lambda: body(ks, 0, tq, False))
        pl.when(one & two & jnp.logical_not(plain))(lambda: body(ks, 0, tq))
        pl.when(one & jnp.logical_not(two))(lambda: body(ks, 0, half))
        pl.when(two & jnp.logical_not(one))(lambda: body(ks, half, half))
        return 0

    lax.fori_loop(0, steps, step, 0)


def window(own, total, limit):
    first = lax.axis_index("mp") * own
    radius = -(-(limit - 1) // own)
    return jnp.maximum(first - radius * own, 0), jnp.minimum(first + (radius + 1) * own, total)

def fill_segments(kseg, ends, count, total):
    def one(n, _):
        at = pl.multiple_of(n * 256, 256)
        place = at + lax.broadcasted_iota(jnp.int32, (256, LANES), 0)
        kseg[pl.ds(at, 256), :] = segment_of(place, ends, count)
        return 0
    lax.fori_loop(0, total // 256, one, 0)

def tile_lanes(x, n):
    return x if n == 1 else jnp.concatenate([x] * n, axis=1)

def lane_start(ks, q_at, g, reach, off, nq):
    d = (ks - q_at) // LANES + g
    return pl.multiple_of(off - LANES * jnp.clip(d, -reach, reach + nq - 1), LANES)

def fwd_kernel(cfg, lens_ref, strip, q_ref, k_ref, vt_ref, ctx_ref, lse_ref, kseg, top, tot, acc):
    tq, tk, limit, rows_dev, count, own, total, hp = cfg
    reach, off, width = strip_sizes(limit, tq)
    ends = ends_list(lens_ref, rows_dev, count)
    @pl.when(pl.program_id(0) == 0)
    def _():
        fill_segments(kseg, ends, count, total)
    first = lax.axis_index("mp") * own
    w_high = window(own, total, limit)[1]
    lane = lax.broadcasted_iota(jnp.int32, (tq, LANES), 1)
    for qt in range(own // tq):
        rows = slice(qt * tq, (qt + 1) * tq)
        q_at = first + qt * tq
        halves = []
        for h in range(hp):
            q2 = q_ref[rows, h // 2 * LANES : h // 2 * LANES + LANES]
            halves.append(jnp.where((lane < 64) == (h % 2 == 0), q2, jnp.zeros_like(q2)))
        qseg = segment_of(q_at + lax.broadcasted_iota(jnp.int32, (1, tq), 1), ends, count)
        top[...] = jnp.full(top.shape, 2 * NEG, jnp.float32)
        tot[...] = jnp.zeros_like(tot)
        acc[...] = jnp.zeros_like(acc)

        def body(ks, skip, lanes, masked=True):
            nq = lanes // LANES
            at = slice(skip, skip + lanes)
            same = tile_lanes(kseg[pl.ds(ks, tk), :], nq) == qseg[:, at] if masked else None
            starts = [lane_start(ks, q_at + skip, g, reach, off, nq) for g in range(tk // LANES)]
            raws, news, fades, lows = [], [], [], []
            for h in range(hp):
                kc = k_ref[pl.ds(ks, tk), h // 2 * LANES : h // 2 * LANES + LANES]
                raws.append(lax.dot_general(kc, halves[h][at], (((1,), (1,)), ((), ())), preferred_element_type=jnp.float32))
            for h in range(hp):
                bias = jnp.concatenate([strip[h, :, pl.ds(one, lanes)] for one in starts], axis=0)
                raws[h] = jnp.where(same, raws[h] + bias, NEG) if masked else raws[h] + bias
                old = top[h : h + 1, at]
                new = jnp.maximum(old, jnp.max(raws[h], axis=0, keepdims=True))
                top[h : h + 1, at] = new
                news.append(new)
                fades.append(jnp.exp(old - new))
            for h in range(hp):
                p = jnp.exp(raws[h] - news[h])
                tot[h : h + 1, at] = tot[h : h + 1, at] * fades[h] + jnp.sum(p, axis=0, keepdims=True)
                lows.append(p.astype(jnp.bfloat16))
            for h in range(hp):
                acc[h, :, at] = acc[h, :, at] * fades[h] + jnp.dot(
                    vt_ref[h * 64 : h * 64 + 64, pl.ds(ks, tk)], lows[h], preferred_element_type=jnp.float32
                )

        for_chunks(body, q_at, tq, tk, min(256, tq), ends, count, w_high)
        for pair in range(hp // 2):
            both = jnp.concatenate([acc[h] / tot[h : h + 1, :] for h in (2 * pair, 2 * pair + 1)], axis=0)
            ctx_ref[rows, pair * LANES : pair * LANES + LANES] = both.T.astype(jnp.bfloat16)
        for h in range(hp):
            lse_ref[h // 2, h % 2 : h % 2 + 1, rows] = top[h : h + 1, :] + jnp.log(tot[h : h + 1, :])


def attend(lengths, strips, q, k, vt, limit, tq, tk, hp):
    own, inner = q.shape
    total = k.shape[0]
    steps = inner // 64 // hp
    lanes = hp * 64
    rows_dev, count = lengths.shape
    width = strips.shape[2]
    cfg = (tq, tk, limit, rows_dev, count, own, total, hp)
    smem = pl.BlockSpec(memory_space=pltpu.SMEM)
    return pl.pallas_call(
        functools.partial(fwd_kernel, cfg),
        grid=(steps,),
        in_specs=[smem,
            pl.BlockSpec((hp, LANES, width), lambda p: (p, 0, 0)),
            pl.BlockSpec((own, lanes), lambda p: (0, p)),
            pl.BlockSpec((total, lanes), lambda p: (0, p)),
            pl.BlockSpec((lanes, total), lambda p: (p, 0))],
        out_specs=[pl.BlockSpec((own, lanes), lambda p: (0, p)),
                   pl.BlockSpec((hp // 2, 2, own), lambda p: (p, 0, 0))],
        out_shape=[jax.ShapeDtypeStruct((own, inner), jnp.bfloat16), jax.ShapeDtypeStruct((inner // LANES, 2, own), jnp.float32)],
        scratch_shapes=[pltpu.VMEM((total, LANES), jnp.int32), pltpu.VMEM((hp, tq), jnp.float32), pltpu.VMEM((hp, tq), jnp.float32),
                        pltpu.VMEM((hp, 64, tq), jnp.float32)],
        compiler_params=pltpu.CompilerParams(vmem_limit_bytes=56 * 2**20),
        name="attend",
    )(lengths, strips, q, k, vt)


def bwd_kernel(cfg, lens_ref, strip, q_ref, k_ref, kt_ref, v_ref, ctx_ref, do_ref, lse_ref,
               dq_ref, dk_ref, dv_ref, dstrip, kseg, dk_acc, dv_acc, dq_acc):
    tq, tk, limit, rows_dev, count, own, total, hp = cfg
    reach, off, width = strip_sizes(limit, tq)
    nq = tq // LANES
    ends = ends_list(lens_ref, rows_dev, count)
    @pl.when(pl.program_id(0) == 0)
    def _():
        fill_segments(kseg, ends, count, total)
    dstrip[...] = jnp.zeros_like(dstrip)
    dk_acc[...] = jnp.zeros_like(dk_acc)
    dv_acc[...] = jnp.zeros_like(dv_acc)
    first = lax.axis_index("mp") * own
    w_high = window(own, total, limit)[1]
    lane = lax.broadcasted_iota(jnp.int32, (tq, LANES), 1)
    for qt in range(own // tq):
        rows = slice(qt * tq, (qt + 1) * tq)
        q_at = first + qt * tq
        q_half, do_half, delta, lse = [], [], [], []
        for pair in range(hp // 2):
            lanes = slice(pair * LANES, pair * LANES + LANES)
            q2 = q_ref[rows, lanes]
            do2 = do_ref[rows, lanes]
            prod = (do2.astype(jnp.float32) * ctx_ref[rows, lanes].astype(jnp.float32)).T
            for hh in range(2):
                keep = (lane < 64) == (hh == 0)
                q_half.append(jnp.where(keep, q2, jnp.zeros_like(q2)))
                do_half.append(jnp.where(keep, do2, jnp.zeros_like(do2)))
                delta.append(jnp.sum(prod[hh * 64 : hh * 64 + 64], axis=0, keepdims=True))
                lse.append(lse_ref[pair, hh : hh + 1, rows])
        qseg = segment_of(q_at + lax.broadcasted_iota(jnp.int32, (1, tq), 1), ends, count)
        dq_acc[...] = jnp.zeros_like(dq_acc)

        def body(ks, skip, span, masked=True):
            nq = span // LANES
            at = slice(skip, skip + span)
            same = tile_lanes(kseg[pl.ds(ks, tk), :], nq) == qseg[:, at] if masked else None
            starts = [lane_start(ks, q_at + skip, g, reach, off, nq) for g in range(tk // LANES)]
            for pair in range(hp // 2):
                lanes = slice(pair * LANES, pair * LANES + LANES)
                kc = k_ref[pl.ds(ks, tk), lanes]
                vc = v_ref[pl.ds(ks, tk), lanes]
                dk_part = dv_part = None
                for h in (2 * pair, 2 * pair + 1):
                    s = lax.dot_general(kc, q_half[h][at], (((1,), (1,)), ((), ())), preferred_element_type=jnp.float32)
                    bias = jnp.concatenate([strip[h, :, pl.ds(one, span)] for one in starts], axis=0)
                    s = s + (bias - lse[h][:, at])
                    p = jnp.exp(jnp.where(same, s, NEG) if masked else s)
                    dp = lax.dot_general(vc, do_half[h][at], (((1,), (1,)), ((), ())), preferred_element_type=jnp.float32)
                    ds = p * (dp - delta[h][:, at])
                    for g, one in enumerate(starts):
                        dstrip[h, :, pl.ds(one, span)] += ds[g * LANES : (g + 1) * LANES, :]
                    pb = p.astype(jnp.bfloat16)
                    dsb = ds.astype(jnp.bfloat16)
                    dv_one = jnp.dot(pb, do_half[h][at], preferred_element_type=jnp.float32)
                    dk_one = jnp.dot(dsb, q_half[h][at], preferred_element_type=jnp.float32)
                    dv_part = dv_one if dv_part is None else dv_part + dv_one
                    dk_part = dk_one if dk_part is None else dk_part + dk_one
                    dq_acc[h, :, at] += jnp.dot(kt_ref[h * 64 : h * 64 + 64, pl.ds(ks, tk)], dsb, preferred_element_type=jnp.float32)
                dv_acc[pl.ds(ks, tk), lanes] += dv_part
                dk_acc[pl.ds(ks, tk), lanes] += dk_part

        for_chunks(body, q_at, tq, tk, min(256, tq), ends, count, w_high)
        for pair in range(hp // 2):
            dq_ref[rows, pair * LANES : pair * LANES + LANES] = jnp.concatenate([dq_acc[2 * pair], dq_acc[2 * pair + 1]], axis=0).T.astype(jnp.bfloat16)
    dk_ref[...] = dk_acc[...].astype(jnp.bfloat16)
    dv_ref[...] = dv_acc[...].astype(jnp.bfloat16)


def attend_back(lengths, strips, q, k, kt, v, ctx, do, lse, limit, tq, tk, hp):
    own, inner = q.shape
    total = k.shape[0]
    steps = inner // 64 // hp
    lanes = hp * 64
    rows_dev, count = lengths.shape
    width = strips.shape[2]
    cfg = (tq, tk, limit, rows_dev, count, own, total, hp)
    smem = pl.BlockSpec(memory_space=pltpu.SMEM)
    tall = pl.BlockSpec((total, lanes), lambda p: (0, p))
    short = pl.BlockSpec((own, lanes), lambda p: (0, p))
    band = pl.BlockSpec((hp, LANES, width), lambda p: (p, 0, 0))
    return pl.pallas_call(
        functools.partial(bwd_kernel, cfg),
        grid=(steps,),
        in_specs=[smem, band,
            short, tall, pl.BlockSpec((lanes, total), lambda p: (p, 0)), tall, short, short,
            pl.BlockSpec((hp // 2, 2, own), lambda p: (p, 0, 0))],
        out_specs=[short, tall, tall, band],
        out_shape=[jax.ShapeDtypeStruct((own, inner), jnp.bfloat16), jax.ShapeDtypeStruct((total, inner), jnp.bfloat16),
                   jax.ShapeDtypeStruct((total, inner), jnp.bfloat16), jax.ShapeDtypeStruct(strips.shape, jnp.float32)],
        scratch_shapes=[pltpu.VMEM((total, LANES), jnp.int32),
                        pltpu.VMEM((total, lanes), jnp.float32), pltpu.VMEM((total, lanes), jnp.float32),
                        pltpu.VMEM((hp, 64, tq), jnp.float32)],
        compiler_params=pltpu.CompilerParams(vmem_limit_bytes=60 * 2**20),
        name="attend_back",
    )(lengths, strips, q, k, kt, v, ctx, do, lse)


MESH = pl.DeviceIdType.MESH
GROUP = 8


def flip(index, bit):
    return index + bit * (1 - 2 * ((index // bit) % 2))


class Links:
    def __init__(self, send_sems, recv_sems, batch, place):
        self.send_sems, self.recv_sems = send_sems, recv_sems
        self.batch, self.place = batch, place
        self.slots = {}
        self.sent = []

    def slot(self, key):
        return self.slots.setdefault(key, len(self.slots))

    def copy(self, key, src, dst, target):
        n = self.slot(key)
        return pltpu.make_async_remote_copy(
            src_ref=src, dst_ref=dst, send_sem=self.send_sems.at[n], recv_sem=self.recv_sems.at[n],
            device_id=target, device_id_type=MESH)

    def send(self, key, src, dst, target, when=None):
        def go():
            self.copy(key, src, dst, target).start()
        self.sent.append((key, src, dst, target, when))
        if when is None:
            go()
        else:
            pl.when(when)(go)

    def take(self, key, dst, when=None, then=None):
        def go():
            self.copy(key, dst, dst, (self.batch, self.place)).wait_recv()
            if then is not None:
                then()
        if when is None:
            go()
        else:
            pl.when(when)(go)

    def drain(self):
        for key, src, dst, target, when in self.sent:
            def go():
                self.copy(key, src, dst, target).wait_send()
            if when is None:
                go()
            else:
                pl.when(when)(go)


def greet(batch, place, count):
    bar = pltpu.get_barrier_semaphore()
    for bit in (1, 2, 4):
        pl.semaphore_signal(bar, inc=1, device_id=(flip(batch, bit), place), device_id_type=MESH)
    for way in range(1 - count, count):
        if way != 0:
            @pl.when((place + way >= 0) & (place + way < count))
            def _():
                pl.semaphore_signal(bar, inc=1, device_id=(batch, place + way), device_id_type=MESH)
    pl.semaphore_wait(bar, 3 + count - 1)


def both(a, b):
    return a if b is None else (b if a is None else a & b)


class PlaneGather:
    def __init__(self, links, key, view, ref, sub, when=None):
        self.l, self.key, self.view, self.ref, self.sub, self.when = links, key, view, ref, sub, when

    def put(self, path, sub, half, bit):
        region = self.view(self.ref, sub, half)
        self.l.send((self.key, path), region, region, (flip(self.l.batch, bit), self.l.place), self.when)

    def start(self):
        self.put("x", self.sub, None, 2)
        self.put("y", self.sub, None, 4)
        self.put("c", self.sub, None, 1)

    def middle(self):
        sub = self.sub
        self.l.take((self.key, "x"), self.view(self.ref, flip(sub, 2), None), self.when)
        self.put("xy", flip(sub, 2), 0, 4)
        self.put("xc", flip(sub, 2), None, 1)
        self.l.take((self.key, "y"), self.view(self.ref, flip(sub, 4), None), self.when)
        self.put("yx", flip(sub, 4), 1, 2)
        self.put("yc", flip(sub, 4), None, 1)

    def far(self):
        sub = self.sub
        diagonal = flip(flip(sub, 2), 4)
        self.l.take((self.key, "xy"), self.view(self.ref, diagonal, 0), self.when)
        self.put("0c", diagonal, 0, 1)
        self.l.take((self.key, "yx"), self.view(self.ref, diagonal, 1), self.when)
        self.put("1c", diagonal, 1, 1)

    def end(self):
        sub = flip(self.sub, 1)
        diagonal = flip(flip(sub, 2), 4)
        self.l.take((self.key, "c"), self.view(self.ref, sub, None), self.when)
        self.l.take((self.key, "xc"), self.view(self.ref, flip(sub, 2), None), self.when)
        self.l.take((self.key, "yc"), self.view(self.ref, flip(sub, 4), None), self.when)
        self.l.take((self.key, "0c"), self.view(self.ref, diagonal, 0), self.when)
        self.l.take((self.key, "1c"), self.view(self.ref, diagonal, 1), self.when)


def half_rows(half, rows):
    return pl.ds(0, rows) if half is None else pl.ds(half * (rows // 2), rows // 2)


PIECES = 4
ORDER = "X0 T S0-2 a123 X1 f1 S2-5 ma123 X2 f2 S5-8 ra123 mf1 X3 f3 x1 za123 P0 mf2 P1+ rf1 mf3 P1- rf23 S8-12 x2 P2"
EPS = 1e-06


def unit_norm(values):
    return lax.rsqrt(jnp.mean(values * values, axis=1, keepdims=True) + EPS)


def dot_nt(a, b):
    return lax.dot_general(a, b, (((1,), (1,)), ((), ())), preferred_element_type=jnp.float32)


def dot_nn(a, b):
    return jnp.dot(a, b, preferred_element_type=jnp.float32)


def gather_kernel(count, radius, tok_ref, gain_ref, wq_ref, wk_ref, wv_ref, wo_ref, wg_ref, wu_ref, wd_ref, rel_ref, kinds_ref,
                  xs_out, was_out, wfs_ref, q_out, k_out, kt_out, v_out, vt_out, strips_out,
                  xs, was, q_v, k_v, kt_v, v_v, vt_v, wf, rel_all, table, strip_v, send_sems, recv_sems, local_sems):
    batch, place = lax.axis_index("batch"), lax.axis_index("mp")
    sub = batch % GROUP
    links = Links(send_sems, recv_sems, batch, place)
    own, width = tok_ref.shape
    rows_a = was.shape[3]
    rows_f = wf.shape[2]
    step = own // PIECES
    local = []

    def copy_local(src, dst):
        one = pltpu.make_async_copy(src, dst, local_sems.at[len(local)])
        local.append(one)
        return one

    own_a = [copy_local(ref, was.at[n, place]) for n, ref in enumerate((wq_ref, wk_ref, wv_ref, wo_ref))]
    own_d = copy_local(wd_ref, wf.at[2])
    for one in own_a + [own_d]:
        one.start()
    gain = gain_ref[...].reshape(1, width)
    for p in range(PIECES):
        rows = pl.ds(p * step, step)
        values = tok_ref[rows, :].astype(jnp.float32)
        xs[place, rows] = (values * unit_norm(values) * gain).astype(xs.dtype)
    for n, ref in enumerate((wg_ref, wu_ref)):
        turn = ref[...].T
        for g in range(GROUP):
            wf[n, g] = turn[g * rows_f : (g + 1) * rows_f]
    for one in own_a + [own_d]:
        one.wait()
    copy_local(wf, wfs_ref.at[:, place]).start()
    greet(batch, place, count)

    def view_a(mm):
        return lambda ref, s, half: ref.at[s // 2, mm, s % 2, half_rows(half, rows_a)]

    def view_f(mm):
        return lambda ref, s, half: ref.at[:, mm, s, half_rows(half, rows_f)]

    def inside(n):
        return (n >= 0) & (n < count)

    for way in (1, -1):
        ok = inside(place + way)
        target = (batch, place + way)
        links.send(("a", way, 1), view_a(place)(was, sub, None), view_a(place)(was, sub, None), target, ok)
        links.send(("f", way, 1), wf.at[:, sub], view_f(place)(wfs_ref, sub, None), target, ok)
    rel_all[place, 0 : rel_ref.shape[0], :] = rel_ref[...]
    for d in range(1, count):
        for way in (1, -1):
            links.send(("r", way, d), rel_all.at[place], rel_all.at[place], (batch, place + way * d), inside(place + way * d))
    def x_send(p):
        rows = pl.ds(p * step, step)
        for way in (1, -1):
            links.send(("x", way, 1, p), xs.at[place, rows], xs.at[place, rows], (batch, place + way), inside(place + way))

    for n in range(count):
        @pl.when((n - place > radius) | (place - n > radius))
        def _():
            def blank(p, _):
                xs[n, pl.ds(p * step, step)] = jnp.zeros((step, width), xs.dtype)
                return 0
            lax.fori_loop(0, PIECES, blank, 0)
            for ref in (k_v, v_v):
                ref[pl.ds(n * own, own)] = jnp.zeros((own, ref.shape[1]), ref.dtype)
            for ref in (kt_v, vt_v):
                ref[:, pl.ds(n * own, own)] = jnp.zeros((ref.shape[0], own), ref.dtype)

    gathers = {}

    def weights_arrive(kind, dist):
        for way in (1, -1):
            source = place - way * dist
            ok = inside(source)
            view, ref = (view_a(source), was) if kind == "a" else (view_f(source), wfs_ref)
            region = view(ref, sub, None)
            links.take((kind, way, dist), region, ok)
            if dist < count - 1:
                links.send((kind, way, dist + 1), region, region, (batch, place + way), ok & inside(place + way))
            gather = PlaneGather(links, ("g", kind, way, dist), view, ref, sub, ok)
            gather.start()
            gathers[kind, way, dist] = gather

    def x_arrive(dist, p):
        for way in (1, -1):
            source = place - way * dist
            ok = inside(source)
            region = xs.at[source, pl.ds(p * step, step)]
            links.take(("x", way, dist, p), region, ok)
            if dist < radius:
                links.send(("x", way, dist + 1, p), region, region, (batch, place + way), ok & inside(place + way))

    def stage(name, kind, dist):
        for way in (1, -1):
            getattr(gathers[kind, way, dist], name)()

    heads = table.shape[0]
    span = table.shape[1]
    kinds = rel_ref.shape[1]

    def make_table():
        for d in range(1, count):
            for way in (1, -1):
                links.take(("r", way, d), rel_all.at[place - way * d], inside(place - way * d))
        per = heads // count
        joined = jnp.concatenate([rel_all[n, 0:per, :] for n in range(count)], axis=0)
        for at in range(0, span, 512):
            lanes = pl.ds(at, min(512, span - at))
            kind = kinds_ref[:, lanes]
            total = jnp.zeros((heads, kind.shape[1]), jnp.float32)
            for b in range(NB_MAX):
                if b < kinds:
                    total = total + jnp.where(kind == b, joined[:, b : b + 1], 0.0)
            table[:, lanes] = total

    strip_copies = []

    def make_strip(h):
        slot = h % 2
        if h >= 2:
            strip_copies[h - 2].wait()
        row = table[h : h + 1, :]
        strip_v[slot] = pltpu.roll(jnp.broadcast_to(row, (LANES, span)), 0, 1, stride=1, stride_axis=0)
        one = pltpu.make_async_copy(strip_v.at[slot], strips_out.at[h], local_sems.at[8 + slot])
        one.start()
        strip_copies.append(one)

    inner = was.shape[1] * was.shape[2] * rows_a

    def weight_tile(kind, n):
        return was[kind, n].reshape(2 * rows_a, width)

    def project(block, when):
        def go():
            x = xs[block]
            def one(n, _):
                at = pl.multiple_of(n * 2 * rows_a, 64)
                kt_v[pl.ds(at, 2 * rows_a), pl.ds(pl.multiple_of(block * own, LANES), own)] = dot_nt(weight_tile(1, n), x).astype(kt_v.dtype)
                vt_v[pl.ds(at, 2 * rows_a), pl.ds(pl.multiple_of(block * own, LANES), own)] = dot_nt(weight_tile(2, n), x).astype(vt_v.dtype)
                return 0
            lax.fori_loop(0, count, one, 0)
            rows = pl.ds(pl.multiple_of(block * own, LANES), own)
            tile = 256
            for at in range(0, inner, tile):
                wk = was[1].reshape(inner, width)[at : at + tile]
                wv = was[2].reshape(inner, width)[at : at + tile]
                k_v[rows, at : at + tile] = dot_nt(x, wk).astype(k_v.dtype)
                v_v[rows, at : at + tile] = dot_nt(x, wv).astype(v_v.dtype)
        if when is None:
            go()
        else:
            pl.when(when)(go)

    def project_q():
        x = xs[place]
        tile = 256
        for at in range(0, inner, tile):
            wq = was[0].reshape(inner, width)[at : at + tile]
            q_v[:, at : at + tile] = dot_nt(x, wq).astype(q_v.dtype)

    saves = []

    def save_block(block, when):
        rows = pl.ds(pl.multiple_of(block * own, LANES), own)
        for src, dst in ((k_v, k_out), (v_v, v_out)):
            saves.append((pltpu.make_async_copy(src.at[rows], dst.at[rows], local_sems.at[10 + len(saves)]), when))
        for src, dst in ((kt_v, kt_out), (vt_v, vt_out)):
            saves.append((pltpu.make_async_copy(src.at[:, rows], dst.at[:, rows], local_sems.at[10 + len(saves)]), when))
        for one, ok in saves[-4:]:
            one.start() if ok is None else pl.when(ok)(one.start)

    dists = range(1, count)

    def run(order):
        for op in order.split():
            name, arg = op[0], op[1:]
            if name == "T":
                make_table()
            elif name == "S":
                for h in range(*[int(one) for one in arg.split("-")]):
                    make_strip(h)
            elif name in "af":
                for d in arg:
                    if int(d) in dists:
                        weights_arrive(name, int(d))
            elif name in "mrz":
                for d in arg[1:]:
                    if int(d) in dists:
                        stage({"m": "middle", "r": "far", "z": "end"}[name], arg[0], int(d))
            elif name == "X":
                for p in arg:
                    x_send(int(p))
            elif name == "x":
                for p in arg[1:] or "0123":
                    if int(arg[0]) <= radius:
                        x_arrive(int(arg[0]), int(p))
            elif name == "P":
                d = int(arg[0])
                if d == 0:
                    project_q()
                    copy_local(q_v, q_out).start()
                    project(place, None)
                    save_block(place, None)
                elif d <= radius:
                    for way in (1, -1) if len(arg) == 1 else ((1,) if arg[1] == "+" else (-1,)):
                        project(place + way * d, inside(place + way * d))
                        save_block(place + way * d, inside(place + way * d))

    run(ORDER)
    copy_local(was, was_out).start()
    copy_local(xs, xs_out).start()
    for n in range(count):
        save_block(n, (n - place > radius) | (place - n > radius))
    for d in dists:
        stage("end", "f", d)
    links.drain()
    for one in local[5:] + strip_copies[-2:]:
        one.wait()
    for one, ok in saves:
        one.wait() if ok is None else pl.when(ok)(one.wait)


NB_MAX = 128


def gather(tokens, gain, w_heads, w_hidden, rel, kinds, count, radius, heads):
    own, width = tokens.shape
    bf = jnp.bfloat16
    total = own * count
    half_a = w_heads[0].shape[0] // 2
    part = w_hidden[2].shape[0] // GROUP
    inner = count * 2 * half_a
    span = kinds.shape[1]
    vm = pl.BlockSpec(memory_space=pltpu.VMEM)
    hb = pl.BlockSpec(memory_space=pl.ANY)
    shapes = [
        ((count, own, width), bf),
        ((4, count, 2, half_a, width), bf),
        ((3, count, GROUP, part, width), bf),
        ((own, inner), bf), ((total, inner), bf), ((inner, total), bf), ((total, inner), bf), ((inner, total), bf),
        ((heads, LANES, span), jnp.float32),
    ]
    return pl.pallas_call(
        functools.partial(gather_kernel, count, radius),
        in_specs=[vm, vm] + [hb] * 4 + [vm, vm, hb, vm, vm],
        out_specs=[hb] * len(shapes),
        out_shape=[jax.ShapeDtypeStruct(*one) for one in shapes],
        scratch_shapes=[pltpu.VMEM(*shapes[n]) for n in (0, 1, 3, 4, 5, 6, 7)] + [
            pltpu.VMEM((3, GROUP, part, width), bf),
            pltpu.VMEM((count, 8, rel.shape[1]), jnp.float32),
            pltpu.VMEM((heads, span), jnp.float32),
            pltpu.VMEM((2, LANES, span), jnp.float32),
            pltpu.SemaphoreType.DMA((170,)),
            pltpu.SemaphoreType.DMA((170,)),
            pltpu.SemaphoreType.DMA((64,)),
        ],
        compiler_params=pltpu.CompilerParams(collective_id=1, has_side_effects=True, vmem_limit_bytes=60 * 2**20),
        name="gather",
    )(tokens, gain, *[one.reshape(2, half_a, width) for one in w_heads], *w_hidden[:2], w_hidden[2].reshape(GROUP, part, width), rel, kinds)


def ffn_kernel(count, tok_ref, cot_ref, ctx_ref, gain_ref, was_ref, wfs_ref,
               out_ref, middle_ref, do_ref, raw_out_ref, gain_out, keep_out, fx_out, fy_out,
               wo, wf, normed, middle, act, raw, got, send_sems, recv_sems, local_sems):
    batch, place = lax.axis_index("batch"), lax.axis_index("mp")
    sub = batch % GROUP
    core, xx, yy = sub % 2, (sub // 2) % 2, sub // 4
    links = Links(send_sems, recv_sems, batch, place)
    sibling = (flip(batch, 1), place)
    own, width = tok_ref.shape
    gain_two = gain_ref[...].reshape(1, width)
    hidden = wf.shape[1]
    per = hidden // count
    part = per // GROUP
    half = part // 2
    bf = jnp.bfloat16
    loads = [pltpu.make_async_copy(was_ref.at[3], wo, local_sems.at[0])]
    for n in range(count):
        rows = pl.ds(n * per, per)
        loads += [pltpu.make_async_copy(wfs_ref.at[t, rows], wf.at[t, rows], local_sems.at[1 + 3 * n + t]) for t in range(3)]
    for one in loads:
        one.start()
    bar = pltpu.get_barrier_semaphore()
    pl.semaphore_signal(bar, inc=1, device_id=sibling, device_id_type=MESH)
    loads[0].wait()
    tile = 256
    for at in range(0, own, tile):
        rows = slice(at, at + tile)
        mid = tok_ref[rows, :].astype(jnp.float32) + dot_nn(ctx_ref[rows, :], wo[...])
        middle[rows, :] = mid
        normed[rows, :] = (mid * unit_norm(mid) * gain_two).astype(bf)
    pl.semaphore_wait(bar, 1)

    def products(j):
        if j * tile % per == 0:
            n = j * tile // per
            for one in loads[1 + 3 * n : 4 + 3 * n]:
                one.wait()
        rows = slice(j * tile, (j + 1) * tile)
        return dot_nt(normed[...], wf[0, rows, :]), dot_nt(normed[...], wf[1, rows, :]), dot_nt(cot_ref[...], wf[2, rows, :])

    ahead = products(0)
    tiles = hidden // tile
    for j in range(tiles):
        gate, up, back = ahead
        if j + 1 < tiles:
            ahead = products(j + 1)
        cols = slice(j * tile, (j + 1) * tile)
        squared = 0.044715 * (gate * gate)
        t = jnp.tanh(0.7978845608028654 * gate * (1.0 + squared))
        half_up = 0.5 * (1.0 + t)
        gelu = gate * half_up
        slope = half_up + 0.5 * gate * (1.0 - t * t) * (0.7978845608028654 * (1.0 + 3.0 * squared))
        act[0, :, cols] = (back * up * slope).astype(bf)
        act[1, :, cols] = (back * gelu).astype(bf)
        act[2, :, cols] = (gelu * up).astype(bf)
        n, r = j * tile // per, j * tile % per // part
        for t_id in range(3):
            value = dot_nn(act[t_id, :, cols].T, cot_ref[...] if t_id == 2 else normed[...]).astype(bf)
            for s in range(tile // part):
                raw[t_id, n, (r + s) // 2, (r + s) % 2] = value[s * part : (s + 1) * part]
        if (j + 1) * tile % per == 0:
            for t_id in range(3):
                links.send(("f1", t_id, n), raw.at[t_id, n, :, 1 - core], got.at[t_id, n], sibling)
    saves = []

    def settle(n):
        for t in range(3):
            links.take(("f1", t, n), got.at[t, n])
            for s in range(GROUP // 2):
                got[t, n, s] = got[t, n, s] + raw[t, n, s, core]
            whole = got.at[t, n].reshape(2, 2, part, width)
            for src, dst in ((whole, keep_out.at[t, n]), (whole.at[:, 1 - xx, pl.ds(0, half)], fx_out.at[t, n]),
                             (whole.at[1 - yy, :, pl.ds(half, half)], fy_out.at[t, n])):
                one = pltpu.make_async_copy(src, dst, local_sems.at[1 + 3 * count + len(saves)])
                one.start()
                saves.append(one)

    for n in range(count - 1):
        settle(n)
    for at in range(0, own, tile):
        rows = slice(at, at + tile)
        mid = middle[rows, :]
        out_ref[rows, :] = (mid + dot_nn(act[2, rows, :], wf[2])).astype(bf)
        s = unit_norm(mid)
        n2 = mid * s
        gn = dot_nn(act[0, rows, :], wf[0]) + dot_nn(act[1, rows, :], wf[1])
        e = gn * gain_two
        grad = cot_ref[rows, :].astype(jnp.float32) + s * (e - n2 * jnp.mean(e * n2, axis=1, keepdims=True))
        middle_ref[rows, :] = grad
        normed[rows, :] = grad.astype(bf)
        gain = jnp.sum(gn * n2, axis=0, keepdims=True)
        gain_out[...] = gain if at == 0 else gain_out[...] + gain
    for at in range(0, width, tile):
        cols = slice(at, at + tile)
        do_ref[:, cols] = dot_nt(normed[...], wo[cols, :]).astype(bf)
        raw_out_ref[cols, :] = dot_nn(ctx_ref[:, cols].T, normed[...]).astype(bf)
    settle(count - 1)
    links.drain()
    for one in saves:
        one.wait()


def ffn(tokens, cotangent, context, gain, was, wfs, count):
    own, width = tokens.shape
    hidden = wfs.shape[1]
    part = hidden // count // GROUP
    bf = jnp.bfloat16
    vm = pl.BlockSpec(memory_space=pltpu.VMEM)
    hb = pl.BlockSpec(memory_space=pl.ANY)
    return pl.pallas_call(
        functools.partial(ffn_kernel, count),
        in_specs=[vm, vm, vm, vm, hb, hb],
        out_specs=[vm] * 5 + [hb] * 3,
        out_shape=[
            jax.ShapeDtypeStruct((own, width), bf),
            jax.ShapeDtypeStruct((own, width), jnp.float32),
            jax.ShapeDtypeStruct(context.shape, bf),
            jax.ShapeDtypeStruct((context.shape[1], width), bf),
            jax.ShapeDtypeStruct((1, width), jnp.float32),
            jax.ShapeDtypeStruct((3, count, 2, 2, part, width), bf),
            jax.ShapeDtypeStruct((3, count, 2, part // 2, width), bf),
            jax.ShapeDtypeStruct((3, count, 2, part // 2, width), bf),
        ],
        scratch_shapes=[
            pltpu.VMEM((was.shape[1], width), bf),
            pltpu.VMEM((3, hidden, width), bf),
            pltpu.VMEM((own, width), bf),
            pltpu.VMEM((own, width), jnp.float32),
            pltpu.VMEM((3, own, hidden), bf),
            pltpu.VMEM((3, count, GROUP // 2, 2, part, width), bf),
            pltpu.VMEM((3, count, GROUP // 2, part, width), bf),
            pltpu.SemaphoreType.DMA((3 * count,)),
            pltpu.SemaphoreType.DMA((3 * count,)),
            pltpu.SemaphoreType.DMA((1 + 12 * count,)),
        ],
        compiler_params=pltpu.CompilerParams(collective_id=3, has_side_effects=True, vmem_limit_bytes=60 * 2**20),
        name="ffn",
    )(tokens, cotangent, context, gain, was, wfs)


FINISH_ORDER = "F B X0123 O R12 l w0 R0 Q A w1 x0123 C w2 f0123 S0-3 m w3 S3-6 n w4 S6-12 b g t0 M t1 a G t2 r N e D"


def finish_kernel(count, radius, buckets, scale, gain_ref, tiny_ref, kinds_ref,
                  dq_ref, dk_ref, dv_ref, xs_ref, was_ref, raw_out_ref, keep_ref, fx_ref, fy_ref, strips_ref,
                  full_a, full_f, gn_out, side_ref, total_ref,
                  dq, dk, dv, xs, wq, wk, wv, ga, got_a1, got_ax, got_ay, got_ay2, got_ax2,
                  keep_f, got_fx, got_fy, got_fy2, got_fx2, from_a, from_f,
                  gx, own_acc, got_x, rows8, small, tiny, tiny_z, side_z, strip_v, send_sems, recv_sems, local_sems):
    batch, place = lax.axis_index("batch"), lax.axis_index("mp")
    sub = batch % GROUP
    core, xx, yy = sub % 2, (sub // 2) % 2, sub // 4
    links = Links(send_sems, recv_sems, batch, place)
    rows_a, rows_f = ga.shape[4], keep_f.shape[4]
    ha, hf = rows_a // 2, rows_f // 2
    own, width = gn_out.shape
    step = own // PIECES
    bf = jnp.bfloat16
    f32 = jnp.float32
    sibling, x_near, y_near = [(flip(batch, bit), place) for bit in (1, 2, 4)]

    def inside(n):
        return (n >= 0) & (n < count)

    used = [0]

    def load(src, dst, start=True):
        one = pltpu.make_async_copy(src, dst, local_sems.at[used[0]])
        used[0] += 1
        if start:
            one.start()
        return one

    load_f = [(load(keep_ref.at[t], keep_f.at[t]), load(fx_ref.at[t], got_fx.at[t]), load(fy_ref.at[t], got_fy.at[t])) for t in range(3)]
    load_k = [load(dk_ref, dk), load(was_ref.at[1], wk), load(dv_ref, dv), load(was_ref.at[2], wv)]
    load_x = [load(xs_ref, xs), load(dq_ref, dq), load(was_ref.at[0], wq)]
    load_o = load(raw_out_ref, ga.at[1, 1])
    heads = strips_ref.shape[0]
    load_s = {}

    def load_strip(n):
        load_s[n] = pltpu.make_async_copy(strips_ref.at[n // 2, pl.ds(n % 2 * 64, 64)], strip_v.at[n % 2], local_sems.at[40 + n % 2])
        load_s[n].start()

    load_strip(0)
    load_strip(1)

    def one_f(t):
        def go(n, _):
            for i in range(2):
                keep_f[t, n, i, xx, pl.ds(0, hf)] = keep_f[t, n, i, xx, pl.ds(0, hf)] + got_fx[t, n, i]
                keep_f[t, n, yy, i, pl.ds(hf, hf)] = keep_f[t, n, yy, i, pl.ds(hf, hf)] + got_fy[t, n, i]
            return 0
        lax.fori_loop(0, count, go, 0)

    def first_f():
        for t in range(3):
            for one in load_f[t]:
                one.wait()
            one_f(t)
            if t == 0:
                greet(batch, place, count)
            links.send(("fy2", t), keep_f.at[t, :, 1 - yy, xx, pl.ds(0, hf)], got_fy2.at[t], y_near)
            links.send(("fx2", t), keep_f.at[t, :, yy, 1 - xx, pl.ds(hf, hf)], got_fx2.at[t], x_near)

    rows8[...] = jnp.zeros_like(rows8)

    def block_part(block, local):
        tile = 256
        for at in range(0, own, tile):
            rows = pl.ds(pl.multiple_of(block * own + at, tile), tile)
            value = dot_nn(dk[rows, :], wk[...]) + dot_nn(dv[rows, :], wv[...])
            if local:
                value = value + dot_nn(dq[at : at + tile, :], wq[...])
                own_acc[at : at + tile, :] = value
            else:
                gx[block, at : at + tile] = value.astype(bf)
            prod = value * xs[block, at : at + tile].astype(f32)
            acc = prod[0:8]
            for r in range(8, tile, 8):
                acc = acc + prod[r : r + 8]
            rows8[...] = rows8[...] + acc

    def x_send(way, level, p):
        rows = pl.ds(p * step, step)
        links.send(("x", way, level, p), gx.at[place + way * level, rows], got_x.at[0 if way > 0 else 1, level - 1, rows],
                   (batch, place + way), inside(place + way * level))

    def x_step(level, p):
        rows = pl.ds(p * step, step)
        for side, way in ((0, 1), (1, -1)):
            dest = place + way * (level - 1)
            behind = inside(place - way)
            def add():
                got_x[side, level - 1, rows] = got_x[side, level - 1, rows] + gx[dest, rows]
            links.take(("x", way, level, p), got_x.at[side, level - 1, rows], behind & inside(dest), add)
            links.send(("x", way, level - 1, p), got_x.at[side, level - 1, rows], got_x.at[side, level - 2, rows],
                       (batch, place + way), behind & inside(dest))

    def x_first(level, p):
        rows = pl.ds(p * step, step)
        for side, way in ((0, 1), (1, -1)):
            dest = place + way * (level - 1)
            links.send(("x0", way, level - 1, p), gx.at[jnp.clip(dest, 0, count - 1), rows], got_x.at[side, level - 2, rows],
                       (batch, place + way), jnp.logical_not(inside(place - way)) & inside(dest))

    inner = wq.shape[0]

    def raw_grad(kind, left, right):
        for c in range(0, inner, 256):
            value = dot_nn(left(c).T, right()).astype(bf)
            at = c
            while at < c + 256:
                n, r = at // (2 * rows_a), at % (2 * rows_a)
                h, r = r // rows_a, r % rows_a
                size = min(rows_a - r, c + 256 - at)
                ga[kind // 2, kind % 2, n, h, r : r + size] = value[at - c : at - c + size]
                at += size
        links.send(("a1", kind), ga.at[kind // 2, kind % 2, :, 1 - core], got_a1.at[kind // 2, kind % 2], sibling)

    def last_f(t):
        links.take(("fy2", t), got_fy2.at[t])
        links.take(("fx2", t), got_fx2.at[t])
        def one(n, _):
            keep_f[t, n, yy, xx, pl.ds(0, hf)] = keep_f[t, n, yy, xx, pl.ds(0, hf)] + got_fy2[t, n]
            keep_f[t, n, yy, xx, pl.ds(hf, hf)] = keep_f[t, n, yy, xx, pl.ds(hf, hf)] + got_fx2[t, n]
            return 0
        lax.fori_loop(0, count, one, 0)

    def unit(t, n):
        return keep_f.at[t, n, yy, xx]

    def line(t, hop, rank):
        for side, way in ((0, 1), (1, -1)):
            here = place == (hop if way > 0 else count - 1 - hop)
            n = count - 1 - rank if way > 0 else rank
            if hop > 0:
                def add():
                    ref, more = unit(t, n), from_f.at[t, side, n]
                    ref[...] = ref[...] + more[...]
                links.take(("z", t, side, n, hop - 1), from_f.at[t, side, n], here, add)
            links.send(("z", t, side, n, hop), unit(t, n), from_f.at[t, side, n], (batch, place + way), here)

    def line_a():
        for d in range(count - 1, 0, -1):
            for way in (1, -1):
                dest = place + way * d
                links.send(("za", way, d), ga.at[yy, xx, jnp.clip(dest, 0, count - 1), core], from_a.at[place], (batch, dest), inside(dest))

    def view_a(ref, s, half):
        return ref.at[s // 2, s % 2, half_rows(half, rows_a)]

    def view_f(t):
        return lambda ref, s, half: ref.at[t, s, half_rows(half, rows_f)]

    gathers = {}

    def finish(t):
        for side, way in ((0, 1), (1, -1)):
            for hop in range(count - 1):
                n = hop + 1 if way > 0 else count - 2 - hop
                def add():
                    ref, more = unit(t, n), from_f.at[t, side, n]
                    ref[...] = ref[...] + more[...]
                links.take(("z", t, side, n, hop), from_f.at[t, side, n], place == n, add)
        full_f[t, sub] = keep_f[t, place, yy, xx]
        gathers[t] = PlaneGather(links, ("g", t), view_f(t), full_f, sub)
        gathers[t].start()

    def finish_a():
        from_a[place] = ga[yy, xx, place, core]
        for d in range(1, count):
            for way in (1, -1):
                links.take(("za", way, d), from_a.at[place - way * d], inside(place - way * d))
        total = from_a[0].astype(f32)
        for n in range(1, count):
            total = total + from_a[n].astype(f32)
        full_a[sub // 2, sub % 2] = total.astype(bf)
        gathers["a"] = PlaneGather(links, ("g", "a"), view_a, full_a, sub)
        gathers["a"].start()

    def a_core(kind):
        i, j = kind // 2, kind % 2
        links.take(("a1", kind), got_a1.at[i, j])
        for n in range(count):
            ga[i, j, n, core] = ga[i, j, n, core] + got_a1[i, j, n]

    def a_middle():
        links.take(("ax",), got_ax)
        links.take(("ay",), got_ay)
        for n in range(count):
            for i in range(2):
                ga[i, xx, n, core, pl.ds(0, ha)] = ga[i, xx, n, core, pl.ds(0, ha)] + got_ax[i, n]
                ga[yy, i, n, core, pl.ds(ha, ha)] = ga[yy, i, n, core, pl.ds(ha, ha)] + got_ay[i, n]
        links.send(("ay2",), ga.at[1 - yy, xx, :, core, pl.ds(0, ha)], got_ay2, y_near)
        links.send(("ax2",), ga.at[yy, 1 - xx, :, core, pl.ds(ha, ha)], got_ax2, x_near)

    def a_last():
        links.take(("ay2",), got_ay2)
        links.take(("ax2",), got_ax2)
        for n in range(count):
            ga[yy, xx, n, core, pl.ds(0, ha)] = ga[yy, xx, n, core, pl.ds(0, ha)] + got_ay2[n]
            ga[yy, xx, n, core, pl.ds(ha, ha)] = ga[yy, xx, n, core, pl.ds(ha, ha)] + got_ax2[n]

    sums = {}

    def strip_sum(h):
        span = strip_v.shape[2]
        eight = None
        for n in (2 * h, 2 * h + 1):
            load_s[n].wait()
            for g in range(8):
                shift = 8 * g + 64 * (n % 2)
                part = strip_v[n % 2, 8 * g : 8 * g + 8, :]
                part = part if shift == 0 else pltpu.roll(part, span - shift, 1)
                eight = part if eight is None else eight + part
            if n + 2 < 2 * heads:
                load_strip(n + 2)
        flat = eight[0:1, :]
        for r in range(1, 8):
            flat = flat + pltpu.roll(eight[r : r + 1, :], span - r, 1)
        sums[h] = flat

    def tiny_step(n):
        links.take(("s", n), tiny.at[2 * n + 1])
        before = small if n == 0 else tiny.at[2 * n]
        tiny[2 * n + 2] = before[...] + tiny[2 * n + 1]
        if n < 2:
            links.send(("s", n + 1), tiny.at[2 * n + 2], tiny.at[2 * n + 3], (flip(batch, 2 << n), place))
        else:
            tiny_z[place] = tiny[6]
            for d in range(1, count):
                for way in (1, -1):
                    links.send(("sz", way, d), tiny.at[6], tiny_z.at[place], (batch, place + way * d), inside(place + way * d))

    def parts(level):
        for way in (1, -1):
            @pl.when(inside(place + way * level))
            def _():
                block_part(place + way * level, False)

    def wave(n):
        for hop in range(count - 2, -1, -1):
            rank = n - 2 * hop
            if 0 <= rank < count - 1 - hop:
                for t in range(3):
                    line(t, hop, rank)

    def raw_out_part():
        load_o.wait()
        links.send(("a1", 3), ga.at[1, 1, :, 1 - core], got_a1.at[1, 1], sibling)

    def far_part():
        for one in load_k + load_x:
            one.wait()
        for way in (1, -1):
            @pl.when(inside(place + way * radius))
            def _():
                block_part(place + way * radius, False)

    def raw_part(kind):
        if kind == 0:
            raw_grad(0, lambda c: dq[:, c : c + 256], lambda: xs[place])
        else:
            side = dk if kind == 1 else dv
            raw_grad(kind, lambda c: side[:, c : c + 256], lambda: xs[...].reshape(count * own, width))

    def near_parts():
        for level in range(radius - 1, 0, -1):
            parts(level)

    def a_first():
        for kind in (3, 1, 2, 0):
            a_core(kind)
        links.send(("ax",), ga.at[:, 1 - xx, :, core, pl.ds(0, ha)], got_ax, x_near)
        links.send(("ay",), ga.at[1 - yy, :, :, core, pl.ds(ha, ha)], got_ay, y_near)

    def buckets_part():
        diag = jnp.concatenate([sums[h] for h in range(heads)], axis=0)
        small[...] = jnp.zeros_like(small)
        small[0:1, :] = jnp.sum(rows8[...], axis=0, keepdims=True) / gain_ref[...].reshape(1, width)
        small[1:2, :] = tiny_ref[...]
        bucket_lane = lax.broadcasted_iota(jnp.int32, (heads, LANES), 1)
        rel = jnp.zeros((heads, LANES), f32)
        for b in range(buckets):
            rel = jnp.where(bucket_lane == b, jnp.sum(jnp.where(kinds_ref[...] == b, diag, 0.0), axis=1, keepdims=True), rel)
        per = width // LANES
        for h in range(heads):
            small[2 + h // per : 3 + h // per, h % per * LANES : (h % per + 1) * LANES] = rel[h : h + 1, :]
        links.send(("s", 0), small, tiny.at[1], sibling)

    def gn_part():
        for p in range(PIECES):
            rows = pl.ds(p * step, step)
            for side, way in ((0, 1), (1, -1)):
                ok = inside(place - way)
                near = inside(place - 2 * way)
                if radius > 1:
                    links.take(("x", way, 1, p), got_x.at[side, 0, rows], ok & near)
                    links.take(("x0", way, 1, p), got_x.at[side, 0, rows], ok & jnp.logical_not(near))
                else:
                    links.take(("x", way, 1, p), got_x.at[side, 0, rows], ok)
                def blank():
                    got_x[side, 0, rows] = jnp.zeros((step, width), bf)
                pl.when(jnp.logical_not(ok))(blank)
            gn_out[rows, :] = own_acc[rows, :] + got_x[0, 0, rows].astype(f32) + got_x[1, 0, rows].astype(f32)

    def each(act):
        for t in range(3):
            act(t)

    def levels(act, p):
        for level in range(radius, 1, -1):
            act(level, p)

    simple = {
        "F": first_f, "B": far_part, "O": raw_out_part, "Q": near_parts, "A": a_first, "C": lambda: block_part(place, True),
        "m": a_middle, "n": lambda: (a_last(), line_a()), "b": buckets_part, "a": finish_a, "G": gn_part,
        "l": lambda: each(last_f), "g": lambda: each(finish), "M": lambda: each(lambda t: gathers[t].middle()),
        "r": lambda: each(lambda t: gathers[t].far()), "e": lambda: each(lambda t: gathers[t].end()),
        "N": lambda: gathers["a"].middle(), "D": lambda: gathers["a"].far(),
    }
    for op in FINISH_ORDER.split():
        name, arg = op[0], op[1:]
        if name == "S":
            for h in range(*[int(one) for one in arg.split("-")]):
                if h < heads:
                    strip_sum(h)
        elif name in "XxfRwt":
            for one in arg:
                {"X": lambda p: [x_send(way, radius, p) for way in (1, -1)], "x": lambda p: levels(x_step, p), "f": lambda p: levels(x_first, p),
                 "R": raw_part, "w": wave, "t": tiny_step}[name](int(one))
        else:
            simple[name]()

    def squares(read, blocks):
        def one(n, acc):
            value = read(n).astype(f32) * scale
            for r in range(0, value.shape[0], 8):
                acc = acc + value[r : r + 8] * value[r : r + 8]
            return acc
        return jnp.sum(lax.fori_loop(0, blocks, one, jnp.zeros((8, width), f32)), axis=0, keepdims=True)

    f_sums = [squares(lambda n: full_f[t, n], GROUP) for t in range(3)]
    for d in range(1, count):
        for way in (1, -1):
            links.take(("sz", way, d), tiny_z.at[place - way * d], inside(place - way * d))
    summed = tiny_z[0]
    for n in range(1, count):
        summed = summed + tiny_z[n]
    total_ref[...] = summed
    gathers["a"].end()
    a_sums = [squares(lambda n: full_a[s, n], 2) for s in range(4)]
    side_z[place] = jnp.concatenate(a_sums + f_sums + [jnp.zeros((1, width), f32)], axis=0)
    for d in range(1, count):
        for way in (1, -1):
            links.send(("q", way, d), side_z.at[place], side_z.at[place], (batch, place + way * d), inside(place + way * d))
    for d in range(1, count):
        for way in (1, -1):
            links.take(("q", way, d), side_z.at[place - way * d], inside(place - way * d))
    summed = side_z[0]
    for n in range(1, count):
        summed = summed + side_z[n]
    side_ref[...] = summed
    links.drain()


def finish(gain, tiny, kinds, dq, dk, dv, xs, was, raw_out, keep, fx, fy, strips, count, radius, buckets, scale):
    own = dq.shape[0]
    width = gain.shape[0]
    total, inner = dk.shape
    heads, _, span = strips.shape
    part = keep.shape[4]
    half_a = inner // count // 2
    bf = jnp.bfloat16
    vm = pl.BlockSpec(memory_space=pltpu.VMEM)
    hb = pl.BlockSpec(memory_space=pl.ANY)
    V = lambda *s: pltpu.VMEM(s + (width,), bf)
    F = lambda *s: pltpu.VMEM(s, jnp.float32)
    O = lambda *s: jax.ShapeDtypeStruct(s, jnp.float32)
    return pl.pallas_call(
        functools.partial(finish_kernel, count, radius, buckets, scale),
        in_specs=[vm] * 3 + [hb] * 10,
        out_specs=[vm] * 5,
        out_shape=[
            jax.ShapeDtypeStruct((4, 2, half_a, width), bf), jax.ShapeDtypeStruct((3, GROUP, part, width), bf),
            O(own, width), O(8, width), O(8, width),
        ],
        scratch_shapes=[
            pltpu.VMEM((own, inner), bf), pltpu.VMEM((total, inner), bf), pltpu.VMEM((total, inner), bf), V(count, own),
            V(inner), V(inner), V(inner),
            V(2, 2, count, 2, half_a), V(2, 2, count, half_a), V(2, count, half_a // 2), V(2, count, half_a // 2), V(count, half_a // 2), V(count, half_a // 2),
            V(3, count, 2, 2, part), V(3, count, 2, part // 2), V(3, count, 2, part // 2), V(3, count, part // 2), V(3, count, part // 2),
            V(count, half_a), V(3, 2, count, part),
            V(count, own), F(own, width), V(2, radius, own), F(8, width),
            F(8, width), F(7, 8, width), F(count, 8, width), F(count, 8, width), F(2, 64, span),
            pltpu.SemaphoreType.DMA((240,)), pltpu.SemaphoreType.DMA((240,)), pltpu.SemaphoreType.DMA((48,)),
        ],
        compiler_params=pltpu.CompilerParams(collective_id=2, has_side_effects=True, vmem_limit_bytes=63 * 2**20),
        name="finish",
    )(gain, tiny, kinds, dq, dk, dv, xs, was, raw_out, keep, fx, fy, strips)


def emit_kernel(heads, kinds, scale, totals, tok_ref, mid_ref, gn_ref, layer_ref, gain_ref, a_ref, f_ref, side_ref, sums_ref,
                layer_out, tokens_out, gq, gk, gv, go, gg, gu, gd, rel_out, g1_out, g2_out, model_out, heads_out, units_out, rows_out):
    n = pl.program_id(0)
    f32 = jnp.float32
    layer_out[...] = layer_ref[...]
    x = tok_ref[...].astype(f32)
    s = unit_norm(x)
    n1 = x * s
    e = gn_ref[...] * gain_ref[...].reshape(1, gain_ref.shape[0])
    tokens_out[...] = (mid_ref[...] + s * (e - n1 * jnp.mean(e * n1, axis=1, keepdims=True))).astype(tokens_out.dtype)
    inner_total, hidden_total, width = totals
    shard = a_ref.shape[0] // 4
    hidden = f_ref.shape[0] // 3

    def part(ref, at, size, straight, turned, stat, row):
        for c in range(0, size, LANES):
            rows = min(LANES, size - c)
            value = ref[at + c : at + c + rows, :].astype(f32) * scale
            if rows < LANES:
                value = jnp.concatenate([value, jnp.zeros((LANES - rows, LANES), f32)], axis=0)
            turn = value.T
            if straight is not None:
                straight[c : c + rows, :] = value[:rows]
            if turned is not None:
                turned[:, c : c + rows] = turn[:, :rows]
            more = jnp.sum(turn * turn, axis=0, keepdims=True)[:, :rows] * (1.0 / width)
            old = stat[row : row + 1, c : c + rows]
            stat[row : row + 1, c : c + rows] = jnp.where(n == 0, TINY, old) + more

    for row, (straight, turned) in enumerate(((gq, None), (gk, None), (gv, None), (go, None))):
        part(a_ref, row * shard, shard, straight, turned, heads_out, row)
    for row, (straight, turned) in enumerate(((None, gg), (None, gu), (gd, None))):
        part(f_ref, row * hidden, hidden, straight, turned, units_out, row)

    @pl.when(n == 0)
    def _():
        model_out[0:4, :] = side_ref[0:4, :] * (1.0 / inner_total) + TINY
        model_out[4:5, :] = side_ref[6:7, :] * (1.0 / hidden_total) + TINY
        rows_out[...] = side_ref[4:6, :] * (1.0 / hidden_total) + TINY
        g1_out[...] = (sums_ref[0:1, :] * scale).reshape(g1_out.shape)
        g2_out[...] = (sums_ref[1:2, :] * scale).reshape(g2_out.shape)
        place = lax.axis_index("mp")
        per = width // LANES
        rel = jnp.concatenate([sums_ref[2 + h // per : 3 + h // per, h % per * LANES : (h % per + 1) * LANES] for h in range(heads)], axis=0)
        own_heads = rel_out.shape[0]
        mine = jnp.zeros((8, LANES), f32)
        for m in range(heads // own_heads):
            block = jnp.concatenate([rel[m * own_heads : (m + 1) * own_heads], jnp.zeros((8 - own_heads, LANES), f32)], axis=0)
            mine = jnp.where(place == m, block, mine)
        rel_out[...] = mine[:own_heads, :kinds] * scale


def emit(tokens, middle, gn, layer, gain, full_a, full_f, side, sums, heads, own_heads, kinds, scale, count):
    own, width = tokens.shape
    inner, hidden = full_a.shape[0] // 4, full_f.shape[0] // 3
    steps = width // LANES
    pieces = max(n for n in range(1, steps + 1) if own % n == 0 and own // n % 16 == 0)
    rows = pl.BlockSpec((own // pieces, width), lambda n: (jnp.minimum(n, pieces - 1), 0))
    whole = lambda *s: pl.BlockSpec(s, lambda n: (0,) * len(s))
    down = lambda r: pl.BlockSpec((LANES, r), lambda n: (n, 0))
    across = lambda r: pl.BlockSpec((r, LANES), lambda n: (0, n))
    O = lambda *s: jax.ShapeDtypeStruct(s, jnp.float32)
    totals = (float(inner * count), float(hidden * count), width)
    return pl.pallas_call(
        functools.partial(emit_kernel, heads, kinds, scale, totals),
        grid=(steps,),
        in_specs=[rows, rows, rows, rows, whole(width), across(4 * inner), across(3 * hidden),
                  whole(8, width), whole(8, width)],
        out_specs=[rows, rows, across(inner), across(inner), across(inner), across(inner), down(hidden), down(hidden), across(hidden),
                   whole(own_heads, kinds), whole(width), whole(width), whole(5, width), whole(4, inner), whole(3, hidden), whole(2, width)],
        out_shape=[
            jax.ShapeDtypeStruct((own, width), jnp.bfloat16), jax.ShapeDtypeStruct((own, width), jnp.bfloat16),
            O(inner, width), O(inner, width), O(inner, width), O(inner, width), O(width, hidden), O(width, hidden), O(hidden, width),
            O(own_heads, kinds), O(width), O(width), O(5, width), O(4, inner), O(3, hidden), O(2, width),
        ],
        compiler_params=pltpu.CompilerParams(vmem_limit_bytes=60 * 2**20),
        name="emit",
    )(tokens, middle, gn, layer, gain, full_a, full_f, side, sums)


def on_device(tokens, cotangent, lengths, buckets, w_query, w_key, w_value, w_out, w_gate, w_up, w_down, rel_table, gain_one, gain_two):
    bf = jnp.bfloat16
    count = lax.axis_size("mp")
    batches = lax.axis_size("batch")
    own, width = tokens.shape
    total = own * count
    inner = w_query.shape[1]
    hidden_rows = w_gate.shape[1]
    limit = (buckets.shape[0] + 1) // 2
    radius = min(count - 1, -(-(limit - 1) // own))
    kinds = rel_table.shape[0]
    heads = rel_table.shape[1] * count

    kind_row = bucket_kinds(buckets, TQ)[None]
    rows_one, wa_all, wf_all, q, k, kt, v, vt, strips = gather(
        tokens, gain_one, (w_query.T, w_key.T, w_value.T, w_out), (w_gate, w_up, w_down), rel_table.T, kind_row, count, radius, heads
    )
    was = wa_all.reshape(4, count * inner, width)
    wfs = wf_all.reshape(3, count * hidden_rows, width)
    context, lse = attend(lengths, strips, q, k, vt, limit, TQ, TK, HP_F)

    layer_out, grad_middle, grad_context, raw_out, gain_two_part, keep, fx, fy = ffn(
        tokens, cotangent, context, gain_two, was, wfs, count
    )
    got_fx = lax.ppermute(fx, "batch", [(n, n ^ 2) for n in range(batches)])
    got_fy = lax.ppermute(fy, "batch", [(n, n ^ 4) for n in range(batches)])
    grad_q, grad_k, grad_v, grad_strips = attend_back(
        lengths, strips, q, k, kt, v, context, grad_context, lse, limit, TQ, TK, HP_B
    )
    scale = (total * batches) ** -0.5
    one_group = batches == GROUP
    full_a, full_f, grad_norm_one, side, sums = finish(
        gain_one, gain_two_part, kind_row, grad_q, grad_k, grad_v, rows_one, was,
        raw_out.reshape(count, 2, inner // 2, width), keep, got_fx, got_fy, grad_strips, count, radius, kinds, scale
    )
    full_a = full_a.reshape(4 * inner, width)
    full_f = full_f.reshape(3 * hidden_rows, width)
    if not one_group:
        full_a, full_f, sums = [one / GROUP for one in lax.psum((full_a.astype(jnp.float32), full_f.astype(jnp.float32), sums), "batch")]
        squares = [jnp.sum((one * scale) ** 2, axis=0) for one in (*jnp.split(full_a, 4), *jnp.split(full_f, 3))]
        side = lax.psum(jnp.stack(squares + [squares[0]]), "mp")
    outs = emit(
        tokens, grad_middle, grad_norm_one, layer_out, gain_one, full_a, full_f, side, sums,
        heads, rel_table.shape[1], kinds, scale, count
    )
    return (*outs[:2], *[one.T for one in outs[2:5]], *outs[5:9], outs[9].T, *outs[10:])


TQ = 512
TK = 256
HP_F = 4
HP_B = 2


def solution(mesh):
    in_specs = (
        P(("batch", "mp"), None),
        P(("batch", "mp"), None),
        P("batch", None),
        P(),
        P(None, "mp"),
        P(None, "mp"),
        P(None, "mp"),
        P("mp", None),
        P(None, "mp"),
        P(None, "mp"),
        P("mp", None),
        P(None, "mp"),
        P(),
        P(),
    )
    out_specs = (
        P(("batch", "mp"), None),
        P(("batch", "mp"), None),
        P(None, "mp"),
        P(None, "mp"),
        P(None, "mp"),
        P("mp", None),
        P(None, "mp"),
        P(None, "mp"),
        P("mp", None),
        P(None, "mp"),
        P(),
        P(),
        P(),
        P(None, "mp"),
        P(None, "mp"),
        P(),
    )
    return jax.shard_map(
        on_device, mesh=mesh, in_specs=in_specs, out_specs=out_specs, check_vma=False
    )
```

```python
import functools

import jax
import jax.numpy as jnp
from jax import lax
from jax.experimental import pallas as pl
from jax.experimental.pallas import tpu as pltpu
from jax.sharding import PartitionSpec as P

TINY = 1e-30

NEG = -1e9
LANES = 128

def strip_sizes(limit, tq):
    reach = -(-limit // LANES)
    nq = tq // LANES
    off = LANES * (reach + nq)
    return reach, off, off + LANES * reach + tq

def bucket_kinds(buckets, tq):
    limit = (buckets.shape[0] + 1) // 2
    _, off, width = strip_sizes(limit, tq)
    shift = off - (limit - 1)
    return jnp.pad(lax.rev(buckets, (0,)), (shift, width - shift - buckets.shape[0]))


def ends_list(lens_ref, rows_dev, count):
    total = jnp.int32(0)
    ends = []
    for r in range(rows_dev):
        for c in range(count):
            total = total + lens_ref[r, c]
            ends.append(total)
    return ends

def segment_of(place, ends, count):
    seg = jnp.zeros_like(place)
    pad = jnp.zeros_like(place)
    for n, end in enumerate(ends):
        past = place >= end
        seg = seg + jnp.where(past, 1, 0)
        if n % count == count - 2:
            pad = pad + jnp.where(past, 1, 0)
        if n % count == count - 1:
            pad = pad - jnp.where(past, 1, 0)
    return jnp.where(pad > 0, place + 4096, seg)

def key_range(first, last, ends, count):
    low = jnp.int32(0)
    high = ends[-1]
    for n, end in enumerate(ends):
        is_pad_next = n % count == count - 2
        low = jnp.where(first >= end, jnp.maximum(low, first if is_pad_next else end), low)
    for n in range(len(ends) - 1, -1, -1):
        is_pad = n % count == count - 1
        high = jnp.where(last < ends[n], (last + 1) if is_pad else ends[n], high)
    return low, high


def for_chunks(body, q_at, tq, tk, half, ends, count, w_high):
    ranges = [key_range(q_at + at, q_at + at + half - 1, ends, count) for at in range(0, tq, half)]
    start, high = ranges[0][0], ranges[-1][1]
    alike = start == key_range(q_at + tq - 1, q_at + tq - 1, ends, count)[0]
    low = (start // LANES) * LANES
    steps = (high - low + tk - 1) // tk
    low = jnp.minimum(low, w_high - steps * tk)

    def step(c, _):
        ks = pl.multiple_of(low + c * tk, LANES)
        if len(ranges) == 1:
            body(ks, 0, tq)
            return 0
        one, two = [(ks < stop) & (ks + tk > begin) for begin, stop in ranges]
        plain = alike & (ks >= start) & (ks + tk <= high)
        pl.when(plain)(lambda: body(ks, 0, tq, False))
        pl.when(one & two & jnp.logical_not(plain))(lambda: body(ks, 0, tq))
        pl.when(one & jnp.logical_not(two))(lambda: body(ks, 0, half))
        pl.when(two & jnp.logical_not(one))(lambda: body(ks, half, half))
        return 0

    lax.fori_loop(0, steps, step, 0)


def window(own, total, limit):
    first = lax.axis_index("mp") * own
    radius = -(-(limit - 1) // own)
    return jnp.maximum(first - radius * own, 0), jnp.minimum(first + (radius + 1) * own, total)

def fill_segments(kseg, ends, count, total):
    def one(n, _):
        at = pl.multiple_of(n * 256, 256)
        place = at + lax.broadcasted_iota(jnp.int32, (256, LANES), 0)
        kseg[pl.ds(at, 256), :] = segment_of(place, ends, count)
        return 0
    lax.fori_loop(0, total // 256, one, 0)

def tile_lanes(x, n):
    return x if n == 1 else jnp.concatenate([x] * n, axis=1)

def lane_start(ks, q_at, g, reach, off, nq):
    d = (ks - q_at) // LANES + g
    return pl.multiple_of(off - LANES * jnp.clip(d, -reach, reach + nq - 1), LANES)

def fwd_kernel(cfg, lens_ref, strip, q_ref, k_ref, vt_ref, ctx_ref, lse_ref, kseg, top, tot, acc):
    tq, tk, limit, rows_dev, count, own, total, hp = cfg
    reach, off, width = strip_sizes(limit, tq)
    ends = ends_list(lens_ref, rows_dev, count)
    @pl.when(pl.program_id(0) == 0)
    def _():
        fill_segments(kseg, ends, count, total)
    first = lax.axis_index("mp") * own
    w_high = window(own, total, limit)[1]
    lane = lax.broadcasted_iota(jnp.int32, (tq, LANES), 1)
    for qt in range(own // tq):
        rows = slice(qt * tq, (qt + 1) * tq)
        q_at = first + qt * tq
        halves = []
        for h in range(hp):
            q2 = q_ref[rows, h // 2 * LANES : h // 2 * LANES + LANES]
            halves.append(jnp.where((lane < 64) == (h % 2 == 0), q2, jnp.zeros_like(q2)))
        qseg = segment_of(q_at + lax.broadcasted_iota(jnp.int32, (1, tq), 1), ends, count)
        top[...] = jnp.full(top.shape, 2 * NEG, jnp.float32)
        tot[...] = jnp.zeros_like(tot)
        acc[...] = jnp.zeros_like(acc)

        def body(ks, skip, lanes, masked=True):
            nq = lanes // LANES
            at = slice(skip, skip + lanes)
            same = tile_lanes(kseg[pl.ds(ks, tk), :], nq) == qseg[:, at] if masked else None
            starts = [lane_start(ks, q_at + skip, g, reach, off, nq) for g in range(tk // LANES)]
            raws, news, fades, lows = [], [], [], []
            for h in range(hp):
                kc = k_ref[pl.ds(ks, tk), h // 2 * LANES : h // 2 * LANES + LANES]
                raws.append(lax.dot_general(kc, halves[h][at], (((1,), (1,)), ((), ())), preferred_element_type=jnp.float32))
            for h in range(hp):
                bias = jnp.concatenate([strip[h, :, pl.ds(one, lanes)] for one in starts], axis=0)
                raws[h] = jnp.where(same, raws[h] + bias, NEG) if masked else raws[h] + bias
                old = top[h : h + 1, at]
                new = jnp.maximum(old, jnp.max(raws[h], axis=0, keepdims=True))
                top[h : h + 1, at] = new
                news.append(new)
                fades.append(jnp.exp(old - new))
            for h in range(hp):
                p = jnp.exp(raws[h] - news[h])
                tot[h : h + 1, at] = tot[h : h + 1, at] * fades[h] + jnp.sum(p, axis=0, keepdims=True)
                lows.append(p.astype(jnp.bfloat16))
            for h in range(hp):
                acc[h, :, at] = acc[h, :, at] * fades[h] + jnp.dot(
                    vt_ref[h * 64 : h * 64 + 64, pl.ds(ks, tk)], lows[h], preferred_element_type=jnp.float32
                )

        for_chunks(body, q_at, tq, tk, min(256, tq), ends, count, w_high)
        for pair in range(hp // 2):
            both = jnp.concatenate([acc[h] / tot[h : h + 1, :] for h in (2 * pair, 2 * pair + 1)], axis=0)
            ctx_ref[rows, pair * LANES : pair * LANES + LANES] = both.T.astype(jnp.bfloat16)
        for h in range(hp):
            lse_ref[h // 2, h % 2 : h % 2 + 1, rows] = top[h : h + 1, :] + jnp.log(tot[h : h + 1, :])


def attend(lengths, strips, q, k, vt, limit, tq, tk, hp):
    own, inner = q.shape
    total = k.shape[0]
    steps = inner // 64 // hp
    lanes = hp * 64
    rows_dev, count = lengths.shape
    width = strips.shape[2]
    cfg = (tq, tk, limit, rows_dev, count, own, total, hp)
    smem = pl.BlockSpec(memory_space=pltpu.SMEM)
    return pl.pallas_call(
        functools.partial(fwd_kernel, cfg),
        grid=(steps,),
        in_specs=[smem,
            pl.BlockSpec((hp, LANES, width), lambda p: (p, 0, 0)),
            pl.BlockSpec((own, lanes), lambda p: (0, p)),
            pl.BlockSpec((total, lanes), lambda p: (0, p)),
            pl.BlockSpec((lanes, total), lambda p: (p, 0))],
        out_specs=[pl.BlockSpec((own, lanes), lambda p: (0, p)),
                   pl.BlockSpec((hp // 2, 2, own), lambda p: (p, 0, 0))],
        out_shape=[jax.ShapeDtypeStruct((own, inner), jnp.bfloat16), jax.ShapeDtypeStruct((inner // LANES, 2, own), jnp.float32)],
        scratch_shapes=[pltpu.VMEM((total, LANES), jnp.int32), pltpu.VMEM((hp, tq), jnp.float32), pltpu.VMEM((hp, tq), jnp.float32),
                        pltpu.VMEM((hp, 64, tq), jnp.float32)],
        compiler_params=pltpu.CompilerParams(vmem_limit_bytes=56 * 2**20),
        name="attend",
    )(lengths, strips, q, k, vt)


def bwd_kernel(cfg, lens_ref, strip, q_ref, k_ref, kt_ref, v_ref, ctx_ref, do_ref, lse_ref,
               dq_ref, dk_ref, dv_ref, dstrip, kseg, dk_acc, dv_acc, dq_acc):
    tq, tk, limit, rows_dev, count, own, total, hp = cfg
    reach, off, width = strip_sizes(limit, tq)
    nq = tq // LANES
    ends = ends_list(lens_ref, rows_dev, count)
    @pl.when(pl.program_id(0) == 0)
    def _():
        fill_segments(kseg, ends, count, total)
    dstrip[...] = jnp.zeros_like(dstrip)
    dk_acc[...] = jnp.zeros_like(dk_acc)
    dv_acc[...] = jnp.zeros_like(dv_acc)
    first = lax.axis_index("mp") * own
    w_high = window(own, total, limit)[1]
    lane = lax.broadcasted_iota(jnp.int32, (tq, LANES), 1)
    for qt in range(own // tq):
        rows = slice(qt * tq, (qt + 1) * tq)
        q_at = first + qt * tq
        q_half, do_half, delta, lse = [], [], [], []
        for pair in range(hp // 2):
            lanes = slice(pair * LANES, pair * LANES + LANES)
            q2 = q_ref[rows, lanes]
            do2 = do_ref[rows, lanes]
            prod = (do2.astype(jnp.float32) * ctx_ref[rows, lanes].astype(jnp.float32)).T
            for hh in range(2):
                keep = (lane < 64) == (hh == 0)
                q_half.append(jnp.where(keep, q2, jnp.zeros_like(q2)))
                do_half.append(jnp.where(keep, do2, jnp.zeros_like(do2)))
                delta.append(jnp.sum(prod[hh * 64 : hh * 64 + 64], axis=0, keepdims=True))
                lse.append(lse_ref[pair, hh : hh + 1, rows])
        qseg = segment_of(q_at + lax.broadcasted_iota(jnp.int32, (1, tq), 1), ends, count)
        dq_acc[...] = jnp.zeros_like(dq_acc)

        def body(ks, skip, span, masked=True):
            nq = span // LANES
            at = slice(skip, skip + span)
            same = tile_lanes(kseg[pl.ds(ks, tk), :], nq) == qseg[:, at] if masked else None
            starts = [lane_start(ks, q_at + skip, g, reach, off, nq) for g in range(tk // LANES)]
            for pair in range(hp // 2):
                lanes = slice(pair * LANES, pair * LANES + LANES)
                kc = k_ref[pl.ds(ks, tk), lanes]
                vc = v_ref[pl.ds(ks, tk), lanes]
                dk_part = dv_part = None
                for h in (2 * pair, 2 * pair + 1):
                    s = lax.dot_general(kc, q_half[h][at], (((1,), (1,)), ((), ())), preferred_element_type=jnp.float32)
                    bias = jnp.concatenate([strip[h, :, pl.ds(one, span)] for one in starts], axis=0)
                    s = s + (bias - lse[h][:, at])
                    p = jnp.exp(jnp.where(same, s, NEG) if masked else s)
                    dp = lax.dot_general(vc, do_half[h][at], (((1,), (1,)), ((), ())), preferred_element_type=jnp.float32)
                    ds = p * (dp - delta[h][:, at])
                    for g, one in enumerate(starts):
                        dstrip[h, :, pl.ds(one, span)] += ds[g * LANES : (g + 1) * LANES, :]
                    pb = p.astype(jnp.bfloat16)
                    dsb = ds.astype(jnp.bfloat16)
                    dv_one = jnp.dot(pb, do_half[h][at], preferred_element_type=jnp.float32)
                    dk_one = jnp.dot(dsb, q_half[h][at], preferred_element_type=jnp.float32)
                    dv_part = dv_one if dv_part is None else dv_part + dv_one
                    dk_part = dk_one if dk_part is None else dk_part + dk_one
                    dq_acc[h, :, at] += jnp.dot(kt_ref[h * 64 : h * 64 + 64, pl.ds(ks, tk)], dsb, preferred_element_type=jnp.float32)
                dv_acc[pl.ds(ks, tk), lanes] += dv_part
                dk_acc[pl.ds(ks, tk), lanes] += dk_part

        for_chunks(body, q_at, tq, tk, min(256, tq), ends, count, w_high)
        for pair in range(hp // 2):
            dq_ref[rows, pair * LANES : pair * LANES + LANES] = jnp.concatenate([dq_acc[2 * pair], dq_acc[2 * pair + 1]], axis=0).T.astype(jnp.bfloat16)
    dk_ref[...] = dk_acc[...].astype(jnp.bfloat16)
    dv_ref[...] = dv_acc[...].astype(jnp.bfloat16)


def attend_back(lengths, strips, q, k, kt, v, ctx, do, lse, limit, tq, tk, hp):
    own, inner = q.shape
    total = k.shape[0]
    steps = inner // 64 // hp
    lanes = hp * 64
    rows_dev, count = lengths.shape
    width = strips.shape[2]
    cfg = (tq, tk, limit, rows_dev, count, own, total, hp)
    smem = pl.BlockSpec(memory_space=pltpu.SMEM)
    tall = pl.BlockSpec((total, lanes), lambda p: (0, p))
    short = pl.BlockSpec((own, lanes), lambda p: (0, p))
    band = pl.BlockSpec((hp, LANES, width), lambda p: (p, 0, 0))
    return pl.pallas_call(
        functools.partial(bwd_kernel, cfg),
        grid=(steps,),
        in_specs=[smem, band,
            short, tall, pl.BlockSpec((lanes, total), lambda p: (p, 0)), tall, short, short,
            pl.BlockSpec((hp // 2, 2, own), lambda p: (p, 0, 0))],
        out_specs=[short, tall, tall, band],
        out_shape=[jax.ShapeDtypeStruct((own, inner), jnp.bfloat16), jax.ShapeDtypeStruct((total, inner), jnp.bfloat16),
                   jax.ShapeDtypeStruct((total, inner), jnp.bfloat16), jax.ShapeDtypeStruct(strips.shape, jnp.float32)],
        scratch_shapes=[pltpu.VMEM((total, LANES), jnp.int32),
                        pltpu.VMEM((total, lanes), jnp.float32), pltpu.VMEM((total, lanes), jnp.float32),
                        pltpu.VMEM((hp, 64, tq), jnp.float32)],
        compiler_params=pltpu.CompilerParams(vmem_limit_bytes=60 * 2**20),
        name="attend_back",
    )(lengths, strips, q, k, kt, v, ctx, do, lse)


MESH = pl.DeviceIdType.MESH
GROUP = 8


def flip(index, bit):
    return index + bit * (1 - 2 * ((index // bit) % 2))


class Links:
    def __init__(self, send_sems, recv_sems, batch, place):
        self.send_sems, self.recv_sems = send_sems, recv_sems
        self.batch, self.place = batch, place
        self.slots = {}
        self.sent = []

    def slot(self, key):
        return self.slots.setdefault(key, len(self.slots))

    def copy(self, key, src, dst, target):
        n = self.slot(key)
        return pltpu.make_async_remote_copy(
            src_ref=src, dst_ref=dst, send_sem=self.send_sems.at[n], recv_sem=self.recv_sems.at[n],
            device_id=target, device_id_type=MESH)

    def send(self, key, src, dst, target, when=None):
        def go():
            self.copy(key, src, dst, target).start()
        self.sent.append((key, src, dst, target, when))
        if when is None:
            go()
        else:
            pl.when(when)(go)

    def take(self, key, dst, when=None, then=None):
        def go():
            self.copy(key, dst, dst, (self.batch, self.place)).wait_recv()
            if then is not None:
                then()
        if when is None:
            go()
        else:
            pl.when(when)(go)

    def drain(self):
        for key, src, dst, target, when in self.sent:
            def go():
                self.copy(key, src, dst, target).wait_send()
            if when is None:
                go()
            else:
                pl.when(when)(go)


def greet(batch, place, count):
    bar = pltpu.get_barrier_semaphore()
    for bit in (1, 2, 4):
        pl.semaphore_signal(bar, inc=1, device_id=(flip(batch, bit), place), device_id_type=MESH)
    for way in range(1 - count, count):
        if way != 0:
            @pl.when((place + way >= 0) & (place + way < count))
            def _():
                pl.semaphore_signal(bar, inc=1, device_id=(batch, place + way), device_id_type=MESH)
    pl.semaphore_wait(bar, 3 + count - 1)


def both(a, b):
    return a if b is None else (b if a is None else a & b)


class PlaneGather:
    def __init__(self, links, key, view, ref, sub, when=None):
        self.l, self.key, self.view, self.ref, self.sub, self.when = links, key, view, ref, sub, when

    def put(self, path, sub, half, bit):
        region = self.view(self.ref, sub, half)
        self.l.send((self.key, path), region, region, (flip(self.l.batch, bit), self.l.place), self.when)

    def start(self):
        self.put("x", self.sub, None, 2)
        self.put("y", self.sub, None, 4)
        self.put("c", self.sub, None, 1)

    def middle(self):
        sub = self.sub
        self.l.take((self.key, "x"), self.view(self.ref, flip(sub, 2), None), self.when)
        self.put("xy", flip(sub, 2), 0, 4)
        self.put("xc", flip(sub, 2), None, 1)
        self.l.take((self.key, "y"), self.view(self.ref, flip(sub, 4), None), self.when)
        self.put("yx", flip(sub, 4), 1, 2)
        self.put("yc", flip(sub, 4), None, 1)

    def far(self):
        sub = self.sub
        diagonal = flip(flip(sub, 2), 4)
        self.l.take((self.key, "xy"), self.view(self.ref, diagonal, 0), self.when)
        self.put("0c", diagonal, 0, 1)
        self.l.take((self.key, "yx"), self.view(self.ref, diagonal, 1), self.when)
        self.put("1c", diagonal, 1, 1)

    def end(self):
        sub = flip(self.sub, 1)
        diagonal = flip(flip(sub, 2), 4)
        self.l.take((self.key, "c"), self.view(self.ref, sub, None), self.when)
        self.l.take((self.key, "xc"), self.view(self.ref, flip(sub, 2), None), self.when)
        self.l.take((self.key, "yc"), self.view(self.ref, flip(sub, 4), None), self.when)
        self.l.take((self.key, "0c"), self.view(self.ref, diagonal, 0), self.when)
        self.l.take((self.key, "1c"), self.view(self.ref, diagonal, 1), self.when)


def half_rows(half, rows):
    return pl.ds(0, rows) if half is None else pl.ds(half * (rows // 2), rows // 2)


PIECES = 4
ORDER = (
    "X0", "T", "S0-2", "a123", "X1", "f1", "S2-5", "ma123", "X2", "f2", "S5-8", "ra123", "mf1", "X3", "f3",
    "x1", "za123", "P0", "mf2", "P1+", "rf1", "mf3", "P1-", "rf23", "S8-12", "x2", "P2",
)
EPS = 1e-06


def unit_norm(values):
    return lax.rsqrt(jnp.mean(values * values, axis=1, keepdims=True) + EPS)


def dot_nt(a, b):
    return lax.dot_general(a, b, (((1,), (1,)), ((), ())), preferred_element_type=jnp.float32)


def dot_nn(a, b):
    return jnp.dot(a, b, preferred_element_type=jnp.float32)


def gather_kernel(count, radius, tok_ref, gain_ref, wq_ref, wk_ref, wv_ref, wo_ref, wg_ref, wu_ref, wd_ref, rel_ref, kinds_ref,
                  xs_out, was_out, wfs_ref, q_out, k_out, kt_out, v_out, vt_out, strips_out,
                  xs, was, q_v, k_v, kt_v, v_v, vt_v, wf, rel_all, table, strip_v, send_sems, recv_sems, local_sems):
    batch, place = lax.axis_index("batch"), lax.axis_index("mp")
    sub = batch % GROUP
    links = Links(send_sems, recv_sems, batch, place)
    own, width = tok_ref.shape
    rows_a = was.shape[3]
    rows_f = wf.shape[2]
    step = own // PIECES
    local = []

    def copy_local(src, dst):
        one = pltpu.make_async_copy(src, dst, local_sems.at[len(local)])
        local.append(one)
        return one

    own_a = [copy_local(ref, was.at[n, place]) for n, ref in enumerate((wq_ref, wk_ref, wv_ref, wo_ref))]
    own_d = copy_local(wd_ref, wf.at[2])
    for one in own_a + [own_d]:
        one.start()
    gain = gain_ref[...].reshape(1, width)
    for p in range(PIECES):
        rows = pl.ds(p * step, step)
        values = tok_ref[rows, :].astype(jnp.float32)
        xs[place, rows] = (values * unit_norm(values) * gain).astype(xs.dtype)
    for n, ref in enumerate((wg_ref, wu_ref)):
        turn = ref[...].T
        for g in range(GROUP):
            wf[n, g] = turn[g * rows_f : (g + 1) * rows_f]
    for one in own_a + [own_d]:
        one.wait()
    copy_local(wf, wfs_ref.at[:, place]).start()
    greet(batch, place, count)

    def view_a(mm):
        return lambda ref, s, half: ref.at[s // 2, mm, s % 2, half_rows(half, rows_a)]

    def view_f(mm):
        return lambda ref, s, half: ref.at[:, mm, s, half_rows(half, rows_f)]

    def inside(n):
        return (n >= 0) & (n < count)

    for way in (1, -1):
        ok = inside(place + way)
        target = (batch, place + way)
        links.send(("a", way, 1), view_a(place)(was, sub, None), view_a(place)(was, sub, None), target, ok)
        links.send(("f", way, 1), wf.at[:, sub], view_f(place)(wfs_ref, sub, None), target, ok)
    rel_all[place, 0 : rel_ref.shape[0], :] = rel_ref[...]
    for d in range(1, count):
        for way in (1, -1):
            links.send(("r", way, d), rel_all.at[place], rel_all.at[place], (batch, place + way * d), inside(place + way * d))
    def x_send(p):
        rows = pl.ds(p * step, step)
        for way in (1, -1):
            links.send(("x", way, 1, p), xs.at[place, rows], xs.at[place, rows], (batch, place + way), inside(place + way))

    for n in range(count):
        @pl.when((n - place > radius) | (place - n > radius))
        def _():
            def blank(p, _):
                xs[n, pl.ds(p * step, step)] = jnp.zeros((step, width), xs.dtype)
                return 0
            lax.fori_loop(0, PIECES, blank, 0)
            for ref in (k_v, v_v):
                ref[pl.ds(n * own, own)] = jnp.zeros((own, ref.shape[1]), ref.dtype)
            for ref in (kt_v, vt_v):
                ref[:, pl.ds(n * own, own)] = jnp.zeros((ref.shape[0], own), ref.dtype)

    gathers = {}

    def weights_arrive(kind, dist):
        for way in (1, -1):
            source = place - way * dist
            ok = inside(source)
            view, ref = (view_a(source), was) if kind == "a" else (view_f(source), wfs_ref)
            region = view(ref, sub, None)
            links.take((kind, way, dist), region, ok)
            if dist < count - 1:
                links.send((kind, way, dist + 1), region, region, (batch, place + way), ok & inside(place + way))
            gather = PlaneGather(links, ("g", kind, way, dist), view, ref, sub, ok)
            gather.start()
            gathers[kind, way, dist] = gather

    def x_arrive(dist, p):
        for way in (1, -1):
            source = place - way * dist
            ok = inside(source)
            region = xs.at[source, pl.ds(p * step, step)]
            links.take(("x", way, dist, p), region, ok)
            if dist < radius:
                links.send(("x", way, dist + 1, p), region, region, (batch, place + way), ok & inside(place + way))

    def stage(name, kind, dist):
        for way in (1, -1):
            getattr(gathers[kind, way, dist], name)()

    heads = table.shape[0]
    span = table.shape[1]
    kinds = rel_ref.shape[1]

    def make_table():
        for d in range(1, count):
            for way in (1, -1):
                links.take(("r", way, d), rel_all.at[place - way * d], inside(place - way * d))
        per = heads // count
        joined = jnp.concatenate([rel_all[n, 0:per, :] for n in range(count)], axis=0)
        for at in range(0, span, 512):
            lanes = pl.ds(at, min(512, span - at))
            kind = kinds_ref[:, lanes]
            total = jnp.zeros((heads, kind.shape[1]), jnp.float32)
            for b in range(NB_MAX):
                if b < kinds:
                    total = total + jnp.where(kind == b, joined[:, b : b + 1], 0.0)
            table[:, lanes] = total

    strip_copies = []

    def make_strip(h):
        slot = h % 2
        if h >= 2:
            strip_copies[h - 2].wait()
        row = table[h : h + 1, :]
        strip_v[slot] = pltpu.roll(jnp.broadcast_to(row, (LANES, span)), 0, 1, stride=1, stride_axis=0)
        one = pltpu.make_async_copy(strip_v.at[slot], strips_out.at[h], local_sems.at[8 + slot])
        one.start()
        strip_copies.append(one)

    inner = was.shape[1] * was.shape[2] * rows_a

    def weight_tile(kind, n):
        return was[kind, n].reshape(2 * rows_a, width)

    def project(block, when, first=0, size=None):
        size = own if size is None else size

        def go():
            x = xs[block, first : first + size]
            at_block = block * own + first
            def one(n, _):
                at = pl.multiple_of(n * 2 * rows_a, 64)
                kt_v[pl.ds(at, 2 * rows_a), pl.ds(pl.multiple_of(at_block, LANES), size)] = dot_nt(weight_tile(1, n), x).astype(kt_v.dtype)
                vt_v[pl.ds(at, 2 * rows_a), pl.ds(pl.multiple_of(at_block, LANES), size)] = dot_nt(weight_tile(2, n), x).astype(vt_v.dtype)
                return 0
            lax.fori_loop(0, count, one, 0)
            rows = pl.ds(pl.multiple_of(at_block, LANES), size)
            tile = 256
            for at in range(0, inner, tile):
                wk = was[1].reshape(inner, width)[at : at + tile]
                wv = was[2].reshape(inner, width)[at : at + tile]
                k_v[rows, at : at + tile] = dot_nt(x, wk).astype(k_v.dtype)
                v_v[rows, at : at + tile] = dot_nt(x, wv).astype(v_v.dtype)
        if when is None:
            go()
        else:
            pl.when(when)(go)

    def project_q():
        x = xs[place]
        tile = 256
        for at in range(0, inner, tile):
            wq = was[0].reshape(inner, width)[at : at + tile]
            q_v[:, at : at + tile] = dot_nt(x, wq).astype(q_v.dtype)

    saves = []

    def save_block(block, when):
        rows = pl.ds(pl.multiple_of(block * own, LANES), own)
        for src, dst in ((k_v, k_out), (v_v, v_out)):
            saves.append((pltpu.make_async_copy(src.at[rows], dst.at[rows], local_sems.at[10 + len(saves)]), when))
        for src, dst in ((kt_v, kt_out), (vt_v, vt_out)):
            saves.append((pltpu.make_async_copy(src.at[:, rows], dst.at[:, rows], local_sems.at[10 + len(saves)]), when))
        for one, ok in saves[-4:]:
            one.start() if ok is None else pl.when(ok)(one.start)

    dists = range(1, count)

    def run(order):
        for op in order:
            name, arg = op[0], op[1:]
            if name == "T":
                make_table()
            elif name == "S":
                for h in range(*[int(one) for one in arg.split("-")]):
                    make_strip(h)
            elif name in "af":
                for d in arg:
                    if int(d) in dists:
                        weights_arrive(name, int(d))
            elif name in "mrz":
                for d in arg[1:]:
                    if int(d) in dists:
                        stage({"m": "middle", "r": "far", "z": "end"}[name], arg[0], int(d))
            elif name == "X":
                for p in arg:
                    x_send(int(p))
            elif name == "x":
                for p in arg[1:] or "0123":
                    if int(arg[0]) <= radius:
                        x_arrive(int(arg[0]), int(p))
            elif name == "P":
                d = int(arg[0])
                if d == 0:
                    project_q()
                    copy_local(q_v, q_out).start()
                    project(place, None)
                    save_block(place, None)
                elif d <= radius:
                    ways = (1, -1) if arg[1:] not in ("+", "-") else ((1,) if arg[1] == "+" else (-1,))
                    for way in ways:
                        ok = inside(place + way * d)
                        if arg[1:] in ("0", "1"):
                            project(place + way * d, ok, int(arg[1]) * (own // 2), own // 2)
                        else:
                            project(place + way * d, ok)
                        if arg[1:] != "0":
                            save_block(place + way * d, ok)

    run(ORDER)
    copy_local(was, was_out).start()
    copy_local(xs, xs_out).start()
    for n in range(count):
        save_block(n, (n - place > radius) | (place - n > radius))
    for d in dists:
        stage("end", "f", d)
    links.drain()
    for one in local[5:] + strip_copies[-2:]:
        one.wait()
    for one, ok in saves:
        one.wait() if ok is None else pl.when(ok)(one.wait)


NB_MAX = 128


def gather(tokens, gain, w_heads, w_hidden, rel, kinds, count, radius, heads):
    own, width = tokens.shape
    bf = jnp.bfloat16
    total = own * count
    half_a = w_heads[0].shape[0] // 2
    part = w_hidden[2].shape[0] // GROUP
    inner = count * 2 * half_a
    span = kinds.shape[1]
    vm = pl.BlockSpec(memory_space=pltpu.VMEM)
    hb = pl.BlockSpec(memory_space=pl.ANY)
    shapes = [
        ((count, own, width), bf),
        ((4, count, 2, half_a, width), bf),
        ((3, count, GROUP, part, width), bf),
        ((own, inner), bf), ((total, inner), bf), ((inner, total), bf), ((total, inner), bf), ((inner, total), bf),
        ((heads, LANES, span), jnp.float32),
    ]
    return pl.pallas_call(
        functools.partial(gather_kernel, count, radius),
        in_specs=[vm, vm] + [hb] * 4 + [vm, vm, hb, vm, vm],
        out_specs=[hb] * len(shapes),
        out_shape=[jax.ShapeDtypeStruct(*one) for one in shapes],
        scratch_shapes=[pltpu.VMEM(*shapes[n]) for n in (0, 1, 3, 4, 5, 6, 7)] + [
            pltpu.VMEM((3, GROUP, part, width), bf),
            pltpu.VMEM((count, 8, rel.shape[1]), jnp.float32),
            pltpu.VMEM((heads, span), jnp.float32),
            pltpu.VMEM((2, LANES, span), jnp.float32),
            pltpu.SemaphoreType.DMA((170,)),
            pltpu.SemaphoreType.DMA((170,)),
            pltpu.SemaphoreType.DMA((64,)),
        ],
        compiler_params=pltpu.CompilerParams(collective_id=1, has_side_effects=True, vmem_limit_bytes=60 * 2**20),
        name="gather",
    )(tokens, gain, *[one.reshape(2, half_a, width) for one in w_heads], *w_hidden[:2], w_hidden[2].reshape(GROUP, part, width), rel, kinds)


def ffn_kernel(count, tok_ref, cot_ref, ctx_ref, gain_ref, was_ref, wfs_ref,
               out_ref, middle_ref, do_ref, raw_out_ref, gain_out, keep_out, fx_out, fy_out,
               wo, wf, normed, middle, act, raw, got, send_sems, recv_sems, local_sems):
    batch, place = lax.axis_index("batch"), lax.axis_index("mp")
    sub = batch % GROUP
    core, xx, yy = sub % 2, (sub // 2) % 2, sub // 4
    links = Links(send_sems, recv_sems, batch, place)
    sibling = (flip(batch, 1), place)
    own, width = tok_ref.shape
    gain_two = gain_ref[...].reshape(1, width)
    hidden = wf.shape[1]
    per = hidden // count
    part = per // GROUP
    half = part // 2
    bf = jnp.bfloat16
    loads = [pltpu.make_async_copy(was_ref.at[3], wo, local_sems.at[0])]
    for n in range(count):
        rows = pl.ds(n * per, per)
        loads += [pltpu.make_async_copy(wfs_ref.at[t, rows], wf.at[t, rows], local_sems.at[1 + 3 * n + t]) for t in range(3)]
    for one in loads:
        one.start()
    bar = pltpu.get_barrier_semaphore()
    pl.semaphore_signal(bar, inc=1, device_id=sibling, device_id_type=MESH)
    loads[0].wait()
    tile = 256
    for at in range(0, own, tile):
        rows = slice(at, at + tile)
        mid = tok_ref[rows, :].astype(jnp.float32) + dot_nn(ctx_ref[rows, :], wo[...])
        middle[rows, :] = mid
        normed[rows, :] = (mid * unit_norm(mid) * gain_two).astype(bf)
    pl.semaphore_wait(bar, 1)

    def products(j):
        if j * tile % per == 0:
            n = j * tile // per
            for one in loads[1 + 3 * n : 4 + 3 * n]:
                one.wait()
        rows = slice(j * tile, (j + 1) * tile)
        return dot_nt(normed[...], wf[0, rows, :]), dot_nt(normed[...], wf[1, rows, :]), dot_nt(cot_ref[...], wf[2, rows, :])

    ahead = products(0)
    tiles = hidden // tile
    for j in range(tiles):
        gate, up, back = ahead
        if j + 1 < tiles:
            ahead = products(j + 1)
        cols = slice(j * tile, (j + 1) * tile)
        squared = 0.044715 * (gate * gate)
        t = jnp.tanh(0.7978845608028654 * gate * (1.0 + squared))
        half_up = 0.5 * (1.0 + t)
        gelu = gate * half_up
        slope = half_up + 0.5 * gate * (1.0 - t * t) * (0.7978845608028654 * (1.0 + 3.0 * squared))
        act[0, :, cols] = (back * up * slope).astype(bf)
        act[1, :, cols] = (back * gelu).astype(bf)
        act[2, :, cols] = (gelu * up).astype(bf)
        n, r = j * tile // per, j * tile % per // part
        for t_id in range(3):
            value = dot_nn(act[t_id, :, cols].T, cot_ref[...] if t_id == 2 else normed[...]).astype(bf)
            for s in range(tile // part):
                raw[t_id, n, (r + s) // 2, (r + s) % 2] = value[s * part : (s + 1) * part]
        if (j + 1) * tile % per == 0:
            for t_id in range(3):
                links.send(("f1", t_id, n), raw.at[t_id, n, :, 1 - core], got.at[t_id, n], sibling)
    saves = []

    def settle(n):
        for t in range(3):
            links.take(("f1", t, n), got.at[t, n])
            for s in range(GROUP // 2):
                got[t, n, s] = got[t, n, s] + raw[t, n, s, core]
            whole = got.at[t, n].reshape(2, 2, part, width)
            for src, dst in ((whole, keep_out.at[t, n]), (whole.at[:, 1 - xx, pl.ds(0, half)], fx_out.at[t, n]),
                             (whole.at[1 - yy, :, pl.ds(half, half)], fy_out.at[t, n])):
                one = pltpu.make_async_copy(src, dst, local_sems.at[1 + 3 * count + len(saves)])
                one.start()
                saves.append(one)

    for n in range(count - 1):
        settle(n)
    for at in range(0, own, tile):
        rows = slice(at, at + tile)
        mid = middle[rows, :]
        out_ref[rows, :] = (mid + dot_nn(act[2, rows, :], wf[2])).astype(bf)
        s = unit_norm(mid)
        n2 = mid * s
        gn = dot_nn(act[0, rows, :], wf[0]) + dot_nn(act[1, rows, :], wf[1])
        e = gn * gain_two
        grad = cot_ref[rows, :].astype(jnp.float32) + s * (e - n2 * jnp.mean(e * n2, axis=1, keepdims=True))
        middle_ref[rows, :] = grad
        normed[rows, :] = grad.astype(bf)
        gain = jnp.sum(gn * n2, axis=0, keepdims=True)
        gain_out[...] = gain if at == 0 else gain_out[...] + gain
    for at in range(0, width, tile):
        cols = slice(at, at + tile)
        do_ref[:, cols] = dot_nt(normed[...], wo[cols, :]).astype(bf)
        raw_out_ref[cols, :] = dot_nn(ctx_ref[:, cols].T, normed[...]).astype(bf)
    settle(count - 1)
    links.drain()
    for one in saves:
        one.wait()


def ffn(tokens, cotangent, context, gain, was, wfs, count):
    own, width = tokens.shape
    hidden = wfs.shape[1]
    part = hidden // count // GROUP
    bf = jnp.bfloat16
    vm = pl.BlockSpec(memory_space=pltpu.VMEM)
    hb = pl.BlockSpec(memory_space=pl.ANY)
    return pl.pallas_call(
        functools.partial(ffn_kernel, count),
        in_specs=[vm, vm, vm, vm, hb, hb],
        out_specs=[vm] * 5 + [hb] * 3,
        out_shape=[
            jax.ShapeDtypeStruct((own, width), bf),
            jax.ShapeDtypeStruct((own, width), jnp.float32),
            jax.ShapeDtypeStruct(context.shape, bf),
            jax.ShapeDtypeStruct((context.shape[1], width), bf),
            jax.ShapeDtypeStruct((1, width), jnp.float32),
            jax.ShapeDtypeStruct((3, count, 2, 2, part, width), bf),
            jax.ShapeDtypeStruct((3, count, 2, part // 2, width), bf),
            jax.ShapeDtypeStruct((3, count, 2, part // 2, width), bf),
        ],
        scratch_shapes=[
            pltpu.VMEM((was.shape[1], width), bf),
            pltpu.VMEM((3, hidden, width), bf),
            pltpu.VMEM((own, width), bf),
            pltpu.VMEM((own, width), jnp.float32),
            pltpu.VMEM((3, own, hidden), bf),
            pltpu.VMEM((3, count, GROUP // 2, 2, part, width), bf),
            pltpu.VMEM((3, count, GROUP // 2, part, width), bf),
            pltpu.SemaphoreType.DMA((3 * count,)),
            pltpu.SemaphoreType.DMA((3 * count,)),
            pltpu.SemaphoreType.DMA((1 + 12 * count,)),
        ],
        compiler_params=pltpu.CompilerParams(collective_id=3, has_side_effects=True, vmem_limit_bytes=60 * 2**20),
        name="ffn",
    )(tokens, cotangent, context, gain, was, wfs)


FINISH_ORDER = (
    "H", "F", "B", "X0123", "L", "O", "R12", "l", "w0", "R0", "Q", "A", "w1", "x0123", "C", "w2", "f0123",
    "K", "S0-3", "m", "w3", "S3-6", "n", "w4", "S6-12", "b", "g", "t0", "M", "t1", "a", "G", "t2", "r", "e",
    "q", "N", "D",
)


def finish_kernel(count, radius, buckets, scale, gain_ref, tiny_ref, kinds_ref,
                  dq_ref, dk_ref, dv_ref, xs_ref, was_ref, raw_out_ref, keep_ref, fx_ref, fy_ref, strips_ref,
                  full_a, full_f, gn_out, side_ref, total_ref,
                  dq, dk, dv, xs, wq, wk, wv, ga, got_a1, got_ax, got_ay, got_ay2, got_ax2,
                  keep_f, got_fx, got_fy, got_fy2, got_fx2, from_a, from_f,
                  gx, own_acc, got_x, rows8, small, tiny, tiny_z, side_z, strip_v, send_sems, recv_sems, local_sems):
    batch, place = lax.axis_index("batch"), lax.axis_index("mp")
    sub = batch % GROUP
    core, xx, yy = sub % 2, (sub // 2) % 2, sub // 4
    links = Links(send_sems, recv_sems, batch, place)
    rows_a, rows_f = ga.shape[4], keep_f.shape[4]
    ha, hf = rows_a // 2, rows_f // 2
    own, width = gn_out.shape
    step = own // PIECES
    bf = jnp.bfloat16
    f32 = jnp.float32
    sibling, x_near, y_near = [(flip(batch, bit), place) for bit in (1, 2, 4)]

    def inside(n):
        return (n >= 0) & (n < count)

    used = [0]

    def load(src, dst, start=True):
        one = pltpu.make_async_copy(src, dst, local_sems.at[used[0]])
        used[0] += 1
        if start:
            one.start()
        return one

    load_f = [(load(keep_ref.at[t], keep_f.at[t]), load(fx_ref.at[t], got_fx.at[t]), load(fy_ref.at[t], got_fy.at[t])) for t in range(3)]
    load_w = [load(was_ref.at[1], wk), load(was_ref.at[2], wv)]
    load_d = {}

    def load_block(r):
        rows = pl.ds(pl.multiple_of((place + r) % count * own, LANES), own)
        load_d[r] = [load(dk_ref.at[rows], dk.at[rows]), load(dv_ref.at[rows], dv.at[rows])]

    far = sorted({radius % count, -radius % count})
    for r in far:
        load_block(r)
    for r in range(count):
        if r not in far:
            load_block(r)
    load_x = [load(xs_ref, xs), load(dq_ref, dq), load(was_ref.at[0], wq)]
    load_o = load(raw_out_ref, ga.at[1, 1])
    heads = strips_ref.shape[0]
    lanes_low = (strips_ref.shape[2] - strip_v.shape[2] + LANES) // 2
    load_s = {}

    def load_strip(n):
        load_s[n] = pltpu.make_async_copy(strips_ref.at[n // 2, pl.ds(n % 2 * 64, 64), pl.ds(lanes_low, strip_v.shape[2])], strip_v.at[n % 2], local_sems.at[40 + n % 2])
        load_s[n].start()

    load_strip(0)
    load_strip(1)

    def one_f(t):
        def go(n, _):
            for i in range(2):
                keep_f[t, n, i, xx, pl.ds(0, hf)] = keep_f[t, n, i, xx, pl.ds(0, hf)] + got_fx[t, n, i]
                keep_f[t, n, yy, i, pl.ds(hf, hf)] = keep_f[t, n, yy, i, pl.ds(hf, hf)] + got_fy[t, n, i]
            return 0
        lax.fori_loop(0, count, go, 0)

    def first_f():
        for t in range(3):
            for one in load_f[t]:
                one.wait()
            one_f(t)
            links.send(("fy2", t), keep_f.at[t, :, 1 - yy, xx, pl.ds(0, hf)], got_fy2.at[t], y_near)
            links.send(("fx2", t), keep_f.at[t, :, yy, 1 - xx, pl.ds(hf, hf)], got_fx2.at[t], x_near)

    rows8[...] = jnp.zeros_like(rows8)

    def block_part(block, local):
        tile = 256
        for at in range(0, own, tile):
            rows = pl.ds(pl.multiple_of(block * own + at, tile), tile)
            value = dot_nn(dk[rows, :], wk[...]) + dot_nn(dv[rows, :], wv[...])
            if local:
                value = value + dot_nn(dq[at : at + tile, :], wq[...])
                own_acc[at : at + tile, :] = value
                gain_rows(value, block, at)
            else:
                gx[block, at : at + tile] = value.astype(bf)

    def gain_rows(value, block, at):
        prod = value * xs[block, at : at + value.shape[0]].astype(f32)
        acc = prod[0:8]
        for r in range(8, value.shape[0], 8):
            acc = acc + prod[r : r + 8]
        rows8[...] = rows8[...] + acc

    def gains_part():
        for level in range(1, radius + 1):
            for way in (1, -1):
                @pl.when(inside(place + way * level))
                def _():
                    for at in range(0, own, 256):
                        gain_rows(gx[place + way * level, at : at + 256].astype(f32), place + way * level, at)

    def x_send(way, level, p):
        rows = pl.ds(p * step, step)
        links.send(("x", way, level, p), gx.at[place + way * level, rows], got_x.at[0 if way > 0 else 1, level - 1, rows],
                   (batch, place + way), inside(place + way * level))

    def x_step(level, p):
        rows = pl.ds(p * step, step)
        for side, way in ((0, 1), (1, -1)):
            dest = place + way * (level - 1)
            behind = inside(place - way)
            def add():
                got_x[side, level - 1, rows] = got_x[side, level - 1, rows] + gx[dest, rows]
            links.take(("x", way, level, p), got_x.at[side, level - 1, rows], behind & inside(dest), add)
            links.send(("x", way, level - 1, p), got_x.at[side, level - 1, rows], got_x.at[side, level - 2, rows],
                       (batch, place + way), behind & inside(dest))

    def x_first(level, p):
        rows = pl.ds(p * step, step)
        for side, way in ((0, 1), (1, -1)):
            dest = place + way * (level - 1)
            links.send(("x0", way, level - 1, p), gx.at[jnp.clip(dest, 0, count - 1), rows], got_x.at[side, level - 2, rows],
                       (batch, place + way), jnp.logical_not(inside(place - way)) & inside(dest))

    inner = wq.shape[0]

    def raw_grad(kind, left, right):
        for c in range(0, inner, 256):
            value = dot_nn(left(c).T, right()).astype(bf)
            at = c
            while at < c + 256:
                n, r = at // (2 * rows_a), at % (2 * rows_a)
                h, r = r // rows_a, r % rows_a
                size = min(rows_a - r, c + 256 - at)
                ga[kind // 2, kind % 2, n, h, r : r + size] = value[at - c : at - c + size]
                at += size
        links.send(("a1", kind), ga.at[kind // 2, kind % 2, :, 1 - core], got_a1.at[kind // 2, kind % 2], sibling)

    def last_f(t):
        links.take(("fy2", t), got_fy2.at[t])
        links.take(("fx2", t), got_fx2.at[t])
        def one(n, _):
            keep_f[t, n, yy, xx, pl.ds(0, hf)] = keep_f[t, n, yy, xx, pl.ds(0, hf)] + got_fy2[t, n]
            keep_f[t, n, yy, xx, pl.ds(hf, hf)] = keep_f[t, n, yy, xx, pl.ds(hf, hf)] + got_fx2[t, n]
            return 0
        lax.fori_loop(0, count, one, 0)

    def unit(t, n):
        return keep_f.at[t, n, yy, xx]

    def line(t, hop, rank):
        for side, way in ((0, 1), (1, -1)):
            here = place == (hop if way > 0 else count - 1 - hop)
            n = count - 1 - rank if way > 0 else rank
            if hop > 0:
                def add():
                    ref, more = unit(t, n), from_f.at[t, side, n]
                    ref[...] = ref[...] + more[...]
                links.take(("z", t, side, n, hop - 1), from_f.at[t, side, n], here, add)
            links.send(("z", t, side, n, hop), unit(t, n), from_f.at[t, side, n], (batch, place + way), here)

    def line_a():
        for d in range(count - 1, 0, -1):
            for way in (1, -1):
                dest = place + way * d
                links.send(("za", way, d), ga.at[yy, xx, jnp.clip(dest, 0, count - 1), core], from_a.at[place], (batch, dest), inside(dest))

    def view_a(ref, s, half):
        return ref.at[s // 2, s % 2, half_rows(half, rows_a)]

    def view_f(t):
        return lambda ref, s, half: ref.at[t, s, half_rows(half, rows_f)]

    gathers = {}

    def finish(t):
        for side, way in ((0, 1), (1, -1)):
            for hop in range(count - 1):
                n = hop + 1 if way > 0 else count - 2 - hop
                def add():
                    ref, more = unit(t, n), from_f.at[t, side, n]
                    ref[...] = ref[...] + more[...]
                links.take(("z", t, side, n, hop), from_f.at[t, side, n], place == n, add)
        full_f[t, sub] = keep_f[t, place, yy, xx]
        gathers[t] = PlaneGather(links, ("g", t), view_f(t), full_f, sub)
        gathers[t].start()

    def finish_a():
        from_a[place] = ga[yy, xx, place, core]
        for d in range(1, count):
            for way in (1, -1):
                links.take(("za", way, d), from_a.at[place - way * d], inside(place - way * d))
        total = from_a[0].astype(f32)
        for n in range(1, count):
            total = total + from_a[n].astype(f32)
        full_a[sub // 2, sub % 2] = total.astype(bf)
        gathers["a"] = PlaneGather(links, ("g", "a"), view_a, full_a, sub)
        gathers["a"].start()

    def a_core(kind):
        i, j = kind // 2, kind % 2
        links.take(("a1", kind), got_a1.at[i, j])
        for n in range(count):
            ga[i, j, n, core] = ga[i, j, n, core] + got_a1[i, j, n]

    def a_middle():
        links.take(("ax",), got_ax)
        links.take(("ay",), got_ay)
        for n in range(count):
            for i in range(2):
                ga[i, xx, n, core, pl.ds(0, ha)] = ga[i, xx, n, core, pl.ds(0, ha)] + got_ax[i, n]
                ga[yy, i, n, core, pl.ds(ha, ha)] = ga[yy, i, n, core, pl.ds(ha, ha)] + got_ay[i, n]
        links.send(("ay2",), ga.at[1 - yy, xx, :, core, pl.ds(0, ha)], got_ay2, y_near)
        links.send(("ax2",), ga.at[yy, 1 - xx, :, core, pl.ds(ha, ha)], got_ax2, x_near)

    def a_last():
        links.take(("ay2",), got_ay2)
        links.take(("ax2",), got_ax2)
        for n in range(count):
            ga[yy, xx, n, core, pl.ds(0, ha)] = ga[yy, xx, n, core, pl.ds(0, ha)] + got_ay2[n]
            ga[yy, xx, n, core, pl.ds(ha, ha)] = ga[yy, xx, n, core, pl.ds(ha, ha)] + got_ax2[n]

    sums = {}

    def strip_sum(h):
        span = strip_v.shape[2]
        eight = None
        for n in (2 * h, 2 * h + 1):
            load_s[n].wait()
            for g in range(8):
                shift = 8 * g + 64 * (n % 2)
                part = strip_v[n % 2, 8 * g : 8 * g + 8, :]
                part = part if shift == 0 else pltpu.roll(part, span - shift, 1)
                eight = part if eight is None else eight + part
            if n + 2 < 2 * heads:
                load_strip(n + 2)
        flat = eight[0:1, :]
        for r in range(1, 8):
            flat = flat + pltpu.roll(eight[r : r + 1, :], span - r, 1)
        sums[h] = flat

    def tiny_step(n):
        links.take(("s", n), tiny.at[2 * n + 1])
        before = small if n == 0 else tiny.at[2 * n]
        tiny[2 * n + 2] = before[...] + tiny[2 * n + 1]
        if n < 2:
            links.send(("s", n + 1), tiny.at[2 * n + 2], tiny.at[2 * n + 3], (flip(batch, 2 << n), place))
        else:
            tiny_z[place] = tiny[6]
            for d in range(1, count):
                for way in (1, -1):
                    links.send(("sz", way, d), tiny.at[6], tiny_z.at[place], (batch, place + way * d), inside(place + way * d))

    def parts(level):
        for way in (1, -1):
            @pl.when(inside(place + way * level))
            def _():
                block_part(place + way * level, False)

    def wave(n):
        for hop in range(count - 2, -1, -1):
            rank = n - 2 * hop
            if 0 <= rank < count - 1 - hop:
                for t in range(3):
                    line(t, hop, rank)

    def raw_out_part():
        load_o.wait()
        links.send(("a1", 3), ga.at[1, 1, :, 1 - core], got_a1.at[1, 1], sibling)

    def far_part():
        for one in load_w + [one for r in far for one in load_d[r]]:
            one.wait()
        for way in (1, -1):
            @pl.when(inside(place + way * radius))
            def _():
                block_part(place + way * radius, False)

    def rest_loaded():
        for one in load_x + [one for r in range(count) if r not in far for one in load_d[r]]:
            one.wait()

    def raw_part(kind):
        if kind == 0:
            raw_grad(0, lambda c: dq[:, c : c + 256], lambda: xs[place])
        else:
            side = dk if kind == 1 else dv
            raw_grad(kind, lambda c: side[:, c : c + 256], lambda: xs[...].reshape(count * own, width))

    def near_parts():
        for level in range(radius - 1, 0, -1):
            parts(level)

    def a_first():
        for kind in (3, 1, 2, 0):
            a_core(kind)
        links.send(("ax",), ga.at[:, 1 - xx, :, core, pl.ds(0, ha)], got_ax, x_near)
        links.send(("ay",), ga.at[1 - yy, :, :, core, pl.ds(ha, ha)], got_ay, y_near)

    def buckets_part():
        diag = jnp.concatenate([sums[h] for h in range(heads)], axis=0)
        small[...] = jnp.zeros_like(small)
        small[0:1, :] = jnp.sum(rows8[...], axis=0, keepdims=True) / gain_ref[...].reshape(1, width)
        small[1:2, :] = tiny_ref[...]
        kinds = kinds_ref[:, lanes_low : lanes_low + strip_v.shape[2]]
        bucket_lane = lax.broadcasted_iota(jnp.int32, (heads, LANES), 1)
        rel = jnp.zeros((heads, LANES), f32)
        for b in range(buckets):
            rel = jnp.where(bucket_lane == b, jnp.sum(jnp.where(kinds == b, diag, 0.0), axis=1, keepdims=True), rel)
        per = width // LANES
        for h in range(heads):
            small[2 + h // per : 3 + h // per, h % per * LANES : (h % per + 1) * LANES] = rel[h : h + 1, :]
        links.send(("s", 0), small, tiny.at[1], sibling)

    def gn_part():
        for p in range(PIECES):
            rows = pl.ds(p * step, step)
            for side, way in ((0, 1), (1, -1)):
                ok = inside(place - way)
                near = inside(place - 2 * way)
                if radius > 1:
                    links.take(("x", way, 1, p), got_x.at[side, 0, rows], ok & near)
                    links.take(("x0", way, 1, p), got_x.at[side, 0, rows], ok & jnp.logical_not(near))
                else:
                    links.take(("x", way, 1, p), got_x.at[side, 0, rows], ok)
                def blank():
                    got_x[side, 0, rows] = jnp.zeros((step, width), bf)
                pl.when(jnp.logical_not(ok))(blank)
            gn_out[rows, :] = own_acc[rows, :] + got_x[0, 0, rows].astype(f32) + got_x[1, 0, rows].astype(f32)

    def each(act):
        for t in range(3):
            act(t)

    def levels(act, p):
        for level in range(radius, 1, -1):
            act(level, p)

    def squares(read, blocks):
        def one(n, acc):
            value = read(n).astype(f32) * scale
            for r in range(0, value.shape[0], 8):
                acc = acc + value[r : r + 8] * value[r : r + 8]
            return acc
        return jnp.sum(lax.fori_loop(0, blocks, one, jnp.zeros((8, width), f32)), axis=0, keepdims=True)

    f_sums = []

    simple = {
        "F": first_f, "B": far_part, "O": raw_out_part, "Q": near_parts, "A": a_first, "C": lambda: block_part(place, True),
        "m": a_middle, "n": lambda: (a_last(), line_a()), "b": buckets_part, "a": finish_a, "G": gn_part,
        "l": lambda: each(last_f), "g": lambda: each(finish), "M": lambda: each(lambda t: gathers[t].middle()),
        "r": lambda: each(lambda t: gathers[t].far()), "e": lambda: each(lambda t: gathers[t].end()),
        "H": lambda: greet(batch, place, count), "L": rest_loaded, "K": gains_part, "q": lambda: each(lambda t: f_sums.append(squares(lambda n: full_f[t, n], GROUP))), "N": lambda: gathers["a"].middle(), "D": lambda: gathers["a"].far(),
    }
    for op in FINISH_ORDER:
        name, arg = op[0], op[1:]
        if name == "S":
            for h in range(*[int(one) for one in arg.split("-")]):
                if h < heads:
                    strip_sum(h)
        elif name in "XxfRwt":
            for one in arg:
                {"X": lambda p: [x_send(way, radius, p) for way in (1, -1)], "x": lambda p: levels(x_step, p), "f": lambda p: levels(x_first, p),
                 "R": raw_part, "w": wave, "t": tiny_step}[name](int(one))
        else:
            simple[name]()

    for d in range(1, count):
        for way in (1, -1):
            links.take(("sz", way, d), tiny_z.at[place - way * d], inside(place - way * d))
    summed = tiny_z[0]
    for n in range(1, count):
        summed = summed + tiny_z[n]
    total_ref[...] = summed
    gathers["a"].end()
    a_sums = [squares(lambda n: full_a[s, n], 2) for s in range(4)]
    side_z[place] = jnp.concatenate(a_sums + f_sums + [jnp.zeros((1, width), f32)], axis=0)
    for d in range(1, count):
        for way in (1, -1):
            links.send(("q", way, d), side_z.at[place], side_z.at[place], (batch, place + way * d), inside(place + way * d))
    for d in range(1, count):
        for way in (1, -1):
            links.take(("q", way, d), side_z.at[place - way * d], inside(place - way * d))
    summed = side_z[0]
    for n in range(1, count):
        summed = summed + side_z[n]
    side_ref[...] = summed
    links.drain()


def finish(gain, tiny, kinds, dq, dk, dv, xs, was, raw_out, keep, fx, fy, strips, count, radius, buckets, limit, scale):
    own = dq.shape[0]
    width = gain.shape[0]
    total, inner = dk.shape
    heads, _, span = strips.shape
    part = keep.shape[4]
    half_a = inner // count // 2
    bf = jnp.bfloat16
    vm = pl.BlockSpec(memory_space=pltpu.VMEM)
    hb = pl.BlockSpec(memory_space=pl.ANY)
    V = lambda *s: pltpu.VMEM(s + (width,), bf)
    F = lambda *s: pltpu.VMEM(s, jnp.float32)
    O = lambda *s: jax.ShapeDtypeStruct(s, jnp.float32)
    return pl.pallas_call(
        functools.partial(finish_kernel, count, radius, buckets, scale),
        in_specs=[vm] * 3 + [hb] * 10,
        out_specs=[vm] * 5,
        out_shape=[
            jax.ShapeDtypeStruct((4, 2, half_a, width), bf), jax.ShapeDtypeStruct((3, GROUP, part, width), bf),
            O(own, width), O(8, width), O(8, width),
        ],
        scratch_shapes=[
            pltpu.VMEM((own, inner), bf), pltpu.VMEM((total, inner), bf), pltpu.VMEM((total, inner), bf), V(count, own),
            V(inner), V(inner), V(inner),
            V(2, 2, count, 2, half_a), V(2, 2, count, half_a), V(2, count, half_a // 2), V(2, count, half_a // 2), V(count, half_a // 2), V(count, half_a // 2),
            V(3, count, 2, 2, part), V(3, count, 2, part // 2), V(3, count, 2, part // 2), V(3, count, part // 2), V(3, count, part // 2),
            V(count, half_a), V(3, 2, count, part),
            V(count, own), F(own, width), V(2, radius, own), F(8, width),
            F(8, width), F(7, 8, width), F(count, 8, width), F(count, 8, width), F(2, 64, 2 * limit + LANES),
            pltpu.SemaphoreType.DMA((240,)), pltpu.SemaphoreType.DMA((240,)), pltpu.SemaphoreType.DMA((48,)),
        ],
        compiler_params=pltpu.CompilerParams(collective_id=2, has_side_effects=True, vmem_limit_bytes=63 * 2**20),
        name="finish",
    )(gain, tiny, kinds, dq, dk, dv, xs, was, raw_out, keep, fx, fy, strips)


def emit_kernel(heads, kinds, scale, totals, tok_ref, mid_ref, gn_ref, layer_ref, gain_ref, a_ref, f_ref, side_ref, sums_ref,
                layer_out, tokens_out, gq, gk, gv, go, gg, gu, gd, rel_out, g1_out, g2_out, model_out, heads_out, units_out, rows_out):
    n = pl.program_id(0)
    f32 = jnp.float32
    layer_out[...] = layer_ref[...]
    x = tok_ref[...].astype(f32)
    s = unit_norm(x)
    n1 = x * s
    e = gn_ref[...] * gain_ref[...].reshape(1, gain_ref.shape[0])
    tokens_out[...] = (mid_ref[...] + s * (e - n1 * jnp.mean(e * n1, axis=1, keepdims=True))).astype(tokens_out.dtype)
    inner_total, hidden_total, width = totals
    shard = a_ref.shape[0] // 4
    hidden = f_ref.shape[0] // 3

    def part(ref, at, size, straight, turned, stat, row):
        for c in range(0, size, LANES):
            rows = min(LANES, size - c)
            value = ref[at + c : at + c + rows, :].astype(f32) * scale
            if rows < LANES:
                value = jnp.concatenate([value, jnp.zeros((LANES - rows, LANES), f32)], axis=0)
            turn = value.T
            if straight is not None:
                straight[c : c + rows, :] = value[:rows]
            if turned is not None:
                turned[:, c : c + rows] = turn[:, :rows]
            more = jnp.sum(turn * turn, axis=0, keepdims=True)[:, :rows] * (1.0 / width)
            old = stat[row : row + 1, c : c + rows]
            stat[row : row + 1, c : c + rows] = jnp.where(n == 0, TINY, old) + more

    for row, (straight, turned) in enumerate(((gq, None), (gk, None), (gv, None), (go, None))):
        part(a_ref, row * shard, shard, straight, turned, heads_out, row)
    for row, (straight, turned) in enumerate(((None, gg), (None, gu), (gd, None))):
        part(f_ref, row * hidden, hidden, straight, turned, units_out, row)

    @pl.when(n == 0)
    def _():
        model_out[0:4, :] = side_ref[0:4, :] * (1.0 / inner_total) + TINY
        model_out[4:5, :] = side_ref[6:7, :] * (1.0 / hidden_total) + TINY
        rows_out[...] = side_ref[4:6, :] * (1.0 / hidden_total) + TINY
        g1_out[...] = (sums_ref[0:1, :] * scale).reshape(g1_out.shape)
        g2_out[...] = (sums_ref[1:2, :] * scale).reshape(g2_out.shape)
        place = lax.axis_index("mp")
        per = width // LANES
        rel = jnp.concatenate([sums_ref[2 + h // per : 3 + h // per, h % per * LANES : (h % per + 1) * LANES] for h in range(heads)], axis=0)
        own_heads = rel_out.shape[0]
        mine = jnp.zeros((8, LANES), f32)
        for m in range(heads // own_heads):
            block = jnp.concatenate([rel[m * own_heads : (m + 1) * own_heads], jnp.zeros((8 - own_heads, LANES), f32)], axis=0)
            mine = jnp.where(place == m, block, mine)
        rel_out[...] = mine[:own_heads, :kinds] * scale


def emit(tokens, middle, gn, layer, gain, full_a, full_f, side, sums, heads, own_heads, kinds, scale, count):
    own, width = tokens.shape
    inner, hidden = full_a.shape[0] // 4, full_f.shape[0] // 3
    steps = width // LANES
    pieces = max(n for n in range(1, steps + 1) if own % n == 0 and own // n % 16 == 0)
    rows = pl.BlockSpec((own // pieces, width), lambda n: (jnp.minimum(n, pieces - 1), 0))
    whole = lambda *s: pl.BlockSpec(s, lambda n: (0,) * len(s))
    down = lambda r: pl.BlockSpec((LANES, r), lambda n: (n, 0))
    across = lambda r: pl.BlockSpec((r, LANES), lambda n: (0, n))
    O = lambda *s: jax.ShapeDtypeStruct(s, jnp.float32)
    totals = (float(inner * count), float(hidden * count), width)
    return pl.pallas_call(
        functools.partial(emit_kernel, heads, kinds, scale, totals),
        grid=(steps,),
        in_specs=[rows, rows, rows, rows, whole(width), across(4 * inner), across(3 * hidden),
                  whole(8, width), whole(8, width)],
        out_specs=[rows, rows, across(inner), across(inner), across(inner), across(inner), down(hidden), down(hidden), across(hidden),
                   whole(own_heads, kinds), whole(width), whole(width), whole(5, width), whole(4, inner), whole(3, hidden), whole(2, width)],
        out_shape=[
            jax.ShapeDtypeStruct((own, width), jnp.bfloat16), jax.ShapeDtypeStruct((own, width), jnp.bfloat16),
            O(inner, width), O(inner, width), O(inner, width), O(inner, width), O(width, hidden), O(width, hidden), O(hidden, width),
            O(own_heads, kinds), O(width), O(width), O(5, width), O(4, inner), O(3, hidden), O(2, width),
        ],
        compiler_params=pltpu.CompilerParams(vmem_limit_bytes=60 * 2**20),
        name="emit",
    )(tokens, middle, gn, layer, gain, full_a, full_f, side, sums)


def on_device(tokens, cotangent, lengths, buckets, w_query, w_key, w_value, w_out, w_gate, w_up, w_down, rel_table, gain_one, gain_two):
    bf = jnp.bfloat16
    count = lax.axis_size("mp")
    batches = lax.axis_size("batch")
    own, width = tokens.shape
    total = own * count
    inner = w_query.shape[1]
    hidden_rows = w_gate.shape[1]
    limit = (buckets.shape[0] + 1) // 2
    radius = min(count - 1, -(-(limit - 1) // own))
    kinds = rel_table.shape[0]
    heads = rel_table.shape[1] * count

    kind_row = bucket_kinds(buckets, TQ)[None]
    rows_one, wa_all, wf_all, q, k, kt, v, vt, strips = gather(
        tokens, gain_one, (w_query.T, w_key.T, w_value.T, w_out), (w_gate, w_up, w_down), rel_table.T, kind_row, count, radius, heads
    )
    was = wa_all.reshape(4, count * inner, width)
    wfs = wf_all.reshape(3, count * hidden_rows, width)
    context, lse = attend(lengths, strips, q, k, vt, limit, TQ, TK, HP_F)

    layer_out, grad_middle, grad_context, raw_out, gain_two_part, keep, fx, fy = ffn(
        tokens, cotangent, context, gain_two, was, wfs, count
    )
    got_fx = lax.ppermute(fx, "batch", [(n, n ^ 2) for n in range(batches)])
    got_fy = lax.ppermute(fy, "batch", [(n, n ^ 4) for n in range(batches)])
    grad_q, grad_k, grad_v, grad_strips = attend_back(
        lengths, strips, q, k, kt, v, context, grad_context, lse, limit, TQ, TK, HP_B
    )
    scale = (total * batches) ** -0.5
    one_group = batches == GROUP
    full_a, full_f, grad_norm_one, side, sums = finish(
        gain_one, gain_two_part, kind_row, grad_q, grad_k, grad_v, rows_one, was,
        raw_out.reshape(count, 2, inner // 2, width), keep, got_fx, got_fy, grad_strips, count, radius, kinds, limit, scale
    )
    full_a = full_a.reshape(4 * inner, width)
    full_f = full_f.reshape(3 * hidden_rows, width)
    if not one_group:
        full_a, full_f, sums = [one / GROUP for one in lax.psum((full_a.astype(jnp.float32), full_f.astype(jnp.float32), sums), "batch")]
        squares = [jnp.sum((one * scale) ** 2, axis=0) for one in (*jnp.split(full_a, 4), *jnp.split(full_f, 3))]
        side = lax.psum(jnp.stack(squares + [squares[0]]), "mp")
    outs = emit(
        tokens, grad_middle, grad_norm_one, layer_out, gain_one, full_a, full_f, side, sums,
        heads, rel_table.shape[1], kinds, scale, count
    )
    return (*outs[:2], *[one.T for one in outs[2:5]], *outs[5:9], outs[9].T, *outs[10:])


TQ = 512
TK = 256
HP_F = 4
HP_B = 2


def solution(mesh):
    in_specs = (
        P(("batch", "mp"), None),
        P(("batch", "mp"), None),
        P("batch", None),
        P(),
        P(None, "mp"),
        P(None, "mp"),
        P(None, "mp"),
        P("mp", None),
        P(None, "mp"),
        P(None, "mp"),
        P("mp", None),
        P(None, "mp"),
        P(),
        P(),
    )
    out_specs = (
        P(("batch", "mp"), None),
        P(("batch", "mp"), None),
        P(None, "mp"),
        P(None, "mp"),
        P(None, "mp"),
        P("mp", None),
        P(None, "mp"),
        P(None, "mp"),
        P("mp", None),
        P(None, "mp"),
        P(),
        P(),
        P(),
        P(None, "mp"),
        P(None, "mp"),
        P(),
    )
    return jax.shard_map(
        on_device, mesh=mesh, in_specs=in_specs, out_specs=out_specs, check_vma=False
    )
```
